32 devices in a mesh: seq: 8 (over z, y), item: 4 (over x, core).
Axes of the slice: x: 2, y: 2, z: 4, core: 2. Of those that a mesh axis runs over, the one named last changes fastest.
Arguments:
- byte_rows: bfloat16 [4, 8192, 768], P('item', 'seq'), may hold values from -6 to 6
- item_lengths: int32 [4, 4], P('item'), may hold values from 1 to 4096, 8192 in all within a row
- cont_mask: int32 [4, 8192], P('item', 'seq'), may hold values 0 or 1
- bound_mask: int32 [4, 8192], P('item', 'seq'), may hold values 0 or 1
- out_cot: bfloat16 [4, 8192, 768], P('item', 'seq'), may hold values from -6 to 6
- proj_cot: bfloat16 [4, 8192, 1536], P('item', 'seq'), may hold values from -6 to 6
- w_qkv: float32 [3, 768, 768], P(None, ('seq', 'item')), may hold values from -0.21875 to 0.21875
- w_out: float32 [768, 768], P(('seq', 'item')), may hold values from -0.875 to 0.875
- w_up: float32 [768, 3072], P(('seq', 'item')), may hold values from -0.21875 to 0.21875
- w_down: float32 [3072, 768], P(('seq', 'item')), may hold values from -0.109375 to 0.109375
- w_proj: float32 [768, 1536], P(('seq', 'item')), may hold values from -0.21875 to 0.21875
- gains: float32 [2, 768], P(None, ('seq', 'item')), may hold values from 0.35 to 2.2
- row_qkv: float32 [3, 768], P(None, ('seq', 'item')), may hold values from 308.0192 to 4915.2
- col_qkv: float32 [3, 768], replicated, may hold values from 308.0192 to 4915.2
- row_out: float32 [768], P(('seq', 'item')), may hold values from 62.2592 to 983.04
- col_out: float32 [768], replicated, may hold values from 62.2592 to 983.04
- row_up: float32 [768], P(('seq', 'item')), may hold values from 491.52 to 7864.32
- col_up: float32 [3072], replicated, may hold values from 491.52 to 7864.32
- row_down: float32 [3072], P(('seq', 'item')), may hold values from 1966.08 to 31457.28
- col_down: float32 [768], replicated, may hold values from 1966.08 to 31457.28
- row_proj: float32 [768], P(('seq', 'item')), may hold values from 1114.112 to 17694.72
- col_proj: float32 [1536], replicated, may hold values from 1114.112 to 17694.72
- gain_var: float32 [2, 768], P(None, ('seq', 'item')), may hold values from 3080.192 to 49152
Outputs:
- byte_out: bfloat16 [4, 8192, 768], P('item', 'seq')
- projected: bfloat16 [4, 8192, 1536], P('item', 'seq')
- grad_in: bfloat16 [4, 8192, 768], P('item', 'seq')
- grad_qkv: float32 [3, 768, 768], P(None, ('seq', 'item'))
- grad_out: float32 [768, 768], P(('seq', 'item'))
- grad_up: float32 [768, 3072], P(('seq', 'item'))
- grad_down: float32 [3072, 768], P(('seq', 'item'))
- grad_proj: float32 [768, 1536], P(('seq', 'item'))
- grad_gains: float32 [2, 768], P(None, ('seq', 'item'))
- new_qkv: float32 [3, 768, 768], P(None, ('seq', 'item'))
- new_out: float32 [768, 768], P(('seq', 'item'))
- new_up: float32 [768, 3072], P(('seq', 'item'))
- new_down: float32 [3072, 768], P(('seq', 'item'))
- new_proj: float32 [768, 1536], P(('seq', 'item'))
- new_gains: float32 [2, 768], P(None, ('seq', 'item'))
- row_qkv_new: float32 [3, 768], P(None, ('seq', 'item'))
- col_qkv_new: float32 [3, 768], replicated
- row_out_new: float32 [768], P(('seq', 'item'))
- col_out_new: float32 [768], replicated
- row_up_new: float32 [768], P(('seq', 'item'))
- col_up_new: float32 [3072], replicated
- row_down_new: float32 [3072], P(('seq', 'item'))
- col_down_new: float32 [768], replicated
- row_proj_new: float32 [768], P(('seq', 'item'))
- col_proj_new: float32 [1536], replicated
- gain_var_new: float32 [2, 768], P(None, ('seq', 'item'))
The draws below stay inside these ranges and needn't reach their ends.
Inputs may be any that keep to these rules, and one draw needn't show every extreme that they name: `item_lengths`: each row lists the lengths of the items laid end to end in one group's stream; they sum to 8192, and in each row one is exactly 4096.
All inputs are finite; a program needn't handle non-finite values. No bound on the sum of `cont_mask` or of `bound_mask` on one device may be relied on, other than what follows from the above.
Results may differ from the reference program's by a relative error of at most 0.013.
The reference program's roundings to bfloat16 on the way count: a program that leaves them out, or rounds other values in their place, can miss the bound.
Values may be sent and summed in bfloat16 or wider, within the bound.
A program may use at most 512 MiB of HBM per device.

```python
import math
import jax
import jax.numpy as jnp
import numpy as np
from jax import lax

D = 768
HEADS = 12
HDIM = 64
FF = 3072
PROJ = 1536
WINDOW = 1536
STEP = 10
GROUPS = 4
STREAM = 8192
MAXLEN = 4096
NITEMS = 4
QBLOCK = 512


def draw_gains(key, part):
    key = jax.random.fold_in(key, 7)
    lowest, rise, under, over = (0.5, 0.9, 0.7, 1.5)
    ramp = jnp.arange(D, dtype=jnp.float32) / (D - 1)
    noise = jax.random.uniform(key, (2, D), jnp.float32, under, over)
    return (lowest + rise * ramp)[None, :] * noise


def plant(array, stream_key, low, high):
    longest = array.shape.index(max(array.shape))
    spots = []
    for shift in (0, 1):
        where = [jax.random.randint(jax.random.fold_in(stream_key, axis), (), 0, length) for axis, length in enumerate(array.shape)]
        where[longest] = (where[longest] + shift) % array.shape[longest]
        spots.append(tuple(where))
    return array.at[spots[0]].set(low).at[spots[1]].set(high)


def block_scale(rng, shape, cuts, smallest, high):
    level = 1.0
    for axis_at, shards_of in cuts:
        heights = jax.random.uniform(jax.random.fold_in(jax.random.fold_in(rng, 6), axis_at), (shards_of,), jnp.float32, smallest / len(cuts), high / len(cuts))
        level = level * jnp.repeat(jnp.exp(heights), shape[axis_at] // shards_of).reshape((-1,) + (1,) * (len(shape) - 1 - axis_at))
    return level


def length_profile(count, total, most, lean):
    loads = [(1 << 20) // math.isqrt(rank ** lean) + 1 for rank in range(2, count + 1)]
    rest, holding = total - most - (count - 1), [1] * (count - 1)
    while rest > 0:
        free = [i for i in range(count - 1) if holding[i] < most]
        pool, remaining = sum([loads[i] for i in free]), rest
        for i in free:
            addition = min(most - holding[i], max(1, remaining * loads[i] // pool), rest)
            holding[i] = holding[i] + addition
            rest = rest - addition
    return np.array([most] + holding)


def ragged(stream_key, number_of, total, most, lean):
    if number_of == 2:
        one = jax.random.randint(stream_key, (), max(1, total - most), min(most, total - 1) + 1)
        return jnp.stack([one, total - one])
    sizes = jnp.asarray(length_profile(number_of, total, most, lean), jnp.int32)
    twos = (number_of - 1) // 2
    giver, receiver = sizes[1:1 + 2 * twos:2], sizes[2:2 + 2 * twos:2]
    room = jnp.minimum(giver - 1, most - receiver)
    moved = jax.random.randint(jax.random.fold_in(stream_key, 1), (twos,), 0, 1 << 20) % (room + 1)
    sizes = sizes.at[1:1 + 2 * twos:2].set(giver - moved).at[2:2 + 2 * twos:2].set(receiver + moved)
    return sizes[jax.random.permutation(jax.random.fold_in(stream_key, 2), number_of)]


def scatter_about(key, shape, scale, reach, pieces=(), held_as=jnp.bfloat16):
    entries = scale * jax.random.normal(key, shape, jnp.float32)
    if pieces:
        entries = entries * block_scale(key, shape, pieces, -0.22, 0.18)
    return jnp.clip(entries, -reach, reach).astype(held_as)


def setup_inputs(seed: int = 0) -> dict:
    arg_keys = jax.random.split(jax.random.key(seed), 24)
    byte_rows = scatter_about(arg_keys[0], (GROUPS, STREAM, D), 1.0, 6.0, ((0, 4), (1, 8)))
    item_lengths = jax.vmap(lambda own: ragged(own, NITEMS, STREAM, MAXLEN, 2))(jax.random.split(arg_keys[1], GROUPS)).reshape((GROUPS, NITEMS)).astype(jnp.int32)
    cont_mask = plant((jax.random.randint(arg_keys[2], (GROUPS, STREAM), 0, 4) < 1).astype(jnp.int32), jax.random.fold_in(arg_keys[2], 1), 0, 1)
    bound_mask = plant((jax.random.randint(arg_keys[3], (GROUPS, STREAM), 0, 3) < 1).astype(jnp.int32), jax.random.fold_in(arg_keys[3], 1), 0, 1)
    out_cot = scatter_about(arg_keys[4], (GROUPS, STREAM, D), 1.0, 6.0, ((0, 4), (1, 8)))
    proj_cot = scatter_about(arg_keys[5], (GROUPS, STREAM, PROJ), 1.0, 6.0, ((0, 4), (1, 8)))
    w_qkv = scatter_about(arg_keys[6], (3, D, D), D ** -0.5, 0.21875, ((1, 32),), jnp.float32)
    w_out = scatter_about(arg_keys[7], (D, D), (D // 16) ** -0.5, 0.875, ((0, 32),), jnp.float32)
    w_up = scatter_about(arg_keys[8], (D, FF), D ** -0.5, 0.21875, ((0, 32),), jnp.float32)
    w_down = scatter_about(arg_keys[9], (FF, D), FF ** -0.5, 0.109375, ((0, 32),), jnp.float32)
    w_proj = scatter_about(arg_keys[10], (D, PROJ), D ** -0.5, 0.21875, ((0, 32),), jnp.float32)
    gains = draw_gains(jax.random.fold_in(arg_keys[23], 71), 0)
    row_qkv = jnp.clip(jnp.exp(math.log(4915.2) - 2.7699257 * jax.random.uniform(arg_keys[12], (3, D), jnp.float32) ** block_scale(arg_keys[12], (3, D), ((1, 32),), -0.2, 0.2)), 308.0192, 4915.2)
    col_qkv = jnp.clip(jnp.exp(jax.random.uniform(arg_keys[13], (3, D), jnp.float32, math.log(308.0192), math.log(4915.2))), 308.0192, 4915.2)
    row_out = jnp.clip(jnp.exp(math.log(983.04) - 2.7593435 * jax.random.uniform(arg_keys[14], (D,), jnp.float32) ** block_scale(arg_keys[14], (D,), ((0, 32),), -0.2, 0.2)), 62.2592, 983.04)
    col_out = jnp.clip(jnp.exp(jax.random.uniform(arg_keys[15], (D,), jnp.float32, math.log(62.2592), math.log(983.04))), 62.2592, 983.04)
    row_up = jnp.clip(jnp.exp(math.log(7864.32) - 2.7725887 * jax.random.uniform(arg_keys[16], (D,), jnp.float32) ** block_scale(arg_keys[16], (D,), ((0, 32),), -0.2, 0.2)), 491.52, 7864.32)
    col_up = jnp.clip(jnp.exp(jax.random.uniform(arg_keys[17], (FF,), jnp.float32, math.log(491.52), math.log(7864.32))), 491.52, 7864.32)
    row_down = jnp.clip(jnp.exp(math.log(31457.28) - 2.7725887 * jax.random.uniform(arg_keys[18], (FF,), jnp.float32) ** block_scale(arg_keys[18], (FF,), ((0, 32),), -0.2, 0.2)), 1966.08, 31457.28)
    col_down = jnp.clip(jnp.exp(jax.random.uniform(arg_keys[19], (D,), jnp.float32, math.log(1966.08), math.log(31457.28))), 1966.08, 31457.28)
    row_proj = jnp.clip(jnp.exp(math.log(17694.72) - 2.7652086 * jax.random.uniform(arg_keys[20], (D,), jnp.float32) ** block_scale(arg_keys[20], (D,), ((0, 32),), -0.2, 0.2)), 1114.112, 17694.72)
    col_proj = jnp.clip(jnp.exp(jax.random.uniform(arg_keys[21], (PROJ,), jnp.float32, math.log(1114.112), math.log(17694.72))), 1114.112, 17694.72)
    gain_var = jnp.clip(jnp.exp(math.log(49152.0) - 2.7699256 * jax.random.uniform(arg_keys[22], (2, D), jnp.float32) ** block_scale(arg_keys[22], (2, D), ((1, 32),), -0.2, 0.2)), 3080.192, 49152.0)
    return {"byte_rows": byte_rows, "item_lengths": item_lengths, "cont_mask": cont_mask, "bound_mask": bound_mask, "out_cot": out_cot, "proj_cot": proj_cot, "w_qkv": w_qkv, "w_out": w_out, "w_up": w_up, "w_down": w_down, "w_proj": w_proj, "gains": gains, "row_qkv": row_qkv, "col_qkv": col_qkv, "row_out": row_out, "col_out": col_out, "row_up": row_up, "col_up": col_up, "row_down": row_down, "col_down": col_down, "row_proj": row_proj, "col_proj": col_proj, "gain_var": gain_var}


HIGHEST_PRECISION = lax.Precision.HIGHEST
EPSILON = 1e-06
TINY_SQUARE = 1e-30
WEIGHT_RATE = 0.02
GAIN_RATE = 0.2
SCORE_FLOOR = -1e+30

@jax.custom_vjp
def low(v):
    return lax.optimization_barrier(v.astype(jnp.bfloat16)).astype(jnp.float32)

@jax.custom_vjp
def low_back(v):
    return v

def low_keep(v):
    return (low(v), None)

def low_pass(kept, grad):
    return (grad,)

def back_keep(v):
    return (v, None)

def back_low(kept, grad):
    return (low(grad),)
low.defvjp(low_keep, low_pass)
low_back.defvjp(back_keep, back_low)

def matmul(left, right):
    return jnp.matmul(left, right, precision=HIGHEST_PRECISION)

def rms_scale(values, gain):
    return values * lax.rsqrt(lax.optimization_barrier(jnp.mean(values * values, axis=-1, keepdims=True)) + EPSILON) * gain

def gelu_tanh(values):
    return 0.5 * values * (1.0 + jnp.tanh(0.7978845608028654 * (values + 0.044715 * values * values * values)))

def item_numbers(lengths):
    positions = jnp.arange(STREAM, dtype=jnp.int32)
    item_ends = jnp.cumsum(lengths, dtype=jnp.int32)
    return lax.optimization_barrier(jnp.sum((item_ends[None, :] <= positions[:, None]).astype(jnp.int32), axis=1, dtype=jnp.int32))

def attend_group(queries, keys, values, items):
    scale = HDIM ** (-0.5)
    keys_padded = jnp.concatenate([jnp.zeros((WINDOW, HEADS, HDIM), keys.dtype), keys], axis=0)
    values_padded = jnp.concatenate([jnp.zeros((WINDOW, HEADS, HDIM), values.dtype), values], axis=0)
    items_padded = jnp.concatenate([jnp.full((WINDOW,), -1, jnp.int32), items.astype(jnp.int32)])

    def block(index):
        first = index * QBLOCK
        query_block = lax.dynamic_slice_in_dim(queries, first, QBLOCK, 0)
        key_block = lax.dynamic_slice_in_dim(keys_padded, first, QBLOCK + WINDOW, 0)
        value_block = lax.dynamic_slice_in_dim(values_padded, first, QBLOCK + WINDOW, 0)
        query_pos = first + jnp.arange(QBLOCK, dtype=jnp.int32)
        key_pos = first - WINDOW + jnp.arange(QBLOCK + WINDOW, dtype=jnp.int32)
        query_item = lax.dynamic_slice_in_dim(items.astype(jnp.int32), first, QBLOCK, 0)
        key_item = lax.dynamic_slice_in_dim(items_padded, first, QBLOCK + WINDOW, 0)
        allowed = (key_pos[None, :] <= query_pos[:, None]) & (key_pos[None, :] > query_pos[:, None] - WINDOW)
        allowed = allowed & (key_pos[None, :] >= 0) & (key_item[None, :] == query_item[:, None])
        raw = jnp.einsum('qhd,khd->hqk', query_block, key_block, precision=HIGHEST_PRECISION) * scale
        scores = jnp.where(allowed[None], low_back(raw), SCORE_FLOOR)
        row_max = lax.optimization_barrier(jnp.max(scores, axis=-1, keepdims=True))
        weights = jnp.exp(scores - row_max)
        weights = weights / lax.optimization_barrier(jnp.sum(weights, axis=-1, keepdims=True))
        return jnp.einsum('hqk,khd->qhd', low(weights), value_block, precision=HIGHEST_PRECISION)
    blocks = lax.map(jax.checkpoint(block), jnp.arange(STREAM // QBLOCK, dtype=jnp.int32))
    return blocks.reshape(STREAM, HEADS * HDIM)

def factored(weight, grad, row_state, col_state, decay):
    square = grad * grad + TINY_SQUARE
    row_new = decay * row_state + (1.0 - decay) * lax.optimization_barrier(jnp.mean(square, axis=-1))
    col_new = decay * col_state + (1.0 - decay) * lax.optimization_barrier(jnp.mean(square, axis=-2))
    row_mean = lax.optimization_barrier(jnp.mean(row_new, axis=-1, keepdims=True))
    second = row_new[..., :, None] * col_new[..., None, :] / row_mean[..., None]
    return (weight - WEIGHT_RATE * grad * lax.rsqrt(second), row_new, col_new)

def reference(byte_rows, item_lengths, cont_mask, bound_mask, out_cot, proj_cot, w_qkv, w_out, w_up, w_down, w_proj, gains, row_qkv, col_qkv, row_out, col_out, row_up, col_up, row_down, col_down, row_proj, col_proj, gain_var):
    items = jax.vmap(item_numbers)(item_lengths)
    boundary = (bound_mask * (1 - cont_mask)).astype(jnp.float32)[..., None]

    def forward(inputs, qkv_weight, out_weight, up_weight, down_weight, proj_weight, gain_values):
        weight_qkv = low(qkv_weight)
        weight_out = low(out_weight)
        weight_up = low(up_weight)
        weight_down = low(down_weight)
        weight_proj = low(proj_weight)
        gain_low = low(gain_values)
        normed = low(rms_scale(inputs, gain_low[0]))
        heads_in = []
        for slot in range(3):
            projected_slot = low_back(low(matmul(normed, weight_qkv[slot])))
            heads_in.append(projected_slot.reshape(GROUPS, STREAM, HEADS, HDIM))
        attended = jax.vmap(attend_group)(heads_in[0], heads_in[1], heads_in[2], items)
        attended = low_back(low(attended))
        resid = inputs + low_back(matmul(attended, weight_out))
        normed_two = low(rms_scale(resid, gain_low[1]))
        hidden_pre = low_back(matmul(normed_two, weight_up))
        activated = low(gelu_tanh(hidden_pre))
        output = resid + low_back(matmul(activated, weight_down))
        projected_rows = boundary * matmul(low(output), weight_proj)
        return (output, projected_rows)
    (output, projected_rows), backward = jax.vjp(forward, byte_rows.astype(jnp.float32), w_qkv, w_out, w_up, w_down, w_proj, gains)
    grads = backward((out_cot.astype(jnp.float32), proj_cot.astype(jnp.float32)))
    input_grad, grad_qkv, grad_out, grad_up, grad_down, grad_proj, grad_gains = grads
    decay = 1.0 - STEP ** (-0.8)
    new_qkv, row_qkv_new, col_qkv_new = factored(w_qkv, grad_qkv, row_qkv, col_qkv, decay)
    new_out, row_out_new, col_out_new = factored(w_out, grad_out, row_out, col_out, decay)
    new_up, row_up_new, col_up_new = factored(w_up, grad_up, row_up, col_up, decay)
    new_down, row_down_new, col_down_new = factored(w_down, grad_down, row_down, col_down, decay)
    new_proj, row_proj_new, col_proj_new = factored(w_proj, grad_proj, row_proj, col_proj, decay)
    gain_var_new = decay * gain_var + (1.0 - decay) * (grad_gains * grad_gains + TINY_SQUARE)
    new_gains = gains - GAIN_RATE * grad_gains * lax.rsqrt(gain_var_new)
    return (output.astype(jnp.bfloat16), projected_rows.astype(jnp.bfloat16), input_grad.astype(jnp.bfloat16), grad_qkv, grad_out, grad_up, grad_down, grad_proj, grad_gains, new_qkv, new_out, new_up, new_down, new_proj, new_gains, row_qkv_new, col_qkv_new, row_out_new, col_out_new, row_up_new, col_up_new, row_down_new, col_down_new, row_proj_new, col_proj_new, gain_var_new)
```

```python
import functools
import jax
import jax.numpy as jnp
from jax import lax
from jax.experimental import pallas as pl
from jax.experimental.pallas import tpu as pltpu
from jax.sharding import PartitionSpec as P

WINDOW = 1536
HEADS = 12
NEG = -1e30
QB = 256
NT = (((1,), (1,)), ((), ()))
TN = (((0,), (0,)), ((), ()))
f32 = jnp.float32
bf = jnp.bfloat16


def dot(a, b, dims=None):
    if dims is None:
        return jnp.dot(a, b, preferred_element_type=f32)
    return lax.dot_general(a, b, dims, preferred_element_type=f32)


def halves(x):
    lane = lax.broadcasted_iota(jnp.int32, x.shape, 1)
    zero = jnp.zeros_like(x)
    return jnp.where(lane < 64, x, zero), jnp.where(lane < 64, zero, x)


def fwd_kernel(lo_ref, q_ref, k_ref, v_ref, o_ref, lse_ref, bias):
    hp, qb = pl.program_id(0), pl.program_id(1)
    span = WINDOW + QB

    @pl.when(hp == 0)
    def _():
        base = qb * QB
        kpos = base + lax.broadcasted_iota(jnp.int32, (QB, span), 1)
        qpos = WINDOW + base + lax.broadcasted_iota(jnp.int32, (QB, span), 0)
        ok = (kpos >= lo_ref[...]) & (kpos <= qpos)
        bias[qb] = jnp.where(ok, 0.0, NEG)

    start = pl.multiple_of(qb * QB, QB)
    kw = k_ref[pl.ds(start, span), :]
    vw = v_ref[pl.ds(start, span), :]
    outs, lses = [], []
    for qh in halves(q_ref[...]):
        s = dot(qh, kw, NT) + bias[qb]
        m = jnp.max(s, axis=1, keepdims=True)
        p = jnp.exp(s - m)
        l = jnp.sum(p, axis=1, keepdims=True)
        outs.append(dot(p.astype(bf), vw) * (1.0 / l))
        lses.append(m + jnp.log(l))
    lane = lax.broadcasted_iota(jnp.int32, (QB, 128), 1)
    o_ref[...] = jnp.where(lane < 64, outs[0], outs[1]).astype(bf)
    both = jnp.where(lane == 0, lses[0], lses[1])
    lse_ref[0] = both.T[:8]


def attend(q, k, v, lo):
    rows, width = q.shape
    ext = k.shape[0]
    nq, nh = rows // QB, width // 128
    return pl.pallas_call(
        fwd_kernel,
        grid=(nh, nq),
        in_specs=[
            pl.BlockSpec((QB, 1), lambda h, i: (i, 0)),
            pl.BlockSpec((QB, 128), lambda h, i: (i, h)),
            pl.BlockSpec((ext, 128), lambda h, i: (0, h)),
            pl.BlockSpec((ext, 128), lambda h, i: (0, h)),
        ],
        out_specs=[
            pl.BlockSpec((QB, 128), lambda h, i: (i, h)),
            pl.BlockSpec((1, 8, QB), lambda h, i: (h, 0, i)),
        ],
        out_shape=[
            jax.ShapeDtypeStruct((rows, width), bf),
            jax.ShapeDtypeStruct((nh, 8, rows), f32),
        ],
        scratch_shapes=[pltpu.VMEM((nq, QB, WINDOW + QB), f32)],
        compiler_params=pltpu.CompilerParams(vmem_limit_bytes=50 * 2**20),
        cost_estimate=pl.CostEstimate(flops=4 * rows * 1792 * 768 * 3, bytes_accessed=14 * 2**20, transcendentals=0),
        name="attend",
    )(lo, q, k, v)


def bwd_kernel(lo_ref, q_ref, do_ref, o_ref, lse_ref, k_ref, v_ref, dq_ref, dk_ref, dv_ref, bias, dk_acc, dv_acc):
    hp, qb = pl.program_id(0), pl.program_id(1)
    span = WINDOW + QB
    tiles = span // QB
    start = pl.multiple_of(qb * QB, QB)

    @pl.when(hp == 0)
    def _():
        base = qb * QB
        kpos = base + lax.broadcasted_iota(jnp.int32, (span, QB), 0)
        qpos = WINDOW + base + lax.broadcasted_iota(jnp.int32, (span, QB), 1)
        ok = (kpos >= lo_ref[...]) & (kpos <= qpos)
        bias[qb] = jnp.where(ok, 0.0, NEG)

    @pl.when(qb == 0)
    def _():
        dk_acc[...] = jnp.zeros_like(dk_acc)
        dv_acc[...] = jnp.zeros_like(dv_acc)

    q0, q1 = halves(q_ref[...])
    do = do_ref[...]
    d0, d1 = halves(do)
    prod = do.astype(f32) * o_ref[...].astype(f32)
    row = lax.broadcasted_iota(jnp.int32, (8, 128), 0)
    lane = lax.broadcasted_iota(jnp.int32, (8, 128), 1)
    pick = jnp.where(row == lane // 64, 1.0, 0.0).astype(f32)
    delta = lax.dot_general(pick, prod, NT, precision=lax.Precision.HIGHEST, preferred_element_type=f32)
    qcat = jnp.concatenate([q0, q1], axis=0)
    dcat = jnp.concatenate([d0, d1], axis=0)
    lse = lse_ref[0]
    dq = [jnp.zeros((QB, 128), f32), jnp.zeros((QB, 128), f32)]
    for t in range(tiles):
        at = pl.ds(pl.multiple_of(start + t * QB, QB), QB)
        kt = k_ref[at, :]
        vt = v_ref[at, :]
        pbs, dss = [], []
        mask = bias[qb, t * QB : (t + 1) * QB, :]
        for h, (qh, dh) in enumerate(((q0, d0), (q1, d1))):
            s = dot(kt, qh, NT) + mask
            p = jnp.exp(s - lse[h : h + 1])
            dp = dot(vt, dh, NT)
            ds = (p * (dp - delta[h : h + 1])).astype(bf)
            pbs.append(p.astype(bf))
            dss.append(ds)
            dq[h] = dq[h] + dot(ds, kt, TN)
        dv_acc[at, :] += dot(jnp.concatenate(pbs, axis=1), dcat)
        dk_acc[at, :] += dot(jnp.concatenate(dss, axis=1), qcat)
    lane = lax.broadcasted_iota(jnp.int32, (QB, 128), 1)
    dq_ref[...] = (jnp.where(lane < 64, dq[0], dq[1]) * 0.125).astype(bf)

    @pl.when(qb == pl.num_programs(1) - 1)
    def _():
        dk_ref[...] = dk_acc[...].astype(bf)
        dv_ref[...] = dv_acc[...].astype(bf)


def attend_back(q, do, o, lse, k, v, lo_row):
    rows, width = q.shape
    ext = k.shape[0]
    nq, nh = rows // QB, width // 128
    blk = pl.BlockSpec((QB, 128), lambda h, i: (i, h))
    full = pl.BlockSpec((ext, 128), lambda h, i: (0, h))
    return pl.pallas_call(
        bwd_kernel,
        grid=(nh, nq),
        in_specs=[pl.BlockSpec((1, QB), lambda h, i: (0, i)), blk, blk, blk, pl.BlockSpec((1, 8, QB), lambda h, i: (h, 0, i)), full, full],
        out_specs=[blk, full, full],
        out_shape=[
            jax.ShapeDtypeStruct((rows, width), bf),
            jax.ShapeDtypeStruct((ext, width), bf),
            jax.ShapeDtypeStruct((ext, width), bf),
        ],
        scratch_shapes=[
            pltpu.VMEM((nq, WINDOW + QB, QB), f32),
            pltpu.VMEM((ext, 128), f32),
            pltpu.VMEM((ext, 128), f32),
        ],
        compiler_params=pltpu.CompilerParams(vmem_limit_bytes=56 * 2**20),
        cost_estimate=pl.CostEstimate(flops=10 * rows * 1792 * 768 * 3, bytes_accessed=24 * 2**20, transcendentals=0),
        name="attend_back",
    )(lo_row, q, do, o, lse, k, v)


AXES = ("seq", "item")
MESH = pl.DeviceIdType.MESH


def grid_of(seq, item):
    side = 1
    while side * side * 4 <= seq:
        side *= 2
    return (seq // side, side, item // 2)


def my_place(dims):
    seq, item = lax.axis_index("seq"), lax.axis_index("item")
    return (seq // dims[1], lax.rem(seq, dims[1]), item // 2, lax.rem(item, 2))


def device_at(dims, place):
    z, y, x, c = place
    return (z * dims[1] + y, x * 2 + c)


def moved(dims, place, dim, by):
    to = list(place)
    to[dim] = lax.rem(place[dim] + by, dims[dim])
    return tuple(to)


def sibling(place):
    return place[:3] + (1 - place[3],)


def peers(dims, place):
    found = [sibling(place)]
    for dim in range(3):
        found += [moved(dims, place, dim, by) for by in range(1, dims[dim])]
    return [device_at(dims, p) for p in found]


def meet(targets):
    barrier = pltpu.get_barrier_semaphore()
    for target in targets:
        pl.semaphore_signal(barrier, inc=1, device_id=target, device_id_type=MESH)
    pl.semaphore_wait(barrier, len(targets))


class Spread:
    def __init__(self, dims, place, own, out, rows, cols, order, send, recv):
        self.dims, self.place, self.own, self.out = dims, place, own, out
        self.rows, self.cols, self.order = rows, cols, order
        self.send, self.recv = send, recv

    def span(self, core):
        half = self.out.shape[-1] // 2
        return pl.ds(pl.multiple_of(core * half + self.cols[0], 128), self.cols[1])

    def region(self, stage, by=0, core=None):
        held = self.order[:stage]
        at = []
        for dim in range(3):
            if dim in held:
                at.append(slice(None))
            elif by and dim == self.order[stage]:
                at.append(lax.rem(self.place[dim] + self.dims[dim] - by, self.dims[dim]))
            else:
                at.append(self.place[dim])
        core = self.place[3] if core is None else core
        return self.out.at[tuple(at) + (self.rows, self.span(core))]

    def slots(self, stage):
        first = sum(self.dims[d] - 1 for d in self.order[:stage])
        return [(by, first + by - 1) for by in range(1, self.dims[self.order[stage]])]

    def hops(self, stage):
        for by, slot in self.slots(stage):
            block = self.region(stage)
            source = self.own.at[self.rows, self.span(self.place[3])] if stage == 0 else block
            target = device_at(self.dims, moved(self.dims, self.place, self.order[stage], by))
            yield pltpu.make_async_remote_copy(
                src_ref=source, dst_ref=block, send_sem=self.send.at[slot], recv_sem=self.recv.at[slot],
                device_id=target, device_id_type=MESH,
            )

    def shares(self, stage, core=None):
        count = sum(d - 1 for d in self.dims)
        for by, slot in self.slots(stage):
            block = self.region(stage, by, core)
            yield pltpu.make_async_remote_copy(
                src_ref=block, dst_ref=block, send_sem=self.send.at[count + slot], recv_sem=self.recv.at[count + slot],
                device_id=device_at(self.dims, sibling(self.place)), device_id_type=MESH,
            )

    def start(self):
        for copy in self.hops(0):
            copy.start()

    def advance(self, stage):
        for copy in self.hops(stage):
            copy.wait_recv()
        if stage < 2:
            for copy in self.hops(stage + 1):
                copy.start()
        for copy in self.shares(stage):
            copy.start()

    def finish(self):
        for stage in range(3):
            for copy in self.hops(stage):
                copy.wait_send()
            for copy in self.shares(stage):
                copy.wait_send()
            for copy in self.shares(stage, 1 - self.place[3]):
                copy.wait_recv()


def keep_own(own, out, place, sem):
    return pltpu.make_async_copy(own, out.at[place[0], place[1], place[2]], sem)


def copies_of(dims):
    return 2 * sum(d - 1 for d in dims)


def halves_of(shape):
    rows, cols = shape
    half = cols // 2
    if half % 256 == 0:
        return [((0, rows), (0, half // 2)), ((0, rows), (half // 2, half // 2))]
    cut = rows // 32 * 16
    return [((0, cut), (0, half)), ((cut, rows - cut), (0, half))]


ORDERS = ((0, 1, 2), (0, 2, 1))


def pieces_of(dims, place, owns, outs, shapes, send, recv):
    made = []
    for own, out, shape in zip(owns, outs, shapes):
        turn = len(made) // 2 % 2
        for order, (rows, cols) in zip(ORDERS[turn:] + ORDERS[:turn], halves_of(shape)):
            at = len(made)
            made.append(Spread(dims, place, own, out, pl.ds(*rows), cols, order, send.at[at], recv.at[at]))
    return made


def first_kernel(dims, shapes, window, *refs):
    n = len(shapes)
    names = iter(refs)
    take = lambda k: [next(names) for _ in range(k)]
    (x_ref,) = take(1)
    shards = take(n)
    blocks = take(n)
    outs = take(4)
    (halo_ref,) = take(1)
    wide = take(n)
    swap_send, swap_recv, send, recv, own_sem, halo_send, halo_recv = take(7)
    place = my_place(dims)
    c = place[3]
    seq, item = lax.axis_index("seq"), lax.axis_index("item")
    count = dims[0] * dims[1]
    rows = x_ref.shape[0]
    hops = -(-window // rows)
    targets = peers(dims, place)
    around = [(lax.rem(seq + d, count), item) for d in range(1, hops + 1)]
    behind = [(lax.rem(seq + count - d, count), item) for d in range(1, hops + 1)]
    meet(targets + around + behind)

    mate = device_at(dims, sibling(place))
    swaps = []
    for k in range(n):
        half = shapes[k][0] // 2
        mine = wide[k].at[pl.ds(pl.multiple_of(c * half, 8), half)]
        mine[...] = shards[k][...]
        swap = pltpu.make_async_remote_copy(
            src_ref=shards[k], dst_ref=mine, send_sem=swap_send.at[k], recv_sem=swap_recv.at[k],
            device_id=mate, device_id_type=MESH,
        )
        swap.start()
        swaps.append(swap)
    halo = []
    for d in range(1, hops + 1):
        need = min(rows, window - (d - 1) * rows)
        start = window - (d - 1) * rows - need
        halo.append(
            pltpu.make_async_remote_copy(
                src_ref=x_ref.at[pl.ds(rows - need, need)], dst_ref=halo_ref.at[pl.ds(start, need)],
                send_sem=halo_send.at[d - 1], recv_sem=halo_recv.at[d - 1],
                device_id=around[d - 1], device_id_type=MESH,
            )
        )
    pieces = pieces_of(dims, place, blocks[:4], outs, shapes[:4], send, recv)
    keeps = [keep_own(blocks[k], outs[k], place, own_sem.at[k]) for k in range(4)]
    for k in range(n):
        swaps[k].wait()
        blocks[k][...] = wide[k][...].astype(blocks[k].dtype)
        if k < 4:
            keeps[k].start()
            for piece in pieces[2 * k : 2 * k + 2]:
                piece.start()
    for d in range(1, hops + 1):
        pl.when(seq + d < count)(halo[d - 1].start)
    for keep in keeps:
        keep.wait()
    for stage in range(3):
        for piece in pieces:
            piece.advance(stage)
    for piece in pieces:
        piece.finish()
    for d in range(1, hops + 1):
        pl.when(seq + d < count)(halo[d - 1].wait_send)
        pl.when(seq >= d)(halo[d - 1].wait_recv)


def first_gather(x, shards, dims, window):
    shapes = [(2 * s.shape[0], s.shape[1]) for s in shards]
    n = len(shapes)
    outs = [jax.ShapeDtypeStruct(dims + shape, bf) for shape in shapes[:4]]
    vmem = pl.BlockSpec(memory_space=pltpu.VMEM)
    hbm = pl.BlockSpec(memory_space=pl.ANY)
    hops = -(-window // x.shape[0])
    copies = copies_of(dims)
    dma = pltpu.SemaphoreType.DMA
    got = pl.pallas_call(
        functools.partial(first_kernel, dims, shapes, window),
        in_specs=[hbm] + [vmem] * n,
        out_specs=[vmem] * n + [hbm] * 5,
        out_shape=[jax.ShapeDtypeStruct(shape, bf) for shape in shapes]
        + outs
        + [jax.ShapeDtypeStruct((window, x.shape[1]), x.dtype)],
        scratch_shapes=[pltpu.VMEM(shape, f32) for shape in shapes]
        + [dma((n,)), dma((n,)), dma((8, copies)), dma((8, copies)), dma((4,)), dma((hops,)), dma((hops,))],
        compiler_params=pltpu.CompilerParams(
            collective_id=1, has_side_effects=True, vmem_limit_bytes=32 * 2**20
        ),
        name="first_gather",
    )(x, *shards)
    return got[:n], got[n : n + 4], got[n + 4]


GATHER_STEPS = ((0, 0, -1), (0, 1, -1), (0, 2, -1), (5, 0, 0), (5, 1, 0), (5, 3, -1), (8, 0, 1), (8, 1, 1), (12, 2, 0), (13, 0, 2), (13, 1, 2), (16, 2, 1), (19, 3, 0), (23, 2, 2), (23, 3, 1), (23, 3, 2))


def attend_gather_kernel(dims, shapes, steps, lo_ref, q_ref, k_ref, v_ref, *refs):
    n = len(shapes)
    blocks, refs = refs[:n], refs[n:]
    o_ref, lse_ref, refs = refs[0], refs[1], refs[2:]
    outs, refs = refs[:n], refs[n:]
    bias, send, recv, own_sem = refs
    place = my_place(dims)
    step = pl.program_id(0) * pl.num_programs(1) + pl.program_id(1)
    pieces = pieces_of(dims, place, blocks, outs, shapes, send, recv)
    keeps = [keep_own(blocks[k], outs[k], place, own_sem.at[k]) for k in range(n)]
    for at in sorted({s for s, _, _ in steps}):

        @pl.when(step == at)
        def _():
            if at == 0:
                meet(peers(dims, place))
                for keep in keeps:
                    keep.start()
            for _, k, what in [e for e in steps if e[0] == at]:
                if what == 0:
                    keeps[k].wait()
                for piece in pieces[2 * k : 2 * k + 2]:
                    if what < 0:
                        piece.start()
                    else:
                        piece.advance(what)

    fwd_kernel(lo_ref, q_ref, k_ref, v_ref, o_ref, lse_ref, bias)

    @pl.when(step == pl.num_programs(0) * pl.num_programs(1) - 1)
    def _():
        for piece in pieces:
            piece.finish()


def attend_gather(q, k, v, lo, blocks, dims):
    rows, width = q.shape
    ext = k.shape[0]
    nq, nh = rows // QB, width // 128
    shapes = [b.shape for b in blocks]
    n = len(shapes)
    hbm = pl.BlockSpec(memory_space=pl.ANY)
    dma = pltpu.SemaphoreType.DMA
    copies = copies_of(dims)
    got = pl.pallas_call(
        functools.partial(attend_gather_kernel, dims, shapes, GATHER_STEPS),
        grid=(nh, nq),
        in_specs=[
            pl.BlockSpec((QB, 1), lambda h, i: (i, 0)),
            pl.BlockSpec((QB, 128), lambda h, i: (i, h)),
            pl.BlockSpec((ext, 128), lambda h, i: (0, h)),
            pl.BlockSpec((ext, 128), lambda h, i: (0, h)),
        ]
        + [hbm] * n,
        out_specs=[
            pl.BlockSpec((QB, 128), lambda h, i: (i, h)),
            pl.BlockSpec((1, 8, QB), lambda h, i: (h, 0, i)),
        ]
        + [hbm] * n,
        out_shape=[
            jax.ShapeDtypeStruct((rows, width), bf),
            jax.ShapeDtypeStruct((nh, 8, rows), f32),
        ]
        + [jax.ShapeDtypeStruct(dims + shape, bf) for shape in shapes],
        scratch_shapes=[
            pltpu.VMEM((nq, QB, WINDOW + QB), f32),
            dma((2 * n, copies)),
            dma((2 * n, copies)),
            dma((n,)),
        ],
        compiler_params=pltpu.CompilerParams(
            collective_id=2, has_side_effects=True, vmem_limit_bytes=50 * 2**20
        ),
        cost_estimate=pl.CostEstimate(flops=4 * rows * 1792 * 768 * 3, bytes_accessed=14 * 2**20, transcendentals=0),
        name="attend_gather",
    )(lo, q, k, v, *blocks)
    return got[0], got[1], got[2:]


EPSILON = 1e-06
TINY_SQUARE = 1e-30
WEIGHT_RATE = 0.02
GAIN_RATE = 0.2
STEP = 10


def sum_kernel(sizes, x_ref, o_ref, inbox, send_sem, recv_sem):
    place = {name: lax.axis_index(name) for name, _ in sizes}
    partners = []
    for name, size in sizes:
        bit = 1
        while bit < size:
            mine = place[name]
            low = lax.rem(mine // bit, 2)
            other = mine + bit * (1 - 2 * low)
            partners.append(tuple(other if n == name else place[n] for n in ("seq", "item")))
            bit *= 2
    barrier = pltpu.get_barrier_semaphore()
    for partner in partners:
        pl.semaphore_signal(barrier, inc=1, device_id=partner, device_id_type=MESH)
    pl.semaphore_wait(barrier, len(partners))
    o_ref[0] = x_ref[...]
    for stage, partner in enumerate(partners):
        copy = pltpu.make_async_remote_copy(
            src_ref=o_ref.at[stage],
            dst_ref=inbox.at[stage],
            send_sem=send_sem.at[stage],
            recv_sem=recv_sem.at[stage],
            device_id=partner,
            device_id_type=MESH,
        )
        copy.start()
        copy.wait()
        o_ref[stage + 1] = o_ref[stage] + inbox[stage]


def sum_all(x, sizes):
    stages = sum(size.bit_length() - 1 for _, size in sizes)
    held = pl.pallas_call(
        functools.partial(sum_kernel, sizes),
        out_shape=jax.ShapeDtypeStruct((stages + 1,) + x.shape, x.dtype),
        in_specs=[pl.BlockSpec(memory_space=pltpu.VMEM)],
        out_specs=pl.BlockSpec(memory_space=pltpu.VMEM),
        scratch_shapes=[
            pltpu.VMEM((stages,) + x.shape, x.dtype),
            pltpu.SemaphoreType.DMA((stages,)),
            pltpu.SemaphoreType.DMA((stages,)),
        ],
        compiler_params=pltpu.CompilerParams(collective_id=0, has_side_effects=True),
        name="sum_all",
    )(x)
    return held[stages]


def from_behind(block, axis, distance):
    devices = range(lax.axis_size(axis))
    route = [(i - distance, i) for i in devices if i - distance in devices]
    return lax.ppermute(block, axis, route)


def norm_rows(values, gain):
    return values * lax.rsqrt(jnp.mean(values * values, axis=-1, keepdims=True) + EPSILON) * gain


def gelu_tanh(values):
    return (
        0.5
        * values
        * (1.0 + jnp.tanh(0.7978845608028654 * (values + 0.044715 * values * values * values)))
    )


def finish_update(weight, grad, row_new, col_state, col_total, rows_all, row_mean, decay):
    col_new = decay * col_state + (1.0 - decay) * col_total / rows_all
    second = row_new[..., :, None] * col_new[..., None, :] / row_mean
    return (weight - WEIGHT_RATE * grad * lax.rsqrt(second), col_new)


def local(
    byte_rows, item_lengths, cont_mask, bound_mask, out_cot, proj_cot,
    w_qkv, w_out, w_up, w_down, w_proj, gains,
    row_qkv, col_qkv, row_out, col_out, row_up, col_up, row_down, col_down, row_proj, col_proj, gain_var,
):
    sizes = tuple((name, lax.axis_size(name)) for name in ("item", "seq"))
    count = lax.axis_size("item") * lax.axis_size("seq")
    rows_dev, width = byte_rows.shape[1:]
    ff = w_up.shape[1]
    proj = w_proj.shape[1]
    shard = width // count
    shard_ff = ff // count
    nu, npj = ff // width, proj // width
    low = bf

    dims = grid_of(lax.axis_size("seq"), lax.axis_size("item"))
    paired = shard % 8 == 0 and rows_dev % QB == 0
    inputs_low = byte_rows[0]
    if paired:
        gain_block = jnp.pad(gains.reshape(1, 2 * shard), ((0, 15), (0, 256 - 2 * shard)))
        shards = [w_qkv[0], w_qkv[1], w_qkv[2], gain_block, w_out, w_proj, w_up, w_down]
        blocks, first, halo_rows = first_gather(inputs_low, shards, dims, WINDOW)
        weight_qkv = [w.reshape(width, width) for w in first[:3]]
        gain_full = first[3].reshape(count // 2, 2, 16, 256)[:, :, 0, : 2 * shard]
        gain_full = gain_full.reshape(count, 2, shard).transpose(1, 0, 2).reshape(2, width).astype(f32)
    else:
        weight_qkv = lax.all_gather(w_qkv.astype(low), AXES, axis=1, tiled=True)
        gain_full = lax.all_gather(gains.astype(low), AXES, axis=1, tiled=True).astype(f32)
        weight_out, weight_proj, weight_up, weight_down = [
            lax.all_gather(w.astype(low), AXES, axis=0, tiled=True) for w in (w_out, w_proj, w_up, w_down)
        ]

    inputs = inputs_low.astype(f32)
    hop_total = -(-WINDOW // rows_dev)
    offset = lax.axis_index("seq") * rows_dev
    if not paired:
        halo = []
        for distance in range(hop_total, 0, -1):
            need = min(rows_dev, WINDOW - (distance - 1) * rows_dev)
            halo.append(from_behind(inputs_low[rows_dev - need :], "seq", distance))
        halo_rows = jnp.concatenate(halo, axis=0)
    before = offset - WINDOW + jnp.arange(WINDOW, dtype=jnp.int32)
    halo_rows = jnp.where(before[:, None] >= 0, halo_rows, 0)
    normed = norm_rows(inputs, gain_full[0]).astype(low)
    halo_normed = norm_rows(halo_rows.astype(f32), gain_full[0]).astype(low)
    ext_normed = jnp.concatenate([halo_normed, normed], axis=0)
    queries = dot(normed, weight_qkv[0]).astype(low) * jnp.asarray(0.125, low)
    ext_keys = dot(ext_normed, weight_qkv[1]).astype(low)
    ext_values = dot(ext_normed, weight_qkv[2]).astype(low)

    ends = jnp.cumsum(item_lengths[0], dtype=jnp.int32)
    pos = offset + jnp.arange(rows_dev, dtype=jnp.int32)
    begin = jnp.max(jnp.where(ends[None, :] <= pos[:, None], ends[None, :], 0), axis=1)
    lo = jnp.maximum(begin, pos - WINDOW + 1) - offset + WINDOW

    if paired:
        attended, lse, rest = attend_gather(queries, ext_keys, ext_values, lo[:, None], blocks[4:], dims)
        weight_out, weight_proj, weight_up, weight_down = [
            w.reshape(-1, w.shape[-1]) for w in rest
        ]
    else:
        attended, lse = attend(queries, ext_keys, ext_values, lo[:, None])

    resid = inputs + dot(attended, weight_out)
    normed_two = norm_rows(resid, gain_full[1]).astype(low)
    hidden_pre = dot(normed_two, weight_up)
    activated = gelu_tanh(hidden_pre).astype(low)
    output = resid + dot(activated, weight_down)
    output_low = output.astype(low)
    boundary = (bound_mask[0] * (1 - cont_mask[0])).astype(f32)[:, None]
    projected = (boundary * dot(output_low, weight_proj)).astype(low)
    proj_grad = (boundary * proj_cot[0].astype(f32)).astype(low)
    grad_proj = dot(output_low, proj_grad, TN)
    output_grad = out_cot[0].astype(f32) + dot(proj_grad, weight_proj, NT)
    output_grad_low = output_grad.astype(low)
    grad_down = dot(activated, output_grad_low, TN)
    act_grad = dot(output_grad_low, weight_down, NT)
    _, gelu_back = jax.vjp(gelu_tanh, hidden_pre)
    pre_grad = gelu_back(act_grad)[0].astype(low)
    grad_up = dot(normed_two, pre_grad, TN)
    normed_two_grad = dot(pre_grad, weight_up, NT)
    _, norm_two_back = jax.vjp(norm_rows, resid, gain_full[1])
    resid_norm_grad, gain_two_grad = norm_two_back(normed_two_grad)
    resid_grad = output_grad + resid_norm_grad
    resid_grad_low = resid_grad.astype(low)
    grad_out = dot(attended, resid_grad_low, TN)
    attended_grad = dot(resid_grad_low, weight_out, NT).astype(low)

    at_up, at_proj = shard, shard * (1 + nu)
    at_down = shard * (1 + nu + npj)

    def tall(grad, n):
        return grad.astype(low).reshape(count, shard, n, width).transpose(0, 2, 1, 3).reshape(count, n * shard, width)

    parts = jnp.concatenate(
        [tall(grad_out, 1), tall(grad_up, nu), tall(grad_proj, npj), grad_down.astype(low).reshape(count, shard_ff, width)],
        axis=1,
    )
    summed = lax.psum_scatter(parts, AXES, scatter_dimension=0, tiled=False).astype(f32)

    def broad(at, n):
        return summed[at : at + n * shard].reshape(n, shard, width).transpose(1, 0, 2).reshape(shard, n * width)

    sum_out, sum_up, sum_proj, sum_down = broad(0, 1), broad(at_up, nu), broad(at_proj, npj), summed[at_down:]

    query_grad, ext_key_grad, ext_value_grad = attend_back(
        queries, attended_grad, attended, lse, ext_keys, ext_values, lo[None, :]
    )
    ext_back = dot(ext_key_grad, weight_qkv[1], NT) + dot(ext_value_grad, weight_qkv[2], NT)
    returned = []
    for distance in range(1, hop_total + 1):
        need = min(rows_dev, WINDOW - (distance - 1) * rows_dev)
        upper = WINDOW - (distance - 1) * rows_dev
        returned.append(from_behind(ext_back[upper - need : upper].astype(low), "seq", -distance))
    grad_qkv = jnp.stack(
        [dot(normed, query_grad, TN), dot(ext_normed, ext_key_grad, TN), dot(ext_normed, ext_value_grad, TN)]
    )
    parts = grad_qkv.astype(low).reshape(3, count, shard, width).transpose(1, 0, 2, 3).reshape(count, 3 * shard, width)
    sum_qkv = lax.psum_scatter(parts, AXES, scatter_dimension=0, tiled=False).astype(f32).reshape(3, shard, width)

    normed_grad = ext_back[WINDOW:] + dot(query_grad, weight_qkv[0], NT)
    for block in returned:
        need = block.shape[0]
        normed_grad = normed_grad.at[rows_dev - need :].add(block.astype(f32))
    _, norm_one_back = jax.vjp(norm_rows, inputs, gain_full[0])
    input_norm_grad, gain_one_grad = norm_one_back(normed_grad)
    input_grad = (resid_grad + input_norm_grad).astype(low)

    decay = 1.0 - STEP ** (-0.8)
    square_qkv = sum_qkv * sum_qkv + TINY_SQUARE
    square_out = sum_out * sum_out + TINY_SQUARE
    square_up = sum_up * sum_up + TINY_SQUARE
    square_down = sum_down * sum_down + TINY_SQUARE
    square_proj = sum_proj * sum_proj + TINY_SQUARE
    row_qkv_new = decay * row_qkv + (1.0 - decay) * jnp.mean(square_qkv, axis=-1)
    row_out_new = decay * row_out + (1.0 - decay) * jnp.mean(square_out, axis=-1)
    row_up_new = decay * row_up + (1.0 - decay) * jnp.mean(square_up, axis=-1)
    row_down_new = decay * row_down + (1.0 - decay) * jnp.mean(square_down, axis=-1)
    row_proj_new = decay * row_proj + (1.0 - decay) * jnp.mean(square_proj, axis=-1)
    row_sums = jnp.concatenate(
        [
            jnp.sum(row_qkv_new, axis=1),
            jnp.sum(row_out_new)[None],
            jnp.sum(row_up_new)[None],
            jnp.sum(row_down_new)[None],
            jnp.sum(row_proj_new)[None],
        ]
    )
    stats = [
        jnp.sum(square_qkv, axis=1).reshape(-1),
        jnp.sum(square_out, axis=0),
        jnp.sum(square_up, axis=0),
        jnp.sum(square_down, axis=0),
        jnp.sum(square_proj, axis=0),
        gain_one_grad,
        gain_two_grad,
        row_sums,
    ]
    flat = jnp.concatenate(stats)
    used = flat.shape[0]
    padded = -(-used // 1024) * 1024
    flat = jnp.pad(flat, (0, padded - used)).reshape(padded // 128, 128)
    flat = sum_all(flat, sizes).reshape(-1)
    totals, at = [], 0
    for part in stats:
        totals.append(flat[at : at + part.shape[0]])
        at += part.shape[0]
    col_qkv_total, col_out_total, col_up_total, col_down_total, col_proj_total, gain_one, gain_two, row_totals = totals
    col_qkv_total = col_qkv_total.reshape(3, width)
    mine = lax.axis_index("seq") * lax.axis_size("item") + lax.axis_index("item")
    sum_gains = lax.dynamic_slice_in_dim(jnp.stack([gain_one, gain_two]), mine * shard, shard, 1)
    row_counts = jnp.array([width, width, width, width, width, ff, width], f32)
    row_means = row_totals / row_counts
    new_qkv, col_qkv_new = finish_update(
        w_qkv, sum_qkv, row_qkv_new, col_qkv, col_qkv_total, width, row_means[:3][:, None, None], decay
    )
    new_out, col_out_new = finish_update(w_out, sum_out, row_out_new, col_out, col_out_total, width, row_means[3], decay)
    new_up, col_up_new = finish_update(w_up, sum_up, row_up_new, col_up, col_up_total, width, row_means[4], decay)
    new_down, col_down_new = finish_update(
        w_down, sum_down, row_down_new, col_down, col_down_total, ff, row_means[5], decay
    )
    new_proj, col_proj_new = finish_update(
        w_proj, sum_proj, row_proj_new, col_proj, col_proj_total, width, row_means[6], decay
    )
    gain_var_new = decay * gain_var + (1.0 - decay) * (sum_gains * sum_gains + TINY_SQUARE)
    new_gains = gains - GAIN_RATE * sum_gains * lax.rsqrt(gain_var_new)
    return (
        output_low[None], projected[None], input_grad[None],
        sum_qkv, sum_out, sum_up, sum_down, sum_proj, sum_gains,
        new_qkv, new_out, new_up, new_down, new_proj, new_gains,
        row_qkv_new, col_qkv_new, row_out_new, col_out_new, row_up_new, col_up_new,
        row_down_new, col_down_new, row_proj_new, col_proj_new, gain_var_new,
    )


def solution(mesh):
    in_specs = (
        P("item", "seq", None),
        P("item", None),
        P("item", "seq"),
        P("item", "seq"),
        P("item", "seq", None),
        P("item", "seq", None),
        P(None, ("seq", "item"), None),
        P(("seq", "item"), None),
        P(("seq", "item"), None),
        P(("seq", "item"), None),
        P(("seq", "item"), None),
        P(None, ("seq", "item")),
        P(None, ("seq", "item")),
        P(),
        P(("seq", "item")),
        P(),
        P(("seq", "item")),
        P(),
        P(("seq", "item")),
        P(),
        P(("seq", "item")),
        P(),
        P(None, ("seq", "item")),
    )
    out_specs = (
        P("item", "seq", None),
        P("item", "seq", None),
        P("item", "seq", None),
        P(None, ("seq", "item"), None),
        P(("seq", "item"), None),
        P(("seq", "item"), None),
        P(("seq", "item"), None),
        P(("seq", "item"), None),
        P(None, ("seq", "item")),
        P(None, ("seq", "item"), None),
        P(("seq", "item"), None),
        P(("seq", "item"), None),
        P(("seq", "item"), None),
        P(("seq", "item"), None),
        P(None, ("seq", "item")),
        P(None, ("seq", "item")),
        P(),
        P(("seq", "item")),
        P(),
        P(("seq", "item")),
        P(),
        P(("seq", "item")),
        P(),
        P(("seq", "item")),
        P(),
        P(None, ("seq", "item")),
    )
    return jax.shard_map(local, mesh=mesh, in_specs=in_specs, out_specs=out_specs, check_vma=False)
```

```python
import functools
import jax
import jax.numpy as jnp
from jax import lax
from jax.experimental import pallas as pl
from jax.experimental.pallas import tpu as pltpu
from jax.sharding import PartitionSpec as P

WINDOW = 1536
HEADS = 12
NEG = -1e30
QB = 256
NT = (((1,), (1,)), ((), ()))
TN = (((0,), (0,)), ((), ()))
f32 = jnp.float32
bf = jnp.bfloat16


def dot(a, b, dims=None):
    if dims is None:
        return jnp.dot(a, b, preferred_element_type=f32)
    return lax.dot_general(a, b, dims, preferred_element_type=f32)


def halves(x):
    lane = lax.broadcasted_iota(jnp.int32, x.shape, 1)
    zero = jnp.zeros_like(x)
    return jnp.where(lane < 64, x, zero), jnp.where(lane < 64, zero, x)


def fwd_kernel(lo_ref, q_ref, k_ref, v_ref, o_ref, lse_ref, bias):
    hp, qb = pl.program_id(0), pl.program_id(1)
    span = WINDOW + QB

    @pl.when(hp == 0)
    def _():
        base = qb * QB
        kpos = base + lax.broadcasted_iota(jnp.int32, (QB, span), 1)
        qpos = WINDOW + base + lax.broadcasted_iota(jnp.int32, (QB, span), 0)
        ok = (kpos >= lo_ref[...]) & (kpos <= qpos)
        bias[qb] = jnp.where(ok, 0.0, NEG)

    start = pl.multiple_of(qb * QB, QB)
    kw = k_ref[pl.ds(start, span), :]
    vw = v_ref[pl.ds(start, span), :]
    outs, lses = [], []
    for qh in halves(q_ref[...]):
        s = dot(qh, kw, NT) + bias[qb]
        m = jnp.max(s, axis=1, keepdims=True)
        p = jnp.exp(s - m)
        l = jnp.sum(p, axis=1, keepdims=True)
        outs.append(dot(p.astype(bf), vw) * (1.0 / l))
        lses.append(m + jnp.log(l))
    lane = lax.broadcasted_iota(jnp.int32, (QB, 128), 1)
    o_ref[...] = jnp.where(lane < 64, outs[0], outs[1]).astype(bf)
    both = jnp.where(lane == 0, lses[0], lses[1])
    lse_ref[0] = both.T[:8]


def attend(q, k, v, lo):
    rows, width = q.shape
    ext = k.shape[0]
    nq, nh = rows // QB, width // 128
    return pl.pallas_call(
        fwd_kernel,
        grid=(nh, nq),
        in_specs=[
            pl.BlockSpec((QB, 1), lambda h, i: (i, 0)),
            pl.BlockSpec((QB, 128), lambda h, i: (i, h)),
            pl.BlockSpec((ext, 128), lambda h, i: (0, h)),
            pl.BlockSpec((ext, 128), lambda h, i: (0, h)),
        ],
        out_specs=[
            pl.BlockSpec((QB, 128), lambda h, i: (i, h)),
            pl.BlockSpec((1, 8, QB), lambda h, i: (h, 0, i)),
        ],
        out_shape=[
            jax.ShapeDtypeStruct((rows, width), bf),
            jax.ShapeDtypeStruct((nh, 8, rows), f32),
        ],
        scratch_shapes=[pltpu.VMEM((nq, QB, WINDOW + QB), f32)],
        compiler_params=pltpu.CompilerParams(vmem_limit_bytes=50 * 2**20),
        cost_estimate=pl.CostEstimate(flops=4 * rows * 1792 * 768 * 3, bytes_accessed=14 * 2**20, transcendentals=0),
        name="attend",
    )(lo, q, k, v)


AXES = ("seq", "item")
MESH = pl.DeviceIdType.MESH


def grid_of(seq, item):
    side = 1
    while side * side * 4 <= seq:
        side *= 2
    return (seq // side, side, item // 2)


def my_place(dims):
    seq, item = lax.axis_index("seq"), lax.axis_index("item")
    return (seq // dims[1], lax.rem(seq, dims[1]), item // 2, lax.rem(item, 2))


def device_at(dims, place):
    z, y, x, c = place
    return (z * dims[1] + y, x * 2 + c)


def moved(dims, place, dim, by):
    to = list(place)
    to[dim] = lax.rem(place[dim] + by, dims[dim])
    return tuple(to)


def sibling(place):
    return place[:3] + (1 - place[3],)


def peers(dims, place):
    found = [sibling(place)]
    for dim in range(3):
        found += [moved(dims, place, dim, by) for by in range(1, dims[dim])]
    return [device_at(dims, p) for p in found]


def meet(targets):
    barrier = pltpu.get_barrier_semaphore()
    for target in targets:
        pl.semaphore_signal(barrier, inc=1, device_id=target, device_id_type=MESH)
    pl.semaphore_wait(barrier, len(targets))


class Spread:
    def __init__(self, dims, place, own, out, rows, cols, order, send, recv):
        self.dims, self.place, self.own, self.out = dims, place, own, out
        self.rows, self.cols, self.order = rows, cols, order
        self.send, self.recv = send, recv

    def span(self, core):
        half = self.out.shape[-1] // 2
        return pl.ds(pl.multiple_of(core * half + self.cols[0], 128), self.cols[1])

    def region(self, stage, by=0, core=None):
        held = self.order[:stage]
        at = []
        for dim in range(3):
            if dim in held:
                at.append(slice(None))
            elif by and dim == self.order[stage]:
                at.append(lax.rem(self.place[dim] + self.dims[dim] - by, self.dims[dim]))
            else:
                at.append(self.place[dim])
        core = self.place[3] if core is None else core
        return self.out.at[tuple(at) + (self.rows, self.span(core))]

    def slots(self, stage):
        first = sum(self.dims[d] - 1 for d in self.order[:stage])
        return [(by, first + by - 1) for by in range(1, self.dims[self.order[stage]])]

    def hops(self, stage):
        for by, slot in self.slots(stage):
            block = self.region(stage)
            source = self.own.at[self.rows, self.span(self.place[3])] if stage == 0 else block
            target = device_at(self.dims, moved(self.dims, self.place, self.order[stage], by))
            yield pltpu.make_async_remote_copy(
                src_ref=source, dst_ref=block, send_sem=self.send.at[slot], recv_sem=self.recv.at[slot],
                device_id=target, device_id_type=MESH,
            )

    def shares(self, stage, core=None):
        count = sum(d - 1 for d in self.dims)
        for by, slot in self.slots(stage):
            block = self.region(stage, by, core)
            yield pltpu.make_async_remote_copy(
                src_ref=block, dst_ref=block, send_sem=self.send.at[count + slot], recv_sem=self.recv.at[count + slot],
                device_id=device_at(self.dims, sibling(self.place)), device_id_type=MESH,
            )

    def start(self):
        for copy in self.hops(0):
            copy.start()

    def advance(self, stage):
        for copy in self.hops(stage):
            copy.wait_recv()
        if stage < 2:
            for copy in self.hops(stage + 1):
                copy.start()
        for copy in self.shares(stage):
            copy.start()

    def finish(self):
        for stage in range(3):
            for copy in self.hops(stage):
                copy.wait_send()
            for copy in self.shares(stage):
                copy.wait_send()
            for copy in self.shares(stage, 1 - self.place[3]):
                copy.wait_recv()


def keep_own(own, out, place, sem):
    return pltpu.make_async_copy(own, out.at[place[0], place[1], place[2]], sem)


def copies_of(dims):
    return 2 * sum(d - 1 for d in dims)


def halves_of(shape):
    rows, cols = shape
    half = cols // 2
    if half % 256 == 0:
        return [((0, rows), (0, half // 2)), ((0, rows), (half // 2, half // 2))]
    cut = rows // 32 * 16
    return [((0, cut), (0, half)), ((cut, rows - cut), (0, half))]


ORDERS = ((0, 1, 2), (0, 2, 1))


def pieces_of(dims, place, owns, outs, shapes, send, recv):
    made = []
    for own, out, shape in zip(owns, outs, shapes):
        turn = len(made) // 2 % 2
        for order, (rows, cols) in zip(ORDERS[turn:] + ORDERS[:turn], halves_of(shape)):
            at = len(made)
            made.append(Spread(dims, place, own, out, pl.ds(*rows), cols, order, send.at[at], recv.at[at]))
    return made


def first_kernel(dims, shapes, window, *refs):
    n = len(shapes)
    names = iter(refs)
    take = lambda k: [next(names) for _ in range(k)]
    (x_ref,) = take(1)
    shards = take(n)
    blocks = take(n)
    outs = take(4)
    (halo_ref,) = take(1)
    wide = take(n)
    swap_send, swap_recv, send, recv, own_sem, halo_send, halo_recv = take(7)
    place = my_place(dims)
    c = place[3]
    seq, item = lax.axis_index("seq"), lax.axis_index("item")
    count = dims[0] * dims[1]
    rows = x_ref.shape[0]
    hops = -(-window // rows)
    targets = peers(dims, place)
    around = [(lax.rem(seq + d, count), item) for d in range(1, hops + 1)]
    behind = [(lax.rem(seq + count - d, count), item) for d in range(1, hops + 1)]
    meet(targets + around + behind)

    mate = device_at(dims, sibling(place))
    swaps = []
    for k in range(n):
        half = shapes[k][0] // 2
        mine = wide[k].at[pl.ds(pl.multiple_of(c * half, 8), half)]
        mine[...] = shards[k][...]
        swap = pltpu.make_async_remote_copy(
            src_ref=shards[k], dst_ref=mine, send_sem=swap_send.at[k], recv_sem=swap_recv.at[k],
            device_id=mate, device_id_type=MESH,
        )
        swap.start()
        swaps.append(swap)
    halo = []
    for d in range(1, hops + 1):
        need = min(rows, window - (d - 1) * rows)
        start = window - (d - 1) * rows - need
        halo.append(
            pltpu.make_async_remote_copy(
                src_ref=x_ref.at[pl.ds(rows - need, need)], dst_ref=halo_ref.at[pl.ds(start, need)],
                send_sem=halo_send.at[d - 1], recv_sem=halo_recv.at[d - 1],
                device_id=around[d - 1], device_id_type=MESH,
            )
        )
    pieces = pieces_of(dims, place, blocks[:4], outs, shapes[:4], send, recv)
    keeps = [keep_own(blocks[k], outs[k], place, own_sem.at[k]) for k in range(4)]
    for k in range(n):
        swaps[k].wait()
        blocks[k][...] = wide[k][...].astype(blocks[k].dtype)
        if k < 4:
            keeps[k].start()
            for piece in pieces[2 * k : 2 * k + 2]:
                piece.start()
    for d in range(1, hops + 1):
        pl.when(seq + d < count)(halo[d - 1].start)
    for keep in keeps:
        keep.wait()
    for stage in range(3):
        for piece in pieces:
            piece.advance(stage)
    for piece in pieces:
        piece.finish()
    for d in range(1, hops + 1):
        pl.when(seq + d < count)(halo[d - 1].wait_send)
        pl.when(seq >= d)(halo[d - 1].wait_recv)


def first_gather(x, shards, dims, window):
    shapes = [(2 * s.shape[0], s.shape[1]) for s in shards]
    n = len(shapes)
    outs = [jax.ShapeDtypeStruct(dims + shape, bf) for shape in shapes[:4]]
    vmem = pl.BlockSpec(memory_space=pltpu.VMEM)
    hbm = pl.BlockSpec(memory_space=pl.ANY)
    hops = -(-window // x.shape[0])
    copies = copies_of(dims)
    dma = pltpu.SemaphoreType.DMA
    got = pl.pallas_call(
        functools.partial(first_kernel, dims, shapes, window),
        in_specs=[hbm] + [vmem] * n,
        out_specs=[vmem] * n + [hbm] * 5,
        out_shape=[jax.ShapeDtypeStruct(shape, bf) for shape in shapes]
        + outs
        + [jax.ShapeDtypeStruct((window, x.shape[1]), x.dtype)],
        scratch_shapes=[pltpu.VMEM(shape, f32) for shape in shapes]
        + [dma((n,)), dma((n,)), dma((8, copies)), dma((8, copies)), dma((4,)), dma((hops,)), dma((hops,))],
        compiler_params=pltpu.CompilerParams(
            collective_id=1, has_side_effects=True, vmem_limit_bytes=32 * 2**20
        ),
        name="first_gather",
    )(x, *shards)
    return got[:n], got[n : n + 4], got[n + 4]


GATHER_STEPS = ((0, 0, -1), (0, 1, -1), (0, 2, -1), (5, 0, 0), (5, 1, 0), (5, 3, -1), (8, 0, 1), (8, 1, 1), (12, 2, 0), (13, 0, 2), (13, 1, 2), (16, 2, 1), (19, 3, 0), (23, 2, 2), (23, 3, 1), (23, 3, 2))


def attend_gather_kernel(dims, shapes, steps, lo_ref, q_ref, k_ref, v_ref, *refs):
    n = len(shapes)
    blocks, refs = refs[:n], refs[n:]
    o_ref, lse_ref, refs = refs[0], refs[1], refs[2:]
    outs, refs = refs[:n], refs[n:]
    bias, send, recv, own_sem = refs
    place = my_place(dims)
    step = pl.program_id(0) * pl.num_programs(1) + pl.program_id(1)
    pieces = pieces_of(dims, place, blocks, outs, shapes, send, recv)
    keeps = [keep_own(blocks[k], outs[k], place, own_sem.at[k]) for k in range(n)]
    for at in sorted({s for s, _, _ in steps}):

        @pl.when(step == at)
        def _():
            if at == 0:
                meet(peers(dims, place))
                for keep in keeps:
                    keep.start()
            for _, k, what in [e for e in steps if e[0] == at]:
                if what == 0:
                    keeps[k].wait()
                for piece in pieces[2 * k : 2 * k + 2]:
                    if what < 0:
                        piece.start()
                    else:
                        piece.advance(what)

    fwd_kernel(lo_ref, q_ref, k_ref, v_ref, o_ref, lse_ref, bias)

    @pl.when(step == pl.num_programs(0) * pl.num_programs(1) - 1)
    def _():
        for piece in pieces:
            piece.finish()


def attend_gather(q, k, v, lo, blocks, dims):
    rows, width = q.shape
    ext = k.shape[0]
    nq, nh = rows // QB, width // 128
    shapes = [b.shape for b in blocks]
    n = len(shapes)
    hbm = pl.BlockSpec(memory_space=pl.ANY)
    dma = pltpu.SemaphoreType.DMA
    copies = copies_of(dims)
    got = pl.pallas_call(
        functools.partial(attend_gather_kernel, dims, shapes, GATHER_STEPS),
        grid=(nh, nq),
        in_specs=[
            pl.BlockSpec((QB, 1), lambda h, i: (i, 0)),
            pl.BlockSpec((QB, 128), lambda h, i: (i, h)),
            pl.BlockSpec((ext, 128), lambda h, i: (0, h)),
            pl.BlockSpec((ext, 128), lambda h, i: (0, h)),
        ]
        + [hbm] * n,
        out_specs=[
            pl.BlockSpec((QB, 128), lambda h, i: (i, h)),
            pl.BlockSpec((1, 8, QB), lambda h, i: (h, 0, i)),
        ]
        + [hbm] * n,
        out_shape=[
            jax.ShapeDtypeStruct((rows, width), bf),
            jax.ShapeDtypeStruct((nh, 8, rows), f32),
        ]
        + [jax.ShapeDtypeStruct(dims + shape, bf) for shape in shapes],
        scratch_shapes=[
            pltpu.VMEM((nq, QB, WINDOW + QB), f32),
            dma((2 * n, copies)),
            dma((2 * n, copies)),
            dma((n,)),
        ],
        compiler_params=pltpu.CompilerParams(
            collective_id=2, has_side_effects=True, vmem_limit_bytes=50 * 2**20
        ),
        cost_estimate=pl.CostEstimate(flops=4 * rows * 1792 * 768 * 3, bytes_accessed=14 * 2**20, transcendentals=0),
        name="attend_gather",
    )(lo, q, k, v, *blocks)
    return got[0], got[1], got[2:]


def piece_cuts(shape):
    return [(pl.ds(*rows), pl.ds(*cols)) for rows, cols in halves_of(shape)]


class Collapse:
    def __init__(self, dims, place, shape, turn, grad, out, buffers, send, recv):
        self.dims, self.place, self.shape = dims, place, shape
        self.grad, self.out, self.send, self.recv = grad, out, send, recv
        self.acc, self.box0, self.box1, self.box2, self.box3, self.fin, self.box4 = buffers
        z, y, x, c = place
        far_x, far_y = device_at(dims, (z, y, 1 - x, c)), device_at(dims, (z, 1 - y, x, c))
        every = slice(None)
        by_x = [(far_x, (every, every, 1 - x), (every, every, x)), (far_y, (every, 1 - y, x), (every, y, x))]
        by_y = [(far_y, (every, 1 - y, every), (every, y, every)), (far_x, (every, y, 1 - x), (every, y, x))]
        ways = [by_x, by_y] if turn == 0 else [by_y, by_x]
        self.pieces = list(zip(piece_cuts(shape), ways))

    def columns(self, core):
        half = self.shape[1] // 2
        return pl.ds(pl.multiple_of(core * half, 128), half)

    def copy(self, slot, source, target, device):
        return pltpu.make_async_remote_copy(
            src_ref=source, dst_ref=target, send_sem=self.send.at[slot], recv_sem=self.recv.at[slot],
            device_id=device, device_id_type=MESH,
        )

    def copies(self, stage):
        z, y, x, c = self.place
        mate = device_at(self.dims, sibling(self.place))
        every = slice(None)
        if stage == 0:
            source = self.grad.at[every, every, every, every, self.columns(1 - c)]
            return [self.copy(0, source, self.box0, mate)]
        if stage == 4:
            half = self.shape[0] // 2
            source = self.fin.at[pl.ds(pl.multiple_of((1 - c) * half, 8), half)]
            return [self.copy(1, source, self.box4, mate)]
        made = []
        for at, (cut, ways) in enumerate(self.pieces):
            first = 2 + at * (2 + self.dims[0] - 1)
            if stage in (1, 2):
                device, give, _ = ways[stage - 1]
                box = (self.box1 if stage == 1 else self.box2).at[(every,) * (3 - stage) + cut]
                made.append(self.copy(first + stage - 1, self.acc.at[give + cut], box, device))
            else:
                for by in range(1, self.dims[0]):
                    to = lax.rem(z + by, self.dims[0])
                    made.append(
                        self.copy(
                            first + 1 + by, self.acc.at[(to, y, x) + cut], self.box3.at[(by - 1,) + cut],
                            device_at(self.dims, (to, y, x, c)),
                        )
                    )
        return made

    def local(self, sem):
        every = slice(None)
        source = self.grad.at[every, every, every, every, self.columns(self.place[3])]
        return pltpu.make_async_copy(source, self.acc, sem)

    def start(self, stage):
        for copy in self.copies(stage):
            copy.start()

    def add(self, stage):
        for copy in self.copies(stage):
            copy.wait_recv()
        z, y, x, c = self.place
        dims = self.dims
        if stage == 0:

            def body(i, carry):
                a, b, d = i // (dims[1] * dims[2]), lax.rem(i // dims[2], dims[1]), lax.rem(i, dims[2])
                self.acc[a, b, d] = self.acc[a, b, d] + self.box0[a, b, d]
                return carry

            lax.fori_loop(0, dims[0] * dims[1] * dims[2], body, 0)
        elif stage == 1:
            for cut, ways in self.pieces:
                by_x = not isinstance(ways[0][2][2], slice)

                def body(i, carry):
                    a, b = i // 2, lax.rem(i, 2)
                    at = ((a, b, x) if by_x else (a, y, b)) + cut
                    self.acc[at] = self.acc[at] + self.box1[(a, b) + cut]
                    return carry

                lax.fori_loop(0, dims[0] * 2, body, 0)
        elif stage == 2:

            def body(a, carry):
                self.acc[a, y, x] = self.acc[a, y, x] + self.box2[a]
                return carry

            lax.fori_loop(0, dims[0], body, 0)
        elif stage == 3:
            total = self.acc[z, y, x].astype(f32)
            for by in range(1, dims[0]):
                total = total + self.box3[by - 1].astype(f32)
            self.fin[...] = total
        else:
            half = self.shape[0] // 2
            mine = self.fin[pl.ds(pl.multiple_of(c * half, 8), half)]
            other = self.box4[...]
            width = self.shape[1] // 2
            self.out[:, :width] = jnp.where(c == 0, mine, other)
            self.out[:, width:] = jnp.where(c == 0, other, mine)

    def finish(self):
        for stage in range(5):
            for copy in self.copies(stage):
                copy.wait_send()


def collapse_scratch(dims, shapes):
    found = []
    for rows, cols in shapes:
        half = cols // 2
        found += [
            pltpu.VMEM(dims + (rows, half), bf),
            pltpu.VMEM(dims + (rows, half), bf),
            pltpu.VMEM((dims[0], 2, rows, half), bf),
            pltpu.VMEM((dims[0], rows, half), bf),
            pltpu.VMEM((dims[0] - 1, rows, half), bf),
            pltpu.VMEM((rows, half), f32),
            pltpu.VMEM((rows // 2, half), f32),
        ]
    dma = pltpu.SemaphoreType.DMA
    n = len(shapes)
    slots = 2 + 2 * (2 + dims[0] - 1)
    return found + [dma((n, slots)), dma((n, slots)), dma((n,))]


def collapses_of(dims, place, shapes, grads, outs, scratch):
    n = len(shapes)
    send, recv, local_sem = scratch[7 * n :]
    made = [
        Collapse(dims, place, shapes[k], k % 2, grads[k], outs[k], scratch[7 * k : 7 * k + 7], send.at[k], recv.at[k])
        for k in range(n)
    ]
    return made, [made[k].local(local_sem.at[k]) for k in range(n)]


def run_collapse(sums, locals_, k, stage):
    if stage < 0:
        locals_[k].start()
        sums[k].start(0)
        return
    if stage == 0:
        locals_[k].wait()
    sums[k].add(stage)
    if stage < 4:
        sums[k].start(stage + 1)


SUM_STEPS = (
    (0, 2, -1), (0, 3, -1), (0, 1, -1), (0, 0, -1),
    (3, 2, 0), (6, 3, 0), (8, 2, 1), (10, 2, 2), (10, 1, 0), (10, 0, 0), (11, 3, 1), (13, 3, 2),
    (15, 2, 3), (15, 1, 1), (15, 0, 1), (17, 1, 2), (17, 0, 2), (18, 3, 3), (18, 2, 4), (22, 1, 3), (22, 0, 3), (22, 3, 4),
    (23, 1, 4), (23, 0, 4),
)


def back_block(lo_ref, q_ref, do_ref, o_ref, lse_ref, k_ref, v_ref, kt_ref, dq_ref, dk_ref, dv_ref, bias, dk_acc, dv_acc):
    hp, qb = pl.program_id(0), pl.program_id(1)
    span = WINDOW + QB
    start = pl.multiple_of(qb * QB, QB)

    @pl.when(hp == 0)
    def _():
        base = qb * QB
        kpos = base + lax.broadcasted_iota(jnp.int32, (span, QB), 0)
        qpos = WINDOW + base + lax.broadcasted_iota(jnp.int32, (span, QB), 1)
        ok = (kpos >= lo_ref[...]) & (kpos <= qpos)
        bias[qb] = jnp.where(ok, 0.0, NEG)

    @pl.when(qb == 0)
    def _():
        dk_acc[...] = jnp.zeros_like(dk_acc)
        dv_acc[...] = jnp.zeros_like(dv_acc)

    q_heads = halves(q_ref[...])
    do = do_ref[...]
    d_heads = halves(do)
    prod = do.astype(f32) * o_ref[...].astype(f32)
    row = lax.broadcasted_iota(jnp.int32, (8, 128), 0)
    lane = lax.broadcasted_iota(jnp.int32, (8, 128), 1)
    pick = jnp.where(row == lane // 64, 1.0, 0.0).astype(f32)
    delta = lax.dot_general(pick, prod, NT, precision=lax.Precision.HIGHEST, preferred_element_type=f32)
    lse = lse_ref[0]
    at = pl.ds(start, span)
    kw, vw, kt = k_ref[at, :], v_ref[at, :], kt_ref[:, at]
    low_p, low_s, dq = [], [], []
    for h in range(2):
        s = dot(kw, q_heads[h], NT) + bias[qb]
        p = jnp.exp(s - lse[h : h + 1])
        dp = dot(vw, d_heads[h], NT)
        ds = (p * (dp - delta[h : h + 1])).astype(bf)
        low_p.append(p.astype(bf))
        low_s.append(ds)
        dq.append(dot(kt, ds))
    dv_acc[at, :] += dot(jnp.concatenate(low_p, axis=1), jnp.concatenate(d_heads, axis=0))
    dk_acc[at, :] += dot(jnp.concatenate(low_s, axis=1), jnp.concatenate(q_heads, axis=0))
    sub = lax.broadcasted_iota(jnp.int32, (128, QB), 0)
    dq_ref[...] = (jnp.where(sub < 64, dq[0], dq[1]).T * 0.125).astype(bf)

    @pl.when(qb == pl.num_programs(1) - 1)
    def _():
        dk_ref[...] = dk_acc[...].astype(bf)
        dv_ref[...] = dv_acc[...].astype(bf)


def back_sum_kernel(dims, shapes, steps, *refs):
    n = len(shapes)
    ins, grads, refs = refs[:8], refs[8 : 8 + n], refs[8 + n :]
    outs, sums_out, refs = refs[:3], refs[3 : 3 + n], refs[3 + n :]
    own, scratch = refs[:3], refs[3:]
    step = pl.program_id(0) * pl.num_programs(1) + pl.program_id(1)
    if n:
        place = my_place(dims)
        sums, locals_ = collapses_of(dims, place, shapes, grads, sums_out, scratch)
        for at in sorted({s for s, _, _ in steps}):

            @pl.when(step == at)
            def _():
                if at == 0:
                    meet(peers(dims, place))
                for _, k, stage in [e for e in steps if e[0] == at]:
                    run_collapse(sums, locals_, k, stage)

    back_block(*ins, *outs, *own)
    if n:

        @pl.when(step == pl.num_programs(0) * pl.num_programs(1) - 1)
        def _():
            for one in sums:
                one.finish()


def attend_back(q, do, o, lse, k, v, lo_row, grads=(), dims=None):
    rows, width = q.shape
    ext = k.shape[0]
    nq, nh = rows // QB, width // 128
    n = len(grads)
    shapes = [g.shape[3:] for g in grads]
    blk = pl.BlockSpec((QB, 128), lambda h, i: (i, h))
    full = pl.BlockSpec((ext, 128), lambda h, i: (0, h))
    hbm = pl.BlockSpec(memory_space=pl.ANY)
    whole = [pl.BlockSpec((r // 2, c), lambda h, i: (0, 0)) for r, c in shapes]
    got = pl.pallas_call(
        functools.partial(back_sum_kernel, dims, shapes, SUM_STEPS),
        grid=(nh, nq),
        in_specs=[pl.BlockSpec((1, QB), lambda h, i: (0, i)), blk, blk, blk]
        + [pl.BlockSpec((1, 8, QB), lambda h, i: (h, 0, i)), full, full, pl.BlockSpec((128, ext), lambda h, i: (h, 0))]
        + [hbm] * n,
        out_specs=[blk, full, full] + whole,
        out_shape=[
            jax.ShapeDtypeStruct((rows, width), bf),
            jax.ShapeDtypeStruct((ext, width), bf),
            jax.ShapeDtypeStruct((ext, width), bf),
        ]
        + [jax.ShapeDtypeStruct((r // 2, c), f32) for r, c in shapes],
        scratch_shapes=[
            pltpu.VMEM((nq, WINDOW + QB, QB), f32),
            pltpu.VMEM((ext, 128), f32),
            pltpu.VMEM((ext, 128), f32),
        ]
        + (collapse_scratch(dims, shapes) if n else []),
        compiler_params=pltpu.CompilerParams(
            vmem_limit_bytes=60 * 2**20, **(dict(collective_id=3, has_side_effects=True) if n else {})
        ),
        cost_estimate=pl.CostEstimate(flops=10 * rows * 1792 * 768 * 3, bytes_accessed=24 * 2**20, transcendentals=0),
        name="attend_back",
    )(lo_row, q, do, o, lse, k, v, k.T, *grads)
    return got[:3], got[3:]


def last_kernel(dims, shapes, window, *refs):
    n = len(shapes)
    back_ref, grads, refs = refs[0], refs[1 : 1 + n], refs[1 + n :]
    hops = len(refs) - n - (7 * n + 3) - 2
    backs, sums_out, refs = refs[:hops], refs[hops : hops + n], refs[hops + n :]
    scratch, (back_send, back_recv) = refs[:-2], refs[-2:]
    place = my_place(dims)
    seq, item = lax.axis_index("seq"), lax.axis_index("item")
    count = dims[0] * dims[1]
    ahead = [(lax.rem(seq + d, count), item) for d in range(1, hops + 1)]
    behind = [(lax.rem(seq + count - d, count), item) for d in range(1, hops + 1)]
    meet(peers(dims, place) + ahead + behind)
    sums, locals_ = collapses_of(dims, place, shapes, grads, sums_out, scratch)
    for k in range(n):
        run_collapse(sums, locals_, k, -1)
    returns = []
    upper = window
    for d in range(1, hops + 1):
        need = backs[d - 1].shape[0]
        returns.append(
            pltpu.make_async_remote_copy(
                src_ref=back_ref.at[pl.ds(upper - need, need)], dst_ref=backs[d - 1],
                send_sem=back_send.at[d - 1], recv_sem=back_recv.at[d - 1],
                device_id=behind[d - 1], device_id_type=MESH,
            )
        )
        upper -= need
        pl.when(seq >= d)(returns[-1].start)
    for stage in range(5):
        for k in range(n):
            run_collapse(sums, locals_, k, stage)
    for one in sums:
        one.finish()
    for d in range(1, hops + 1):
        pl.when(seq >= d)(returns[d - 1].wait_send)
        pl.when(seq + d < count)(returns[d - 1].wait_recv)


def last_sum(back, grads, dims, rows, window):
    shapes = [g.shape[3:] for g in grads]
    n = len(shapes)
    hops = -(-window // rows)
    needs = [min(rows, window - (d - 1) * rows) for d in range(1, hops + 1)]
    hbm = pl.BlockSpec(memory_space=pl.ANY)
    vmem = pl.BlockSpec(memory_space=pltpu.VMEM)
    got = pl.pallas_call(
        functools.partial(last_kernel, dims, shapes, window),
        in_specs=[hbm] * (1 + n),
        out_specs=[hbm] * hops + [vmem] * n,
        out_shape=[jax.ShapeDtypeStruct((need, back.shape[1]), back.dtype) for need in needs]
        + [jax.ShapeDtypeStruct((r // 2, c), f32) for r, c in shapes],
        scratch_shapes=collapse_scratch(dims, shapes)
        + [pltpu.SemaphoreType.DMA((hops,)), pltpu.SemaphoreType.DMA((hops,))],
        compiler_params=pltpu.CompilerParams(
            collective_id=4, has_side_effects=True, vmem_limit_bytes=40 * 2**20
        ),
        name="last_sum",
    )(back, *grads)
    return got[:hops], got[hops:]


EPSILON = 1e-06
TINY_SQUARE = 1e-30
WEIGHT_RATE = 0.02
GAIN_RATE = 0.2
STEP = 10


def sum_kernel(sizes, x_ref, o_ref, inbox, send_sem, recv_sem):
    place = {name: lax.axis_index(name) for name, _ in sizes}
    partners = []
    for name, size in sizes:
        bit = 1
        while bit < size:
            mine = place[name]
            low = lax.rem(mine // bit, 2)
            other = mine + bit * (1 - 2 * low)
            partners.append(tuple(other if n == name else place[n] for n in ("seq", "item")))
            bit *= 2
    barrier = pltpu.get_barrier_semaphore()
    for partner in partners:
        pl.semaphore_signal(barrier, inc=1, device_id=partner, device_id_type=MESH)
    pl.semaphore_wait(barrier, len(partners))
    o_ref[0] = x_ref[...]
    for stage, partner in enumerate(partners):
        copy = pltpu.make_async_remote_copy(
            src_ref=o_ref.at[stage],
            dst_ref=inbox.at[stage],
            send_sem=send_sem.at[stage],
            recv_sem=recv_sem.at[stage],
            device_id=partner,
            device_id_type=MESH,
        )
        copy.start()
        copy.wait()
        o_ref[stage + 1] = o_ref[stage] + inbox[stage]


def sum_all(x, sizes):
    stages = sum(size.bit_length() - 1 for _, size in sizes)
    held = pl.pallas_call(
        functools.partial(sum_kernel, sizes),
        out_shape=jax.ShapeDtypeStruct((stages + 1,) + x.shape, x.dtype),
        in_specs=[pl.BlockSpec(memory_space=pltpu.VMEM)],
        out_specs=pl.BlockSpec(memory_space=pltpu.VMEM),
        scratch_shapes=[
            pltpu.VMEM((stages,) + x.shape, x.dtype),
            pltpu.SemaphoreType.DMA((stages,)),
            pltpu.SemaphoreType.DMA((stages,)),
        ],
        compiler_params=pltpu.CompilerParams(collective_id=0, has_side_effects=True),
        name="sum_all",
    )(x)
    return held[stages]


def from_behind(block, axis, distance):
    devices = range(lax.axis_size(axis))
    route = [(i - distance, i) for i in devices if i - distance in devices]
    return lax.ppermute(block, axis, route)


def norm_rows(values, gain):
    return values * lax.rsqrt(jnp.mean(values * values, axis=-1, keepdims=True) + EPSILON) * gain


def gelu_tanh(values):
    return (
        0.5
        * values
        * (1.0 + jnp.tanh(0.7978845608028654 * (values + 0.044715 * values * values * values)))
    )


def finish_update(weight, grad, row_new, col_state, col_total, rows_all, row_mean, decay):
    col_new = decay * col_state + (1.0 - decay) * col_total / rows_all
    second = row_new[..., :, None] * col_new[..., None, :] / row_mean
    return (weight - WEIGHT_RATE * grad * lax.rsqrt(second), col_new)


def local(
    byte_rows, item_lengths, cont_mask, bound_mask, out_cot, proj_cot,
    w_qkv, w_out, w_up, w_down, w_proj, gains,
    row_qkv, col_qkv, row_out, col_out, row_up, col_up, row_down, col_down, row_proj, col_proj, gain_var,
):
    sizes = tuple((name, lax.axis_size(name)) for name in ("item", "seq"))
    count = lax.axis_size("item") * lax.axis_size("seq")
    rows_dev, width = byte_rows.shape[1:]
    ff = w_up.shape[1]
    shard = width // count
    low = bf

    dims = grid_of(lax.axis_size("seq"), lax.axis_size("item"))
    paired = shard % 8 == 0 and dims[1:] == (2, 2)
    inputs_low = byte_rows[0]
    if paired:
        gain_block = jnp.pad(gains.reshape(1, 2 * shard), ((0, 15), (0, 256 - 2 * shard)))
        shards = [w_qkv[0], w_qkv[1], w_qkv[2], gain_block, w_out, w_proj, w_up, w_down]
        blocks, first, halo_rows = first_gather(inputs_low, shards, dims, WINDOW)
        weight_qkv = [w.reshape(width, width) for w in first[:3]]
        gain_full = first[3].reshape(count // 2, 2, 16, 256)[:, :, 0, : 2 * shard]
        gain_full = gain_full.reshape(count, 2, shard).transpose(1, 0, 2).reshape(2, width).astype(f32)
    else:
        weight_qkv = lax.all_gather(w_qkv.astype(low), AXES, axis=1, tiled=True)
        gain_full = lax.all_gather(gains.astype(low), AXES, axis=1, tiled=True).astype(f32)
        weight_out, weight_proj, weight_up, weight_down = [
            lax.all_gather(w.astype(low), AXES, axis=0, tiled=True) for w in (w_out, w_proj, w_up, w_down)
        ]

    inputs = inputs_low.astype(f32)
    hop_total = -(-WINDOW // rows_dev)
    offset = lax.axis_index("seq") * rows_dev
    if not paired:
        halo = []
        for distance in range(hop_total, 0, -1):
            need = min(rows_dev, WINDOW - (distance - 1) * rows_dev)
            halo.append(from_behind(inputs_low[rows_dev - need :], "seq", distance))
        halo_rows = jnp.concatenate(halo, axis=0)
    before = offset - WINDOW + jnp.arange(WINDOW, dtype=jnp.int32)
    halo_rows = jnp.where(before[:, None] >= 0, halo_rows, 0)
    normed = norm_rows(inputs, gain_full[0]).astype(low)
    halo_normed = norm_rows(halo_rows.astype(f32), gain_full[0]).astype(low)
    ext_normed = jnp.concatenate([halo_normed, normed], axis=0)
    queries = dot(normed, weight_qkv[0]).astype(low) * jnp.asarray(0.125, low)
    ext_keys = dot(ext_normed, weight_qkv[1]).astype(low)
    ext_values = dot(ext_normed, weight_qkv[2]).astype(low)

    ends = jnp.cumsum(item_lengths[0], dtype=jnp.int32)
    pos = offset + jnp.arange(rows_dev, dtype=jnp.int32)
    begin = jnp.max(jnp.where(ends[None, :] <= pos[:, None], ends[None, :], 0), axis=1)
    lo = jnp.maximum(begin, pos - WINDOW + 1) - offset + WINDOW

    if paired:
        attended, lse, rest = attend_gather(queries, ext_keys, ext_values, lo[:, None], blocks[4:], dims)
        weight_out, weight_proj, weight_up, weight_down = [
            w.reshape(-1, w.shape[-1]) for w in rest
        ]
    else:
        attended, lse = attend(queries, ext_keys, ext_values, lo[:, None])

    resid = inputs + dot(attended, weight_out)
    normed_two = norm_rows(resid, gain_full[1]).astype(low)
    hidden_pre = dot(normed_two, weight_up)
    activated = gelu_tanh(hidden_pre).astype(low)
    output = resid + dot(activated, weight_down)
    output_low = output.astype(low)
    boundary = (bound_mask[0] * (1 - cont_mask[0])).astype(f32)[:, None]
    projected = (boundary * dot(output_low, weight_proj)).astype(low)
    proj_grad = (boundary * proj_cot[0].astype(f32)).astype(low)
    grad_proj = dot(output_low, proj_grad, TN)
    output_grad = out_cot[0].astype(f32) + dot(proj_grad, weight_proj, NT)
    output_grad_low = output_grad.astype(low)
    grad_down = dot(activated, output_grad_low, TN)
    act_grad = dot(output_grad_low, weight_down, NT)
    _, gelu_back = jax.vjp(gelu_tanh, hidden_pre)
    pre_grad = gelu_back(act_grad)[0].astype(low)
    grad_up = dot(normed_two, pre_grad, TN)
    normed_two_grad = dot(pre_grad, weight_up, NT)
    _, norm_two_back = jax.vjp(norm_rows, resid, gain_full[1])
    resid_norm_grad, gain_two_grad = norm_two_back(normed_two_grad)
    resid_grad = output_grad + resid_norm_grad
    resid_grad_low = resid_grad.astype(low)
    grad_out = dot(attended, resid_grad_low, TN)
    attended_grad = dot(resid_grad_low, weight_out, NT).astype(low)

    low_grads = [g.astype(low) for g in (grad_out, grad_proj, grad_up, grad_down)]
    if paired:
        apart = [g.reshape(dims + (-1, g.shape[1])) for g in low_grads]
        (query_grad, ext_key_grad, ext_value_grad), sums = attend_back(
            queries, attended_grad, attended, lse, ext_keys, ext_values, lo[None, :], apart, dims
        )
    else:
        (query_grad, ext_key_grad, ext_value_grad), _ = attend_back(
            queries, attended_grad, attended, lse, ext_keys, ext_values, lo[None, :]
        )
        sums = [lax.psum_scatter(g, AXES, scatter_dimension=0, tiled=True).astype(f32) for g in low_grads]
    sum_out, sum_proj, sum_up, sum_down = sums
    ext_back = dot(ext_key_grad, weight_qkv[1], NT) + dot(ext_value_grad, weight_qkv[2], NT)
    halo_back = ext_back[:WINDOW].astype(low)
    grads_qkv = [
        dot(normed, query_grad, TN).astype(low),
        dot(ext_normed, ext_key_grad, TN).astype(low),
        dot(ext_normed, ext_value_grad, TN).astype(low),
    ]
    if paired:
        apart = [g.reshape(dims + (-1, width)) for g in grads_qkv]
        returned, sums = last_sum(halo_back, apart, dims, rows_dev, WINDOW)
        pieces = lax.axis_size("seq")
        returned = [
            jnp.where(lax.axis_index("seq") + d + 1 < pieces, block, 0) for d, block in enumerate(returned)
        ]
    else:
        returned = []
        for distance in range(1, hop_total + 1):
            need = min(rows_dev, WINDOW - (distance - 1) * rows_dev)
            upper = WINDOW - (distance - 1) * rows_dev
            returned.append(from_behind(halo_back[upper - need : upper], "seq", -distance))
        sums = [lax.psum_scatter(g, AXES, scatter_dimension=0, tiled=True).astype(f32) for g in grads_qkv]
    sum_qkv = jnp.stack(sums)
    normed_grad = ext_back[WINDOW:] + dot(query_grad, weight_qkv[0], NT)
    for block in returned:
        need = block.shape[0]
        normed_grad = normed_grad.at[rows_dev - need :].add(block.astype(f32))
    _, norm_one_back = jax.vjp(norm_rows, inputs, gain_full[0])
    input_norm_grad, gain_one_grad = norm_one_back(normed_grad)
    input_grad = (resid_grad + input_norm_grad).astype(low)

    decay = 1.0 - STEP ** (-0.8)
    square_qkv = sum_qkv * sum_qkv + TINY_SQUARE
    square_out = sum_out * sum_out + TINY_SQUARE
    square_up = sum_up * sum_up + TINY_SQUARE
    square_down = sum_down * sum_down + TINY_SQUARE
    square_proj = sum_proj * sum_proj + TINY_SQUARE
    row_qkv_new = decay * row_qkv + (1.0 - decay) * jnp.mean(square_qkv, axis=-1)
    row_out_new = decay * row_out + (1.0 - decay) * jnp.mean(square_out, axis=-1)
    row_up_new = decay * row_up + (1.0 - decay) * jnp.mean(square_up, axis=-1)
    row_down_new = decay * row_down + (1.0 - decay) * jnp.mean(square_down, axis=-1)
    row_proj_new = decay * row_proj + (1.0 - decay) * jnp.mean(square_proj, axis=-1)
    row_sums = jnp.concatenate(
        [
            jnp.sum(row_qkv_new, axis=1),
            jnp.sum(row_out_new)[None],
            jnp.sum(row_up_new)[None],
            jnp.sum(row_down_new)[None],
            jnp.sum(row_proj_new)[None],
        ]
    )
    stats = [
        jnp.sum(square_qkv, axis=1).reshape(-1),
        jnp.sum(square_out, axis=0),
        jnp.sum(square_up, axis=0),
        jnp.sum(square_down, axis=0),
        jnp.sum(square_proj, axis=0),
        gain_one_grad,
        gain_two_grad,
        row_sums,
    ]
    flat = jnp.concatenate(stats)
    used = flat.shape[0]
    padded = -(-used // 1024) * 1024
    flat = jnp.pad(flat, (0, padded - used)).reshape(padded // 128, 128)
    flat = sum_all(flat, sizes).reshape(-1)
    totals, at = [], 0
    for part in stats:
        totals.append(flat[at : at + part.shape[0]])
        at += part.shape[0]
    col_qkv_total, col_out_total, col_up_total, col_down_total, col_proj_total, gain_one, gain_two, row_totals = totals
    col_qkv_total = col_qkv_total.reshape(3, width)
    mine = lax.axis_index("seq") * lax.axis_size("item") + lax.axis_index("item")
    sum_gains = lax.dynamic_slice_in_dim(jnp.stack([gain_one, gain_two]), mine * shard, shard, 1)
    row_counts = jnp.array([width, width, width, width, width, ff, width], f32)
    row_means = row_totals / row_counts
    new_qkv, col_qkv_new = finish_update(
        w_qkv, sum_qkv, row_qkv_new, col_qkv, col_qkv_total, width, row_means[:3][:, None, None], decay
    )
    new_out, col_out_new = finish_update(w_out, sum_out, row_out_new, col_out, col_out_total, width, row_means[3], decay)
    new_up, col_up_new = finish_update(w_up, sum_up, row_up_new, col_up, col_up_total, width, row_means[4], decay)
    new_down, col_down_new = finish_update(
        w_down, sum_down, row_down_new, col_down, col_down_total, ff, row_means[5], decay
    )
    new_proj, col_proj_new = finish_update(
        w_proj, sum_proj, row_proj_new, col_proj, col_proj_total, width, row_means[6], decay
    )
    gain_var_new = decay * gain_var + (1.0 - decay) * (sum_gains * sum_gains + TINY_SQUARE)
    new_gains = gains - GAIN_RATE * sum_gains * lax.rsqrt(gain_var_new)
    return (
        output_low[None], projected[None], input_grad[None],
        sum_qkv, sum_out, sum_up, sum_down, sum_proj, sum_gains,
        new_qkv, new_out, new_up, new_down, new_proj, new_gains,
        row_qkv_new, col_qkv_new, row_out_new, col_out_new, row_up_new, col_up_new,
        row_down_new, col_down_new, row_proj_new, col_proj_new, gain_var_new,
    )


def solution(mesh):
    in_specs = (
        P("item", "seq", None),
        P("item", None),
        P("item", "seq"),
        P("item", "seq"),
        P("item", "seq", None),
        P("item", "seq", None),
        P(None, ("seq", "item"), None),
        P(("seq", "item"), None),
        P(("seq", "item"), None),
        P(("seq", "item"), None),
        P(("seq", "item"), None),
        P(None, ("seq", "item")),
        P(None, ("seq", "item")),
        P(),
        P(("seq", "item")),
        P(),
        P(("seq", "item")),
        P(),
        P(("seq", "item")),
        P(),
        P(("seq", "item")),
        P(),
        P(None, ("seq", "item")),
    )
    out_specs = (
        P("item", "seq", None),
        P("item", "seq", None),
        P("item", "seq", None),
        P(None, ("seq", "item"), None),
        P(("seq", "item"), None),
        P(("seq", "item"), None),
        P(("seq", "item"), None),
        P(("seq", "item"), None),
        P(None, ("seq", "item")),
        P(None, ("seq", "item"), None),
        P(("seq", "item"), None),
        P(("seq", "item"), None),
        P(("seq", "item"), None),
        P(("seq", "item"), None),
        P(None, ("seq", "item")),
        P(None, ("seq", "item")),
        P(),
        P(("seq", "item")),
        P(),
        P(("seq", "item")),
        P(),
        P(("seq", "item")),
        P(),
        P(("seq", "item")),
        P(),
        P(None, ("seq", "item")),
    )
    return jax.shard_map(local, mesh=mesh, in_specs=in_specs, out_specs=out_specs, check_vma=False)
```

```python
import functools
import jax
import jax.numpy as jnp
from jax import lax
from jax.experimental import pallas as pl
from jax.experimental.pallas import tpu as pltpu
from jax.sharding import PartitionSpec as P

WINDOW = 1536
HEADS = 12
NEG = -1e30
EPSILON = 1e-06
TINY_SQUARE = 1e-30
WEIGHT_RATE = 0.02
GAIN_RATE = 0.2
STEP = 10
QB = 256
NT = (((1,), (1,)), ((), ()))
TN = (((0,), (0,)), ((), ()))
f32 = jnp.float32
bf = jnp.bfloat16


def dot(a, b, dims=None):
    if dims is None:
        return jnp.dot(a, b, preferred_element_type=f32)
    return lax.dot_general(a, b, dims, preferred_element_type=f32)


def halves(x):
    lane = lax.broadcasted_iota(jnp.int32, x.shape, 1)
    zero = jnp.zeros_like(x)
    return jnp.where(lane < 64, x, zero), jnp.where(lane < 64, zero, x)


def fwd_kernel(lo_ref, q_ref, k_ref, v_ref, o_ref, lse_ref, bias):
    hp, qb = pl.program_id(0), pl.program_id(1)
    span = WINDOW + QB

    @pl.when(hp == 0)
    def _():
        base = qb * QB
        kpos = base + lax.broadcasted_iota(jnp.int32, (QB, span), 1)
        qpos = WINDOW + base + lax.broadcasted_iota(jnp.int32, (QB, span), 0)
        ok = (kpos >= lo_ref[...]) & (kpos <= qpos)
        bias[qb] = jnp.where(ok, 0.0, NEG)

    start = pl.multiple_of(qb * QB, QB)
    kw = k_ref[pl.ds(start, span), :]
    vw = v_ref[pl.ds(start, span), :]
    outs, lses = [], []
    for qh in halves(q_ref[...]):
        s = dot(qh, kw, NT) + bias[qb]
        m = jnp.max(s, axis=1, keepdims=True)
        p = jnp.exp(s - m)
        l = jnp.sum(p, axis=1, keepdims=True)
        outs.append(dot(p.astype(bf), vw) * (1.0 / l))
        lses.append(m + jnp.log(l))
    lane = lax.broadcasted_iota(jnp.int32, (QB, 128), 1)
    o_ref[...] = jnp.where(lane < 64, outs[0], outs[1]).astype(bf)
    both = jnp.where(lane == 0, lses[0], lses[1])
    lse_ref[0] = both.T[:8]


def attend(q, k, v, lo):
    rows, width = q.shape
    ext = k.shape[0]
    nq, nh = rows // QB, width // 128
    return pl.pallas_call(
        fwd_kernel,
        grid=(nh, nq),
        in_specs=[
            pl.BlockSpec((QB, 1), lambda h, i: (i, 0)),
            pl.BlockSpec((QB, 128), lambda h, i: (i, h)),
            pl.BlockSpec((ext, 128), lambda h, i: (0, h)),
            pl.BlockSpec((ext, 128), lambda h, i: (0, h)),
        ],
        out_specs=[
            pl.BlockSpec((QB, 128), lambda h, i: (i, h)),
            pl.BlockSpec((1, 8, QB), lambda h, i: (h, 0, i)),
        ],
        out_shape=[
            jax.ShapeDtypeStruct((rows, width), bf),
            jax.ShapeDtypeStruct((nh, 8, rows), f32),
        ],
        scratch_shapes=[pltpu.VMEM((nq, QB, WINDOW + QB), f32)],
        compiler_params=pltpu.CompilerParams(vmem_limit_bytes=50 * 2**20),
        cost_estimate=pl.CostEstimate(flops=4 * rows * 1792 * 768 * 3, bytes_accessed=14 * 2**20, transcendentals=0),
        name="attend",
    )(lo, q, k, v)


AXES = ("seq", "item")
MESH = pl.DeviceIdType.MESH


def grid_of(seq, item):
    side = 1
    while side * side * 4 <= seq:
        side *= 2
    return (seq // side, side, item // 2)


def my_place(dims):
    seq, item = lax.axis_index("seq"), lax.axis_index("item")
    return (seq // dims[1], lax.rem(seq, dims[1]), item // 2, lax.rem(item, 2))


def device_at(dims, place):
    z, y, x, c = place
    return (z * dims[1] + y, x * 2 + c)


def moved(dims, place, dim, by):
    to = list(place)
    to[dim] = lax.rem(place[dim] + by, dims[dim])
    return tuple(to)


def sibling(place):
    return place[:3] + (1 - place[3],)


def peers(dims, place):
    found = [sibling(place)]
    for dim in range(3):
        found += [moved(dims, place, dim, by) for by in range(1, dims[dim])]
    return [device_at(dims, p) for p in found]


def meet(targets):
    barrier = pltpu.get_barrier_semaphore()
    for target in targets:
        pl.semaphore_signal(barrier, inc=1, device_id=target, device_id_type=MESH)
    pl.semaphore_wait(barrier, len(targets))


class Spread:
    def __init__(self, dims, place, own, out, rows, cols, order, send, recv):
        self.dims, self.place, self.own, self.out = dims, place, own, out
        self.rows, self.cols, self.order = rows, cols, order
        self.send, self.recv = send, recv

    def span(self, core):
        half = self.out.shape[-1] // 2
        return pl.ds(pl.multiple_of(core * half + self.cols[0], 128), self.cols[1])

    def region(self, stage, by=0, core=None):
        held = self.order[:stage]
        at = []
        for dim in range(3):
            if dim in held:
                at.append(slice(None))
            elif by and dim == self.order[stage]:
                at.append(lax.rem(self.place[dim] + self.dims[dim] - by, self.dims[dim]))
            else:
                at.append(self.place[dim])
        core = self.place[3] if core is None else core
        return self.out.at[tuple(at) + (self.rows, self.span(core))]

    def slots(self, stage):
        first = sum(self.dims[d] - 1 for d in self.order[:stage])
        return [(by, first + by - 1) for by in range(1, self.dims[self.order[stage]])]

    def hops(self, stage):
        for by, slot in self.slots(stage):
            block = self.region(stage)
            source = self.own.at[self.rows, self.span(self.place[3])] if stage == 0 else block
            target = device_at(self.dims, moved(self.dims, self.place, self.order[stage], by))
            yield pltpu.make_async_remote_copy(
                src_ref=source, dst_ref=block, send_sem=self.send.at[slot], recv_sem=self.recv.at[slot],
                device_id=target, device_id_type=MESH,
            )

    def shares(self, stage, core=None):
        count = sum(d - 1 for d in self.dims)
        for by, slot in self.slots(stage):
            block = self.region(stage, by, core)
            yield pltpu.make_async_remote_copy(
                src_ref=block, dst_ref=block, send_sem=self.send.at[count + slot], recv_sem=self.recv.at[count + slot],
                device_id=device_at(self.dims, sibling(self.place)), device_id_type=MESH,
            )

    def start(self):
        for copy in self.hops(0):
            copy.start()

    def advance(self, stage):
        for copy in self.hops(stage):
            copy.wait_recv()
        if stage < 2:
            for copy in self.hops(stage + 1):
                copy.start()
        for copy in self.shares(stage):
            copy.start()

    def finish(self):
        for stage in range(3):
            for copy in self.hops(stage):
                copy.wait_send()
            for copy in self.shares(stage):
                copy.wait_send()
            for copy in self.shares(stage, 1 - self.place[3]):
                copy.wait_recv()


def keep_own(own, out, place, sem):
    return pltpu.make_async_copy(own, out.at[place[0], place[1], place[2]], sem)


def copies_of(dims):
    return 2 * sum(d - 1 for d in dims)


def halves_of(shape):
    rows, cols = shape
    half = cols // 2
    if half % 256 == 0:
        return [((0, rows), (0, half // 2)), ((0, rows), (half // 2, half // 2))]
    cut = rows // 32 * 16
    return [((at, count), (0, half)) for at, count in ((0, cut), (cut, rows - cut)) if count]


ORDERS = ((0, 1, 2), (0, 2, 1))


def pieces_of(dims, place, owns, outs, shapes, send, recv):
    made, at = [], 0
    for k, (own, out, shape) in enumerate(zip(owns, outs, shapes)):
        turn = k % 2
        pieces = []
        for order, (rows, cols) in zip(ORDERS[turn:] + ORDERS[:turn], halves_of(shape)):
            pieces.append(Spread(dims, place, own, out, pl.ds(*rows), cols, order, send.at[at], recv.at[at]))
            at += 1
        made.append(pieces)
    return made


def begin(pieces):
    for piece in pieces:
        piece.start()


def advance(pieces, stage):
    for piece in pieces:
        piece.advance(stage)


def lower_bounds(lengths_ref, pos, offset):
    begin = jnp.zeros_like(pos)
    end = jnp.int32(0)
    for j in range(lengths_ref.shape[1]):
        end = end + lengths_ref[0, j]
        begin = jnp.where(end <= pos, end, begin)
    return jnp.maximum(begin, pos - (WINDOW - 1)) - offset + WINDOW


def norm_block(values, gain):
    x = values.astype(f32)
    return (x * lax.rsqrt(jnp.mean(x * x, axis=-1, keepdims=True) + EPSILON) * gain).astype(bf)


REST_STEPS = ((2, 2, 0), (2, 3, -1), (5, 2, 1), (9, 3, 0), (9, 2, 2), (13, 3, 1), (17, 3, 2))


def front_kernel(dims, shapes, count, lengths_ref, x_ref, gains_ref, qkv_ref, out_ref_, proj_ref, up_ref, down_ref, *refs):
    names = iter(refs)
    take = lambda k: [next(names) for _ in range(k)]
    o_ref, lse_ref, q_out, k_out, v_out, n_out = take(6)
    w_outs = take(4)
    rest_outs = take(4)
    halo, normed, q_scr, k_scr, v_scr, gain_scr, gain_own, bias = take(8)
    wide, blocks = take(8), take(8)
    first = take(4)
    swap_send, swap_recv, send, recv, keep_sem, halo_send, halo_recv, out_sem = take(8)

    place = my_place(dims)
    c = place[3]
    seq, item = lax.axis_index("seq"), lax.axis_index("item")
    rows, width = x_ref.shape
    hops = -(-WINDOW // rows)
    around = [(lax.rem(seq + d, count), item) for d in range(1, hops + 1)]
    behind = [(lax.rem(seq + count - d, count), item) for d in range(1, hops + 1)]
    with jax.named_scope("meet"):
        meet(peers(dims, place) + around + behind)

    mate = device_at(dims, sibling(place))
    shard = gains_ref.shape[1]
    gain_own[...] = jnp.zeros_like(gain_own)
    gain_own[0:2, 0:shard] = gains_ref[...]
    mine = seq * (dims[2] * 2) + item
    gain_own[...] = pltpu.roll(gain_own[...], mine * shard, 1)
    shards = [qkv_ref.at[0], qkv_ref.at[1], qkv_ref.at[2], gain_own, out_ref_, proj_ref, up_ref, down_ref]
    swaps = []
    for k in range(8):
        half = shapes[k][0] // 2
        part = wide[k].at[pl.ds(pl.multiple_of(c * half, 8), half)]
        part[...] = shards[k][...]
        swaps.append(
            pltpu.make_async_remote_copy(
                src_ref=shards[k], dst_ref=part, send_sem=swap_send.at[k], recv_sem=swap_recv.at[k],
                device_id=mate, device_id_type=MESH,
            )
        )
        swaps[k].start()
    outs = first + rest_outs
    keeps = [keep_own(blocks[k], outs[k], place, keep_sem.at[k]) for k in range(8)]
    pieces = pieces_of(dims, place, blocks, outs, shapes, send, recv)

    def ready(k):
        swaps[k].wait()
        blocks[k][...] = wide[k][...].astype(bf)
        keeps[k].start()

    with jax.named_scope("swap"):
        for k in (3, 0, 1, 2):
            ready(k)
            begin(pieces[k])
    halos = []
    for d in range(1, hops + 1):
        need = min(rows, WINDOW - (d - 1) * rows)
        start = WINDOW - (d - 1) * rows - need
        halos.append(
            pltpu.make_async_remote_copy(
                src_ref=x_ref.at[pl.ds(rows - need, need)], dst_ref=halo.at[pl.ds(start, need)],
                send_sem=halo_send.at[d - 1], recv_sem=halo_recv.at[d - 1],
                device_id=around[d - 1], device_id_type=MESH,
            )
        )
        pl.when(seq + d < count)(halos[-1].start)
    with jax.named_scope("swap_rest"):
        for k in (4, 5, 6, 7):
            ready(k)
        for k in range(8):
            keeps[k].wait()
    for stage in range(3):
        with jax.named_scope("first_%d" % stage):
            for k in (3, 0, 1, 2):
                advance(pieces[k], stage)
        if stage == 0:
            begin(pieces[4])
            begin(pieces[5])
        if stage == 1:
            begin(pieces[6])
    with jax.named_scope("first_end"):
        for k in range(4):
            for piece in pieces[k]:
                piece.finish()
    total = first[3][...].astype(f32).reshape(dims[0] * dims[1] * dims[2] * 2, 8, width)
    gain_scr[...] = jnp.sum(total, axis=0)

    weights = [first[k] for k in range(3)]
    ext0 = WINDOW

    def project(slot, target, at, scale=None):
        got = dot(normed[at, :], weights[slot][...].reshape(width, width)).astype(bf)
        return got if scale is None else got * jnp.asarray(scale, bf)

    def own_rows(i, carry):
        at = pl.ds(pl.multiple_of(i * QB, QB), QB)
        ext = pl.ds(pl.multiple_of(ext0 + i * QB, QB), QB)
        normed[ext, :] = norm_block(x_ref[at, :], gain_scr[0:1])
        q_scr[at, :] = project(0, q_scr, ext, 0.125)
        k_scr[ext, :] = project(1, k_scr, ext)
        v_scr[ext, :] = project(2, v_scr, ext)
        return carry

    with jax.named_scope("own_rows"):
        lax.fori_loop(0, rows // QB, own_rows, 0)
    with jax.named_scope("rest_45_0"):
        advance(pieces[4], 0)
        advance(pieces[5], 0)
    with jax.named_scope("wait_halo"):
        for d in range(1, hops + 1):
            pl.when(seq >= d)(halos[d - 1].wait_recv)

    def halo_rows(i, carry):
        at = pl.ds(pl.multiple_of(i * QB, QB), QB)
        pos = seq * rows - WINDOW + i * QB + lax.broadcasted_iota(jnp.int32, (QB, width), 0)
        block = jnp.where(pos >= 0, halo[at, :].astype(f32), 0.0)
        normed[at, :] = norm_block(block, gain_scr[0:1])
        k_scr[at, :] = project(1, k_scr, at)
        v_scr[at, :] = project(2, v_scr, at)
        return carry

    with jax.named_scope("halo_rows"):
        lax.fori_loop(0, WINDOW // QB, halo_rows, 0)
    with jax.named_scope("rest_45_1"):
        advance(pieces[4], 1)
        advance(pieces[5], 1)
    saved = [
        pltpu.make_async_copy(a, b, out_sem.at[n])
        for n, (a, b) in enumerate(
            zip([q_scr, k_scr, v_scr, normed] + first[:3] + [gain_scr], [q_out, k_out, v_out, n_out] + w_outs)
        )
    ]
    for copy in saved:
        copy.start()

    nq = rows // QB
    span = WINDOW + QB

    def block(step, carry):
        hp, qb = step // nq, lax.rem(step, nq)
        for at in sorted({s for s, _, _ in REST_STEPS}):

            @pl.when(step == at)
            def _():
                if at == 2:
                    advance(pieces[4], 2)
                    advance(pieces[5], 2)
                for _, k, what in [e for e in REST_STEPS if e[0] == at]:
                    with jax.named_scope("rest_%d_%d" % (k, what + 1)):
                        if what < 0:
                            begin(pieces[4 + k])
                        else:
                            advance(pieces[4 + k], what)

        base = pl.multiple_of(qb * QB, QB)

        @pl.when(hp == 0)
        def _():
            pos = seq * rows + base + lax.broadcasted_iota(jnp.int32, (QB, 1), 0)
            lo = lower_bounds(lengths_ref, pos, seq * rows)
            kpos = base + lax.broadcasted_iota(jnp.int32, (QB, span), 1)
            qpos = WINDOW + base + lax.broadcasted_iota(jnp.int32, (QB, span), 0)
            bias[qb] = jnp.where((kpos >= lo) & (kpos <= qpos), 0.0, NEG)

        lanes = pl.ds(pl.multiple_of(hp * 128, 128), 128)
        kw = k_scr[pl.ds(base, span), lanes]
        vw = v_scr[pl.ds(base, span), lanes]
        found, lses = [], []
        for qh in halves(q_scr[pl.ds(base, QB), lanes]):
            s = dot(qh, kw, NT) + bias[qb]
            m = jnp.max(s, axis=1, keepdims=True)
            p = jnp.exp(s - m)
            l = jnp.sum(p, axis=1, keepdims=True)
            found.append(dot(p.astype(bf), vw) * (1.0 / l))
            lses.append(m + jnp.log(l))
        lane = lax.broadcasted_iota(jnp.int32, (QB, 128), 1)
        o_ref[pl.ds(base, QB), lanes] = jnp.where(lane < 64, found[0], found[1]).astype(bf)
        lse_ref[hp, :, pl.ds(base, QB)] = jnp.where(lane == 0, lses[0], lses[1]).T[:8]
        return carry

    with jax.named_scope("attention"):
        lax.fori_loop(0, nq * (width // 128), block, 0)
    with jax.named_scope("rest_end"):
        for k in range(4, 8):
            for piece in pieces[k]:
                piece.finish()
    for d in range(1, hops + 1):
        pl.when(seq + d < count)(halos[d - 1].wait_send)
    for copy in saved:
        copy.wait()


def front(lengths, x, gains, w_qkv, others, dims, count):
    rows, width = x.shape
    shard = w_qkv.shape[1]
    ext = WINDOW + rows
    shapes = [(2 * shard, width)] * 3 + [(16, width)] + [(2 * w.shape[0], w.shape[1]) for w in others]
    hops = -(-WINDOW // rows)
    copies = copies_of(dims)
    vmem = pl.BlockSpec(memory_space=pltpu.VMEM)
    hbm = pl.BlockSpec(memory_space=pl.ANY)
    dma = pltpu.SemaphoreType.DMA
    count_pieces = sum(len(halves_of(s)) for s in shapes)
    nh, nq = width // 128, rows // QB
    sds = jax.ShapeDtypeStruct
    got = pl.pallas_call(
        functools.partial(front_kernel, dims, shapes, count),
        in_specs=[pl.BlockSpec(memory_space=pltpu.SMEM)] + [vmem] * 7,
        out_specs=[vmem] * 2 + [hbm] * 12,
        out_shape=[
            sds((rows, width), bf), sds((nh, 8, rows), f32),
            sds((rows, width), bf), sds((ext, width), bf), sds((ext, width), bf), sds((ext, width), bf),
        ]
        + [sds(dims + shapes[0], bf)] * 3 + [sds((8, width), f32)]
        + [sds(dims + s, bf) for s in shapes[4:]],
        scratch_shapes=[
            pltpu.VMEM((WINDOW, width), bf), pltpu.VMEM((ext, width), bf), pltpu.VMEM((rows, width), bf),
            pltpu.VMEM((ext, width), bf), pltpu.VMEM((ext, width), bf), pltpu.VMEM((8, width), f32),
            pltpu.VMEM((8, width), f32), pltpu.VMEM((nq, QB, WINDOW + QB), f32),
        ]
        + [pltpu.VMEM(s, f32) for s in shapes]
        + [pltpu.VMEM(s, bf) for s in shapes]
        + [pltpu.VMEM(dims + s, bf) for s in shapes[:4]]
        + [
            dma((8,)), dma((8,)), dma((count_pieces, copies)), dma((count_pieces, copies)), dma((8,)),
            dma((hops,)), dma((hops,)), dma((8,)),
        ],
        compiler_params=pltpu.CompilerParams(
            collective_id=1, has_side_effects=True, vmem_limit_bytes=60 * 2**20
        ),
        cost_estimate=pl.CostEstimate(flops=4 * rows * 1792 * 768 * 3, bytes_accessed=14 * 2**20, transcendentals=0),
        name="front",
    )(lengths, x, gains, w_qkv, *others)
    return got


def piece_cuts(shape):
    return [(pl.ds(*rows), pl.ds(*cols)) for rows, cols in halves_of(shape)]


class Collapse:
    def __init__(self, dims, place, shape, turn, grad, out, buffers, send, recv):
        self.dims, self.place, self.shape = dims, place, shape
        self.grad, self.out, self.send, self.recv = grad, out, send, recv
        self.acc, self.box0, self.box1, self.box2, self.box3, self.fin, self.box4 = buffers
        z, y, x, c = place
        far_x, far_y = device_at(dims, (z, y, 1 - x, c)), device_at(dims, (z, 1 - y, x, c))
        every = slice(None)
        by_x = [(far_x, (every, every, 1 - x), (every, every, x)), (far_y, (every, 1 - y, x), (every, y, x))]
        by_y = [(far_y, (every, 1 - y, every), (every, y, every)), (far_x, (every, y, 1 - x), (every, y, x))]
        ways = [by_x, by_y] if turn == 0 else [by_y, by_x]
        self.pieces = list(zip(piece_cuts(shape), ways))

    def columns(self, core):
        half = self.shape[1] // 2
        return pl.ds(pl.multiple_of(core * half, 128), half)

    def copy(self, slot, source, target, device):
        return pltpu.make_async_remote_copy(
            src_ref=source, dst_ref=target, send_sem=self.send.at[slot], recv_sem=self.recv.at[slot],
            device_id=device, device_id_type=MESH,
        )

    def copies(self, stage):
        z, y, x, c = self.place
        mate = device_at(self.dims, sibling(self.place))
        every = slice(None)
        if stage == 0:
            source = self.grad.at[every, every, every, every, self.columns(1 - c)]
            return [self.copy(0, source, self.box0, mate)]
        if stage == 4:
            half = self.shape[0] // 2
            source = self.fin.at[pl.ds(pl.multiple_of((1 - c) * half, 8), half)]
            return [self.copy(1, source, self.box4, mate)]
        made = []
        for at, (cut, ways) in enumerate(self.pieces):
            first = 2 + at * (2 + self.dims[0] - 1)
            if stage in (1, 2):
                device, give, _ = ways[stage - 1]
                box = (self.box1 if stage == 1 else self.box2).at[(every,) * (3 - stage) + cut]
                made.append(self.copy(first + stage - 1, self.acc.at[give + cut], box, device))
            else:
                for by in range(1, self.dims[0]):
                    to = lax.rem(z + by, self.dims[0])
                    made.append(
                        self.copy(
                            first + 1 + by, self.acc.at[(to, y, x) + cut], self.box3.at[(by - 1,) + cut],
                            device_at(self.dims, (to, y, x, c)),
                        )
                    )
        return made

    def local(self, sem):
        every = slice(None)
        source = self.grad.at[every, every, every, every, self.columns(self.place[3])]
        return pltpu.make_async_copy(source, self.acc, sem)

    def start(self, stage):
        for copy in self.copies(stage):
            copy.start()

    def add(self, stage):
        for copy in self.copies(stage):
            copy.wait_recv()
        z, y, x, c = self.place
        dims = self.dims
        if stage == 0:

            def body(i, carry):
                a, b, d = i // (dims[1] * dims[2]), lax.rem(i // dims[2], dims[1]), lax.rem(i, dims[2])
                self.acc[a, b, d] = self.acc[a, b, d] + self.box0[a, b, d]
                return carry

            lax.fori_loop(0, dims[0] * dims[1] * dims[2], body, 0)
        elif stage == 1:
            for cut, ways in self.pieces:
                by_x = not isinstance(ways[0][2][2], slice)

                def body(i, carry):
                    a, b = i // 2, lax.rem(i, 2)
                    at = ((a, b, x) if by_x else (a, y, b)) + cut
                    self.acc[at] = self.acc[at] + self.box1[(a, b) + cut]
                    return carry

                lax.fori_loop(0, dims[0] * 2, body, 0)
        elif stage == 2:

            def body(a, carry):
                self.acc[a, y, x] = self.acc[a, y, x] + self.box2[a]
                return carry

            lax.fori_loop(0, dims[0], body, 0)
        elif stage == 3:
            total = self.acc[z, y, x].astype(f32)
            for by in range(1, dims[0]):
                total = total + self.box3[by - 1].astype(f32)
            self.fin[...] = total
        else:
            half = self.shape[0] // 2
            mine = self.fin[pl.ds(pl.multiple_of(c * half, 8), half)]
            other = self.box4[...]
            width = self.shape[1] // 2
            self.out[:, :width] = jnp.where(c == 0, mine, other)
            self.out[:, width:] = jnp.where(c == 0, other, mine)

    def finish(self):
        for stage in range(5):
            for copy in self.copies(stage):
                copy.wait_send()


def collapse_scratch(dims, shapes):
    found = []
    for rows, cols in shapes:
        half = cols // 2
        found += [
            pltpu.VMEM(dims + (rows, half), bf),
            pltpu.VMEM(dims + (rows, half), bf),
            pltpu.VMEM((dims[0], 2, rows, half), bf),
            pltpu.VMEM((dims[0], rows, half), bf),
            pltpu.VMEM((dims[0] - 1, rows, half), bf),
            pltpu.VMEM((rows, half), f32),
            pltpu.VMEM((rows // 2, half), f32),
        ]
    dma = pltpu.SemaphoreType.DMA
    n = len(shapes)
    slots = 2 + 2 * (2 + dims[0] - 1)
    return found + [dma((n, slots)), dma((n, slots)), dma((n,))]


def collapses_of(dims, place, shapes, grads, outs, scratch):
    n = len(shapes)
    send, recv, local_sem = scratch[7 * n :]
    made = [
        Collapse(dims, place, shapes[k], k % 2, grads[k], outs[k], scratch[7 * k : 7 * k + 7], send.at[k], recv.at[k])
        for k in range(n)
    ]
    return made, [made[k].local(local_sem.at[k]) for k in range(n)]


def run_collapse(sums, locals_, k, stage):
    if stage < 0:
        locals_[k].start()
        sums[k].start(0)
        return
    if stage == 0:
        locals_[k].wait()
    sums[k].add(stage)
    if stage < 4:
        sums[k].start(stage + 1)


SUM_STEPS = (
    (0, 2, -1), (0, 3, -1), (0, 1, -1), (0, 0, -1),
    (3, 2, 0), (6, 3, 0), (8, 2, 1), (10, 2, 2), (10, 1, 0), (10, 0, 0), (11, 3, 1), (13, 3, 2),
    (15, 2, 3), (15, 1, 1), (15, 0, 1), (17, 1, 2), (17, 0, 2), (18, 3, 3), (18, 2, 4), (22, 1, 3), (22, 0, 3), (22, 3, 4),
    (23, 1, 4), (23, 0, 4),
)


def back_block(lo_ref, q_ref, do_ref, o_ref, lse_ref, k_ref, v_ref, dq_ref, dk_ref, dv_ref, bias, dk_acc, dv_acc):
    hp, qb = pl.program_id(0), pl.program_id(1)
    span = WINDOW + QB
    start = pl.multiple_of(qb * QB, QB)

    @pl.when(hp == 0)
    def _():
        base = qb * QB
        kpos = base + lax.broadcasted_iota(jnp.int32, (span, QB), 0)
        qpos = WINDOW + base + lax.broadcasted_iota(jnp.int32, (span, QB), 1)
        ok = (kpos >= lo_ref[...]) & (kpos <= qpos)
        bias[qb] = jnp.where(ok, 0.0, NEG)

    @pl.when(qb == 0)
    def _():
        dk_acc[...] = jnp.zeros_like(dk_acc)
        dv_acc[...] = jnp.zeros_like(dv_acc)

    q_heads = halves(q_ref[...])
    do = do_ref[...]
    d_heads = halves(do)
    prod = do.astype(f32) * o_ref[...].astype(f32)
    row = lax.broadcasted_iota(jnp.int32, (8, 128), 0)
    lane = lax.broadcasted_iota(jnp.int32, (8, 128), 1)
    pick = jnp.where(row == lane // 64, 1.0, 0.0).astype(f32)
    delta = lax.dot_general(pick, prod, NT, precision=lax.Precision.HIGHEST, preferred_element_type=f32)
    lse = lse_ref[0]
    at = pl.ds(start, span)
    kw, vw = k_ref[at, :], v_ref[at, :]
    low_p, low_s, dq = [], [], []
    for h in range(2):
        s = dot(kw, q_heads[h], NT) + bias[qb]
        p = jnp.exp(s - lse[h : h + 1])
        dp = dot(vw, d_heads[h], NT)
        ds = (p * (dp - delta[h : h + 1])).astype(bf)
        low_p.append(p.astype(bf))
        low_s.append(ds)
        dq.append(dot(ds, kw, TN))
    dv_acc[at, :] += dot(jnp.concatenate(low_p, axis=1), jnp.concatenate(d_heads, axis=0))
    dk_acc[at, :] += dot(jnp.concatenate(low_s, axis=1), jnp.concatenate(q_heads, axis=0))
    lane = lax.broadcasted_iota(jnp.int32, (QB, 128), 1)
    dq_ref[...] = (jnp.where(lane < 64, dq[0], dq[1]) * 0.125).astype(bf)

    @pl.when(qb == pl.num_programs(1) - 1)
    def _():
        dk_ref[...] = dk_acc[...].astype(bf)
        dv_ref[...] = dv_acc[...].astype(bf)


def back_sum_kernel(dims, shapes, steps, *refs):
    n = len(shapes)
    ins, grads, refs = refs[:7], refs[7 : 7 + n], refs[7 + n :]
    outs, sums_out, refs = refs[:3], refs[3 : 3 + n], refs[3 + n :]
    own, scratch = refs[:3], refs[3:]
    step = pl.program_id(0) * pl.num_programs(1) + pl.program_id(1)
    if n:
        place = my_place(dims)
        sums, locals_ = collapses_of(dims, place, shapes, grads, sums_out, scratch)
        for at in sorted({s for s, _, _ in steps}):

            @pl.when(step == at)
            def _():
                if at == 0:
                    meet(peers(dims, place))
                for _, k, stage in [e for e in steps if e[0] == at]:
                    with jax.named_scope("reduce_%d_%d" % (k, stage + 1)):
                        run_collapse(sums, locals_, k, stage)

    with jax.named_scope("back_block"):
        back_block(*ins, *outs, *own)
    if n:

        @pl.when(step == pl.num_programs(0) * pl.num_programs(1) - 1)
        def _():
            for one in sums:
                one.finish()


def attend_back(q, do, o, lse, k, v, lo_row, grads=(), dims=None):
    rows, width = q.shape
    ext = k.shape[0]
    nq, nh = rows // QB, width // 128
    n = len(grads)
    shapes = [g.shape[3:] for g in grads]
    blk = pl.BlockSpec((QB, 128), lambda h, i: (i, h))
    full = pl.BlockSpec((ext, 128), lambda h, i: (0, h))
    hbm = pl.BlockSpec(memory_space=pl.ANY)
    whole = [pl.BlockSpec((r // 2, c), lambda h, i: (0, 0)) for r, c in shapes]
    got = pl.pallas_call(
        functools.partial(back_sum_kernel, dims, shapes, SUM_STEPS),
        grid=(nh, nq),
        in_specs=[pl.BlockSpec((1, QB), lambda h, i: (0, i)), blk, blk, blk]
        + [pl.BlockSpec((1, 8, QB), lambda h, i: (h, 0, i)), full, full]
        + [hbm] * n,
        out_specs=[blk, full, full] + whole,
        out_shape=[
            jax.ShapeDtypeStruct((rows, width), bf),
            jax.ShapeDtypeStruct((ext, width), bf),
            jax.ShapeDtypeStruct((ext, width), bf),
        ]
        + [jax.ShapeDtypeStruct((r // 2, c), f32) for r, c in shapes],
        scratch_shapes=[
            pltpu.VMEM((nq, WINDOW + QB, QB), f32),
            pltpu.VMEM((ext, 128), f32),
            pltpu.VMEM((ext, 128), f32),
        ]
        + (collapse_scratch(dims, shapes) if n else []),
        compiler_params=pltpu.CompilerParams(
            vmem_limit_bytes=60 * 2**20, **(dict(collective_id=3, has_side_effects=True) if n else {})
        ),
        cost_estimate=pl.CostEstimate(flops=10 * rows * 1792 * 768 * 3, bytes_accessed=24 * 2**20, transcendentals=0),
        name="attend_back",
    )(lo_row, q, do, o, lse, k, v, *grads)
    return got[:3], got[3:]


ROW_OUT, ROW_UP, ROW_PROJ, ROW_DOWN, ROW_GAIN, ROW_MEAN = 3, 4, 8, 10, 11, 13
STAT_ROWS = 16
DECAY = 1.0 - STEP ** (-0.8)


def pair_partners(dims, place):
    z, y, x, c = place
    found = [sibling(place), (z, y, 1 - x, c), (z, 1 - y, x, c)]
    bit = 1
    while bit < dims[0]:
        low = lax.rem(z // bit, 2)
        found.append((z + bit * (1 - 2 * low), y, x, c))
        bit *= 2
    return [device_at(dims, p) for p in found]


def put_stats(stats, row, total, square_sum, old_rows, lane, columns):
    width = stats.shape[1]
    for j in range(total.shape[1] // width):
        stats[row + j : row + j + 1, :] = total[:, j * width : (j + 1) * width]
    value = DECAY * jnp.sum(old_rows, axis=1, keepdims=True) + (1.0 - DECAY) / columns * square_sum
    at = lax.broadcasted_iota(jnp.int32, (1, width), 1)
    stats[ROW_MEAN : ROW_MEAN + 1, :] += jnp.where(at == lane, value, 0.0)


def last_kernel(
    dims, shapes, count, x_ref, resid_ref, gain_ref, gain_two_ref,
    dq_hbm, dk_hbm, dv_hbm, n_hbm, wq_hbm, wk_hbm, wv_hbm,
    sum_out, sum_proj, sum_up, sum_down, row_qkv, row_out, row_proj, row_up, row_down, *refs,
):
    names = iter(refs)
    take = lambda k: [next(names) for _ in range(k)]
    grad_ref, total_ref = take(2)
    sums_out = take(3)
    dq, dk, dv, normed, flipped, wq, wk, wv = take(8)
    halo_back, own_back, box_near, box_far, stats, inbox = take(6)
    grads = take(3)
    load_sem, back_send, back_recv, stat_send, stat_recv = take(5)
    scratch = list(names)

    place = my_place(dims)
    seq, item = lax.axis_index("seq"), lax.axis_index("item")
    rows, width = x_ref.shape
    boxes = [box_near, box_far]
    hops = len(boxes)
    loads = [
        pltpu.make_async_copy(a, b, load_sem.at[n])
        for n, (a, b) in enumerate(
            [(dk_hbm, dk), (wk_hbm, wk), (dv_hbm, dv), (wv_hbm, wv), (n_hbm, normed), (dq_hbm, dq), (wq_hbm, wq)]
        )
    ]
    for load in loads:
        load.start()
    ahead = [(lax.rem(seq + d, count), item) for d in range(1, hops + 1)]
    behind = [(lax.rem(seq + count - d, count), item) for d in range(1, hops + 1)]
    with jax.named_scope("meet"):
        meet(peers(dims, place) + ahead + behind)
        for load in loads[:4]:
            load.wait()

    returns = []
    upper = WINDOW
    for d in range(1, hops + 1):
        need = boxes[d - 1].shape[0]
        returns.append(
            pltpu.make_async_remote_copy(
                src_ref=halo_back.at[pl.ds(upper - need, need)], dst_ref=boxes[d - 1],
                send_sem=back_send.at[d - 1], recv_sem=back_recv.at[d - 1],
                device_id=behind[d - 1], device_id_type=MESH,
            )
        )
        upper -= need

    def back_of(at):
        return dot(dk[at, :], wk[...].reshape(width, width), NT) + dot(dv[at, :], wv[...].reshape(width, width), NT)

    def halo_block(i, carry):
        at = pl.ds(pl.multiple_of(i * QB, QB), QB)
        halo_back[at, :] = back_of(at).astype(bf)
        return carry

    with jax.named_scope("halo_gradients"):
        upper = WINDOW
        for d in range(1, hops + 1):
            need = boxes[d - 1].shape[0]
            lax.fori_loop((upper - need) // QB, upper // QB, halo_block, 0)
            pl.when(seq >= d)(returns[d - 1].start)
            upper -= need

    sums, locals_ = collapses_of(dims, place, shapes, grads, sums_out, scratch)
    with jax.named_scope("weight_gradients"):
        loads[4].wait()
        flipped[...] = normed[...].T
        for k, part in ((1, dk), (2, dv), (0, dq)):
            if k == 0:
                loads[5].wait()
                loads[6].wait()
            base = WINDOW if k == 0 else 0
            got = dot(flipped[:, base:], part[...])
            grads[k][...] = got.astype(bf).reshape(grads[k].shape)
            run_collapse(sums, locals_, k, -1)

    def own_block(i, carry):
        at = pl.ds(pl.multiple_of(i * QB, QB), QB)
        ext = pl.ds(pl.multiple_of(WINDOW + i * QB, QB), QB)
        own_back[at, :] = back_of(ext) + dot(dq[at, :], wq[...].reshape(width, width), NT)
        return carry

    with jax.named_scope("own_rows"):
        lax.fori_loop(0, rows // QB, own_block, 0)

    stats[0] = jnp.zeros_like(stats[0])
    held = stats.at[0]
    held[ROW_GAIN + 1 : ROW_GAIN + 2, :] = gain_two_ref[...]

    def add_stats(row, grad, old_rows, lane):
        square = grad * grad + TINY_SQUARE
        total = jnp.sum(square, axis=0, keepdims=True)
        put_stats(held, row, total, jnp.sum(total, axis=1, keepdims=True), old_rows, lane, grad.shape[1])

    with jax.named_scope("small_sums"):
        add_stats(ROW_OUT, sum_out[...], row_out[...], 3)
        add_stats(ROW_UP, sum_up[...], row_up[...], 4)
        add_stats(ROW_PROJ, sum_proj[...], row_proj[...], 5)
        add_stats(ROW_DOWN, sum_down[...], row_down[...], 6)

    for stage in range(5):
        with jax.named_scope("reduce_%d" % stage):
            for k in (1, 2, 0):
                run_collapse(sums, locals_, k, stage)
    for k in range(3):
        add_stats(k, sums_out[k][...], row_qkv[k : k + 1, :], k)

    with jax.named_scope("rows_returned"):
        for d in range(1, hops + 1):
            need = boxes[d - 1].shape[0]

            @pl.when(seq + d < count)
            def _():
                returns[d - 1].wait_recv()

                def take_in(i, carry):
                    at = pl.ds(pl.multiple_of(i * QB, QB), QB)
                    to = pl.ds(pl.multiple_of(rows - need + i * QB, QB), QB)
                    own_back[to, :] += boxes[d - 1][at, :].astype(f32)
                    return carry

                lax.fori_loop(0, need // QB, take_in, 0)

    gain = gain_ref[0:1]

    def input_block(i, total):
        at = pl.ds(pl.multiple_of(i * QB, QB), QB)
        x = x_ref[at, :].astype(f32)
        scale = lax.rsqrt(jnp.mean(x * x, axis=-1, keepdims=True) + EPSILON)
        back = own_back[at, :]
        unit = x * scale
        by_gain = back * gain
        inner = jnp.mean(by_gain * unit, axis=-1, keepdims=True)
        grad_ref[at, :] = (resid_ref[at, :] + scale * (by_gain - unit * inner)).astype(bf)
        return total + jnp.sum(back * unit, axis=0, keepdims=True)

    with jax.named_scope("input_gradient"):
        total = lax.fori_loop(0, rows // QB, input_block, jnp.zeros((1, width), f32))
    held[ROW_GAIN : ROW_GAIN + 1, :] = total

    with jax.named_scope("exchange_sums"):
        partners = pair_partners(dims, place)
        for stage, partner in enumerate(partners):
            copy = pltpu.make_async_remote_copy(
                src_ref=stats.at[stage], dst_ref=inbox.at[stage],
                send_sem=stat_send.at[stage], recv_sem=stat_recv.at[stage],
                device_id=partner, device_id_type=MESH,
            )
            copy.start()
            copy.wait()
            stats[stage + 1] = stats[stage] + inbox[stage]

    total_ref[...] = stats[len(partners)]
    for one in sums:
        one.finish()
    for d in range(1, hops + 1):
        pl.when(seq >= d)(returns[d - 1].wait_send)


def last(x, resid_grad, gain, gain_two, dq, dk, dv, normed, weights, sums, old_rows, dims, count):
    rows, width = x.shape
    ext = normed.shape[0]
    shapes = [w.shape[3:] for w in weights]
    hops = -(-WINDOW // rows)
    needs = [min(rows, WINDOW - (d - 1) * rows) for d in range(1, hops + 1)]
    stages = 3 + dims[0].bit_length() - 1
    vmem = pl.BlockSpec(memory_space=pltpu.VMEM)
    hbm = pl.BlockSpec(memory_space=pl.ANY)
    dma = pltpu.SemaphoreType.DMA
    sds = jax.ShapeDtypeStruct
    got = pl.pallas_call(
        functools.partial(last_kernel, dims, shapes, count),
        in_specs=[vmem] * 4 + [hbm] * 7 + [vmem] * 9,
        out_specs=[vmem] * 5,
        out_shape=[sds((rows, width), bf), sds((STAT_ROWS, width), f32)] + [sds((r // 2, c), f32) for r, c in shapes],
        scratch_shapes=[
            pltpu.VMEM((rows, width), bf), pltpu.VMEM((ext, width), bf), pltpu.VMEM((ext, width), bf),
            pltpu.VMEM((ext, width), bf), pltpu.VMEM((width, ext), bf),
        ]
        + [pltpu.VMEM(w.shape, bf) for w in weights]
        + [pltpu.VMEM((WINDOW, width), bf), pltpu.VMEM((rows, width), f32)]
        + [pltpu.VMEM((need, width), bf) for need in needs]
        + [pltpu.VMEM((stages + 1, STAT_ROWS, width), f32), pltpu.VMEM((stages, STAT_ROWS, width), f32)]
        + [pltpu.VMEM(w.shape, bf) for w in weights]
        + [dma((7,)), dma((hops,)), dma((hops,)), dma((stages,)), dma((stages,))]
        + collapse_scratch(dims, shapes),
        compiler_params=pltpu.CompilerParams(
            collective_id=4, has_side_effects=True, vmem_limit_bytes=61 * 2**20
        ),
        name="last",
    )(x, resid_grad, gain, gain_two, dq, dk, dv, normed, *weights, *sums, *old_rows)
    return got[0], got[1], got[2:]


def update_kernel(
    place_ref, total_ref, gains_ref, gain_var_ref,
    w_qkv, w_out, w_proj, w_up, w_down, s_q, s_k, s_v, s_out, s_proj, s_up, s_down,
    row_qkv, row_out, row_proj, row_up, row_down, col_qkv, col_out, col_proj, col_up, col_down,
    g_qkv, g_out, g_proj, g_up, g_down, g_gains, n_qkv, n_out, n_proj, n_up, n_down, n_gains,
    r_qkv, r_out, r_proj, r_up, r_down, c_qkv, c_out, c_proj, c_up, c_down, gain_var_new, flat, tall,
):
    shard = row_out.shape[1]
    shard_down = row_down.shape[1]
    width = total_ref.shape[1]
    flat[...] = jnp.zeros_like(flat)
    flat[0:3, :shard] = row_qkv[...]
    flat[3:4, :shard] = row_out[...]
    flat[4:5, :shard] = row_up[...]
    flat[5:6, :shard] = row_proj[...]
    flat[6:7, :shard_down] = row_down[...]
    olds = flat[...].T
    tall[...] = jnp.zeros_like(tall)

    def one(weight, grad, lane, row, old_col, rows_all, g_out_, n_out_, c_out_):
        count, columns = grad.shape
        square = grad * grad + TINY_SQUARE
        row_new = DECAY * olds[:count, lane : lane + 1] + (1.0 - DECAY) * jnp.mean(square, axis=1, keepdims=True)
        tall[:count, lane : lane + 1] = row_new
        parts = [total_ref[row + j : row + j + 1, :] for j in range(columns // width)]
        col_total = parts[0] if len(parts) == 1 else jnp.concatenate(parts, axis=1)
        col_new = DECAY * old_col + (1.0 - DECAY) * col_total / rows_all
        mean = total_ref[ROW_MEAN : ROW_MEAN + 1, lane : lane + 1] / rows_all
        second = row_new * col_new / mean
        g_out_[...] = grad
        n_out_[...] = weight - WEIGHT_RATE * grad * lax.rsqrt(second)
        c_out_[...] = col_new

    for k, grad in enumerate((s_q, s_k, s_v)):
        one(w_qkv[k], grad[...], k, k, col_qkv[k : k + 1, :], width, g_qkv.at[k], n_qkv.at[k], c_qkv.at[k : k + 1])
    one(w_out[...], s_out[...], 3, ROW_OUT, col_out[...], width, g_out, n_out, c_out)
    one(w_up[...], s_up[...], 4, ROW_UP, col_up[...], width, g_up, n_up, c_up)
    one(w_proj[...], s_proj[...], 5, ROW_PROJ, col_proj[...], width, g_proj, n_proj, c_proj)
    one(w_down[...], s_down[...], 6, ROW_DOWN, col_down[...], col_up.shape[1], g_down, n_down, c_down)
    news = tall[...].T
    r_qkv[...] = news[0:3, :shard]
    r_out[...] = news[3:4, :shard]
    r_up[...] = news[4:5, :shard]
    r_proj[...] = news[5:6, :shard]
    r_down[...] = news[6:7, :shard_down]

    gain_sums = pltpu.roll(total_ref[8:16, :], width - place_ref[0] * shard, 1)
    sums = gain_sums[ROW_GAIN - 8 : ROW_GAIN - 6, :shard]
    var = DECAY * gain_var_ref[...] + (1.0 - DECAY) * (sums * sums + TINY_SQUARE)
    g_gains[...] = sums
    gain_var_new[...] = var
    n_gains[...] = gains_ref[...] - GAIN_RATE * sums * lax.rsqrt(var)


def update(place, totals, gains, gain_var, weights, sums, rows, cols):
    vmem = pl.BlockSpec(memory_space=pltpu.VMEM)
    like = lambda arrays: [jax.ShapeDtypeStruct(a.shape, f32) for a in arrays]
    outs = like(weights) + like([gains]) + like(weights) + like([gains]) + like(rows) + like(cols) + like([gain_var])
    return pl.pallas_call(
        update_kernel,
        in_specs=[pl.BlockSpec(memory_space=pltpu.SMEM)] + [vmem] * (3 + 5 + 7 + 5 + 5),
        out_specs=[vmem] * len(outs),
        out_shape=outs,
        scratch_shapes=[pltpu.VMEM((8, 128), f32), pltpu.VMEM((128, 8), f32)],
        compiler_params=pltpu.CompilerParams(vmem_limit_bytes=32 * 2**20),
        name="update",
    )(place, totals, gains, gain_var, *weights, *sums, *rows, *cols)


def sum_kernel(sizes, x_ref, o_ref, inbox, send_sem, recv_sem):
    place = {name: lax.axis_index(name) for name, _ in sizes}
    partners = []
    for name, size in sizes:
        bit = 1
        while bit < size:
            mine = place[name]
            low = lax.rem(mine // bit, 2)
            other = mine + bit * (1 - 2 * low)
            partners.append(tuple(other if n == name else place[n] for n in ("seq", "item")))
            bit *= 2
    barrier = pltpu.get_barrier_semaphore()
    for partner in partners:
        pl.semaphore_signal(barrier, inc=1, device_id=partner, device_id_type=MESH)
    pl.semaphore_wait(barrier, len(partners))
    o_ref[0] = x_ref[...]
    for stage, partner in enumerate(partners):
        copy = pltpu.make_async_remote_copy(
            src_ref=o_ref.at[stage],
            dst_ref=inbox.at[stage],
            send_sem=send_sem.at[stage],
            recv_sem=recv_sem.at[stage],
            device_id=partner,
            device_id_type=MESH,
        )
        copy.start()
        copy.wait()
        o_ref[stage + 1] = o_ref[stage] + inbox[stage]


def sum_all(x, sizes):
    stages = sum(size.bit_length() - 1 for _, size in sizes)
    held = pl.pallas_call(
        functools.partial(sum_kernel, sizes),
        out_shape=jax.ShapeDtypeStruct((stages + 1,) + x.shape, x.dtype),
        in_specs=[pl.BlockSpec(memory_space=pltpu.VMEM)],
        out_specs=pl.BlockSpec(memory_space=pltpu.VMEM),
        scratch_shapes=[
            pltpu.VMEM((stages,) + x.shape, x.dtype),
            pltpu.SemaphoreType.DMA((stages,)),
            pltpu.SemaphoreType.DMA((stages,)),
        ],
        compiler_params=pltpu.CompilerParams(collective_id=0, has_side_effects=True),
        name="sum_all",
    )(x)
    return held[stages]


def from_behind(block, axis, distance):
    devices = range(lax.axis_size(axis))
    route = [(i - distance, i) for i in devices if i - distance in devices]
    return lax.ppermute(block, axis, route)


def norm_rows(values, gain):
    return values * lax.rsqrt(jnp.mean(values * values, axis=-1, keepdims=True) + EPSILON) * gain


def gelu_tanh(values):
    return (
        0.5
        * values
        * (1.0 + jnp.tanh(0.7978845608028654 * (values + 0.044715 * values * values * values)))
    )


def finish_update(weight, grad, row_new, col_state, col_total, rows_all, row_mean, decay):
    col_new = decay * col_state + (1.0 - decay) * col_total / rows_all
    second = row_new[..., :, None] * col_new[..., None, :] / row_mean
    return (weight - WEIGHT_RATE * grad * lax.rsqrt(second), col_new)


def local(
    byte_rows, item_lengths, cont_mask, bound_mask, out_cot, proj_cot,
    w_qkv, w_out, w_up, w_down, w_proj, gains,
    row_qkv, col_qkv, row_out, col_out, row_up, col_up, row_down, col_down, row_proj, col_proj, gain_var,
):
    sizes = tuple((name, lax.axis_size(name)) for name in ("item", "seq"))
    count = lax.axis_size("item") * lax.axis_size("seq")
    rows_dev, width = byte_rows.shape[1:]
    ff = w_up.shape[1]
    shard = width // count
    low = bf

    dims = grid_of(lax.axis_size("seq"), lax.axis_size("item"))
    paired = shard % 8 == 0 and dims[1:] == (2, 2)
    inputs_low = byte_rows[0]
    inputs = inputs_low.astype(f32)
    if paired:
        got = front(item_lengths, inputs_low, gains, w_qkv, (w_out, w_proj, w_up, w_down), dims, lax.axis_size("seq"))
        attended, lse, queries, ext_keys, ext_values, ext_normed = got[:6]
        split_qkv = got[6:9]
        gain_full = got[9]
        weight_out, weight_proj, weight_up, weight_down = [w.reshape(-1, w.shape[-1]) for w in got[10:]]
    else:
        weight_qkv = lax.all_gather(w_qkv.astype(low), AXES, axis=1, tiled=True)
        gain_full = lax.all_gather(gains.astype(low), AXES, axis=1, tiled=True).astype(f32)
        weight_out, weight_proj, weight_up, weight_down = [
            lax.all_gather(w.astype(low), AXES, axis=0, tiled=True) for w in (w_out, w_proj, w_up, w_down)
        ]

    hop_total = -(-WINDOW // rows_dev)
    offset = lax.axis_index("seq") * rows_dev
    ends = jnp.cumsum(item_lengths[0], dtype=jnp.int32)
    pos = offset + jnp.arange(rows_dev, dtype=jnp.int32)
    begin_at = jnp.max(jnp.where(ends[None, :] <= pos[:, None], ends[None, :], 0), axis=1)
    lo = jnp.maximum(begin_at, pos - WINDOW + 1) - offset + WINDOW
    if not paired:
        halo = []
        for distance in range(hop_total, 0, -1):
            need = min(rows_dev, WINDOW - (distance - 1) * rows_dev)
            halo.append(from_behind(inputs_low[rows_dev - need :], "seq", distance))
        normed = norm_rows(inputs, gain_full[0]).astype(low)
        halo_normed = norm_rows(jnp.concatenate(halo, axis=0).astype(f32), gain_full[0]).astype(low)
        ext_normed = jnp.concatenate([halo_normed, normed], axis=0)
        queries = dot(normed, weight_qkv[0]).astype(low) * jnp.asarray(0.125, low)
        ext_keys = dot(ext_normed, weight_qkv[1]).astype(low)
        ext_values = dot(ext_normed, weight_qkv[2]).astype(low)
        attended, lse = attend(queries, ext_keys, ext_values, lo[:, None])

    resid = inputs + dot(attended, weight_out)
    normed_two = norm_rows(resid, gain_full[1]).astype(low)
    hidden_pre = dot(normed_two, weight_up)
    activated = gelu_tanh(hidden_pre).astype(low)
    output = resid + dot(activated, weight_down)
    output_low = output.astype(low)
    boundary = (bound_mask[0] * (1 - cont_mask[0])).astype(f32)[:, None]
    projected = (boundary * dot(output_low, weight_proj)).astype(low)
    proj_grad = (boundary * proj_cot[0].astype(f32)).astype(low)
    grad_proj = dot(output_low, proj_grad, TN)
    output_grad = out_cot[0].astype(f32) + dot(proj_grad, weight_proj, NT)
    output_grad_low = output_grad.astype(low)
    grad_down = dot(activated, output_grad_low, TN)
    act_grad = dot(output_grad_low, weight_down, NT)
    _, gelu_back = jax.vjp(gelu_tanh, hidden_pre)
    pre_grad = gelu_back(act_grad)[0].astype(low)
    grad_up = dot(normed_two, pre_grad, TN)
    normed_two_grad = dot(pre_grad, weight_up, NT)
    _, norm_two_back = jax.vjp(norm_rows, resid, gain_full[1])
    resid_norm_grad, gain_two_grad = norm_two_back(normed_two_grad)
    resid_grad = output_grad + resid_norm_grad
    resid_grad_low = resid_grad.astype(low)
    grad_out = dot(attended, resid_grad_low, TN)
    attended_grad = dot(resid_grad_low, weight_out, NT).astype(low)

    low_grads = [g.astype(low) for g in (grad_out, grad_proj, grad_up, grad_down)]
    if paired:
        apart = [g.reshape(dims + (-1, g.shape[1])) for g in low_grads]
        (query_grad, ext_key_grad, ext_value_grad), sums = attend_back(
            queries, attended_grad, attended, lse, ext_keys, ext_values, lo[None, :], apart, dims
        )
    else:
        (query_grad, ext_key_grad, ext_value_grad), _ = attend_back(
            queries, attended_grad, attended, lse, ext_keys, ext_values, lo[None, :]
        )
        sums = [lax.psum_scatter(g, AXES, scatter_dimension=0, tiled=True).astype(f32) for g in low_grads]
    sum_out, sum_proj, sum_up, sum_down = sums
    if paired:
        rows = [row_qkv, row_out[None], row_proj[None], row_up[None], row_down[None]]
        cols = [col_qkv, col_out[None], col_proj[None], col_up[None], col_down[None]]
        input_grad, totals, sums_qkv = last(
            inputs_low, resid_grad, gain_full, gain_two_grad[None], query_grad, ext_key_grad, ext_value_grad,
            ext_normed, split_qkv, sums, rows, dims, lax.axis_size("seq"),
        )
        mine = lax.axis_index("seq") * lax.axis_size("item") + lax.axis_index("item")
        done = update(
            mine[None].astype(jnp.int32), totals, gains, gain_var,
            (w_qkv, w_out, w_proj, w_up, w_down), (*sums_qkv, *sums), rows, cols,
        )
        sum_qkv, sum_out, sum_proj, sum_up, sum_down, sum_gains = done[:6]
        new_qkv, new_out, new_proj, new_up, new_down, new_gains = done[6:12]
        row_qkv_new, row_out_new, row_proj_new, row_up_new, row_down_new = [done[12]] + [r[0] for r in done[13:17]]
        col_qkv_new, col_out_new, col_proj_new, col_up_new, col_down_new = [done[17]] + [r[0] for r in done[18:22]]
        gain_var_new = done[22]
        return (
            output_low[None], projected[None], input_grad[None],
            sum_qkv, sum_out, sum_up, sum_down, sum_proj, sum_gains,
            new_qkv, new_out, new_up, new_down, new_proj, new_gains,
            row_qkv_new, col_qkv_new, row_out_new, col_out_new, row_up_new, col_up_new,
            row_down_new, col_down_new, row_proj_new, col_proj_new, gain_var_new,
        )
    ext_back = dot(ext_key_grad, weight_qkv[1], NT) + dot(ext_value_grad, weight_qkv[2], NT)
    halo_back = ext_back[:WINDOW].astype(low)
    grads_qkv = [
        dot(normed, query_grad, TN).astype(low),
        dot(ext_normed, ext_key_grad, TN).astype(low),
        dot(ext_normed, ext_value_grad, TN).astype(low),
    ]
    returned = []
    for distance in range(1, hop_total + 1):
        need = min(rows_dev, WINDOW - (distance - 1) * rows_dev)
        upper = WINDOW - (distance - 1) * rows_dev
        returned.append(from_behind(halo_back[upper - need : upper], "seq", -distance))
    sums = [lax.psum_scatter(g, AXES, scatter_dimension=0, tiled=True).astype(f32) for g in grads_qkv]
    sum_qkv = jnp.stack(sums)
    normed_grad = ext_back[WINDOW:] + dot(query_grad, weight_qkv[0], NT)
    for block in returned:
        need = block.shape[0]
        normed_grad = normed_grad.at[rows_dev - need :].add(block.astype(f32))
    _, norm_one_back = jax.vjp(norm_rows, inputs, gain_full[0])
    input_norm_grad, gain_one_grad = norm_one_back(normed_grad)
    input_grad = (resid_grad + input_norm_grad).astype(low)

    decay = 1.0 - STEP ** (-0.8)
    square_qkv = sum_qkv * sum_qkv + TINY_SQUARE
    square_out = sum_out * sum_out + TINY_SQUARE
    square_up = sum_up * sum_up + TINY_SQUARE
    square_down = sum_down * sum_down + TINY_SQUARE
    square_proj = sum_proj * sum_proj + TINY_SQUARE
    row_qkv_new = decay * row_qkv + (1.0 - decay) * jnp.mean(square_qkv, axis=-1)
    row_out_new = decay * row_out + (1.0 - decay) * jnp.mean(square_out, axis=-1)
    row_up_new = decay * row_up + (1.0 - decay) * jnp.mean(square_up, axis=-1)
    row_down_new = decay * row_down + (1.0 - decay) * jnp.mean(square_down, axis=-1)
    row_proj_new = decay * row_proj + (1.0 - decay) * jnp.mean(square_proj, axis=-1)
    row_sums = jnp.concatenate(
        [
            jnp.sum(row_qkv_new, axis=1),
            jnp.sum(row_out_new)[None],
            jnp.sum(row_up_new)[None],
            jnp.sum(row_down_new)[None],
            jnp.sum(row_proj_new)[None],
        ]
    )
    stats = [
        jnp.sum(square_qkv, axis=1).reshape(-1),
        jnp.sum(square_out, axis=0),
        jnp.sum(square_up, axis=0),
        jnp.sum(square_down, axis=0),
        jnp.sum(square_proj, axis=0),
        gain_one_grad,
        gain_two_grad,
        row_sums,
    ]
    flat = jnp.concatenate(stats)
    used = flat.shape[0]
    padded = -(-used // 1024) * 1024
    flat = jnp.pad(flat, (0, padded - used)).reshape(padded // 128, 128)
    flat = sum_all(flat, sizes).reshape(-1)
    totals, at = [], 0
    for part in stats:
        totals.append(flat[at : at + part.shape[0]])
        at += part.shape[0]
    col_qkv_total, col_out_total, col_up_total, col_down_total, col_proj_total, gain_one, gain_two, row_totals = totals
    col_qkv_total = col_qkv_total.reshape(3, width)
    mine = lax.axis_index("seq") * lax.axis_size("item") + lax.axis_index("item")
    sum_gains = lax.dynamic_slice_in_dim(jnp.stack([gain_one, gain_two]), mine * shard, shard, 1)
    row_counts = jnp.array([width, width, width, width, width, ff, width], f32)
    row_means = row_totals / row_counts
    new_qkv, col_qkv_new = finish_update(
        w_qkv, sum_qkv, row_qkv_new, col_qkv, col_qkv_total, width, row_means[:3][:, None, None], decay
    )
    new_out, col_out_new = finish_update(w_out, sum_out, row_out_new, col_out, col_out_total, width, row_means[3], decay)
    new_up, col_up_new = finish_update(w_up, sum_up, row_up_new, col_up, col_up_total, width, row_means[4], decay)
    new_down, col_down_new = finish_update(
        w_down, sum_down, row_down_new, col_down, col_down_total, ff, row_means[5], decay
    )
    new_proj, col_proj_new = finish_update(
        w_proj, sum_proj, row_proj_new, col_proj, col_proj_total, width, row_means[6], decay
    )
    gain_var_new = decay * gain_var + (1.0 - decay) * (sum_gains * sum_gains + TINY_SQUARE)
    new_gains = gains - GAIN_RATE * sum_gains * lax.rsqrt(gain_var_new)
    return (
        output_low[None], projected[None], input_grad[None],
        sum_qkv, sum_out, sum_up, sum_down, sum_proj, sum_gains,
        new_qkv, new_out, new_up, new_down, new_proj, new_gains,
        row_qkv_new, col_qkv_new, row_out_new, col_out_new, row_up_new, col_up_new,
        row_down_new, col_down_new, row_proj_new, col_proj_new, gain_var_new,
    )


def solution(mesh):
    in_specs = (
        P("item", "seq", None),
        P("item", None),
        P("item", "seq"),
        P("item", "seq"),
        P("item", "seq", None),
        P("item", "seq", None),
        P(None, ("seq", "item"), None),
        P(("seq", "item"), None),
        P(("seq", "item"), None),
        P(("seq", "item"), None),
        P(("seq", "item"), None),
        P(None, ("seq", "item")),
        P(None, ("seq", "item")),
        P(),
        P(("seq", "item")),
        P(),
        P(("seq", "item")),
        P(),
        P(("seq", "item")),
        P(),
        P(("seq", "item")),
        P(),
        P(None, ("seq", "item")),
    )
    out_specs = (
        P("item", "seq", None),
        P("item", "seq", None),
        P("item", "seq", None),
        P(None, ("seq", "item"), None),
        P(("seq", "item"), None),
        P(("seq", "item"), None),
        P(("seq", "item"), None),
        P(("seq", "item"), None),
        P(None, ("seq", "item")),
        P(None, ("seq", "item"), None),
        P(("seq", "item"), None),
        P(("seq", "item"), None),
        P(("seq", "item"), None),
        P(("seq", "item"), None),
        P(None, ("seq", "item")),
        P(None, ("seq", "item")),
        P(),
        P(("seq", "item")),
        P(),
        P(("seq", "item")),
        P(),
        P(("seq", "item")),
        P(),
        P(("seq", "item")),
        P(),
        P(None, ("seq", "item")),
    )
    return jax.shard_map(local, mesh=mesh, in_specs=in_specs, out_specs=out_specs, check_vma=False)
```

```python
import functools
import jax
import jax.numpy as jnp
from jax import lax
from jax.experimental import pallas as pl
from jax.experimental.pallas import tpu as pltpu
from jax.sharding import PartitionSpec as P

WINDOW = 1536
HEADS = 12
NEG = -1e30
EPSILON = 1e-06
TINY_SQUARE = 1e-30
WEIGHT_RATE = 0.02
GAIN_RATE = 0.2
STEP = 10
QB = 256
NT = (((1,), (1,)), ((), ()))
TN = (((0,), (0,)), ((), ()))
f32 = jnp.float32
bf = jnp.bfloat16


def dot(a, b, dims=None):
    if dims is None:
        return jnp.dot(a, b, preferred_element_type=f32)
    return lax.dot_general(a, b, dims, preferred_element_type=f32)


def halves(x):
    lane = lax.broadcasted_iota(jnp.int32, x.shape, 1)
    zero = jnp.zeros_like(x)
    return jnp.where(lane < 64, x, zero), jnp.where(lane < 64, zero, x)


def fwd_kernel(lo_ref, q_ref, k_ref, v_ref, o_ref, lse_ref, bias):
    hp, qb = pl.program_id(0), pl.program_id(1)
    span = WINDOW + QB

    @pl.when(hp == 0)
    def _():
        base = qb * QB
        kpos = base + lax.broadcasted_iota(jnp.int32, (QB, span), 1)
        qpos = WINDOW + base + lax.broadcasted_iota(jnp.int32, (QB, span), 0)
        ok = (kpos >= lo_ref[...]) & (kpos <= qpos)
        bias[qb] = jnp.where(ok, 0.0, NEG)

    start = pl.multiple_of(qb * QB, QB)
    kw = k_ref[pl.ds(start, span), :]
    vw = v_ref[pl.ds(start, span), :]
    outs, lses = [], []
    for qh in halves(q_ref[...]):
        s = dot(qh, kw, NT) + bias[qb]
        m = jnp.max(s, axis=1, keepdims=True)
        p = jnp.exp(s - m)
        l = jnp.sum(p, axis=1, keepdims=True)
        outs.append(dot(p.astype(bf), vw) * (1.0 / l))
        lses.append(m + jnp.log(l))
    lane = lax.broadcasted_iota(jnp.int32, (QB, 128), 1)
    o_ref[...] = jnp.where(lane < 64, outs[0], outs[1]).astype(bf)
    both = jnp.where(lane == 0, lses[0], lses[1])
    lse_ref[0] = both.T[:8]


def attend(q, k, v, lo):
    rows, width = q.shape
    ext = k.shape[0]
    nq, nh = rows // QB, width // 128
    return pl.pallas_call(
        fwd_kernel,
        grid=(nh, nq),
        in_specs=[
            pl.BlockSpec((QB, 1), lambda h, i: (i, 0)),
            pl.BlockSpec((QB, 128), lambda h, i: (i, h)),
            pl.BlockSpec((ext, 128), lambda h, i: (0, h)),
            pl.BlockSpec((ext, 128), lambda h, i: (0, h)),
        ],
        out_specs=[
            pl.BlockSpec((QB, 128), lambda h, i: (i, h)),
            pl.BlockSpec((1, 8, QB), lambda h, i: (h, 0, i)),
        ],
        out_shape=[
            jax.ShapeDtypeStruct((rows, width), bf),
            jax.ShapeDtypeStruct((nh, 8, rows), f32),
        ],
        scratch_shapes=[pltpu.VMEM((nq, QB, WINDOW + QB), f32)],
        compiler_params=pltpu.CompilerParams(vmem_limit_bytes=50 * 2**20),
        cost_estimate=pl.CostEstimate(flops=4 * rows * 1792 * 768 * 3, bytes_accessed=14 * 2**20, transcendentals=0),
        name="attend",
    )(lo, q, k, v)


AXES = ("seq", "item")
MESH = pl.DeviceIdType.MESH


def grid_of(seq, item):
    side = 1
    while side * side * 4 <= seq:
        side *= 2
    return (seq // side, side, item // 2)


def my_place(dims):
    seq, item = lax.axis_index("seq"), lax.axis_index("item")
    return (seq // dims[1], lax.rem(seq, dims[1]), item // 2, lax.rem(item, 2))


def device_at(dims, place):
    z, y, x, c = place
    return (z * dims[1] + y, x * 2 + c)


def moved(dims, place, dim, by):
    to = list(place)
    to[dim] = lax.rem(place[dim] + by, dims[dim])
    return tuple(to)


def sibling(place):
    return place[:3] + (1 - place[3],)


def peers(dims, place):
    found = [sibling(place)]
    for dim in range(3):
        found += [moved(dims, place, dim, by) for by in range(1, dims[dim])]
    return [device_at(dims, p) for p in found]


def meet(targets):
    barrier = pltpu.get_barrier_semaphore()
    for target in targets:
        pl.semaphore_signal(barrier, inc=1, device_id=target, device_id_type=MESH)
    pl.semaphore_wait(barrier, len(targets))


class Spread:
    def __init__(self, dims, place, own, out, rows, cols, order, send, recv):
        self.dims, self.place, self.own, self.out = dims, place, own, out
        self.rows, self.cols, self.order = rows, cols, order
        self.send, self.recv = send, recv

    def span(self, core):
        half = self.out.shape[-1] // 2
        return pl.ds(pl.multiple_of(core * half + self.cols[0], 128), self.cols[1])

    def region(self, stage, by=0, core=None):
        held = self.order[:stage]
        at = []
        for dim in range(3):
            if dim in held:
                at.append(slice(None))
            elif by and dim == self.order[stage]:
                at.append(lax.rem(self.place[dim] + self.dims[dim] - by, self.dims[dim]))
            else:
                at.append(self.place[dim])
        core = self.place[3] if core is None else core
        return self.out.at[tuple(at) + (self.rows, self.span(core))]

    def slots(self, stage):
        first = sum(self.dims[d] - 1 for d in self.order[:stage])
        return [(by, first + by - 1) for by in range(1, self.dims[self.order[stage]])]

    def hops(self, stage):
        for by, slot in self.slots(stage):
            block = self.region(stage)
            source = self.own.at[self.rows, self.span(self.place[3])] if stage == 0 else block
            target = device_at(self.dims, moved(self.dims, self.place, self.order[stage], by))
            yield pltpu.make_async_remote_copy(
                src_ref=source, dst_ref=block, send_sem=self.send.at[slot], recv_sem=self.recv.at[slot],
                device_id=target, device_id_type=MESH,
            )

    def shares(self, stage, core=None):
        count = sum(d - 1 for d in self.dims)
        for by, slot in self.slots(stage):
            block = self.region(stage, by, core)
            yield pltpu.make_async_remote_copy(
                src_ref=block, dst_ref=block, send_sem=self.send.at[count + slot], recv_sem=self.recv.at[count + slot],
                device_id=device_at(self.dims, sibling(self.place)), device_id_type=MESH,
            )

    def start(self):
        for copy in self.hops(0):
            copy.start()

    def advance(self, stage):
        for copy in self.hops(stage):
            copy.wait_recv()
        if stage < 2:
            for copy in self.hops(stage + 1):
                copy.start()
        for copy in self.shares(stage):
            copy.start()

    def finish(self):
        for stage in range(3):
            for copy in self.hops(stage):
                copy.wait_send()
            for copy in self.shares(stage):
                copy.wait_send()
            for copy in self.shares(stage, 1 - self.place[3]):
                copy.wait_recv()


def keep_own(own, out, place, sem):
    return pltpu.make_async_copy(own, out.at[place[0], place[1], place[2]], sem)


def copies_of(dims):
    return 2 * sum(d - 1 for d in dims)


def halves_of(shape):
    rows, cols = shape
    half = cols // 2
    if half % 256 == 0:
        return [((0, rows), (0, half // 2)), ((0, rows), (half // 2, half // 2))]
    cut = rows // 32 * 16
    return [((at, count), (0, half)) for at, count in ((0, cut), (cut, rows - cut)) if count]


ORDERS = ((0, 1, 2), (0, 2, 1))


def pieces_of(dims, place, owns, outs, shapes, send, recv):
    made, at = [], 0
    for k, (own, out, shape) in enumerate(zip(owns, outs, shapes)):
        turn = k % 2
        pieces = []
        for order, (rows, cols) in zip(ORDERS[turn:] + ORDERS[:turn], halves_of(shape)):
            pieces.append(Spread(dims, place, own, out, pl.ds(*rows), cols, order, send.at[at], recv.at[at]))
            at += 1
        made.append(pieces)
    return made


def begin(pieces):
    for piece in pieces:
        piece.start()


def advance(pieces, stage):
    for piece in pieces:
        piece.advance(stage)


def lower_bounds(lengths_ref, pos, offset):
    begin = jnp.zeros_like(pos)
    end = jnp.int32(0)
    for j in range(lengths_ref.shape[1]):
        end = end + lengths_ref[0, j]
        begin = jnp.where(end <= pos, end, begin)
    return jnp.maximum(begin, pos - (WINDOW - 1)) - offset + WINDOW


def norm_block(values, gain):
    x = values.astype(f32)
    return (x * lax.rsqrt(jnp.mean(x * x, axis=-1, keepdims=True) + EPSILON) * gain).astype(bf)


REST_EVENTS = {
    (0, 0): ((0, 0), (1, 0), (2, -1), (3, -1)),
    (1, 0): ((0, 1), (1, 1)),
    (1, 2): ((2, 0), (0, 2), (1, 2)),
    (1, 3): ((3, 0),),
    (1, 4): ((2, 1),),
    (1, 5): ((3, 1), (2, 2)),
}


def front_kernel(dims, shapes, count, lengths_ref, x_ref, gains_ref, qkv_ref, out_ref_, proj_ref, up_ref, down_ref, *refs):
    names = iter(refs)
    take = lambda k: [next(names) for _ in range(k)]
    o_ref, lse_ref, q_out, k_out, v_out, n_out = take(6)
    w_outs = take(4)
    rest_outs = take(4)
    halo, staging, normed, q_scr, k_scr, v_scr, gain_scr, gain_own, bias, o_part, half_stats = take(11)
    wide, blocks = take(8), take(8)
    first = take(4)
    swap_send, swap_recv, send, recv, keep_sem, halo_send, halo_recv, out_sem = take(8)

    place = my_place(dims)
    c = place[3]
    seq, item = lax.axis_index("seq"), lax.axis_index("item")
    rows, width = x_ref.shape
    hops = -(-WINDOW // rows)
    around = [(lax.rem(seq + d, count), item) for d in range(1, hops + 1)]
    behind = [(lax.rem(seq + count - d, count), item) for d in range(1, hops + 1)]
    with jax.named_scope("meet"):
        meet(peers(dims, place) + around + behind)

    mate = device_at(dims, sibling(place))
    shard = gains_ref.shape[1]
    gain_own[...] = jnp.zeros_like(gain_own)
    gain_own[0:2, 0:shard] = gains_ref[...]
    mine = seq * (dims[2] * 2) + item
    gain_own[...] = pltpu.roll(gain_own[...], mine * shard, 1)
    shards = [qkv_ref.at[0], qkv_ref.at[1], qkv_ref.at[2], gain_own, out_ref_, proj_ref, up_ref, down_ref]
    swaps = []
    for k in range(8):
        half = shapes[k][0] // 2
        part = wide[k].at[pl.ds(pl.multiple_of(c * half, 8), half)]
        part[...] = shards[k][...]
        swaps.append(
            pltpu.make_async_remote_copy(
                src_ref=shards[k], dst_ref=part, send_sem=swap_send.at[k], recv_sem=swap_recv.at[k],
                device_id=mate, device_id_type=MESH,
            )
        )
        swaps[k].start()
    outs = first + rest_outs
    keeps = [keep_own(blocks[k], outs[k], place, keep_sem.at[k]) for k in range(8)]
    pieces = pieces_of(dims, place, blocks, outs, shapes, send, recv)

    def ready(k):
        swaps[k].wait()
        blocks[k][...] = wide[k][...].astype(bf)
        keeps[k].start()

    odd = place[1] == 1
    lower, upper = WINDOW - rows, 2 * rows - WINDOW
    part = rows // 4

    def hop(send_slot, slot, source, target, device):
        return pltpu.make_async_remote_copy(
            src_ref=source, dst_ref=target, send_sem=halo_send.at[send_slot], recv_sem=halo_recv.at[slot],
            device_id=device, device_id_type=MESH,
        )

    cuts = [(0, 2 * part), (2 * part, part), (3 * part, part)]
    direct = [
        hop(n, n, x_ref.at[pl.ds(at, size)], halo.at[pl.ds(lower + at, size)], around[0])
        for n, (at, size) in enumerate(cuts)
    ]
    far = hop(3, 3, x_ref.at[pl.ds(upper, lower)], halo.at[pl.ds(0, lower)], around[1])
    aside = hop(4, 4, x_ref.at[pl.ds(0, 2 * part)], staging, behind[0])
    onward = hop(5, 0, staging, halo.at[pl.ds(lower, 2 * part)], around[1])
    has_next, has_far = seq + 1 < count, seq + 2 < count
    odd_next = jnp.logical_and(odd, has_next)
    even_next = jnp.logical_and(jnp.logical_not(odd), has_next)
    relays = jnp.logical_and(jnp.logical_not(odd), has_far)

    with jax.named_scope("swap"):
        for k in (3, 0, 1, 2):
            ready(k)
            begin(pieces[k])
        pl.when(odd_next)(aside.start)
        pl.when(even_next)(direct[2].start)
    with jax.named_scope("swap_rest"):
        for k in (4, 5, 6, 7):
            ready(k)
        for k in range(8):
            keeps[k].wait()
    with jax.named_scope("first_0"):
        for k in (3, 0, 1, 2):
            advance(pieces[k], 0)
        begin(pieces[4])
        begin(pieces[5])
    with jax.named_scope("first_1"):
        for k in (3, 0, 1, 2):
            advance(pieces[k], 1)
        pl.when(has_far)(far.start)
        pl.when(has_next)(direct[1].start)
        pl.when(odd_next)(direct[2].start)
        pl.when(even_next)(direct[0].start)
    with jax.named_scope("relay"):

        @pl.when(relays)
        def _():
            aside.wait_recv()
            onward.start()

    with jax.named_scope("first_2"):
        for k in (3, 0, 1, 2):
            advance(pieces[k], 2)
    with jax.named_scope("first_end"):
        for k in range(4):
            for piece in pieces[k]:
                piece.finish()
    total = first[3][...].astype(f32).reshape(dims[0] * dims[1] * dims[2] * 2, 8, width)
    gain_scr[...] = jnp.sum(total, axis=0)

    weights = [first[k] for k in range(3)]

    def project(slot, at):
        return dot(normed[at, :], weights[slot][...].reshape(width, width)).astype(bf)

    def own_rows(i, carry):
        at = pl.ds(pl.multiple_of(i * QB, QB), QB)
        ext = pl.ds(pl.multiple_of(WINDOW + i * QB, QB), QB)
        normed[ext, :] = norm_block(x_ref[at, :], gain_scr[0:1])
        q_scr[at, :] = project(0, ext) * jnp.asarray(0.125, bf)
        k_scr[ext, :] = project(1, ext)
        v_scr[ext, :] = project(2, ext)
        return carry

    def halo_rows(i, carry):
        at = pl.ds(pl.multiple_of(i * QB, QB), QB)
        pos = seq * rows - WINDOW + i * QB + lax.broadcasted_iota(jnp.int32, (QB, width), 0)
        block = jnp.where(pos >= 0, halo[at, :].astype(f32), 0.0)
        normed[at, :] = norm_block(block, gain_scr[0:1])
        k_scr[at, :] = project(1, at)
        v_scr[at, :] = project(2, at)
        return carry

    nq, pairs = rows // QB, width // 128

    def events(stage, hp):
        for (when, pair), moves in REST_EVENTS.items():
            if when != stage:
                continue

            @pl.when(hp == pair)
            def _():
                for k, what in moves:
                    with jax.named_scope("rest_%d_%d" % (k, what + 1)):
                        if what < 0:
                            begin(pieces[4 + k])
                        else:
                            advance(pieces[4 + k], what)

    lane = lax.broadcasted_iota(jnp.int32, (QB, 128), 1)

    def masks(qb):
        pos = seq * rows + qb * QB + lax.broadcasted_iota(jnp.int32, (QB, 1), 0)
        lo = lower_bounds(lengths_ref, pos, seq * rows)
        kpos = qb * QB + lax.broadcasted_iota(jnp.int32, (QB, WINDOW + QB), 1)
        qpos = WINDOW + qb * QB + lax.broadcasted_iota(jnp.int32, (QB, WINDOW + QB), 0)
        bias[qb] = jnp.where((kpos >= lo) & (kpos <= qpos), 0.0, NEG)

    def own_keys(hp, carry):
        events(0, hp)
        lanes = pl.ds(pl.multiple_of(hp * 128, 128), 128)
        for qb in range(nq):
            at, keys = pl.ds(qb * QB, QB), pl.ds(WINDOW, (qb + 1) * QB)
            kw, vw = k_scr[keys, lanes], v_scr[keys, lanes]
            found, held = [], []
            for qh in halves(q_scr[at, lanes]):
                s = dot(qh, kw, NT) + bias[qb, :, WINDOW - qb * QB :]
                m = jnp.max(s, axis=1, keepdims=True)
                p = jnp.exp(s - m)
                held += [m, jnp.sum(p, axis=1, keepdims=True)]
                found.append(dot(p.astype(bf), vw))
            o_part[at, lanes] = jnp.where(lane < 64, found[0], found[1])
            half_stats[hp, at, :] = jnp.where(
                lane < 2, jnp.where(lane == 0, held[0], held[1]), jnp.where(lane == 2, held[2], held[3])
            )
        return carry

    def halo_keys(hp, carry):
        events(1, hp)
        lanes = pl.ds(pl.multiple_of(hp * 128, 128), 128)
        for qb in range(nq):
            at, keys = pl.ds(qb * QB, QB), pl.ds(qb * QB, WINDOW - qb * QB)
            kw, vw = k_scr[keys, lanes], v_scr[keys, lanes]
            before = half_stats[hp, at, :]
            found, olds, scales, lses = [], [], [], []
            for h, qh in enumerate(halves(q_scr[at, lanes])):
                s = dot(qh, kw, NT) + bias[qb, :, : WINDOW - qb * QB]
                m_own, l_own = before[:, 2 * h : 2 * h + 1], before[:, 2 * h + 1 : 2 * h + 2]
                m = jnp.maximum(m_own, jnp.max(s, axis=1, keepdims=True))
                p = jnp.exp(s - m)
                alpha = jnp.exp(m_own - m)
                l = l_own * alpha + jnp.sum(p, axis=1, keepdims=True)
                found.append(dot(p.astype(bf), vw))
                olds.append(alpha)
                scales.append(1.0 / l)
                lses.append(m + jnp.log(l))
            low_half = lane < 64
            mixed = o_part[at, lanes] * jnp.where(low_half, olds[0], olds[1]) + jnp.where(low_half, found[0], found[1])
            o_ref[at, lanes] = (mixed * jnp.where(low_half, scales[0], scales[1])).astype(bf)
            lse_ref[hp, :, at] = jnp.where(lane == 0, lses[0], lses[1]).T[:8]
        return carry

    with jax.named_scope("own_rows"):
        lax.fori_loop(0, nq, own_rows, 0)
        for qb in range(nq):
            masks(qb)
    with jax.named_scope("own_keys"):
        lax.fori_loop(0, pairs, own_keys, 0)
    with jax.named_scope("wait_halo"):

        @pl.when(seq >= 1)
        def _():
            for copy in direct:
                copy.wait_recv()

        pl.when(seq >= 2)(far.wait_recv)
    with jax.named_scope("halo_rows"):
        lax.fori_loop(0, WINDOW // QB, halo_rows, 0)
    saved = [
        pltpu.make_async_copy(a, b, out_sem.at[n])
        for n, (a, b) in enumerate(
            zip([q_scr, k_scr, v_scr, normed] + first[:3] + [gain_scr], [q_out, k_out, v_out, n_out] + w_outs)
        )
    ]
    for copy in saved:
        copy.start()
    with jax.named_scope("halo_keys"):
        lax.fori_loop(0, pairs, halo_keys, 0)
    with jax.named_scope("rest_end"):
        advance(pieces[7], 2)
        for k in range(4, 8):
            for piece in pieces[k]:
                piece.finish()
        pl.when(has_far)(far.wait_send)
        pl.when(has_next)(direct[1].wait_send)
        pl.when(has_next)(direct[2].wait_send)
        pl.when(even_next)(direct[0].wait_send)
        pl.when(odd_next)(aside.wait_send)
        pl.when(relays)(onward.wait_send)
        for copy in saved:
            copy.wait()


def front(lengths, x, gains, w_qkv, others, dims, count):
    rows, width = x.shape
    shard = w_qkv.shape[1]
    ext = WINDOW + rows
    shapes = [(2 * shard, width)] * 3 + [(16, width)] + [(2 * w.shape[0], w.shape[1]) for w in others]
    copies = copies_of(dims)
    vmem = pl.BlockSpec(memory_space=pltpu.VMEM)
    hbm = pl.BlockSpec(memory_space=pl.ANY)
    dma = pltpu.SemaphoreType.DMA
    count_pieces = sum(len(halves_of(s)) for s in shapes)
    nh, nq = width // 128, rows // QB
    sds = jax.ShapeDtypeStruct
    got = pl.pallas_call(
        functools.partial(front_kernel, dims, shapes, count),
        in_specs=[pl.BlockSpec(memory_space=pltpu.SMEM)] + [vmem] * 7,
        out_specs=[vmem] * 2 + [hbm] * 12,
        out_shape=[
            sds((rows, width), bf), sds((nh, 8, rows), f32),
            sds((rows, width), bf), sds((ext, width), bf), sds((ext, width), bf), sds((ext, width), bf),
        ]
        + [sds(dims + shapes[0], bf)] * 3 + [sds((8, width), f32)]
        + [sds(dims + s, bf) for s in shapes[4:]],
        scratch_shapes=[
            pltpu.VMEM((WINDOW, width), bf), pltpu.VMEM((rows // 2, width), bf), pltpu.VMEM((ext, width), bf),
            pltpu.VMEM((rows, width), bf),
            pltpu.VMEM((ext, width), bf), pltpu.VMEM((ext, width), bf), pltpu.VMEM((8, width), f32),
            pltpu.VMEM((8, width), f32), pltpu.VMEM((nq, QB, WINDOW + QB), f32),
            pltpu.VMEM((rows, width), f32), pltpu.VMEM((nh, rows, 128), f32),
        ]
        + [pltpu.VMEM(s, f32) for s in shapes]
        + [pltpu.VMEM(s, bf) for s in shapes]
        + [pltpu.VMEM(dims + s, bf) for s in shapes[:4]]
        + [
            dma((8,)), dma((8,)), dma((count_pieces, copies)), dma((count_pieces, copies)), dma((8,)),
            dma((6,)), dma((5,)), dma((8,)),
        ],
        compiler_params=pltpu.CompilerParams(
            collective_id=1, has_side_effects=True, vmem_limit_bytes=60 * 2**20
        ),
        cost_estimate=pl.CostEstimate(flops=4 * rows * 1792 * 768 * 3, bytes_accessed=14 * 2**20, transcendentals=0),
        name="front",
    )(lengths, x, gains, w_qkv, *others)
    return got


def piece_cuts(shape):
    return [(pl.ds(*rows), pl.ds(*cols)) for rows, cols in halves_of(shape)]


class Collapse:
    def __init__(self, dims, place, shape, turn, grad, out, buffers, send, recv):
        self.dims, self.place, self.shape = dims, place, shape
        self.grad, self.out, self.send, self.recv = grad, out, send, recv
        self.acc, self.box0, self.box1, self.box2, self.box3, self.fin, self.box4 = buffers
        z, y, x, c = place
        far_x, far_y = device_at(dims, (z, y, 1 - x, c)), device_at(dims, (z, 1 - y, x, c))
        every = slice(None)
        by_x = [(far_x, (every, every, 1 - x), (every, every, x)), (far_y, (every, 1 - y, x), (every, y, x))]
        by_y = [(far_y, (every, 1 - y, every), (every, y, every)), (far_x, (every, y, 1 - x), (every, y, x))]
        ways = [by_x, by_y] if turn == 0 else [by_y, by_x]
        self.pieces = list(zip(piece_cuts(shape), ways))

    def columns(self, core):
        half = self.shape[1] // 2
        return pl.ds(pl.multiple_of(core * half, 128), half)

    def copy(self, slot, source, target, device):
        return pltpu.make_async_remote_copy(
            src_ref=source, dst_ref=target, send_sem=self.send.at[slot], recv_sem=self.recv.at[slot],
            device_id=device, device_id_type=MESH,
        )

    def copies(self, stage):
        z, y, x, c = self.place
        mate = device_at(self.dims, sibling(self.place))
        every = slice(None)
        if stage == 0:
            source = self.grad.at[every, every, every, every, self.columns(1 - c)]
            return [self.copy(0, source, self.box0, mate)]
        if stage == 4:
            half = self.shape[0] // 2
            source = self.fin.at[pl.ds(pl.multiple_of((1 - c) * half, 8), half)]
            return [self.copy(1, source, self.box4, mate)]
        made = []
        for at, (cut, ways) in enumerate(self.pieces):
            first = 2 + at * (2 + self.dims[0] - 1)
            if stage in (1, 2):
                device, give, _ = ways[stage - 1]
                box = (self.box1 if stage == 1 else self.box2).at[(every,) * (3 - stage) + cut]
                made.append(self.copy(first + stage - 1, self.acc.at[give + cut], box, device))
            else:
                for by in range(1, self.dims[0]):
                    to = lax.rem(z + by, self.dims[0])
                    made.append(
                        self.copy(
                            first + 1 + by, self.acc.at[(to, y, x) + cut], self.box3.at[(by - 1,) + cut],
                            device_at(self.dims, (to, y, x, c)),
                        )
                    )
        return made

    def local(self, sem):
        every = slice(None)
        source = self.grad.at[every, every, every, every, self.columns(self.place[3])]
        return pltpu.make_async_copy(source, self.acc, sem)

    def start(self, stage):
        for copy in self.copies(stage):
            copy.start()

    def add(self, stage):
        for copy in self.copies(stage):
            copy.wait_recv()
        z, y, x, c = self.place
        dims = self.dims
        if stage == 0:

            def body(i, carry):
                a, b, d = i // (dims[1] * dims[2]), lax.rem(i // dims[2], dims[1]), lax.rem(i, dims[2])
                self.acc[a, b, d] = self.acc[a, b, d] + self.box0[a, b, d]
                return carry

            lax.fori_loop(0, dims[0] * dims[1] * dims[2], body, 0)
        elif stage == 1:
            for cut, ways in self.pieces:
                by_x = not isinstance(ways[0][2][2], slice)

                def body(i, carry):
                    a, b = i // 2, lax.rem(i, 2)
                    at = ((a, b, x) if by_x else (a, y, b)) + cut
                    self.acc[at] = self.acc[at] + self.box1[(a, b) + cut]
                    return carry

                lax.fori_loop(0, dims[0] * 2, body, 0)
        elif stage == 2:

            def body(a, carry):
                self.acc[a, y, x] = self.acc[a, y, x] + self.box2[a]
                return carry

            lax.fori_loop(0, dims[0], body, 0)
        elif stage == 3:
            total = self.acc[z, y, x].astype(f32)
            for by in range(1, dims[0]):
                total = total + self.box3[by - 1].astype(f32)
            self.fin[...] = total
        else:
            half = self.shape[0] // 2
            mine = self.fin[pl.ds(pl.multiple_of(c * half, 8), half)]
            other = self.box4[...]
            width = self.shape[1] // 2
            self.out[:, :width] = jnp.where(c == 0, mine, other)
            self.out[:, width:] = jnp.where(c == 0, other, mine)

    def finish(self):
        for stage in range(5):
            for copy in self.copies(stage):
                copy.wait_send()


def collapse_scratch(dims, shapes):
    found = []
    for rows, cols in shapes:
        half = cols // 2
        found += [
            pltpu.VMEM(dims + (rows, half), bf),
            pltpu.VMEM(dims + (rows, half), bf),
            pltpu.VMEM((dims[0], 2, rows, half), bf),
            pltpu.VMEM((dims[0], rows, half), bf),
            pltpu.VMEM((dims[0] - 1, rows, half), bf),
            pltpu.VMEM((rows, half), f32),
            pltpu.VMEM((rows // 2, half), f32),
        ]
    dma = pltpu.SemaphoreType.DMA
    n = len(shapes)
    slots = 2 + 2 * (2 + dims[0] - 1)
    return found + [dma((n, slots)), dma((n, slots)), dma((n,))]


def collapses_of(dims, place, shapes, grads, outs, scratch):
    n = len(shapes)
    send, recv, local_sem = scratch[7 * n :]
    made = [
        Collapse(dims, place, shapes[k], k % 2, grads[k], outs[k], scratch[7 * k : 7 * k + 7], send.at[k], recv.at[k])
        for k in range(n)
    ]
    return made, [made[k].local(local_sem.at[k]) for k in range(n)]


def run_collapse(sums, locals_, k, stage):
    if stage < 0:
        locals_[k].start()
        sums[k].start(0)
        return
    if stage == 0:
        locals_[k].wait()
    sums[k].add(stage)
    if stage < 4:
        sums[k].start(stage + 1)


def back_kernel(lo_ref, q_ref, do_ref, o_ref, lse_ref, k_ref, v_ref, dq_ref, dk_ref, dv_ref, bias, dk_acc, dv_acc):
    hp, qb = pl.program_id(0), pl.program_id(1)
    span = WINDOW + QB
    start = pl.multiple_of(qb * QB, QB)

    @pl.when(hp == 0)
    def _():
        base = qb * QB
        kpos = base + lax.broadcasted_iota(jnp.int32, (span, QB), 0)
        qpos = WINDOW + base + lax.broadcasted_iota(jnp.int32, (span, QB), 1)
        ok = (kpos >= lo_ref[...]) & (kpos <= qpos)
        bias[qb] = jnp.where(ok, 0.0, NEG)

    @pl.when(qb == 0)
    def _():
        dk_acc[...] = jnp.zeros_like(dk_acc)
        dv_acc[...] = jnp.zeros_like(dv_acc)

    q_heads = halves(q_ref[...])
    do = do_ref[...]
    d_heads = halves(do)
    prod = do.astype(f32) * o_ref[...].astype(f32)
    row = lax.broadcasted_iota(jnp.int32, (8, 128), 0)
    lane = lax.broadcasted_iota(jnp.int32, (8, 128), 1)
    pick = jnp.where(row == lane // 64, 1.0, 0.0).astype(f32)
    delta = lax.dot_general(pick, prod, NT, precision=lax.Precision.HIGHEST, preferred_element_type=f32)
    lse = lse_ref[0]
    at = pl.ds(start, span)
    kw, vw = k_ref[at, :], v_ref[at, :]
    low_p, low_s, dq = [], [], []
    for h in range(2):
        s = dot(kw, q_heads[h], NT) + bias[qb]
        p = jnp.exp(s - lse[h : h + 1])
        dp = dot(vw, d_heads[h], NT)
        ds = (p * (dp - delta[h : h + 1])).astype(bf)
        low_p.append(p.astype(bf))
        low_s.append(ds)
        dq.append(dot(ds, kw, TN))
    dv_acc[at, :] += dot(jnp.concatenate(low_p, axis=1), jnp.concatenate(d_heads, axis=0))
    dk_acc[at, :] += dot(jnp.concatenate(low_s, axis=1), jnp.concatenate(q_heads, axis=0))
    lane = lax.broadcasted_iota(jnp.int32, (QB, 128), 1)
    dq_ref[...] = (jnp.where(lane < 64, dq[0], dq[1]) * 0.125).astype(bf)

    @pl.when(qb == pl.num_programs(1) - 1)
    def _():
        dk_ref[...] = dk_acc[...].astype(bf)
        dv_ref[...] = dv_acc[...].astype(bf)


def attend_back(q, do, o, lse, k, v, lo_row):
    rows, width = q.shape
    ext = k.shape[0]
    nq, nh = rows // QB, width // 128
    blk = pl.BlockSpec((QB, 128), lambda h, i: (i, h))
    full = pl.BlockSpec((ext, 128), lambda h, i: (0, h))
    return pl.pallas_call(
        back_kernel,
        grid=(nh, nq),
        in_specs=[pl.BlockSpec((1, QB), lambda h, i: (0, i)), blk, blk, blk]
        + [pl.BlockSpec((1, 8, QB), lambda h, i: (h, 0, i)), full, full],
        out_specs=[blk, full, full],
        out_shape=[
            jax.ShapeDtypeStruct((rows, width), bf),
            jax.ShapeDtypeStruct((ext, width), bf),
            jax.ShapeDtypeStruct((ext, width), bf),
        ],
        scratch_shapes=[
            pltpu.VMEM((nq, WINDOW + QB, QB), f32),
            pltpu.VMEM((ext, 128), f32),
            pltpu.VMEM((ext, 128), f32),
        ],
        compiler_params=pltpu.CompilerParams(vmem_limit_bytes=56 * 2**20),
        name="attend_back",
    )(lo_row, q, do, o, lse, k, v)


SUM_EVENTS = {
    (0, 1): ((2, 0),),
    (0, 3): ((2, 1), (1, 0), (0, 0)),
    (0, 4): ((2, 2),),
    (1, 2): ((1, 2), (0, 2), (2, 3)),
    (1, 5): ((2, 4),),
}


def back_kernel_paired(dims, shapes, count, lengths_ref, lse_ref, delta_ref, *refs):
    n = len(shapes)
    names = iter(refs)
    take = lambda k: [next(names) for _ in range(k)]
    sources = take(6)
    grads = take(n)
    dq_out, dk_out, dv_out, near_out, rest_out = take(5)
    sums_out = take(n)
    q, do, k, v, wk, wv = buffers = take(6)
    dk, dv, dq_acc, dk_acc, dv_acc, bias = take(6)
    load_sem, out_sem, back_send, back_recv = take(4)
    scratch = list(names)

    place = my_place(dims)
    seq, item = lax.axis_index("seq"), lax.axis_index("item")
    rows, width = q.shape
    nq, pairs = rows // QB, width // 128
    loads = [pltpu.make_async_copy(a, b, load_sem.at[m]) for m, (a, b) in enumerate(zip(sources, buffers))]
    for load in loads:
        load.start()
    ahead, behind = (lax.rem(seq + 1, count), item), (lax.rem(seq + count - 1, count), item)
    with jax.named_scope("meet"):
        meet(peers(dims, place) + [ahead, behind])
    sums, locals_ = collapses_of(dims, place, shapes, grads, sums_out, scratch)
    for a in (2, 1, 0):
        run_collapse(sums, locals_, a, -1)

    with jax.named_scope("masks"):
        for qb in range(nq):
            pos = seq * rows + qb * QB + lax.broadcasted_iota(jnp.int32, (1, QB), 1)
            lo = lower_bounds(lengths_ref, pos, seq * rows)
            kpos = qb * QB + lax.broadcasted_iota(jnp.int32, (WINDOW + QB, QB), 0)
            qpos = WINDOW + qb * QB + lax.broadcasted_iota(jnp.int32, (WINDOW + QB, QB), 1)
            bias[qb] = jnp.where((kpos >= lo) & (kpos <= qpos), 0.0, NEG).astype(bf)
    with jax.named_scope("load"):
        for load in loads:
            load.wait()

    def events(part, hp):
        for (when, pair), moves in SUM_EVENTS.items():
            if when != part:
                continue

            @pl.when(hp == pair)
            def _():
                for a, stage in moves:
                    with jax.named_scope("reduce_%d_%d" % (a, stage + 1)):
                        run_collapse(sums, locals_, a, stage)

    lane = lax.broadcasted_iota(jnp.int32, (QB, 128), 1)

    def block(hp, lanes, at, keys, mask):
        q_heads, d_heads = halves(q[at, lanes]), halves(do[at, lanes])
        lse, delta = lse_ref[hp, :, at], delta_ref[hp, :, at]
        kw, vw = k[keys, lanes], v[keys, lanes]
        low_p, low_s, found = [], [], []
        for h in range(2):
            s = dot(kw, q_heads[h], NT) + mask.astype(f32)
            p = jnp.exp(s - lse[h : h + 1])
            dp = dot(vw, d_heads[h], NT)
            ds = (p * (dp - delta[h : h + 1])).astype(bf)
            low_p.append(p.astype(bf))
            low_s.append(ds)
            found.append(dot(ds, kw, TN))
        dv_part = dot(jnp.concatenate(low_p, axis=1), jnp.concatenate(d_heads, axis=0))
        dk_part = dot(jnp.concatenate(low_s, axis=1), jnp.concatenate(q_heads, axis=0))
        return jnp.where(lane < 64, found[0], found[1]), dk_part, dv_part

    def halo_keys(hp, carry):
        events(0, hp)
        lanes = pl.ds(pl.multiple_of(hp * 128, 128), 128)
        for qb in range(nq):
            at, size = pl.ds(qb * QB, QB), WINDOW - qb * QB
            keys = pl.ds(qb * QB, size)
            dq_part, dk_part, dv_part = block(hp, lanes, at, keys, bias[qb, :size, :])
            dq_acc[at, lanes] = dq_part
            if qb == 0:
                dk_acc[...] = dk_part
                dv_acc[...] = dv_part
            else:
                dk_acc[keys, :] += dk_part
                dv_acc[keys, :] += dv_part
        dk[0:WINDOW, lanes] = dk_acc[...].astype(bf)
        dv[0:WINDOW, lanes] = dv_acc[...].astype(bf)
        return carry

    with jax.named_scope("halo_keys"):
        lax.fori_loop(0, pairs, halo_keys, 0)

    def halo_rows(i, carry):
        at = pl.ds(pl.multiple_of(i * QB, QB), QB)
        total = dot(dk[at, :], wk[...].reshape(width, width), NT) + dot(dv[at, :], wv[...].reshape(width, width), NT)
        k[at, :] = total.astype(bf)
        return carry

    lower, part = WINDOW - rows, rows // 4
    returned = pltpu.make_async_remote_copy(
        src_ref=k.at[pl.ds(lower, part)], dst_ref=near_out, send_sem=back_send.at[0], recv_sem=back_recv.at[0],
        device_id=behind, device_id_type=MESH,
    )
    for a in (1, 0):
        with jax.named_scope("reduce_%d_2" % a):
            run_collapse(sums, locals_, a, 1)
    with jax.named_scope("halo_rows"):
        lax.fori_loop(lower // QB, (lower + part) // QB, halo_rows, 0)
        pl.when(seq >= 1)(returned.start)
        lax.fori_loop(0, lower // QB, halo_rows, 0)
        lax.fori_loop((lower + part) // QB, WINDOW // QB, halo_rows, 0)
        rest = [
            pltpu.make_async_copy(k.at[pl.ds(0, lower)], rest_out.at[pl.ds(0, lower)], out_sem.at[0]),
            pltpu.make_async_copy(
                k.at[pl.ds(lower + part, rows - part)], rest_out.at[pl.ds(lower, rows - part)], out_sem.at[1]
            ),
        ]
        for copy in rest:
            copy.start()

    def own_keys(hp, carry):
        events(1, hp)
        lanes = pl.ds(pl.multiple_of(hp * 128, 128), 128)
        for qb in reversed(range(nq)):
            at, size = pl.ds(qb * QB, QB), (qb + 1) * QB
            keys, own = pl.ds(WINDOW, size), pl.ds(0, size)
            dq_part, dk_part, dv_part = block(hp, lanes, at, keys, bias[qb, WINDOW - qb * QB :, :])
            q[at, lanes] = ((dq_acc[at, lanes] + dq_part) * 0.125).astype(bf)
            if qb == nq - 1:
                dk_acc[own, :] = dk_part
                dv_acc[own, :] = dv_part
            else:
                dk_acc[own, :] += dk_part
                dv_acc[own, :] += dv_part
        dk[WINDOW:, lanes] = dk_acc[0:rows, :].astype(bf)
        dv[WINDOW:, lanes] = dv_acc[0:rows, :].astype(bf)
        return carry

    with jax.named_scope("own_keys"):
        lax.fori_loop(0, pairs, own_keys, 0)
    stores = rest + [
        pltpu.make_async_copy(a, b, out_sem.at[2 + m]) for m, (a, b) in enumerate([(q, dq_out), (dk, dk_out), (dv, dv_out)])
    ]
    for store in stores[2:]:
        store.start()
    with jax.named_scope("finish"):
        for stage in (3, 4):
            for a in (1, 0):
                run_collapse(sums, locals_, a, stage)
        for one in sums:
            one.finish()
        for store in stores:
            store.wait()

        pl.when(seq >= 1)(returned.wait_send)
        pl.when(seq + 1 < count)(returned.wait_recv)


def back(lengths, lse, delta, arrays, grads, dims, count):
    q, do, k, v, wk, wv = arrays
    rows, width = q.shape
    ext = k.shape[0]
    nq = rows // QB
    shapes = [g.shape[3:] for g in grads]
    vmem = pl.BlockSpec(memory_space=pltpu.VMEM)
    hbm = pl.BlockSpec(memory_space=pl.ANY)
    dma = pltpu.SemaphoreType.DMA
    sds = jax.ShapeDtypeStruct
    part = rows // 4
    got = pl.pallas_call(
        functools.partial(back_kernel_paired, dims, shapes, count),
        in_specs=[pl.BlockSpec(memory_space=pltpu.SMEM), vmem, vmem] + [hbm] * (6 + len(grads)),
        out_specs=[hbm] * 5 + [vmem] * len(grads),
        out_shape=[
            sds((rows, width), bf), sds((ext, width), bf), sds((ext, width), bf),
            sds((part, width), bf), sds((WINDOW - part, width), bf),
        ]
        + [sds((r // 2, c), f32) for r, c in shapes],
        scratch_shapes=[pltpu.VMEM(a.shape, bf) for a in arrays]
        + [
            pltpu.VMEM((ext, width), bf), pltpu.VMEM((ext, width), bf), pltpu.VMEM((rows, width), f32),
            pltpu.VMEM((WINDOW, 128), f32), pltpu.VMEM((WINDOW, 128), f32),
            pltpu.VMEM((nq, WINDOW + QB, QB), bf),
            dma((6,)), dma((5,)), dma((1,)), dma((1,)),
        ]
        + collapse_scratch(dims, shapes),
        compiler_params=pltpu.CompilerParams(
            collective_id=3, has_side_effects=True, vmem_limit_bytes=63 * 2**20
        ),
        name="back",
    )(lengths, lse, delta, *arrays, *grads)
    return got[:5], got[5:]


GELU_A, GELU_B = 0.7978845608028654, 0.044715
MB = 256
PROJ_STEPS = (0, 1, 2, 3)


def middle_kernel(dims, proj_shape, bound_ref, cont_ref, gain_ref, *refs):
    names = iter(refs)
    take = lambda k: [next(names) for _ in range(k)]
    sources = take(8)
    y_out, p_out, dr_out, do_out, gain_out, delta_out, sum_proj, g_out, g_up, g_down = take(10)
    x, o, cot, pcot, wo, wu, wd, wp = buffers = take(8)
    n2, r1, act, slope, low_c, dyl, stage, grad_proj = take(8)
    load_sem, stage_sem, out_sem = take(3)
    scratch = list(names)

    place = my_place(dims)
    loads = [pltpu.make_async_copy(a, b, load_sem.at[k]) for k, (a, b) in enumerate(zip(sources, buffers))]
    for load in loads:
        load.start()
    with jax.named_scope("meet"):
        meet(peers(dims, place))
    (total,), locals_ = collapses_of(dims, place, [proj_shape], [grad_proj], [sum_proj], scratch)

    rows, width = x.shape
    chunks = wu.shape[1] // width
    gain = gain_ref[1:2]
    with jax.named_scope("load"):
        for load in loads:
            load.wait()

    def forward(i, carry):
        at = pl.ds(pl.multiple_of(i * MB, MB), MB)
        r = x[at, :].astype(f32) + dot(o[at, :], wo[...])
        r1[at, :] = r
        scale = lax.rsqrt(jnp.mean(r * r, axis=-1, keepdims=True) + EPSILON)
        n2[at, :] = (r * scale * gain).astype(bf)
        y = r
        for j in range(chunks):
            cols = slice(j * width, (j + 1) * width)
            u = dot(n2[at, :], wu[:, cols])
            square = u * u
            t = jnp.tanh(GELU_A * (u + GELU_B * square * u))
            half = 0.5 * (1.0 + t)
            act[at, cols] = (u * half).astype(bf)
            slope[at, cols] = (half + 0.5 * u * (1.0 - t * t) * (GELU_A + 3.0 * GELU_A * GELU_B * square)).astype(bf)
            y = y + dot(act[at, cols], wd[cols, :])
        low_y = y.astype(bf)
        edge = (bound_ref[:, at] * (1 - cont_ref[:, at])).astype(f32)
        edge = jnp.broadcast_to(edge, (8, MB)).T[:, 0:1]
        c = (edge * pcot[at, :].astype(f32)).astype(bf)
        low_c[at, :] = c
        d = cot[at, :].astype(f32) + dot(c, wp[...], NT)
        dr_out[at, :] = d
        dyl[at, :] = d.astype(bf)
        cot[at, :] = low_y
        pcot[at, :] = (edge * dot(low_y, wp[...])).astype(bf)
        return carry

    with jax.named_scope("forward"):
        lax.fori_loop(0, rows // MB, forward, 0)
    stores = [pltpu.make_async_copy(cot, y_out, out_sem.at[0]), pltpu.make_async_copy(pcot, p_out, out_sem.at[1])]
    for store in stores:
        store.start()

    flying = {}

    def emit(target, left, right):
        tall, wide = left.shape[1] // width, right.shape[1] // width
        for j in range(tall):
            for k in range(wide):
                slot = emit.count % 2
                emit.count += 1
                if slot in flying:
                    flying[slot].wait()
                rows_at, cols_at = slice(j * width, (j + 1) * width), slice(k * width, (k + 1) * width)
                stage[slot] = dot(left[:, rows_at], right[:, cols_at], TN).astype(bf)
                copy = pltpu.make_async_copy(
                    stage.at[slot], target.at[pl.ds(j * width, width), pl.ds(k * width, width)], stage_sem.at[slot]
                )
                copy.start()
                flying[slot] = copy

    emit.count = 0
    with jax.named_scope("grad_proj"):
        for k in range(proj_shape[1] // width):
            cols = slice(k * width, (k + 1) * width)
            got = dot(cot[...], low_c[:, cols], TN).astype(bf)
            grad_proj[:, :, :, :, cols] = got.reshape(dims + (proj_shape[0], width))
        run_collapse([total], locals_, 0, -1)
    with jax.named_scope("grad_down"):
        emit(g_down, act, dyl)

    row = lax.broadcasted_iota(jnp.int32, (16, width), 0)
    lane = lax.broadcasted_iota(jnp.int32, (16, width), 1)
    heads = jnp.where(row == lane // 64, 1.0, 0.0).astype(f32)

    def backward(i, carry):
        for step, when in enumerate(PROJ_STEPS):

            @pl.when(i == when)
            def _():
                with jax.named_scope("reduce_%d" % step):
                    run_collapse([total], locals_, 0, step)

        at = pl.ds(pl.multiple_of(i * MB, MB), MB)
        dn = jnp.zeros((MB, width), f32)
        for j in range(chunks):
            cols = slice(j * width, (j + 1) * width)
            du = (dot(dyl[at, :], wd[cols, :], NT) * slope[at, cols].astype(f32)).astype(bf)
            slope[at, cols] = du
            dn = dn + dot(du, wu[:, cols], NT)
        r = r1[at, :]
        scale = lax.rsqrt(jnp.mean(r * r, axis=-1, keepdims=True) + EPSILON)
        unit = r * scale
        by_gain = dn * gain
        inner = jnp.mean(by_gain * unit, axis=-1, keepdims=True)
        dr = dr_out[at, :] + scale * (by_gain - unit * inner)
        dr_out[at, :] = dr
        low_dr = dr.astype(bf)
        dyl[at, :] = low_dr
        low_do = dot(low_dr, wo[...], NT).astype(bf)
        x[at, :] = low_do
        delta = lax.dot_general(
            heads, low_do.astype(f32) * o[at, :].astype(f32), NT,
            precision=lax.Precision.HIGHEST, preferred_element_type=f32,
        )
        for hp in range(width // 128):
            delta_out[hp, 0:2, at] = delta[2 * hp : 2 * hp + 2]
        return carry + jnp.sum(dn * unit, axis=0, keepdims=True)

    with jax.named_scope("backward"):
        gain_out[...] = lax.fori_loop(0, rows // MB, backward, jnp.zeros((1, width), f32))
    stores.append(pltpu.make_async_copy(x, do_out, out_sem.at[2]))
    stores[-1].start()
    with jax.named_scope("grad_up"):
        emit(g_up, n2, slope)
    with jax.named_scope("grad_out"):
        emit(g_out, o, dyl)
    with jax.named_scope("finish"):
        run_collapse([total], locals_, 0, 4)
        for copy in list(flying.values()) + stores:
            copy.wait()
        total.finish()


def middle(bound, cont, gain, arrays, dims):
    x, o, cot, pcot, wo, wu, wd, wp = arrays
    rows, width = x.shape
    ff, proj = wu.shape[1], wp.shape[1]
    pair = width // (dims[0] * dims[1] * dims[2])
    vmem = pl.BlockSpec(memory_space=pltpu.VMEM)
    hbm = pl.BlockSpec(memory_space=pl.ANY)
    dma = pltpu.SemaphoreType.DMA
    sds = jax.ShapeDtypeStruct
    return pl.pallas_call(
        functools.partial(middle_kernel, dims, (pair, proj)),
        in_specs=[vmem] * 3 + [hbm] * 8,
        out_specs=[hbm, hbm, vmem, hbm, vmem, vmem, vmem, hbm, hbm, hbm],
        out_shape=[
            sds((rows, width), bf), sds((rows, proj), bf), sds((rows, width), f32), sds((rows, width), bf),
            sds((1, width), f32), sds((width // 128, 8, rows), f32), sds((pair // 2, proj), f32),
            sds(wo.shape, bf), sds(wu.shape, bf), sds(wd.shape, bf),
        ],
        scratch_shapes=[pltpu.VMEM(a.shape, bf) for a in arrays]
        + [
            pltpu.VMEM((rows, width), bf), pltpu.VMEM((rows, width), f32), pltpu.VMEM((rows, ff), bf),
            pltpu.VMEM((rows, ff), bf), pltpu.VMEM((rows, proj), bf), pltpu.VMEM((rows, width), bf),
            pltpu.VMEM((2, width, width), bf), pltpu.VMEM(dims + (pair, proj), bf),
            dma((8,)), dma((2,)), dma((3,)),
        ]
        + collapse_scratch(dims, [(pair, proj)]),
        compiler_params=pltpu.CompilerParams(
            collective_id=2, has_side_effects=True, vmem_limit_bytes=62 * 2**20
        ),
        name="middle",
    )(bound, cont, gain, *arrays)


ROW_OUT, ROW_UP, ROW_PROJ, ROW_DOWN, ROW_GAIN, ROW_MEAN = 3, 4, 8, 10, 11, 13
STAT_ROWS = 16
DECAY = 1.0 - STEP ** (-0.8)


def exchange_rounds(dims, place):
    z, y, x, c = place
    plane = [(1, 0), (0, 1), (1, 1)]
    rounds = [
        ([sibling(place)], c),
        ([(z, lax.rem(y + dy, 2), lax.rem(x + dx, 2), c) for dy, dx in plane], y * 2 + x),
        ([moved(dims, place, 0, by) for by in range(1, dims[0])], z),
    ]
    return [([device_at(dims, p) for p in others], number) for others, number in rounds]


def put_stats(stats, row, total, square_sum, old_rows, lane, columns):
    width = stats.shape[1]
    for j in range(total.shape[1] // width):
        stats[row + j : row + j + 1, :] = total[:, j * width : (j + 1) * width]
    value = DECAY * jnp.sum(old_rows, axis=1, keepdims=True) + (1.0 - DECAY) / columns * square_sum
    at = lax.broadcasted_iota(jnp.int32, (1, width), 1)
    stats[ROW_MEAN : ROW_MEAN + 1, :] += jnp.where(at == lane, value, 0.0)


def last_kernel(
    dims, shapes, count, x_hbm, resid_hbm, gain_ref, gain_two_ref,
    dq_hbm, dk_hbm, dv_hbm, n_hbm, wq_hbm, wk_hbm, wv_hbm, near_hbm, rest_hbm,
    sum_out, sum_proj, sum_up, sum_down, row_qkv, row_out, row_proj, row_up, row_down, *refs,
):
    names = iter(refs)
    take = lambda k: [next(names) for _ in range(k)]
    grad_ref, total_ref = take(2)
    sums_out = take(3)
    dq, dk, dv, normed, flipped, wq, wk, wv = take(8)
    own_back, near, rest, box, stats, inbox, x_ref, resid_ref = take(8)
    grads = take(3)
    load_sem, back_send, back_recv, stat_send, stat_recv = take(5)
    scratch = list(names)

    place = my_place(dims)
    seq, item = lax.axis_index("seq"), lax.axis_index("item")
    rows, width = x_ref.shape
    loads = [
        pltpu.make_async_copy(a, b, load_sem.at[n])
        for n, (a, b) in enumerate(
            [
                (rest_hbm, rest), (n_hbm, normed), (dk_hbm, dk), (dv_hbm, dv), (dq_hbm, dq),
                (wk_hbm, wk), (wv_hbm, wv), (wq_hbm, wq), (near_hbm, near),
                (x_hbm, x_ref), (resid_hbm, resid_ref),
            ]
        )
    ]
    for load in loads:
        load.start()
    ahead = [(lax.rem(seq + d, count), item) for d in (1, 2)]
    behind = [(lax.rem(seq + count - d, count), item) for d in (1, 2)]
    with jax.named_scope("meet"):
        meet(peers(dims, place) + ahead + behind + [device_at(dims, place[:1] + (1 - place[1], 1 - place[2], place[3]))])
    far = WINDOW - rows
    near_rows, far_rows = pl.ds(far, rest.shape[0] - far), pl.ds(0, far)
    returned = [
        pltpu.make_async_remote_copy(
            src_ref=rest.at[part], dst_ref=box.at[part], send_sem=back_send.at[m], recv_sem=back_recv.at[m],
            device_id=behind[m], device_id_type=MESH,
        )
        for m, part in enumerate((near_rows, far_rows))
    ]
    loads[0].wait()
    for m in range(2):
        pl.when(seq >= m + 1)(returned[m].start)

    def back_of(at):
        return dot(dk[at, :], wk[...].reshape(width, width), NT) + dot(dv[at, :], wv[...].reshape(width, width), NT)

    sums, locals_ = collapses_of(dims, place, shapes, grads, sums_out, scratch)
    with jax.named_scope("weight_gradients"):
        loads[1].wait()
        flipped[...] = normed[...].T
        for k, part in ((1, dk), (2, dv), (0, dq)):
            loads[(4, 2, 3)[k]].wait()
            base = WINDOW if k == 0 else 0
            got = dot(flipped[:, base:], part[...])
            grads[k][...] = got.astype(bf).reshape(grads[k].shape)
            run_collapse(sums, locals_, k, -1)

    def own_block(i, carry):
        at = pl.ds(pl.multiple_of(i * QB, QB), QB)
        ext = pl.ds(pl.multiple_of(WINDOW + i * QB, QB), QB)
        own_back[at, :] = back_of(ext) + dot(dq[at, :], wq[...].reshape(width, width), NT)
        return carry

    with jax.named_scope("own_rows"):
        for load in loads[5:]:
            load.wait()
        lax.fori_loop(0, rows // QB, own_block, 0)

    stats[0] = jnp.zeros_like(stats[0])
    held = stats.at[0]
    held[ROW_GAIN + 1 : ROW_GAIN + 2, :] = gain_two_ref[...]

    def add_stats(row, grad, old_rows, lane):
        square = grad * grad + TINY_SQUARE
        total = jnp.sum(square, axis=0, keepdims=True)
        put_stats(held, row, total, jnp.sum(total, axis=1, keepdims=True), old_rows, lane, grad.shape[1])

    with jax.named_scope("small_sums"):
        add_stats(ROW_OUT, sum_out[...], row_out[...], 3)
        add_stats(ROW_UP, sum_up[...], row_up[...], 4)
        add_stats(ROW_PROJ, sum_proj[...], row_proj[...], 5)
        add_stats(ROW_DOWN, sum_down[...], row_down[...], 6)

    for stage in range(5):
        with jax.named_scope("reduce_%d" % stage):
            for k in (1, 2, 0):
                run_collapse(sums, locals_, k, stage)
    for k in range(3):
        add_stats(k, sums_out[k][...], row_qkv[k : k + 1, :], k)

    with jax.named_scope("rows_returned"):

        @pl.when(seq + 1 < count)
        def _():
            returned[0].wait_recv()
            size = near.shape[0]
            own_back[0:size, :] += near[...].astype(f32)
            own_back[size:, :] += box[near_rows, :].astype(f32)

        @pl.when(seq + 2 < count)
        def _():
            returned[1].wait_recv()
            own_back[rows - far :, :] += box[far_rows, :].astype(f32)

    gain = gain_ref[0:1]

    def input_block(i, total):
        at = pl.ds(pl.multiple_of(i * QB, QB), QB)
        x = x_ref[at, :].astype(f32)
        scale = lax.rsqrt(jnp.mean(x * x, axis=-1, keepdims=True) + EPSILON)
        back = own_back[at, :]
        unit = x * scale
        by_gain = back * gain
        inner = jnp.mean(by_gain * unit, axis=-1, keepdims=True)
        grad_ref[at, :] = (resid_ref[at, :] + scale * (by_gain - unit * inner)).astype(bf)
        return total + jnp.sum(back * unit, axis=0, keepdims=True)

    with jax.named_scope("input_gradient"):
        total = lax.fori_loop(0, rows // QB, input_block, jnp.zeros((1, width), f32))
    held[ROW_GAIN : ROW_GAIN + 1, :] = total

    rounds = exchange_rounds(dims, place)
    z, y, x, c = place
    senders = [
        [1 - c],
        [lax.rem(y + dy, 2) * 2 + lax.rem(x + dx, 2) for dy, dx in ((1, 0), (0, 1), (1, 1))],
        [lax.rem(z + dims[0] - by, dims[0]) for by in range(1, dims[0])],
    ]

    with jax.named_scope("exchange_sums"):
        slot = 0
        for stage, (others, number) in enumerate(rounds):
            copies = []
            for other in others:
                copies.append(
                    pltpu.make_async_remote_copy(
                        src_ref=stats.at[stage], dst_ref=inbox.at[slot],
                        send_sem=stat_send.at[slot], recv_sem=stat_recv.at[slot],
                        device_id=other, device_id_type=MESH,
                    )
                )
                copies[-1].start()
                slot += 1
            for copy in copies:
                copy.wait()
            base = slot - len(others)
            total = jnp.zeros_like(stats[0])
            for member in range(len(others) + 1):
                term = stats[stage]
                for m in range(len(others)):
                    term = jnp.where(senders[stage][m] == member, inbox[base + m], term)
                total = total + term
            stats[stage + 1] = total
        total_ref[...] = stats[len(rounds)]
    for one in sums:
        one.finish()
    for m in range(2):
        pl.when(seq >= m + 1)(returned[m].wait_send)


def last(x, resid_grad, gain, gain_two, dq, dk, dv, normed, weights, returned, sums, old_rows, dims, count):
    rows, width = x.shape
    ext = normed.shape[0]
    shapes = [w.shape[3:] for w in weights]
    slots = 4 + dims[0] - 1
    vmem = pl.BlockSpec(memory_space=pltpu.VMEM)
    hbm = pl.BlockSpec(memory_space=pl.ANY)
    dma = pltpu.SemaphoreType.DMA
    sds = jax.ShapeDtypeStruct
    got = pl.pallas_call(
        functools.partial(last_kernel, dims, shapes, count),
        in_specs=[hbm] * 2 + [vmem] * 2 + [hbm] * 9 + [vmem] * 9,
        out_specs=[vmem] * 5,
        out_shape=[sds((rows, width), bf), sds((STAT_ROWS, width), f32)] + [sds((r // 2, c), f32) for r, c in shapes],
        scratch_shapes=[
            pltpu.VMEM((rows, width), bf), pltpu.VMEM((ext, width), bf), pltpu.VMEM((ext, width), bf),
            pltpu.VMEM((ext, width), bf), pltpu.VMEM((width, ext), bf),
        ]
        + [pltpu.VMEM(w.shape, bf) for w in weights]
        + [pltpu.VMEM((rows, width), f32)]
        + [pltpu.VMEM(a.shape, bf) for a in (*returned, returned[1])]
        + [pltpu.VMEM((4, STAT_ROWS, width), f32), pltpu.VMEM((slots, STAT_ROWS, width), f32)]
        + [pltpu.VMEM((rows, width), bf), pltpu.VMEM((rows, width), f32)]
        + [pltpu.VMEM(w.shape, bf) for w in weights]
        + [dma((11,)), dma((2,)), dma((2,)), dma((slots,)), dma((slots,))]
        + collapse_scratch(dims, shapes),
        compiler_params=pltpu.CompilerParams(
            collective_id=4, has_side_effects=True, vmem_limit_bytes=61 * 2**20
        ),
        name="last",
    )(x, resid_grad, gain, gain_two, dq, dk, dv, normed, *weights, *returned, *sums, *old_rows)
    return got[0], got[1], got[2:]


def update_kernel(
    place_ref, total_ref, gains_ref, gain_var_ref,
    w_qkv, w_out, w_proj, w_up, w_down, s_q, s_k, s_v, s_out, s_proj, s_up, s_down,
    row_qkv, row_out, row_proj, row_up, row_down, col_qkv, col_out, col_proj, col_up, col_down,
    y_ref, p_ref, d_ref, g_qkv, g_out, g_proj, g_up, g_down, g_gains, n_qkv, n_out, n_proj, n_up, n_down, n_gains,
    r_qkv, r_out, r_proj, r_up, r_down, c_qkv, c_out, c_proj, c_up, c_down, gain_var_new,
    y_out, p_out, d_out, flat, tall, y_held, p_held, d_held, pass_sem,
):
    held = (y_held, p_held, d_held)
    taken = [pltpu.make_async_copy(a, b, pass_sem.at[n]) for n, (a, b) in enumerate(zip((y_ref, p_ref, d_ref), held))]
    passed = [pltpu.make_async_copy(a, b, pass_sem.at[3 + n]) for n, (a, b) in enumerate(zip(held, (y_out, p_out, d_out)))]
    for copy in taken:
        copy.start()
    shard = row_out.shape[1]
    shard_down = row_down.shape[1]
    width = total_ref.shape[1]
    flat[...] = jnp.zeros_like(flat)
    flat[0:3, :shard] = row_qkv[...]
    flat[3:4, :shard] = row_out[...]
    flat[4:5, :shard] = row_up[...]
    flat[5:6, :shard] = row_proj[...]
    flat[6:7, :shard_down] = row_down[...]
    olds = flat[...].T
    tall[...] = jnp.zeros_like(tall)

    def one(weight, grad, lane, row, old_col, rows_all, g_out_, n_out_, c_out_):
        count, columns = grad.shape
        square = grad * grad + TINY_SQUARE
        row_new = DECAY * olds[:count, lane : lane + 1] + (1.0 - DECAY) * jnp.mean(square, axis=1, keepdims=True)
        tall[:count, lane : lane + 1] = row_new
        parts = [total_ref[row + j : row + j + 1, :] for j in range(columns // width)]
        col_total = parts[0] if len(parts) == 1 else jnp.concatenate(parts, axis=1)
        col_new = DECAY * old_col + (1.0 - DECAY) * col_total / rows_all
        mean = total_ref[ROW_MEAN : ROW_MEAN + 1, lane : lane + 1] / rows_all
        second = row_new * col_new / mean
        g_out_[...] = grad
        n_out_[...] = weight - WEIGHT_RATE * grad * lax.rsqrt(second)
        c_out_[...] = col_new

    for k, grad in enumerate((s_q, s_k, s_v)):
        one(w_qkv[k], grad[...], k, k, col_qkv[k : k + 1, :], width, g_qkv.at[k], n_qkv.at[k], c_qkv.at[k : k + 1])
    one(w_out[...], s_out[...], 3, ROW_OUT, col_out[...], width, g_out, n_out, c_out)
    one(w_up[...], s_up[...], 4, ROW_UP, col_up[...], width, g_up, n_up, c_up)
    one(w_proj[...], s_proj[...], 5, ROW_PROJ, col_proj[...], width, g_proj, n_proj, c_proj)
    one(w_down[...], s_down[...], 6, ROW_DOWN, col_down[...], col_up.shape[1], g_down, n_down, c_down)
    for copy, onward in zip(taken, passed):
        copy.wait()
        onward.start()
    news = tall[...].T
    r_qkv[...] = news[0:3, :shard]
    r_out[...] = news[3:4, :shard]
    r_up[...] = news[4:5, :shard]
    r_proj[...] = news[5:6, :shard]
    r_down[...] = news[6:7, :shard_down]

    gain_sums = pltpu.roll(total_ref[8:16, :], width - place_ref[0] * shard, 1)
    sums = gain_sums[ROW_GAIN - 8 : ROW_GAIN - 6, :shard]
    var = DECAY * gain_var_ref[...] + (1.0 - DECAY) * (sums * sums + TINY_SQUARE)
    g_gains[...] = sums
    gain_var_new[...] = var
    n_gains[...] = gains_ref[...] - GAIN_RATE * sums * lax.rsqrt(var)
    for copy in passed:
        copy.wait()


def update(place, totals, gains, gain_var, weights, sums, rows, cols, results):
    vmem = pl.BlockSpec(memory_space=pltpu.VMEM)
    like = lambda arrays: [jax.ShapeDtypeStruct(a.shape, f32) for a in arrays]
    outs = like(weights) + like([gains]) + like(weights) + like([gains]) + like(rows) + like(cols) + like([gain_var])
    hbm = pl.BlockSpec(memory_space=pl.ANY)
    return pl.pallas_call(
        update_kernel,
        in_specs=[pl.BlockSpec(memory_space=pltpu.SMEM)] + [vmem] * (3 + 5 + 7 + 5 + 5) + [hbm] * 3,
        out_specs=[vmem] * len(outs) + [hbm] * 3,
        out_shape=outs + [jax.ShapeDtypeStruct(a.shape, a.dtype) for a in results],
        scratch_shapes=[pltpu.VMEM((8, 128), f32), pltpu.VMEM((128, 8), f32)]
        + [pltpu.VMEM(a.shape, a.dtype) for a in results]
        + [pltpu.SemaphoreType.DMA((6,))],
        compiler_params=pltpu.CompilerParams(vmem_limit_bytes=63 * 2**20),
        name="update",
    )(place, totals, gains, gain_var, *weights, *sums, *rows, *cols, *results)


def sum_kernel(sizes, x_ref, o_ref, inbox, send_sem, recv_sem):
    place = {name: lax.axis_index(name) for name, _ in sizes}
    partners = []
    for name, size in sizes:
        bit = 1
        while bit < size:
            mine = place[name]
            low = lax.rem(mine // bit, 2)
            other = mine + bit * (1 - 2 * low)
            partners.append(tuple(other if n == name else place[n] for n in ("seq", "item")))
            bit *= 2
    barrier = pltpu.get_barrier_semaphore()
    for partner in partners:
        pl.semaphore_signal(barrier, inc=1, device_id=partner, device_id_type=MESH)
    pl.semaphore_wait(barrier, len(partners))
    o_ref[0] = x_ref[...]
    for stage, partner in enumerate(partners):
        copy = pltpu.make_async_remote_copy(
            src_ref=o_ref.at[stage],
            dst_ref=inbox.at[stage],
            send_sem=send_sem.at[stage],
            recv_sem=recv_sem.at[stage],
            device_id=partner,
            device_id_type=MESH,
        )
        copy.start()
        copy.wait()
        o_ref[stage + 1] = o_ref[stage] + inbox[stage]


def sum_all(x, sizes):
    stages = sum(size.bit_length() - 1 for _, size in sizes)
    held = pl.pallas_call(
        functools.partial(sum_kernel, sizes),
        out_shape=jax.ShapeDtypeStruct((stages + 1,) + x.shape, x.dtype),
        in_specs=[pl.BlockSpec(memory_space=pltpu.VMEM)],
        out_specs=pl.BlockSpec(memory_space=pltpu.VMEM),
        scratch_shapes=[
            pltpu.VMEM((stages,) + x.shape, x.dtype),
            pltpu.SemaphoreType.DMA((stages,)),
            pltpu.SemaphoreType.DMA((stages,)),
        ],
        compiler_params=pltpu.CompilerParams(collective_id=0, has_side_effects=True),
        name="sum_all",
    )(x)
    return held[stages]


def from_behind(block, axis, distance):
    devices = range(lax.axis_size(axis))
    route = [(i - distance, i) for i in devices if i - distance in devices]
    return lax.ppermute(block, axis, route)


def norm_rows(values, gain):
    return values * lax.rsqrt(jnp.mean(values * values, axis=-1, keepdims=True) + EPSILON) * gain


def gelu_tanh(values):
    return (
        0.5
        * values
        * (1.0 + jnp.tanh(0.7978845608028654 * (values + 0.044715 * values * values * values)))
    )


def finish_update(weight, grad, row_new, col_state, col_total, rows_all, row_mean, decay):
    col_new = decay * col_state + (1.0 - decay) * col_total / rows_all
    second = row_new[..., :, None] * col_new[..., None, :] / row_mean
    return (weight - WEIGHT_RATE * grad * lax.rsqrt(second), col_new)


def local(
    byte_rows, item_lengths, cont_mask, bound_mask, out_cot, proj_cot,
    w_qkv, w_out, w_up, w_down, w_proj, gains,
    row_qkv, col_qkv, row_out, col_out, row_up, col_up, row_down, col_down, row_proj, col_proj, gain_var,
):
    sizes = tuple((name, lax.axis_size(name)) for name in ("item", "seq"))
    count = lax.axis_size("item") * lax.axis_size("seq")
    rows_dev, width = byte_rows.shape[1:]
    ff = w_up.shape[1]
    shard = width // count
    low = bf

    dims = grid_of(lax.axis_size("seq"), lax.axis_size("item"))
    paired = dims == (4, 2, 2) and shard % 8 == 0 and rows_dev < WINDOW <= 2 * rows_dev
    inputs_low = byte_rows[0]
    if paired:
        got = front(item_lengths, inputs_low, gains, w_qkv, (w_out, w_proj, w_up, w_down), dims, lax.axis_size("seq"))
        attended, lse, queries, ext_keys, ext_values, ext_normed = got[:6]
        split_qkv = got[6:9]
        gain_full = got[9]
        weight_out, weight_proj, weight_up, weight_down = [w.reshape(-1, w.shape[-1]) for w in got[10:]]
    else:
        inputs = inputs_low.astype(f32)
        weight_qkv = lax.all_gather(w_qkv.astype(low), AXES, axis=1, tiled=True)
        gain_full = lax.all_gather(gains.astype(low), AXES, axis=1, tiled=True).astype(f32)
        weight_out, weight_proj, weight_up, weight_down = [
            lax.all_gather(w.astype(low), AXES, axis=0, tiled=True) for w in (w_out, w_proj, w_up, w_down)
        ]

    hop_total = -(-WINDOW // rows_dev)
    if not paired:
        offset = lax.axis_index("seq") * rows_dev
        ends = jnp.cumsum(item_lengths[0], dtype=jnp.int32)
        pos = offset + jnp.arange(rows_dev, dtype=jnp.int32)
        begin_at = jnp.max(jnp.where(ends[None, :] <= pos[:, None], ends[None, :], 0), axis=1)
        lo = jnp.maximum(begin_at, pos - WINDOW + 1) - offset + WINDOW
        halo = []
        for distance in range(hop_total, 0, -1):
            need = min(rows_dev, WINDOW - (distance - 1) * rows_dev)
            halo.append(from_behind(inputs_low[rows_dev - need :], "seq", distance))
        normed = norm_rows(inputs, gain_full[0]).astype(low)
        halo_normed = norm_rows(jnp.concatenate(halo, axis=0).astype(f32), gain_full[0]).astype(low)
        ext_normed = jnp.concatenate([halo_normed, normed], axis=0)
        queries = dot(normed, weight_qkv[0]).astype(low) * jnp.asarray(0.125, low)
        ext_keys = dot(ext_normed, weight_qkv[1]).astype(low)
        ext_values = dot(ext_normed, weight_qkv[2]).astype(low)
        attended, lse = attend(queries, ext_keys, ext_values, lo[:, None])

    if paired:
        output_low, projected, resid_grad, attended_grad, gain_two_grad, delta, sum_proj, *low_grads = middle(
            bound_mask, cont_mask, gain_full,
            (inputs_low, attended, out_cot[0], proj_cot[0], weight_out, weight_up, weight_down, weight_proj), dims,
        )
        apart = [g.reshape(dims + (-1, g.shape[1])) for g in low_grads]
        (query_grad, ext_key_grad, ext_value_grad, *returned), (sum_out, sum_up, sum_down) = back(
            item_lengths, lse, delta, (queries, attended_grad, ext_keys, ext_values, split_qkv[1], split_qkv[2]),
            apart, dims, lax.axis_size("seq"),
        )
        sums = [sum_out, sum_proj, sum_up, sum_down]
    else:
        resid = inputs + dot(attended, weight_out)
        normed_two = norm_rows(resid, gain_full[1]).astype(low)
        hidden_pre = dot(normed_two, weight_up)
        activated = gelu_tanh(hidden_pre).astype(low)
        output = resid + dot(activated, weight_down)
        output_low = output.astype(low)
        boundary = (bound_mask[0] * (1 - cont_mask[0])).astype(f32)[:, None]
        projected = (boundary * dot(output_low, weight_proj)).astype(low)
        proj_grad = (boundary * proj_cot[0].astype(f32)).astype(low)
        grad_proj = dot(output_low, proj_grad, TN)
        output_grad = out_cot[0].astype(f32) + dot(proj_grad, weight_proj, NT)
        output_grad_low = output_grad.astype(low)
        grad_down = dot(activated, output_grad_low, TN)
        act_grad = dot(output_grad_low, weight_down, NT)
        _, gelu_back = jax.vjp(gelu_tanh, hidden_pre)
        pre_grad = gelu_back(act_grad)[0].astype(low)
        grad_up = dot(normed_two, pre_grad, TN)
        normed_two_grad = dot(pre_grad, weight_up, NT)
        _, norm_two_back = jax.vjp(norm_rows, resid, gain_full[1])
        resid_norm_grad, gain_two_grad = norm_two_back(normed_two_grad)
        resid_grad = output_grad + resid_norm_grad
        resid_grad_low = resid_grad.astype(low)
        grad_out = dot(attended, resid_grad_low, TN)
        attended_grad = dot(resid_grad_low, weight_out, NT).astype(low)

        low_grads = [g.astype(low) for g in (grad_out, grad_proj, grad_up, grad_down)]
        query_grad, ext_key_grad, ext_value_grad = attend_back(
            queries, attended_grad, attended, lse, ext_keys, ext_values, lo[None, :]
        )
        sums = [lax.psum_scatter(g, AXES, scatter_dimension=0, tiled=True).astype(f32) for g in low_grads]
        sum_out, sum_proj, sum_up, sum_down = sums
    if paired:
        rows = [row_qkv, row_out[None], row_proj[None], row_up[None], row_down[None]]
        cols = [col_qkv, col_out[None], col_proj[None], col_up[None], col_down[None]]
        input_grad, totals, sums_qkv = last(
            inputs_low, resid_grad, gain_full, gain_two_grad, query_grad, ext_key_grad, ext_value_grad,
            ext_normed, split_qkv, returned, sums, rows, dims, lax.axis_size("seq"),
        )
        mine = lax.axis_index("seq") * lax.axis_size("item") + lax.axis_index("item")
        done = update(
            mine[None].astype(jnp.int32), totals, gains, gain_var,
            (w_qkv, w_out, w_proj, w_up, w_down), (*sums_qkv, *sums), rows, cols,
            (output_low, projected, input_grad),
        )
        sum_qkv, sum_out, sum_proj, sum_up, sum_down, sum_gains = done[:6]
        new_qkv, new_out, new_proj, new_up, new_down, new_gains = done[6:12]
        row_qkv_new, row_out_new, row_proj_new, row_up_new, row_down_new = [done[12]] + [r[0] for r in done[13:17]]
        col_qkv_new, col_out_new, col_proj_new, col_up_new, col_down_new = [done[17]] + [r[0] for r in done[18:22]]
        gain_var_new, output_low, projected, input_grad = done[22:]
        return (
            output_low[None], projected[None], input_grad[None],
            sum_qkv, sum_out, sum_up, sum_down, sum_proj, sum_gains,
            new_qkv, new_out, new_up, new_down, new_proj, new_gains,
            row_qkv_new, col_qkv_new, row_out_new, col_out_new, row_up_new, col_up_new,
            row_down_new, col_down_new, row_proj_new, col_proj_new, gain_var_new,
        )
    ext_back = dot(ext_key_grad, weight_qkv[1], NT) + dot(ext_value_grad, weight_qkv[2], NT)
    halo_back = ext_back[:WINDOW].astype(low)
    grads_qkv = [
        dot(normed, query_grad, TN).astype(low),
        dot(ext_normed, ext_key_grad, TN).astype(low),
        dot(ext_normed, ext_value_grad, TN).astype(low),
    ]
    returned = []
    for distance in range(1, hop_total + 1):
        need = min(rows_dev, WINDOW - (distance - 1) * rows_dev)
        upper = WINDOW - (distance - 1) * rows_dev
        returned.append(from_behind(halo_back[upper - need : upper], "seq", -distance))
    sums = [lax.psum_scatter(g, AXES, scatter_dimension=0, tiled=True).astype(f32) for g in grads_qkv]
    sum_qkv = jnp.stack(sums)
    normed_grad = ext_back[WINDOW:] + dot(query_grad, weight_qkv[0], NT)
    for block in returned:
        need = block.shape[0]
        normed_grad = normed_grad.at[rows_dev - need :].add(block.astype(f32))
    _, norm_one_back = jax.vjp(norm_rows, inputs, gain_full[0])
    input_norm_grad, gain_one_grad = norm_one_back(normed_grad)
    input_grad = (resid_grad + input_norm_grad).astype(low)

    decay = 1.0 - STEP ** (-0.8)
    square_qkv = sum_qkv * sum_qkv + TINY_SQUARE
    square_out = sum_out * sum_out + TINY_SQUARE
    square_up = sum_up * sum_up + TINY_SQUARE
    square_down = sum_down * sum_down + TINY_SQUARE
    square_proj = sum_proj * sum_proj + TINY_SQUARE
    row_qkv_new = decay * row_qkv + (1.0 - decay) * jnp.mean(square_qkv, axis=-1)
    row_out_new = decay * row_out + (1.0 - decay) * jnp.mean(square_out, axis=-1)
    row_up_new = decay * row_up + (1.0 - decay) * jnp.mean(square_up, axis=-1)
    row_down_new = decay * row_down + (1.0 - decay) * jnp.mean(square_down, axis=-1)
    row_proj_new = decay * row_proj + (1.0 - decay) * jnp.mean(square_proj, axis=-1)
    row_sums = jnp.concatenate(
        [
            jnp.sum(row_qkv_new, axis=1),
            jnp.sum(row_out_new)[None],
            jnp.sum(row_up_new)[None],
            jnp.sum(row_down_new)[None],
            jnp.sum(row_proj_new)[None],
        ]
    )
    stats = [
        jnp.sum(square_qkv, axis=1).reshape(-1),
        jnp.sum(square_out, axis=0),
        jnp.sum(square_up, axis=0),
        jnp.sum(square_down, axis=0),
        jnp.sum(square_proj, axis=0),
        gain_one_grad,
        gain_two_grad,
        row_sums,
    ]
    flat = jnp.concatenate(stats)
    used = flat.shape[0]
    padded = -(-used // 1024) * 1024
    flat = jnp.pad(flat, (0, padded - used)).reshape(padded // 128, 128)
    flat = sum_all(flat, sizes).reshape(-1)
    totals, at = [], 0
    for part in stats:
        totals.append(flat[at : at + part.shape[0]])
        at += part.shape[0]
    col_qkv_total, col_out_total, col_up_total, col_down_total, col_proj_total, gain_one, gain_two, row_totals = totals
    col_qkv_total = col_qkv_total.reshape(3, width)
    mine = lax.axis_index("seq") * lax.axis_size("item") + lax.axis_index("item")
    sum_gains = lax.dynamic_slice_in_dim(jnp.stack([gain_one, gain_two]), mine * shard, shard, 1)
    row_counts = jnp.array([width, width, width, width, width, ff, width], f32)
    row_means = row_totals / row_counts
    new_qkv, col_qkv_new = finish_update(
        w_qkv, sum_qkv, row_qkv_new, col_qkv, col_qkv_total, width, row_means[:3][:, None, None], decay
    )
    new_out, col_out_new = finish_update(w_out, sum_out, row_out_new, col_out, col_out_total, width, row_means[3], decay)
    new_up, col_up_new = finish_update(w_up, sum_up, row_up_new, col_up, col_up_total, width, row_means[4], decay)
    new_down, col_down_new = finish_update(
        w_down, sum_down, row_down_new, col_down, col_down_total, ff, row_means[5], decay
    )
    new_proj, col_proj_new = finish_update(
        w_proj, sum_proj, row_proj_new, col_proj, col_proj_total, width, row_means[6], decay
    )
    gain_var_new = decay * gain_var + (1.0 - decay) * (sum_gains * sum_gains + TINY_SQUARE)
    new_gains = gains - GAIN_RATE * sum_gains * lax.rsqrt(gain_var_new)
    return (
        output_low[None], projected[None], input_grad[None],
        sum_qkv, sum_out, sum_up, sum_down, sum_proj, sum_gains,
        new_qkv, new_out, new_up, new_down, new_proj, new_gains,
        row_qkv_new, col_qkv_new, row_out_new, col_out_new, row_up_new, col_up_new,
        row_down_new, col_down_new, row_proj_new, col_proj_new, gain_var_new,
    )


def solution(mesh):
    in_specs = (
        P("item", "seq", None),
        P("item", None),
        P("item", "seq"),
        P("item", "seq"),
        P("item", "seq", None),
        P("item", "seq", None),
        P(None, ("seq", "item"), None),
        P(("seq", "item"), None),
        P(("seq", "item"), None),
        P(("seq", "item"), None),
        P(("seq", "item"), None),
        P(None, ("seq", "item")),
        P(None, ("seq", "item")),
        P(),
        P(("seq", "item")),
        P(),
        P(("seq", "item")),
        P(),
        P(("seq", "item")),
        P(),
        P(("seq", "item")),
        P(),
        P(None, ("seq", "item")),
    )
    out_specs = (
        P("item", "seq", None),
        P("item", "seq", None),
        P("item", "seq", None),
        P(None, ("seq", "item"), None),
        P(("seq", "item"), None),
        P(("seq", "item"), None),
        P(("seq", "item"), None),
        P(("seq", "item"), None),
        P(None, ("seq", "item")),
        P(None, ("seq", "item"), None),
        P(("seq", "item"), None),
        P(("seq", "item"), None),
        P(("seq", "item"), None),
        P(("seq", "item"), None),
        P(None, ("seq", "item")),
        P(None, ("seq", "item")),
        P(),
        P(("seq", "item")),
        P(),
        P(("seq", "item")),
        P(),
        P(("seq", "item")),
        P(),
        P(("seq", "item")),
        P(),
        P(None, ("seq", "item")),
    )
    return jax.shard_map(local, mesh=mesh, in_specs=in_specs, out_specs=out_specs, check_vma=False)
```

```python
import functools
import jax
import jax.numpy as jnp
from jax import lax
from jax.experimental import pallas as pl
from jax.experimental.pallas import tpu as pltpu
from jax.sharding import PartitionSpec as P

WINDOW = 1536
HEADS = 12
NEG = -1e30
EPSILON = 1e-06
TINY_SQUARE = 1e-30
WEIGHT_RATE = 0.02
GAIN_RATE = 0.2
STEP = 10
QB = 256
NT = (((1,), (1,)), ((), ()))
TN = (((0,), (0,)), ((), ()))
f32 = jnp.float32
bf = jnp.bfloat16


def dot(a, b, dims=None):
    if dims is None:
        return jnp.dot(a, b, preferred_element_type=f32)
    return lax.dot_general(a, b, dims, preferred_element_type=f32)


def halves(x):
    lane = lax.broadcasted_iota(jnp.int32, x.shape, 1)
    zero = jnp.zeros_like(x)
    return jnp.where(lane < 64, x, zero), jnp.where(lane < 64, zero, x)


def fwd_kernel(lo_ref, q_ref, k_ref, v_ref, o_ref, lse_ref, bias):
    hp, qb = pl.program_id(0), pl.program_id(1)
    span = WINDOW + QB

    @pl.when(hp == 0)
    def _():
        base = qb * QB
        kpos = base + lax.broadcasted_iota(jnp.int32, (QB, span), 1)
        qpos = WINDOW + base + lax.broadcasted_iota(jnp.int32, (QB, span), 0)
        ok = (kpos >= lo_ref[...]) & (kpos <= qpos)
        bias[qb] = jnp.where(ok, 0.0, NEG)

    start = pl.multiple_of(qb * QB, QB)
    kw = k_ref[pl.ds(start, span), :]
    vw = v_ref[pl.ds(start, span), :]
    outs, lses = [], []
    for qh in halves(q_ref[...]):
        s = dot(qh, kw, NT) + bias[qb]
        m = jnp.max(s, axis=1, keepdims=True)
        p = jnp.exp(s - m)
        l = jnp.sum(p, axis=1, keepdims=True)
        outs.append(dot(p.astype(bf), vw) * (1.0 / l))
        lses.append(m + jnp.log(l))
    lane = lax.broadcasted_iota(jnp.int32, (QB, 128), 1)
    o_ref[...] = jnp.where(lane < 64, outs[0], outs[1]).astype(bf)
    both = jnp.where(lane == 0, lses[0], lses[1])
    lse_ref[0] = both.T[:8]


def attend(q, k, v, lo):
    rows, width = q.shape
    ext = k.shape[0]
    nq, nh = rows // QB, width // 128
    return pl.pallas_call(
        fwd_kernel,
        grid=(nh, nq),
        in_specs=[
            pl.BlockSpec((QB, 1), lambda h, i: (i, 0)),
            pl.BlockSpec((QB, 128), lambda h, i: (i, h)),
            pl.BlockSpec((ext, 128), lambda h, i: (0, h)),
            pl.BlockSpec((ext, 128), lambda h, i: (0, h)),
        ],
        out_specs=[
            pl.BlockSpec((QB, 128), lambda h, i: (i, h)),
            pl.BlockSpec((1, 8, QB), lambda h, i: (h, 0, i)),
        ],
        out_shape=[
            jax.ShapeDtypeStruct((rows, width), bf),
            jax.ShapeDtypeStruct((nh, 8, rows), f32),
        ],
        scratch_shapes=[pltpu.VMEM((nq, QB, WINDOW + QB), f32)],
        compiler_params=pltpu.CompilerParams(vmem_limit_bytes=50 * 2**20),
        cost_estimate=pl.CostEstimate(flops=4 * rows * 1792 * 768 * 3, bytes_accessed=14 * 2**20, transcendentals=0),
        name="attend",
    )(lo, q, k, v)


AXES = ("seq", "item")
MESH = pl.DeviceIdType.MESH


def grid_of(seq, item):
    side = 1
    while side * side * 4 <= seq:
        side *= 2
    return (seq // side, side, item // 2)


def my_place(dims):
    seq, item = lax.axis_index("seq"), lax.axis_index("item")
    return (seq // dims[1], lax.rem(seq, dims[1]), item // 2, lax.rem(item, 2))


def device_at(dims, place):
    z, y, x, c = place
    return (z * dims[1] + y, x * 2 + c)


def moved(dims, place, dim, by):
    to = list(place)
    to[dim] = lax.rem(place[dim] + by, dims[dim])
    return tuple(to)


def sibling(place):
    return place[:3] + (1 - place[3],)


def peers(dims, place):
    found = [sibling(place)]
    for dim in range(3):
        found += [moved(dims, place, dim, by) for by in range(1, dims[dim])]
    return [device_at(dims, p) for p in found]


def meet(targets):
    barrier = pltpu.get_barrier_semaphore()
    for target in targets:
        pl.semaphore_signal(barrier, inc=1, device_id=target, device_id_type=MESH)
    pl.semaphore_wait(barrier, len(targets))


class Spread:
    def __init__(self, dims, place, own, out, rows, cols, order, send, recv):
        self.dims, self.place, self.own, self.out = dims, place, own, out
        self.rows, self.cols, self.order = rows, cols, order
        self.send, self.recv = send, recv

    def span(self, core):
        half = self.out.shape[-1] // 2
        return pl.ds(pl.multiple_of(core * half + self.cols[0], 128), self.cols[1])

    def region(self, stage, by=0, core=None):
        held = self.order[:stage]
        at = []
        for dim in range(3):
            if dim in held:
                at.append(slice(None))
            elif by and dim == self.order[stage]:
                at.append(lax.rem(self.place[dim] + self.dims[dim] - by, self.dims[dim]))
            else:
                at.append(self.place[dim])
        core = self.place[3] if core is None else core
        return self.out.at[tuple(at) + (self.rows, self.span(core))]

    def slots(self, stage):
        first = sum(self.dims[d] - 1 for d in self.order[:stage])
        return [(by, first + by - 1) for by in range(1, self.dims[self.order[stage]])]

    def hops(self, stage):
        for by, slot in self.slots(stage):
            block = self.region(stage)
            source = self.own.at[self.rows, self.span(self.place[3])] if stage == 0 else block
            target = device_at(self.dims, moved(self.dims, self.place, self.order[stage], by))
            yield pltpu.make_async_remote_copy(
                src_ref=source, dst_ref=block, send_sem=self.send.at[slot], recv_sem=self.recv.at[slot],
                device_id=target, device_id_type=MESH,
            )

    def shares(self, stage, core=None):
        count = sum(d - 1 for d in self.dims)
        for by, slot in self.slots(stage):
            block = self.region(stage, by, core)
            yield pltpu.make_async_remote_copy(
                src_ref=block, dst_ref=block, send_sem=self.send.at[count + slot], recv_sem=self.recv.at[count + slot],
                device_id=device_at(self.dims, sibling(self.place)), device_id_type=MESH,
            )

    def begin(self, stage):
        for copy in self.hops(stage):
            copy.start()

    def advance(self, stage, go_on=True):
        for copy in self.hops(stage):
            copy.wait_recv()
        if stage < 2 and go_on:
            self.begin(stage + 1)
        for copy in self.shares(stage):
            copy.start()

    def finish(self, stages=(0, 1, 2)):
        for stage in stages:
            for copy in self.hops(stage):
                copy.wait_send()
            for copy in self.shares(stage):
                copy.wait_send()
            for copy in self.shares(stage, 1 - self.place[3]):
                copy.wait_recv()


def keep_own(own, out, place, sem):
    return pltpu.make_async_copy(own, out.at[place[0], place[1], place[2]], sem)


def copies_of(dims):
    return 2 * sum(d - 1 for d in dims)


def halves_of(shape):
    rows, cols = shape
    half = cols // 2
    if half % 256 == 0:
        return [((0, rows), (0, half // 2)), ((0, rows), (half // 2, half // 2))]
    cut = rows // 32 * 16
    return [((at, count), (0, half)) for at, count in ((0, cut), (cut, rows - cut)) if count]


ORDERS = ((0, 1, 2), (0, 2, 1))


def pieces_of(dims, place, owns, outs, shapes, send, recv):
    made, at = [], 0
    for k, (own, out, shape) in enumerate(zip(owns, outs, shapes)):
        turn = k % 2
        pieces = []
        for order, (rows, cols) in zip(ORDERS[turn:] + ORDERS[:turn], halves_of(shape)):
            pieces.append(Spread(dims, place, own, out, pl.ds(*rows), cols, order, send.at[at], recv.at[at]))
            at += 1
        made.append(pieces)
    return made


def begin(pieces):
    for piece in pieces:
        piece.begin(0)


def advance(pieces, stage):
    for piece in pieces:
        piece.advance(stage)


def lower_bounds(lengths_ref, pos, offset):
    begin = jnp.zeros_like(pos)
    end = jnp.int32(0)
    for j in range(lengths_ref.shape[1]):
        end = end + lengths_ref[0, j]
        begin = jnp.where(end <= pos, end, begin)
    return jnp.maximum(begin, pos - (WINDOW - 1)) - offset + WINDOW


def norm_block(values, gain):
    x = values.astype(f32)
    return (x * lax.rsqrt(jnp.mean(x * x, axis=-1, keepdims=True) + EPSILON) * gain).astype(bf)


REST_EVENTS = {
    (0, 0, 0): ((2, 0),),
    (1, 0, 2): ((2, 1),),
    (1, 1, 2): ((3, 0),),
    (1, 3, 0): ((0, 0), (2, 2)),
    (1, 4, 2): ((3, 1), (0, 1)),
}


def front_kernel(dims, shapes, count, lengths_ref, x_ref, gains_ref, qkv_ref, out_ref_, proj_ref, up_ref, down_ref, *refs):
    names = iter(refs)
    take = lambda k: [next(names) for _ in range(k)]
    o_ref, lse_ref, q_out, k_out, v_out, n_out = take(6)
    w_outs = take(4)
    rest_outs = take(4)
    halo, staging, normed, q_scr, k_scr, v_scr, gain_scr, gain_own, bias, own_mixed, own_top, own_total = take(12)
    wide, blocks = take(8), take(8)
    first = take(4)
    swap_send, swap_recv, send, recv, keep_sem, halo_send, halo_recv, out_sem = take(8)

    place = my_place(dims)
    c = place[3]
    seq, item = lax.axis_index("seq"), lax.axis_index("item")
    rows, width = x_ref.shape
    hops = -(-WINDOW // rows)
    around = [(lax.rem(seq + d, count), item) for d in range(1, hops + 1)]
    behind = [(lax.rem(seq + count - d, count), item) for d in range(1, hops + 1)]
    with jax.named_scope("meet"):
        meet(peers(dims, place) + around + behind)

    mate = device_at(dims, sibling(place))
    shard = gains_ref.shape[1]
    gain_own[...] = jnp.zeros_like(gain_own)
    gain_own[0:2, 0:shard] = gains_ref[...]
    mine = seq * (dims[2] * 2) + item
    gain_own[...] = pltpu.roll(gain_own[...], mine * shard, 1)
    shards = [qkv_ref.at[0], qkv_ref.at[1], qkv_ref.at[2], gain_own, out_ref_, proj_ref, up_ref, down_ref]
    swaps = []
    for k in range(8):
        half = shapes[k][0] // 2
        part = wide[k].at[pl.ds(pl.multiple_of(c * half, 8), half)]
        part[...] = shards[k][...]
        swaps.append(
            pltpu.make_async_remote_copy(
                src_ref=shards[k], dst_ref=part, send_sem=swap_send.at[k], recv_sem=swap_recv.at[k],
                device_id=mate, device_id_type=MESH,
            )
        )
        swaps[k].start()
    outs = first + rest_outs
    keeps = [keep_own(blocks[k], outs[k], place, keep_sem.at[k]) for k in range(8)]
    pieces = pieces_of(dims, place, blocks, outs, shapes, send, recv)

    def ready(k):
        swaps[k].wait()
        blocks[k][...] = wide[k][...].astype(bf)
        keeps[k].start()

    odd = place[1] == 1
    lower, upper = WINDOW - rows, 2 * rows - WINDOW
    part = rows // 4

    def hop(send_slot, slot, source, target, device):
        return pltpu.make_async_remote_copy(
            src_ref=source, dst_ref=target, send_sem=halo_send.at[send_slot], recv_sem=halo_recv.at[slot],
            device_id=device, device_id_type=MESH,
        )

    cuts = [(0, 2 * part), (2 * part, part), (3 * part, part)]
    direct = [
        hop(n, n, x_ref.at[pl.ds(at, size)], halo.at[pl.ds(lower + at, size)], around[0])
        for n, (at, size) in enumerate(cuts)
    ]
    far = hop(3, 3, x_ref.at[pl.ds(upper, lower)], halo.at[pl.ds(0, lower)], around[1])
    aside = hop(4, 4, x_ref.at[pl.ds(0, 2 * part)], staging, behind[0])
    onward = hop(5, 0, staging, halo.at[pl.ds(lower, 2 * part)], around[1])
    has_next, has_far = seq + 1 < count, seq + 2 < count
    odd_next = jnp.logical_and(odd, has_next)
    even_next = jnp.logical_and(jnp.logical_not(odd), has_next)
    relays = jnp.logical_and(jnp.logical_not(odd), has_far)

    with jax.named_scope("swap"):
        for k in (3, 0, 1, 2):
            ready(k)
            begin(pieces[k])
        pl.when(odd_next)(aside.start)
        pl.when(even_next)(direct[2].start)
    with jax.named_scope("swap_rest"):
        for k in (4, 5, 6, 7):
            ready(k)
        for k in range(8):
            keeps[k].wait()
    with jax.named_scope("first_0"):
        for k in (3, 0, 1, 2):
            advance(pieces[k], 0)
        begin(pieces[6])
    with jax.named_scope("first_1"):
        for k in (3, 0, 1, 2):
            advance(pieces[k], 1)
        pl.when(has_far)(far.start)
        pl.when(has_next)(direct[1].start)
        pl.when(odd_next)(direct[2].start)
        pl.when(even_next)(direct[0].start)
    with jax.named_scope("relay"):

        @pl.when(relays)
        def _():
            aside.wait_recv()
            onward.start()

        for k in (7, 4, 5):
            begin(pieces[k])

    with jax.named_scope("first_2"):
        for k in (3, 0, 1, 2):
            advance(pieces[k], 2)
    with jax.named_scope("first_end"):
        for k in range(4):
            for piece in pieces[k]:
                piece.finish()
    total = first[3][...].astype(f32).reshape(dims[0] * dims[1] * dims[2] * 2, 8, width)
    gain_scr[...] = jnp.sum(total, axis=0)

    weights = [first[k] for k in range(3)]

    def project(slot, at):
        return dot(normed[at, :], weights[slot][...].reshape(width, width)).astype(bf)

    def own_rows(i, carry):
        at = pl.ds(pl.multiple_of(i * QB, QB), QB)
        ext = pl.ds(pl.multiple_of(WINDOW + i * QB, QB), QB)
        normed[ext, :] = norm_block(x_ref[at, :], gain_scr[0:1])
        q_scr[at, :] = project(0, ext) * jnp.asarray(0.125, bf)
        k_scr[ext, :] = project(1, ext)
        v_scr[ext, :] = project(2, ext)
        return carry

    def halo_rows(i, carry):
        at = pl.ds(pl.multiple_of(i * QB, QB), QB)
        pos = seq * rows - WINDOW + i * QB + lax.broadcasted_iota(jnp.int32, (QB, width), 0)
        block = jnp.where(pos >= 0, halo[at, :].astype(f32), 0.0)
        normed[at, :] = norm_block(block, gain_scr[0:1])
        k_scr[at, :] = project(1, at)
        v_scr[at, :] = project(2, at)
        return carry

    nq, pairs = rows // QB, width // 128

    def events(stage, hp, qb):
        for (part, pair, block), moves in REST_EVENTS.items():
            if (part, block) != (stage, qb):
                continue

            @pl.when(hp == pair)
            def _():
                for k, what in moves:
                    with jax.named_scope("rest_%d_%d" % (k, what + 1)):
                        advance(pieces[4 + k], what)

    lane = lax.broadcasted_iota(jnp.int32, (QB, 128), 1)

    def masks(qb):
        pos = seq * rows + qb * QB + lax.broadcasted_iota(jnp.int32, (QB, 1), 0)
        lo = lower_bounds(lengths_ref, pos, seq * rows)
        kpos = qb * QB + lax.broadcasted_iota(jnp.int32, (QB, WINDOW + QB), 1)
        qpos = WINDOW + qb * QB + lax.broadcasted_iota(jnp.int32, (QB, WINDOW + QB), 0)
        bias[qb] = jnp.where((kpos >= lo) & (kpos <= qpos), 0.0, NEG)

    low_half = lane < 64

    def both(pair):
        return jnp.where(low_half, pair[0], pair[1])

    def attend_to(at, keys, lanes, mask):
        kw, vw = k_scr[keys, lanes], v_scr[keys, lanes]
        tops, totals, found = [], [], []
        for qh in halves(q_scr[at, lanes]):
            s = dot(qh, kw, NT) + mask
            m = jnp.max(s, axis=1, keepdims=True)
            p = jnp.exp(s - m)
            tops.append(m)
            totals.append(jnp.sum(p, axis=1, keepdims=True))
            found.append(dot(p.astype(bf), vw))
        return both(tops), both(totals), both(found)

    def own_keys(hp, carry):
        lanes = pl.ds(pl.multiple_of(hp * 128, 128), 128)
        for qb in range(nq):
            events(0, hp, qb)
            at, keys = pl.ds(qb * QB, QB), pl.ds(WINDOW, (qb + 1) * QB)
            top, total, mixed = attend_to(at, keys, lanes, bias[qb, :, WINDOW - qb * QB :])
            own_top[hp, at, :] = top
            own_total[hp, at, :] = total
            own_mixed[at, lanes] = mixed
        return carry

    def halo_keys(hp, carry):
        lanes = pl.ds(pl.multiple_of(hp * 128, 128), 128)
        for qb in range(nq):
            events(1, hp, qb)
            at, keys = pl.ds(qb * QB, QB), pl.ds(qb * QB, WINDOW - qb * QB)
            top, total, mixed = attend_to(at, keys, lanes, bias[qb, :, : WINDOW - qb * QB])
            before = own_top[hp, at, :]
            highest = jnp.maximum(before, top)
            by_own, by_halo = jnp.exp(before - highest), jnp.exp(top - highest)
            total = own_total[hp, at, :] * by_own + total * by_halo
            mixed = own_mixed[at, lanes] * by_own + mixed * by_halo
            o_ref[at, lanes] = (mixed * (1.0 / total)).astype(bf)
            logs = (highest + jnp.log(total)).T
            lse_ref[hp, 0:1, at] = logs[0:1]
            lse_ref[hp, 1:2, at] = logs[64:65]
        return carry

    with jax.named_scope("own_rows"):
        lax.fori_loop(0, nq, own_rows, 0)
        for qb in range(nq):
            masks(qb)
    with jax.named_scope("own_keys"):
        lax.fori_loop(0, pairs, own_keys, 0)
    with jax.named_scope("wait_halo"):

        @pl.when(seq >= 1)
        def _():
            for copy in direct:
                copy.wait_recv()

        pl.when(seq >= 2)(far.wait_recv)
    with jax.named_scope("halo_rows"):
        lax.fori_loop(0, WINDOW // QB, halo_rows, 0)
    saved = [
        pltpu.make_async_copy(a, b, out_sem.at[n])
        for n, (a, b) in enumerate(
            zip([q_scr, k_scr, v_scr, normed] + first[:3] + [gain_scr], [q_out, k_out, v_out, n_out] + w_outs)
        )
    ]
    for copy in saved:
        copy.start()
    with jax.named_scope("halo_keys"):
        lax.fori_loop(0, pairs, halo_keys, 0)
    with jax.named_scope("rest_end"):
        for piece in pieces[5]:
            piece.advance(0, False)
        for k in (7, 4):
            advance(pieces[k], 2)
        for k in range(4, 8):
            for piece in pieces[k]:
                piece.finish((0,) if k == 5 else (0, 1, 2))
        pl.when(has_far)(far.wait_send)
        pl.when(has_next)(direct[1].wait_send)
        pl.when(has_next)(direct[2].wait_send)
        pl.when(even_next)(direct[0].wait_send)
        pl.when(odd_next)(aside.wait_send)
        pl.when(relays)(onward.wait_send)
        for copy in saved:
            copy.wait()


def front(lengths, x, gains, w_qkv, others, dims, count):
    rows, width = x.shape
    shard = w_qkv.shape[1]
    ext = WINDOW + rows
    shapes = [(2 * shard, width)] * 3 + [(16, width)] + [(2 * w.shape[0], w.shape[1]) for w in others]
    copies = copies_of(dims)
    vmem = pl.BlockSpec(memory_space=pltpu.VMEM)
    hbm = pl.BlockSpec(memory_space=pl.ANY)
    dma = pltpu.SemaphoreType.DMA
    count_pieces = sum(len(halves_of(s)) for s in shapes)
    nh, nq = width // 128, rows // QB
    sds = jax.ShapeDtypeStruct
    got = pl.pallas_call(
        functools.partial(front_kernel, dims, shapes, count),
        in_specs=[pl.BlockSpec(memory_space=pltpu.SMEM)] + [vmem] * 7,
        out_specs=[vmem] * 2 + [hbm] * 12,
        out_shape=[
            sds((rows, width), bf), sds((nh, 8, rows), f32),
            sds((rows, width), bf), sds((ext, width), bf), sds((ext, width), bf), sds((ext, width), bf),
        ]
        + [sds(dims + shapes[0], bf)] * 3 + [sds((8, width), f32)]
        + [sds(dims + s, bf) for s in shapes[4:]],
        scratch_shapes=[
            pltpu.VMEM((WINDOW, width), bf), pltpu.VMEM((rows // 2, width), bf), pltpu.VMEM((ext, width), bf),
            pltpu.VMEM((rows, width), bf),
            pltpu.VMEM((ext, width), bf), pltpu.VMEM((ext, width), bf), pltpu.VMEM((8, width), f32),
            pltpu.VMEM((8, width), f32), pltpu.VMEM((nq, QB, WINDOW + QB), f32),
            pltpu.VMEM((rows, width), f32), pltpu.VMEM((nh, rows, 128), f32), pltpu.VMEM((nh, rows, 128), f32),
        ]
        + [pltpu.VMEM(s, f32) for s in shapes]
        + [pltpu.VMEM(s, bf) for s in shapes]
        + [pltpu.VMEM(dims + s, bf) for s in shapes[:4]]
        + [
            dma((8,)), dma((8,)), dma((count_pieces, copies)), dma((count_pieces, copies)), dma((8,)),
            dma((6,)), dma((5,)), dma((8,)),
        ],
        compiler_params=pltpu.CompilerParams(
            collective_id=1, has_side_effects=True, vmem_limit_bytes=60 * 2**20
        ),
        cost_estimate=pl.CostEstimate(flops=4 * rows * 1792 * 768 * 3, bytes_accessed=14 * 2**20, transcendentals=0),
        name="front",
    )(lengths, x, gains, w_qkv, *others)
    return got


def piece_cuts(shape):
    return [(pl.ds(*rows), pl.ds(*cols)) for rows, cols in halves_of(shape)]


class Collapse:
    def __init__(self, dims, place, shape, turn, grad, out, buffers, send, recv):
        self.dims, self.place, self.shape = dims, place, shape
        self.grad, self.out, self.send, self.recv = grad, out, send, recv
        self.acc, self.box0, self.box1, self.box2, self.box3, self.fin, self.box4 = buffers
        z, y, x, c = place
        far_x, far_y = device_at(dims, (z, y, 1 - x, c)), device_at(dims, (z, 1 - y, x, c))
        every = slice(None)
        by_x = [(far_x, (every, every, 1 - x), (every, every, x)), (far_y, (every, 1 - y, x), (every, y, x))]
        by_y = [(far_y, (every, 1 - y, every), (every, y, every)), (far_x, (every, y, 1 - x), (every, y, x))]
        ways = [by_x, by_y] if turn == 0 else [by_y, by_x]
        self.pieces = list(zip(piece_cuts(shape), ways))

    def columns(self, core):
        half = self.shape[1] // 2
        return pl.ds(pl.multiple_of(core * half, 128), half)

    def copy(self, slot, source, target, device):
        return pltpu.make_async_remote_copy(
            src_ref=source, dst_ref=target, send_sem=self.send.at[slot], recv_sem=self.recv.at[slot],
            device_id=device, device_id_type=MESH,
        )

    def copies(self, stage):
        z, y, x, c = self.place
        mate = device_at(self.dims, sibling(self.place))
        every = slice(None)
        if stage == 0:
            source = self.grad.at[every, every, every, every, self.columns(1 - c)]
            return [self.copy(0, source, self.box0, mate)]
        if stage == 4:
            half = self.shape[0] // 2
            source = self.fin.at[pl.ds(pl.multiple_of((1 - c) * half, 8), half)]
            return [self.copy(1, source, self.box4, mate)]
        made = []
        for at, (cut, ways) in enumerate(self.pieces):
            first = 2 + at * (2 + self.dims[0] - 1)
            if stage in (1, 2):
                device, give, _ = ways[stage - 1]
                box = (self.box1 if stage == 1 else self.box2).at[(every,) * (3 - stage) + cut]
                made.append(self.copy(first + stage - 1, self.acc.at[give + cut], box, device))
            else:
                for by in range(1, self.dims[0]):
                    to = lax.rem(z + by, self.dims[0])
                    made.append(
                        self.copy(
                            first + 1 + by, self.acc.at[(to, y, x) + cut], self.box3.at[(by - 1,) + cut],
                            device_at(self.dims, (to, y, x, c)),
                        )
                    )
        return made

    def local(self, sem):
        every = slice(None)
        source = self.grad.at[every, every, every, every, self.columns(self.place[3])]
        return pltpu.make_async_copy(source, self.acc, sem)

    def start(self, stage):
        for copy in self.copies(stage):
            copy.start()

    def add(self, stage):
        for copy in self.copies(stage):
            copy.wait_recv()
        z, y, x, c = self.place
        dims = self.dims
        if stage == 0:

            def body(i, carry):
                a, b, d = i // (dims[1] * dims[2]), lax.rem(i // dims[2], dims[1]), lax.rem(i, dims[2])
                self.acc[a, b, d] = self.acc[a, b, d] + self.box0[a, b, d]
                return carry

            lax.fori_loop(0, dims[0] * dims[1] * dims[2], body, 0)
        elif stage == 1:
            for cut, ways in self.pieces:
                by_x = not isinstance(ways[0][2][2], slice)

                def body(i, carry):
                    a, b = i // 2, lax.rem(i, 2)
                    at = ((a, b, x) if by_x else (a, y, b)) + cut
                    self.acc[at] = self.acc[at] + self.box1[(a, b) + cut]
                    return carry

                lax.fori_loop(0, dims[0] * 2, body, 0)
        elif stage == 2:

            def body(a, carry):
                self.acc[a, y, x] = self.acc[a, y, x] + self.box2[a]
                return carry

            lax.fori_loop(0, dims[0], body, 0)
        elif stage == 3:
            total = self.acc[z, y, x].astype(f32)
            for by in range(1, dims[0]):
                total = total + self.box3[by - 1].astype(f32)
            self.fin[...] = total
        else:
            half = self.shape[0] // 2
            mine = self.fin[pl.ds(pl.multiple_of(c * half, 8), half)]
            other = self.box4[...]
            width = self.shape[1] // 2
            self.out[:, :width] = jnp.where(c == 0, mine, other)
            self.out[:, width:] = jnp.where(c == 0, other, mine)

    def finish(self):
        for stage in range(5):
            for copy in self.copies(stage):
                copy.wait_send()


def collapse_scratch(dims, shapes):
    found = []
    for rows, cols in shapes:
        half = cols // 2
        found += [
            pltpu.VMEM(dims + (rows, half), bf),
            pltpu.VMEM(dims + (rows, half), bf),
            pltpu.VMEM((dims[0], 2, rows, half), bf),
            pltpu.VMEM((dims[0], rows, half), bf),
            pltpu.VMEM((dims[0] - 1, rows, half), bf),
            pltpu.VMEM((rows, half), f32),
            pltpu.VMEM((rows // 2, half), f32),
        ]
    dma = pltpu.SemaphoreType.DMA
    n = len(shapes)
    slots = 2 + 2 * (2 + dims[0] - 1)
    return found + [dma((n, slots)), dma((n, slots)), dma((n,))]


def collapses_of(dims, place, shapes, grads, outs, scratch):
    n = len(shapes)
    send, recv, local_sem = scratch[7 * n :]
    made = [
        Collapse(dims, place, shapes[k], k % 2, grads[k], outs[k], scratch[7 * k : 7 * k + 7], send.at[k], recv.at[k])
        for k in range(n)
    ]
    return made, [made[k].local(local_sem.at[k]) for k in range(n)]


def run_collapse(sums, locals_, k, stage):
    if stage < 0:
        locals_[k].start()
        sums[k].start(0)
        return
    if stage == 0:
        locals_[k].wait()
    sums[k].add(stage)
    if stage < 4:
        sums[k].start(stage + 1)


def back_kernel(lo_ref, q_ref, do_ref, o_ref, lse_ref, k_ref, v_ref, dq_ref, dk_ref, dv_ref, bias, dk_acc, dv_acc):
    hp, qb = pl.program_id(0), pl.program_id(1)
    span = WINDOW + QB
    start = pl.multiple_of(qb * QB, QB)

    @pl.when(hp == 0)
    def _():
        base = qb * QB
        kpos = base + lax.broadcasted_iota(jnp.int32, (span, QB), 0)
        qpos = WINDOW + base + lax.broadcasted_iota(jnp.int32, (span, QB), 1)
        ok = (kpos >= lo_ref[...]) & (kpos <= qpos)
        bias[qb] = jnp.where(ok, 0.0, NEG)

    @pl.when(qb == 0)
    def _():
        dk_acc[...] = jnp.zeros_like(dk_acc)
        dv_acc[...] = jnp.zeros_like(dv_acc)

    q_heads = halves(q_ref[...])
    do = do_ref[...]
    d_heads = halves(do)
    prod = do.astype(f32) * o_ref[...].astype(f32)
    row = lax.broadcasted_iota(jnp.int32, (8, 128), 0)
    lane = lax.broadcasted_iota(jnp.int32, (8, 128), 1)
    pick = jnp.where(row == lane // 64, 1.0, 0.0).astype(f32)
    delta = lax.dot_general(pick, prod, NT, precision=lax.Precision.HIGHEST, preferred_element_type=f32)
    lse = lse_ref[0]
    at = pl.ds(start, span)
    kw, vw = k_ref[at, :], v_ref[at, :]
    low_p, low_s, dq = [], [], []
    for h in range(2):
        s = dot(kw, q_heads[h], NT) + bias[qb]
        p = jnp.exp(s - lse[h : h + 1])
        dp = dot(vw, d_heads[h], NT)
        ds = (p * (dp - delta[h : h + 1])).astype(bf)
        low_p.append(p.astype(bf))
        low_s.append(ds)
        dq.append(dot(ds, kw, TN))
    dv_acc[at, :] += dot(jnp.concatenate(low_p, axis=1), jnp.concatenate(d_heads, axis=0))
    dk_acc[at, :] += dot(jnp.concatenate(low_s, axis=1), jnp.concatenate(q_heads, axis=0))
    lane = lax.broadcasted_iota(jnp.int32, (QB, 128), 1)
    dq_ref[...] = (jnp.where(lane < 64, dq[0], dq[1]) * 0.125).astype(bf)

    @pl.when(qb == pl.num_programs(1) - 1)
    def _():
        dk_ref[...] = dk_acc[...].astype(bf)
        dv_ref[...] = dv_acc[...].astype(bf)


def attend_back(q, do, o, lse, k, v, lo_row):
    rows, width = q.shape
    ext = k.shape[0]
    nq, nh = rows // QB, width // 128
    blk = pl.BlockSpec((QB, 128), lambda h, i: (i, h))
    full = pl.BlockSpec((ext, 128), lambda h, i: (0, h))
    return pl.pallas_call(
        back_kernel,
        grid=(nh, nq),
        in_specs=[pl.BlockSpec((1, QB), lambda h, i: (0, i)), blk, blk, blk]
        + [pl.BlockSpec((1, 8, QB), lambda h, i: (h, 0, i)), full, full],
        out_specs=[blk, full, full],
        out_shape=[
            jax.ShapeDtypeStruct((rows, width), bf),
            jax.ShapeDtypeStruct((ext, width), bf),
            jax.ShapeDtypeStruct((ext, width), bf),
        ],
        scratch_shapes=[
            pltpu.VMEM((nq, WINDOW + QB, QB), f32),
            pltpu.VMEM((ext, 128), f32),
            pltpu.VMEM((ext, 128), f32),
        ],
        compiler_params=pltpu.CompilerParams(vmem_limit_bytes=56 * 2**20),
        name="attend_back",
    )(lo_row, q, do, o, lse, k, v)


SUM_EVENTS = {
    (0, 1): ((2, 0), (0, 0)),
    (0, 2): ((1, 0),),
    (0, 3): ((2, 1),),
    (1, 1): ((1, 2), (0, 2)),
    (1, 3): ((2, 3),),
    (1, 5): ((2, 4),),
}
RETURN_STEP = 1


def back_kernel_paired(dims, shapes, count, lengths_ref, lse_ref, delta_ref, *refs):
    n = len(shapes)
    names = iter(refs)
    take = lambda k: [next(names) for _ in range(k)]
    sources = take(6)
    grads = take(n)
    dq_out, dk_out, dv_out, near_out, rest_out = take(5)
    sums_out = take(n)
    q, do, k, v, wk, wv = buffers = take(6)
    dk, dv, dq_acc, dk_acc, dv_acc, bias = take(6)
    load_sem, out_sem, back_send, back_recv = take(4)
    scratch = list(names)

    place = my_place(dims)
    seq, item = lax.axis_index("seq"), lax.axis_index("item")
    rows, width = q.shape
    nq, pairs = rows // QB, width // 128
    loads = [pltpu.make_async_copy(a, b, load_sem.at[m]) for m, (a, b) in enumerate(zip(sources, buffers))]
    for load in loads:
        load.start()
    ahead, behind = (lax.rem(seq + 1, count), item), (lax.rem(seq + count - 1, count), item)
    with jax.named_scope("meet"):
        meet(peers(dims, place) + [ahead, behind])
    sums, locals_ = collapses_of(dims, place, shapes, grads, sums_out, scratch)
    for a in (2, 1, 0):
        run_collapse(sums, locals_, a, -1)

    with jax.named_scope("masks"):
        for qb in range(nq):
            pos = seq * rows + qb * QB + lax.broadcasted_iota(jnp.int32, (1, QB), 1)
            lo = lower_bounds(lengths_ref, pos, seq * rows)
            kpos = qb * QB + lax.broadcasted_iota(jnp.int32, (WINDOW + QB, QB), 0)
            qpos = WINDOW + qb * QB + lax.broadcasted_iota(jnp.int32, (WINDOW + QB, QB), 1)
            bias[qb] = jnp.where((kpos >= lo) & (kpos <= qpos), 0.0, NEG).astype(bf)
    with jax.named_scope("load"):
        for load in loads:
            load.wait()

    def events(part, hp):
        for (when, pair), moves in SUM_EVENTS.items():
            if when != part:
                continue

            @pl.when(hp == pair)
            def _():
                for a, stage in moves:
                    with jax.named_scope("reduce_%d_%d" % (a, stage + 1)):
                        run_collapse(sums, locals_, a, stage)

    lane = lax.broadcasted_iota(jnp.int32, (QB, 128), 1)

    def block(hp, lanes, at, keys, mask):
        q_heads, d_heads = halves(q[at, lanes]), halves(do[at, lanes])
        lse, delta = lse_ref[hp, :, at], delta_ref[hp, :, at]
        kw, vw = k[keys, lanes], v[keys, lanes]
        low_p, low_s, found = [], [], []
        for h in range(2):
            s = dot(kw, q_heads[h], NT) + mask.astype(f32)
            p = jnp.exp(s - lse[h : h + 1])
            dp = dot(vw, d_heads[h], NT)
            ds = (p * (dp - delta[h : h + 1])).astype(bf)
            low_p.append(p.astype(bf))
            low_s.append(ds)
            found.append(dot(ds, kw, TN))
        dv_part = dot(jnp.concatenate(low_p, axis=1), jnp.concatenate(d_heads, axis=0))
        dk_part = dot(jnp.concatenate(low_s, axis=1), jnp.concatenate(q_heads, axis=0))
        return jnp.where(lane < 64, found[0], found[1]), dk_part, dv_part

    def halo_keys(hp, carry):
        events(0, hp)
        lanes = pl.ds(pl.multiple_of(hp * 128, 128), 128)
        for qb in range(nq):
            at, size = pl.ds(qb * QB, QB), WINDOW - qb * QB
            keys = pl.ds(qb * QB, size)
            dq_part, dk_part, dv_part = block(hp, lanes, at, keys, bias[qb, :size, :])
            dq_acc[at, lanes] = dq_part
            if qb == 0:
                dk_acc[...] = dk_part
                dv_acc[...] = dv_part
            else:
                dk_acc[keys, :] += dk_part
                dv_acc[keys, :] += dv_part
        dk[0:WINDOW, lanes] = dk_acc[...].astype(bf)
        dv[0:WINDOW, lanes] = dv_acc[...].astype(bf)
        return carry

    with jax.named_scope("halo_keys"):
        lax.fori_loop(0, pairs, halo_keys, 0)

    def halo_rows(i, carry):
        at = pl.ds(pl.multiple_of(i * QB, QB), QB)
        total = dot(dk[at, :], wk[...].reshape(width, width), NT) + dot(dv[at, :], wv[...].reshape(width, width), NT)
        k[at, :] = total.astype(bf)
        return carry

    lower, part = WINDOW - rows, rows // 4
    returned = [
        pltpu.make_async_remote_copy(
            src_ref=k.at[pl.ds(lower + m * part, part)], dst_ref=near_out.at[pl.ds(m * part, part)],
            send_sem=back_send.at[m], recv_sem=back_recv.at[m], device_id=behind, device_id_type=MESH,
        )
        for m in range(2)
    ]
    for a, stage in ((2, 2), (1, 1), (0, 1)):
        with jax.named_scope("reduce_%d_%d" % (a, stage + 1)):
            run_collapse(sums, locals_, a, stage)
    with jax.named_scope("halo_rows"):
        lax.fori_loop(lower // QB, (lower + part) // QB, halo_rows, 0)
        pl.when(seq >= 1)(returned[0].start)
        lax.fori_loop(0, lower // QB, halo_rows, 0)
        lax.fori_loop((lower + part) // QB, WINDOW // QB, halo_rows, 0)
        rest = [
            pltpu.make_async_copy(k.at[pl.ds(0, lower)], rest_out.at[pl.ds(0, lower)], out_sem.at[0]),
            pltpu.make_async_copy(
                k.at[pl.ds(lower + 2 * part, rows - 2 * part)], rest_out.at[pl.ds(lower, rows - 2 * part)], out_sem.at[1]
            ),
        ]
        rest += [
            pltpu.make_async_copy(a.at[pl.ds(0, WINDOW)], b.at[pl.ds(0, WINDOW)], out_sem.at[2 + m])
            for m, (a, b) in enumerate([(dk, dk_out), (dv, dv_out)])
        ]
        for copy in rest:
            copy.start()

    def own_keys(hp, carry):
        events(1, hp)
        pl.when(jnp.logical_and(hp == RETURN_STEP - place[1], seq >= 1))(returned[1].start)
        lanes = pl.ds(pl.multiple_of(hp * 128, 128), 128)
        for qb in reversed(range(nq)):
            at, size = pl.ds(qb * QB, QB), (qb + 1) * QB
            keys, own = pl.ds(WINDOW, size), pl.ds(0, size)
            dq_part, dk_part, dv_part = block(hp, lanes, at, keys, bias[qb, WINDOW - qb * QB :, :])
            q[at, lanes] = ((dq_acc[at, lanes] + dq_part) * 0.125).astype(bf)
            if qb == nq - 1:
                dk_acc[own, :] = dk_part
                dv_acc[own, :] = dv_part
            else:
                dk_acc[own, :] += dk_part
                dv_acc[own, :] += dv_part
        dk[WINDOW:, lanes] = dk_acc[0:rows, :].astype(bf)
        dv[WINDOW:, lanes] = dv_acc[0:rows, :].astype(bf)
        return carry

    with jax.named_scope("own_keys"):
        lax.fori_loop(0, pairs, own_keys, 0)
    own = pl.ds(WINDOW, rows)
    stores = rest + [
        pltpu.make_async_copy(a, b, out_sem.at[4 + m])
        for m, (a, b) in enumerate([(q, dq_out), (dk.at[own], dk_out.at[own]), (dv.at[own], dv_out.at[own])])
    ]
    for store in stores[4:]:
        store.start()
    with jax.named_scope("finish"):
        for stage in (3, 4):
            for a in (1, 0):
                run_collapse(sums, locals_, a, stage)
        for one in sums:
            one.finish()
        for store in stores:
            store.wait()

        for copy in returned:
            pl.when(seq >= 1)(copy.wait_send)
            pl.when(seq + 1 < count)(copy.wait_recv)


def back(lengths, lse, delta, arrays, grads, dims, count):
    q, do, k, v, wk, wv = arrays
    rows, width = q.shape
    ext = k.shape[0]
    nq = rows // QB
    shapes = [g.shape[3:] for g in grads]
    vmem = pl.BlockSpec(memory_space=pltpu.VMEM)
    hbm = pl.BlockSpec(memory_space=pl.ANY)
    dma = pltpu.SemaphoreType.DMA
    sds = jax.ShapeDtypeStruct
    part = rows // 2
    got = pl.pallas_call(
        functools.partial(back_kernel_paired, dims, shapes, count),
        in_specs=[pl.BlockSpec(memory_space=pltpu.SMEM), vmem, vmem] + [hbm] * (6 + len(grads)),
        out_specs=[hbm] * 5 + [vmem] * len(grads),
        out_shape=[
            sds((rows, width), bf), sds((ext, width), bf), sds((ext, width), bf),
            sds((part, width), bf), sds((WINDOW - part, width), bf),
        ]
        + [sds((r // 2, c), f32) for r, c in shapes],
        scratch_shapes=[pltpu.VMEM(a.shape, bf) for a in arrays]
        + [
            pltpu.VMEM((ext, width), bf), pltpu.VMEM((ext, width), bf), pltpu.VMEM((rows, width), f32),
            pltpu.VMEM((WINDOW, 128), f32), pltpu.VMEM((WINDOW, 128), f32),
            pltpu.VMEM((nq, WINDOW + QB, QB), bf),
            dma((6,)), dma((7,)), dma((2,)), dma((2,)),
        ]
        + collapse_scratch(dims, shapes),
        compiler_params=pltpu.CompilerParams(
            collective_id=3, has_side_effects=True, vmem_limit_bytes=63 * 2**20
        ),
        name="back",
    )(lengths, lse, delta, *arrays, *grads)
    return got[:5], got[5:]


GELU_A, GELU_B = 0.7978845608028654, 0.044715
MB = 512
PROJ_STEPS = (0, 1)
GATHER_STEP = 0


def middle_kernel(dims, proj_shape, bound_ref, cont_ref, gain_ref, *refs):
    names = iter(refs)
    take = lambda k: [next(names) for _ in range(k)]
    sources = take(8)
    y_out, p_out, dr_out, do_out, gain_out, delta_out, sum_proj, g_out, g_up, g_down = take(10)
    x, o, cot, pcot, wo, wu, wd, wp = buffers = take(8)
    n2, r1, act, slope, low_c, dyl, stage, grad_proj = take(8)
    load_sem, stage_sem, out_sem, send, recv = take(5)
    scratch = list(names)

    place = my_place(dims)
    z, y, x_, c = place
    line = (slice(None), y, x_)
    pairs = list(zip(sources[:7], buffers[:7])) + [(sources[7].at[line], wp.at[line])]
    loads = [pltpu.make_async_copy(a, b, load_sem.at[k]) for k, (a, b) in enumerate(pairs)]
    for load in loads:
        load.start()
    with jax.named_scope("meet"):
        meet(peers(dims, place))
    (total,), locals_ = collapses_of(dims, place, [proj_shape], [grad_proj], [sum_proj], scratch)

    rows, width = x.shape
    chunks = wu.shape[1] // width
    gain = gain_ref[1:2]
    pieces = [
        Spread(dims, place, None, wp, pl.ds(*at), cols, order, send.at[k], recv.at[k])
        for k, (order, (at, cols)) in enumerate(zip(ORDERS, halves_of(wp.shape[3:])))
    ]
    with jax.named_scope("load"):
        loads[7].wait()
        for piece in pieces:
            piece.begin(1)
        for load in loads[:7]:
            load.wait()

    def edge_of(at):
        edge = (bound_ref[:, at] * (1 - cont_ref[:, at])).astype(f32)
        return jnp.broadcast_to(edge, (8, MB)).T[:, 0:1]

    def forward(i, carry):
        at = pl.ds(pl.multiple_of(i * MB, MB), MB)
        r = x[at, :].astype(f32) + dot(o[at, :], wo[...])
        r1[at, :] = r
        scale = lax.rsqrt(jnp.mean(r * r, axis=-1, keepdims=True) + EPSILON)
        n2[at, :] = (r * scale * gain).astype(bf)
        y = r
        for j in range(chunks):
            cols = slice(j * width, (j + 1) * width)
            u = dot(n2[at, :], wu[:, cols])
            square = u * u
            t = jnp.tanh(GELU_A * (u + GELU_B * square * u))
            half = 0.5 * (1.0 + t)
            act[at, cols] = (u * half).astype(bf)
            slope[at, cols] = (half + 0.5 * u * (1.0 - t * t) * (GELU_A + 3.0 * GELU_A * GELU_B * square)).astype(bf)
            y = y + dot(act[at, cols], wd[cols, :])
        low_c[at, :] = (edge_of(at) * pcot[at, :].astype(f32)).astype(bf)
        dr_out[at, :] = cot[at, :].astype(f32)
        cot[at, :] = y.astype(bf)

        @pl.when(i == GATHER_STEP)
        def _():
            with jax.named_scope("proj_1"):
                for piece in pieces:
                    piece.advance(1)

        return carry

    def project(i, carry):
        at = pl.ds(pl.multiple_of(i * MB, MB), MB)
        weight = wp[...].reshape(width, wp.shape[-1])
        d = dr_out[at, :] + dot(low_c[at, :], weight, NT)
        dr_out[at, :] = d
        dyl[at, :] = d.astype(bf)
        pcot[at, :] = (edge_of(at) * dot(cot[at, :], weight)).astype(bf)
        return carry

    with jax.named_scope("forward"):
        lax.fori_loop(0, rows // MB, forward, 0)
    with jax.named_scope("proj_2"):
        for piece in pieces:
            piece.advance(2)
        for piece in pieces:
            piece.finish((1, 2))
    with jax.named_scope("project"):
        lax.fori_loop(0, rows // MB, project, 0)
    stores = [pltpu.make_async_copy(cot, y_out, out_sem.at[0]), pltpu.make_async_copy(pcot, p_out, out_sem.at[1])]
    for store in stores:
        store.start()

    flying = {}

    def emit(target, left, right):
        tall, wide = left.shape[1] // width, right.shape[1] // width
        for j in range(tall):
            for k in range(wide):
                slot = emit.count % 2
                emit.count += 1
                if slot in flying:
                    flying[slot].wait()
                rows_at, cols_at = slice(j * width, (j + 1) * width), slice(k * width, (k + 1) * width)
                stage[slot] = dot(left[:, rows_at], right[:, cols_at], TN).astype(bf)
                copy = pltpu.make_async_copy(
                    stage.at[slot], target.at[pl.ds(j * width, width), pl.ds(k * width, width)], stage_sem.at[slot]
                )
                copy.start()
                flying[slot] = copy

    emit.count = 0
    with jax.named_scope("grad_proj"):
        for k in range(proj_shape[1] // width):
            cols = slice(k * width, (k + 1) * width)
            got = dot(cot[...], low_c[:, cols], TN).astype(bf)
            grad_proj[:, :, :, :, cols] = got.reshape(dims + (proj_shape[0], width))
        run_collapse([total], locals_, 0, -1)
    with jax.named_scope("grad_down"):
        emit(g_down, act, dyl)

    row = lax.broadcasted_iota(jnp.int32, (16, width), 0)
    lane = lax.broadcasted_iota(jnp.int32, (16, width), 1)
    heads = jnp.where(row == lane // 64, 1.0, 0.0).astype(f32)

    def backward(i, carry):
        for step, when in enumerate(PROJ_STEPS):

            @pl.when(i == when)
            def _():
                with jax.named_scope("reduce_%d" % step):
                    run_collapse([total], locals_, 0, step)

        at = pl.ds(pl.multiple_of(i * MB, MB), MB)
        dn = jnp.zeros((MB, width), f32)
        for j in range(chunks):
            cols = slice(j * width, (j + 1) * width)
            du = (dot(dyl[at, :], wd[cols, :], NT) * slope[at, cols].astype(f32)).astype(bf)
            slope[at, cols] = du
            dn = dn + dot(du, wu[:, cols], NT)
        r = r1[at, :]
        scale = lax.rsqrt(jnp.mean(r * r, axis=-1, keepdims=True) + EPSILON)
        unit = r * scale
        by_gain = dn * gain
        inner = jnp.mean(by_gain * unit, axis=-1, keepdims=True)
        dr = dr_out[at, :] + scale * (by_gain - unit * inner)
        dr_out[at, :] = dr
        low_dr = dr.astype(bf)
        dyl[at, :] = low_dr
        low_do = dot(low_dr, wo[...], NT).astype(bf)
        x[at, :] = low_do
        delta = lax.dot_general(
            heads, low_do.astype(f32) * o[at, :].astype(f32), NT,
            precision=lax.Precision.HIGHEST, preferred_element_type=f32,
        )
        for hp in range(width // 128):
            delta_out[hp, 0:2, at] = delta[2 * hp : 2 * hp + 2]
        return carry + jnp.sum(dn * unit, axis=0, keepdims=True)

    with jax.named_scope("backward"):
        gain_out[...] = lax.fori_loop(0, rows // MB, backward, jnp.zeros((1, width), f32))
    stores.append(pltpu.make_async_copy(x, do_out, out_sem.at[2]))
    stores[-1].start()
    with jax.named_scope("grad_out"):
        run_collapse([total], locals_, 0, 2)
        emit(g_out, o, dyl)
    with jax.named_scope("grad_up"):
        emit(g_up, n2, slope)
    with jax.named_scope("finish"):
        for stage in (3, 4):
            run_collapse([total], locals_, 0, stage)
        for copy in list(flying.values()) + stores:
            copy.wait()
        total.finish()


def middle(bound, cont, gain, arrays, dims):
    x, o, cot, pcot, wo, wu, wd, wp = arrays
    rows, width = x.shape
    ff, proj = wu.shape[1], wp.shape[-1]
    copies = copies_of(dims)
    pair = width // (dims[0] * dims[1] * dims[2])
    vmem = pl.BlockSpec(memory_space=pltpu.VMEM)
    hbm = pl.BlockSpec(memory_space=pl.ANY)
    dma = pltpu.SemaphoreType.DMA
    sds = jax.ShapeDtypeStruct
    return pl.pallas_call(
        functools.partial(middle_kernel, dims, (pair, proj)),
        in_specs=[vmem] * 3 + [hbm] * 8,
        out_specs=[hbm, hbm, vmem, hbm, vmem, vmem, vmem, hbm, hbm, hbm],
        out_shape=[
            sds((rows, width), bf), sds((rows, proj), bf), sds((rows, width), f32), sds((rows, width), bf),
            sds((1, width), f32), sds((width // 128, 8, rows), f32), sds((pair // 2, proj), f32),
            sds(wo.shape, bf), sds(wu.shape, bf), sds(wd.shape, bf),
        ],
        scratch_shapes=[pltpu.VMEM(a.shape, bf) for a in arrays]
        + [
            pltpu.VMEM((rows, width), bf), pltpu.VMEM((rows, width), f32), pltpu.VMEM((rows, ff), bf),
            pltpu.VMEM((rows, ff), bf), pltpu.VMEM((rows, proj), bf), pltpu.VMEM((rows, width), bf),
            pltpu.VMEM((2, width, width), bf), pltpu.VMEM(dims + (pair, proj), bf),
            dma((8,)), dma((2,)), dma((3,)), dma((2, copies)), dma((2, copies)),
        ]
        + collapse_scratch(dims, [(pair, proj)]),
        compiler_params=pltpu.CompilerParams(
            collective_id=2, has_side_effects=True, vmem_limit_bytes=62 * 2**20
        ),
        name="middle",
    )(bound, cont, gain, *arrays)


ROW_OUT, ROW_UP, ROW_PROJ, ROW_DOWN, ROW_GAIN, ROW_MEAN = 3, 4, 8, 10, 11, 13
STAT_ROWS = 16
DECAY = 1.0 - STEP ** (-0.8)


def exchange_rounds(dims, place):
    z, y, x, c = place
    plane = [(1, 0), (0, 1), (1, 1)]
    rounds = [
        ([sibling(place)], c),
        ([(z, lax.rem(y + dy, 2), lax.rem(x + dx, 2), c) for dy, dx in plane], y * 2 + x),
        ([moved(dims, place, 0, by) for by in range(1, dims[0])], z),
    ]
    return [([device_at(dims, p) for p in others], number) for others, number in rounds]


def put_stats(stats, row, total, square_sum, old_rows, lane, columns):
    width = stats.shape[1]
    for j in range(total.shape[1] // width):
        stats[row + j : row + j + 1, :] = total[:, j * width : (j + 1) * width]
    value = DECAY * jnp.sum(old_rows, axis=1, keepdims=True) + (1.0 - DECAY) / columns * square_sum
    at = lax.broadcasted_iota(jnp.int32, (1, width), 1)
    stats[ROW_MEAN : ROW_MEAN + 1, :] += jnp.where(at == lane, value, 0.0)


def last_kernel(
    dims, shapes, count, x_hbm, resid_hbm, gain_ref, gain_two_ref,
    dq_hbm, dk_hbm, dv_hbm, n_hbm, wq_hbm, wk_hbm, wv_hbm, near_hbm, rest_hbm,
    sum_out, sum_proj, sum_up, sum_down, row_qkv, row_out, row_proj, row_up, row_down, *refs,
):
    names = iter(refs)
    take = lambda k: [next(names) for _ in range(k)]
    grad_ref, total_ref = take(2)
    sums_out = take(3)
    dq, dk, dv, normed, flipped, wq, wk, wv = take(8)
    own_back, near, rest, box, stats, inbox, x_ref, resid_ref = take(8)
    grads = take(3)
    load_sem, back_send, back_recv, stat_send, stat_recv = take(5)
    scratch = list(names)

    place = my_place(dims)
    seq, item = lax.axis_index("seq"), lax.axis_index("item")
    rows, width = x_ref.shape
    loads = [
        pltpu.make_async_copy(a, b, load_sem.at[n])
        for n, (a, b) in enumerate(
            [
                (rest_hbm, rest), (n_hbm, normed), (dk_hbm, dk), (dv_hbm, dv), (dq_hbm, dq),
                (wk_hbm, wk), (wv_hbm, wv), (wq_hbm, wq), (near_hbm, near),
                (x_hbm, x_ref), (resid_hbm, resid_ref),
            ]
        )
    ]
    for load in loads:
        load.start()
    ahead = [(lax.rem(seq + d, count), item) for d in (1, 2)]
    behind = [(lax.rem(seq + count - d, count), item) for d in (1, 2)]
    with jax.named_scope("meet"):
        meet(peers(dims, place) + ahead + behind + [device_at(dims, place[:1] + (1 - place[1], 1 - place[2], place[3]))])
    far = WINDOW - rows
    early = QB
    early_rows, late_rows = pl.ds(far, early), pl.ds(far + early, rest.shape[0] - far - early)
    near_rows, far_rows = pl.ds(far, rest.shape[0] - far), pl.ds(0, far)
    returned = [
        pltpu.make_async_remote_copy(
            src_ref=rest.at[part], dst_ref=box.at[part], send_sem=back_send.at[m], recv_sem=back_recv.at[m],
            device_id=behind[max(m - 1, 0)], device_id_type=MESH,
        )
        for m, part in enumerate((early_rows, late_rows, far_rows))
    ]
    loads[0].wait()
    for m in range(3):
        pl.when(seq >= (1, 1, 2)[m])(returned[m].start)

    def back_of(at):
        return dot(dk[at, :], wk[...].reshape(width, width), NT) + dot(dv[at, :], wv[...].reshape(width, width), NT)

    sums, locals_ = collapses_of(dims, place, shapes, grads, sums_out, scratch)
    with jax.named_scope("weight_gradients"):
        loads[1].wait()
        flipped[...] = normed[...].T
        for k, part in ((1, dk), (2, dv), (0, dq)):
            loads[(4, 2, 3)[k]].wait()
            base = WINDOW if k == 0 else 0
            got = dot(flipped[:, base:], part[...])
            grads[k][...] = got.astype(bf).reshape(grads[k].shape)
            run_collapse(sums, locals_, k, -1)

    def own_block(i, carry):
        at = pl.ds(pl.multiple_of(i * QB, QB), QB)
        ext = pl.ds(pl.multiple_of(WINDOW + i * QB, QB), QB)
        own_back[at, :] = back_of(ext) + dot(dq[at, :], wq[...].reshape(width, width), NT)
        return carry

    with jax.named_scope("own_rows"):
        for load in loads[5:]:
            load.wait()
        lax.fori_loop(0, rows // QB, own_block, 0)

    stats[0] = jnp.zeros_like(stats[0])
    held = stats.at[0]
    held[ROW_GAIN + 1 : ROW_GAIN + 2, :] = gain_two_ref[...]

    def add_stats(row, grad, old_rows, lane):
        square = grad * grad + TINY_SQUARE
        total = jnp.sum(square, axis=0, keepdims=True)
        put_stats(held, row, total, jnp.sum(total, axis=1, keepdims=True), old_rows, lane, grad.shape[1])

    with jax.named_scope("small_sums"):
        add_stats(ROW_OUT, sum_out[...], row_out[...], 3)
        add_stats(ROW_UP, sum_up[...], row_up[...], 4)
        add_stats(ROW_PROJ, sum_proj[...], row_proj[...], 5)
        add_stats(ROW_DOWN, sum_down[...], row_down[...], 6)

    for stage in range(5):
        with jax.named_scope("reduce_%d" % stage):
            for k in (1, 2, 0):
                run_collapse(sums, locals_, k, stage)
    for k in range(3):
        add_stats(k, sums_out[k][...], row_qkv[k : k + 1, :], k)

    with jax.named_scope("rows_returned"):

        @pl.when(seq + 1 < count)
        def _():
            returned[0].wait_recv()
            returned[1].wait_recv()
            size = near.shape[0]
            own_back[0:size, :] += near[...].astype(f32)
            own_back[size:, :] += box[near_rows, :].astype(f32)

        @pl.when(seq + 2 < count)
        def _():
            returned[2].wait_recv()
            own_back[rows - far :, :] += box[far_rows, :].astype(f32)

    gain = gain_ref[0:1]

    def input_block(i, total):
        at = pl.ds(pl.multiple_of(i * QB, QB), QB)
        x = x_ref[at, :].astype(f32)
        scale = lax.rsqrt(jnp.mean(x * x, axis=-1, keepdims=True) + EPSILON)
        back = own_back[at, :]
        unit = x * scale
        by_gain = back * gain
        inner = jnp.mean(by_gain * unit, axis=-1, keepdims=True)
        grad_ref[at, :] = (resid_ref[at, :] + scale * (by_gain - unit * inner)).astype(bf)
        return total + jnp.sum(back * unit, axis=0, keepdims=True)

    with jax.named_scope("input_gradient"):
        total = lax.fori_loop(0, rows // QB, input_block, jnp.zeros((1, width), f32))
    held[ROW_GAIN : ROW_GAIN + 1, :] = total

    rounds = exchange_rounds(dims, place)
    z, y, x, c = place
    senders = [
        [1 - c],
        [lax.rem(y + dy, 2) * 2 + lax.rem(x + dx, 2) for dy, dx in ((1, 0), (0, 1), (1, 1))],
        [lax.rem(z + dims[0] - by, dims[0]) for by in range(1, dims[0])],
    ]

    with jax.named_scope("exchange_sums"):
        slot = 0
        for stage, (others, number) in enumerate(rounds):
            copies = []
            for other in others:
                copies.append(
                    pltpu.make_async_remote_copy(
                        src_ref=stats.at[stage], dst_ref=inbox.at[slot],
                        send_sem=stat_send.at[slot], recv_sem=stat_recv.at[slot],
                        device_id=other, device_id_type=MESH,
                    )
                )
                copies[-1].start()
                slot += 1
            for copy in copies:
                copy.wait()
            base = slot - len(others)
            total = jnp.zeros_like(stats[0])
            for member in range(len(others) + 1):
                term = stats[stage]
                for m in range(len(others)):
                    term = jnp.where(senders[stage][m] == member, inbox[base + m], term)
                total = total + term
            stats[stage + 1] = total
        total_ref[...] = stats[len(rounds)]
    for one in sums:
        one.finish()
    for m in range(3):
        pl.when(seq >= (1, 1, 2)[m])(returned[m].wait_send)


def last(x, resid_grad, gain, gain_two, dq, dk, dv, normed, weights, returned, sums, old_rows, dims, count):
    rows, width = x.shape
    ext = normed.shape[0]
    shapes = [w.shape[3:] for w in weights]
    slots = 4 + dims[0] - 1
    vmem = pl.BlockSpec(memory_space=pltpu.VMEM)
    hbm = pl.BlockSpec(memory_space=pl.ANY)
    dma = pltpu.SemaphoreType.DMA
    sds = jax.ShapeDtypeStruct
    got = pl.pallas_call(
        functools.partial(last_kernel, dims, shapes, count),
        in_specs=[hbm] * 2 + [vmem] * 2 + [hbm] * 9 + [vmem] * 9,
        out_specs=[vmem] * 5,
        out_shape=[sds((rows, width), bf), sds((STAT_ROWS, width), f32)] + [sds((r // 2, c), f32) for r, c in shapes],
        scratch_shapes=[
            pltpu.VMEM((rows, width), bf), pltpu.VMEM((ext, width), bf), pltpu.VMEM((ext, width), bf),
            pltpu.VMEM((ext, width), bf), pltpu.VMEM((width, ext), bf),
        ]
        + [pltpu.VMEM(w.shape, bf) for w in weights]
        + [pltpu.VMEM((rows, width), f32)]
        + [pltpu.VMEM(a.shape, bf) for a in (*returned, returned[1])]
        + [pltpu.VMEM((4, STAT_ROWS, width), f32), pltpu.VMEM((slots, STAT_ROWS, width), f32)]
        + [pltpu.VMEM((rows, width), bf), pltpu.VMEM((rows, width), f32)]
        + [pltpu.VMEM(w.shape, bf) for w in weights]
        + [dma((11,)), dma((3,)), dma((3,)), dma((slots,)), dma((slots,))]
        + collapse_scratch(dims, shapes),
        compiler_params=pltpu.CompilerParams(
            collective_id=4, has_side_effects=True, vmem_limit_bytes=61 * 2**20
        ),
        name="last",
    )(x, resid_grad, gain, gain_two, dq, dk, dv, normed, *weights, *returned, *sums, *old_rows)
    return got[0], got[1], got[2:]


def update_kernel(
    place_ref, total_ref, gains_ref, gain_var_ref,
    w_qkv, w_out, w_proj, w_up, w_down, s_q, s_k, s_v, s_out, s_proj, s_up, s_down,
    row_qkv, row_out, row_proj, row_up, row_down, col_qkv, col_out, col_proj, col_up, col_down,
    y_ref, p_ref, d_ref, g_qkv, g_out, g_proj, g_up, g_down, g_gains, n_qkv, n_out, n_proj, n_up, n_down, n_gains,
    r_qkv, r_out, r_proj, r_up, r_down, c_qkv, c_out, c_proj, c_up, c_down, gain_var_new,
    y_out, p_out, d_out, flat, tall, y_held, p_held, d_held, pass_sem,
):
    held = (y_held, p_held, d_held)
    taken = [pltpu.make_async_copy(a, b, pass_sem.at[n]) for n, (a, b) in enumerate(zip((y_ref, p_ref, d_ref), held))]
    passed = [pltpu.make_async_copy(a, b, pass_sem.at[3 + n]) for n, (a, b) in enumerate(zip(held, (y_out, p_out, d_out)))]
    for copy in taken:
        copy.start()
    shard = row_out.shape[1]
    shard_down = row_down.shape[1]
    width = total_ref.shape[1]
    flat[...] = jnp.zeros_like(flat)
    flat[0:3, :shard] = row_qkv[...]
    flat[3:4, :shard] = row_out[...]
    flat[4:5, :shard] = row_up[...]
    flat[5:6, :shard] = row_proj[...]
    flat[6:7, :shard_down] = row_down[...]
    olds = flat[...].T
    tall[...] = jnp.zeros_like(tall)

    def one(weight, grad, lane, row, old_col, rows_all, g_out_, n_out_, c_out_):
        count, columns = grad.shape
        square = grad * grad + TINY_SQUARE
        row_new = DECAY * olds[:count, lane : lane + 1] + (1.0 - DECAY) * jnp.mean(square, axis=1, keepdims=True)
        tall[:count, lane : lane + 1] = row_new
        parts = [total_ref[row + j : row + j + 1, :] for j in range(columns // width)]
        col_total = parts[0] if len(parts) == 1 else jnp.concatenate(parts, axis=1)
        col_new = DECAY * old_col + (1.0 - DECAY) * col_total / rows_all
        mean = total_ref[ROW_MEAN : ROW_MEAN + 1, lane : lane + 1] / rows_all
        second = row_new * col_new / mean
        g_out_[...] = grad
        n_out_[...] = weight - WEIGHT_RATE * grad * lax.rsqrt(second)
        c_out_[...] = col_new.reshape(c_out_.shape)

    for k, grad in enumerate((s_q, s_k, s_v)):
        one(w_qkv[k], grad[...], k, k, col_qkv[k : k + 1, :], width, g_qkv.at[k], n_qkv.at[k], c_qkv.at[k : k + 1])
    ff = col_up.shape[0]
    one(w_out[...], s_out[...], 3, ROW_OUT, col_out[...].reshape(1, width), width, g_out, n_out, c_out)
    one(w_up[...], s_up[...], 4, ROW_UP, col_up[...].reshape(1, ff), width, g_up, n_up, c_up)
    one(w_proj[...], s_proj[...], 5, ROW_PROJ, col_proj[...].reshape(1, -1), width, g_proj, n_proj, c_proj)
    one(w_down[...], s_down[...], 6, ROW_DOWN, col_down[...].reshape(1, width), ff, g_down, n_down, c_down)
    for copy, onward in zip(taken, passed):
        copy.wait()
        onward.start()
    news = tall[...].T
    r_qkv[...] = news[0:3, :shard]
    r_out[...] = news[3:4, :shard]
    r_up[...] = news[4:5, :shard]
    r_proj[...] = news[5:6, :shard]
    r_down[...] = news[6:7, :shard_down]

    gain_sums = pltpu.roll(total_ref[8:16, :], width - place_ref[0] * shard, 1)
    sums = gain_sums[ROW_GAIN - 8 : ROW_GAIN - 6, :shard]
    var = DECAY * gain_var_ref[...] + (1.0 - DECAY) * (sums * sums + TINY_SQUARE)
    g_gains[...] = sums
    gain_var_new[...] = var
    n_gains[...] = gains_ref[...] - GAIN_RATE * sums * lax.rsqrt(var)
    for copy in passed:
        copy.wait()


def update(place, totals, gains, gain_var, weights, sums, rows, cols, results):
    vmem = pl.BlockSpec(memory_space=pltpu.VMEM)
    like = lambda arrays: [jax.ShapeDtypeStruct(a.shape, f32) for a in arrays]
    outs = like(weights) + like([gains]) + like(weights) + like([gains]) + like(rows) + like(cols) + like([gain_var])
    hbm = pl.BlockSpec(memory_space=pl.ANY)
    return pl.pallas_call(
        update_kernel,
        in_specs=[pl.BlockSpec(memory_space=pltpu.SMEM)] + [vmem] * (3 + 5 + 7 + 5 + 5) + [hbm] * 3,
        out_specs=[vmem] * len(outs) + [hbm] * 3,
        out_shape=outs + [jax.ShapeDtypeStruct(a.shape, a.dtype) for a in results],
        scratch_shapes=[pltpu.VMEM((8, 128), f32), pltpu.VMEM((128, 8), f32)]
        + [pltpu.VMEM(a.shape, a.dtype) for a in results]
        + [pltpu.SemaphoreType.DMA((6,))],
        compiler_params=pltpu.CompilerParams(vmem_limit_bytes=63 * 2**20),
        name="update",
    )(place, totals, gains, gain_var, *weights, *sums, *rows, *cols, *results)


def sum_kernel(sizes, x_ref, o_ref, inbox, send_sem, recv_sem):
    place = {name: lax.axis_index(name) for name, _ in sizes}
    partners = []
    for name, size in sizes:
        bit = 1
        while bit < size:
            mine = place[name]
            low = lax.rem(mine // bit, 2)
            other = mine + bit * (1 - 2 * low)
            partners.append(tuple(other if n == name else place[n] for n in ("seq", "item")))
            bit *= 2
    barrier = pltpu.get_barrier_semaphore()
    for partner in partners:
        pl.semaphore_signal(barrier, inc=1, device_id=partner, device_id_type=MESH)
    pl.semaphore_wait(barrier, len(partners))
    o_ref[0] = x_ref[...]
    for stage, partner in enumerate(partners):
        copy = pltpu.make_async_remote_copy(
            src_ref=o_ref.at[stage],
            dst_ref=inbox.at[stage],
            send_sem=send_sem.at[stage],
            recv_sem=recv_sem.at[stage],
            device_id=partner,
            device_id_type=MESH,
        )
        copy.start()
        copy.wait()
        o_ref[stage + 1] = o_ref[stage] + inbox[stage]


def sum_all(x, sizes):
    stages = sum(size.bit_length() - 1 for _, size in sizes)
    held = pl.pallas_call(
        functools.partial(sum_kernel, sizes),
        out_shape=jax.ShapeDtypeStruct((stages + 1,) + x.shape, x.dtype),
        in_specs=[pl.BlockSpec(memory_space=pltpu.VMEM)],
        out_specs=pl.BlockSpec(memory_space=pltpu.VMEM),
        scratch_shapes=[
            pltpu.VMEM((stages,) + x.shape, x.dtype),
            pltpu.SemaphoreType.DMA((stages,)),
            pltpu.SemaphoreType.DMA((stages,)),
        ],
        compiler_params=pltpu.CompilerParams(collective_id=0, has_side_effects=True),
        name="sum_all",
    )(x)
    return held[stages]


def from_behind(block, axis, distance):
    devices = range(lax.axis_size(axis))
    route = [(i - distance, i) for i in devices if i - distance in devices]
    return lax.ppermute(block, axis, route)


def norm_rows(values, gain):
    return values * lax.rsqrt(jnp.mean(values * values, axis=-1, keepdims=True) + EPSILON) * gain


def gelu_tanh(values):
    return (
        0.5
        * values
        * (1.0 + jnp.tanh(0.7978845608028654 * (values + 0.044715 * values * values * values)))
    )


def finish_update(weight, grad, row_new, col_state, col_total, rows_all, row_mean, decay):
    col_new = decay * col_state + (1.0 - decay) * col_total / rows_all
    second = row_new[..., :, None] * col_new[..., None, :] / row_mean
    return (weight - WEIGHT_RATE * grad * lax.rsqrt(second), col_new)


def local(
    byte_rows, item_lengths, cont_mask, bound_mask, out_cot, proj_cot,
    w_qkv, w_out, w_up, w_down, w_proj, gains,
    row_qkv, col_qkv, row_out, col_out, row_up, col_up, row_down, col_down, row_proj, col_proj, gain_var,
):
    sizes = tuple((name, lax.axis_size(name)) for name in ("item", "seq"))
    count = lax.axis_size("item") * lax.axis_size("seq")
    rows_dev, width = byte_rows.shape[1:]
    ff = w_up.shape[1]
    shard = width // count
    low = bf

    dims = grid_of(lax.axis_size("seq"), lax.axis_size("item"))
    paired = dims == (4, 2, 2) and shard % 8 == 0 and rows_dev < WINDOW <= 2 * rows_dev
    inputs_low = byte_rows[0]
    if paired:
        got = front(item_lengths, inputs_low, gains, w_qkv, (w_out, w_proj, w_up, w_down), dims, lax.axis_size("seq"))
        attended, lse, queries, ext_keys, ext_values, ext_normed = got[:6]
        split_qkv = got[6:9]
        gain_full = got[9]
        weight_out, weight_up, weight_down = [w.reshape(-1, w.shape[-1]) for w in (got[10], got[12], got[13])]
        part_proj = got[11]
    else:
        inputs = inputs_low.astype(f32)
        weight_qkv = lax.all_gather(w_qkv.astype(low), AXES, axis=1, tiled=True)
        gain_full = lax.all_gather(gains.astype(low), AXES, axis=1, tiled=True).astype(f32)
        weight_out, weight_proj, weight_up, weight_down = [
            lax.all_gather(w.astype(low), AXES, axis=0, tiled=True) for w in (w_out, w_proj, w_up, w_down)
        ]

    hop_total = -(-WINDOW // rows_dev)
    if not paired:
        offset = lax.axis_index("seq") * rows_dev
        ends = jnp.cumsum(item_lengths[0], dtype=jnp.int32)
        pos = offset + jnp.arange(rows_dev, dtype=jnp.int32)
        begin_at = jnp.max(jnp.where(ends[None, :] <= pos[:, None], ends[None, :], 0), axis=1)
        lo = jnp.maximum(begin_at, pos - WINDOW + 1) - offset + WINDOW
        halo = []
        for distance in range(hop_total, 0, -1):
            need = min(rows_dev, WINDOW - (distance - 1) * rows_dev)
            halo.append(from_behind(inputs_low[rows_dev - need :], "seq", distance))
        normed = norm_rows(inputs, gain_full[0]).astype(low)
        halo_normed = norm_rows(jnp.concatenate(halo, axis=0).astype(f32), gain_full[0]).astype(low)
        ext_normed = jnp.concatenate([halo_normed, normed], axis=0)
        queries = dot(normed, weight_qkv[0]).astype(low) * jnp.asarray(0.125, low)
        ext_keys = dot(ext_normed, weight_qkv[1]).astype(low)
        ext_values = dot(ext_normed, weight_qkv[2]).astype(low)
        attended, lse = attend(queries, ext_keys, ext_values, lo[:, None])

    if paired:
        output_low, projected, resid_grad, attended_grad, gain_two_grad, delta, sum_proj, *low_grads = middle(
            bound_mask, cont_mask, gain_full,
            (inputs_low, attended, out_cot[0], proj_cot[0], weight_out, weight_up, weight_down, part_proj), dims,
        )
        apart = [g.reshape(dims + (-1, g.shape[1])) for g in low_grads]
        (query_grad, ext_key_grad, ext_value_grad, *returned), (sum_out, sum_up, sum_down) = back(
            item_lengths, lse, delta, (queries, attended_grad, ext_keys, ext_values, split_qkv[1], split_qkv[2]),
            apart, dims, lax.axis_size("seq"),
        )
        sums = [sum_out, sum_proj, sum_up, sum_down]
    else:
        resid = inputs + dot(attended, weight_out)
        normed_two = norm_rows(resid, gain_full[1]).astype(low)
        hidden_pre = dot(normed_two, weight_up)
        activated = gelu_tanh(hidden_pre).astype(low)
        output = resid + dot(activated, weight_down)
        output_low = output.astype(low)
        boundary = (bound_mask[0] * (1 - cont_mask[0])).astype(f32)[:, None]
        projected = (boundary * dot(output_low, weight_proj)).astype(low)
        proj_grad = (boundary * proj_cot[0].astype(f32)).astype(low)
        grad_proj = dot(output_low, proj_grad, TN)
        output_grad = out_cot[0].astype(f32) + dot(proj_grad, weight_proj, NT)
        output_grad_low = output_grad.astype(low)
        grad_down = dot(activated, output_grad_low, TN)
        act_grad = dot(output_grad_low, weight_down, NT)
        _, gelu_back = jax.vjp(gelu_tanh, hidden_pre)
        pre_grad = gelu_back(act_grad)[0].astype(low)
        grad_up = dot(normed_two, pre_grad, TN)
        normed_two_grad = dot(pre_grad, weight_up, NT)
        _, norm_two_back = jax.vjp(norm_rows, resid, gain_full[1])
        resid_norm_grad, gain_two_grad = norm_two_back(normed_two_grad)
        resid_grad = output_grad + resid_norm_grad
        resid_grad_low = resid_grad.astype(low)
        grad_out = dot(attended, resid_grad_low, TN)
        attended_grad = dot(resid_grad_low, weight_out, NT).astype(low)

        low_grads = [g.astype(low) for g in (grad_out, grad_proj, grad_up, grad_down)]
        query_grad, ext_key_grad, ext_value_grad = attend_back(
            queries, attended_grad, attended, lse, ext_keys, ext_values, lo[None, :]
        )
        sums = [lax.psum_scatter(g, AXES, scatter_dimension=0, tiled=True).astype(f32) for g in low_grads]
        sum_out, sum_proj, sum_up, sum_down = sums
    if paired:
        rows = [row_qkv, row_out[None], row_proj[None], row_up[None], row_down[None]]
        cols = [col_qkv, col_out, col_proj, col_up, col_down]
        input_grad, totals, sums_qkv = last(
            inputs_low, resid_grad, gain_full, gain_two_grad, query_grad, ext_key_grad, ext_value_grad,
            ext_normed, split_qkv, returned, sums, rows, dims, lax.axis_size("seq"),
        )
        mine = lax.axis_index("seq") * lax.axis_size("item") + lax.axis_index("item")
        done = update(
            mine[None].astype(jnp.int32), totals, gains, gain_var,
            (w_qkv, w_out, w_proj, w_up, w_down), (*sums_qkv, *sums), rows, cols,
            (output_low, projected, input_grad),
        )
        sum_qkv, sum_out, sum_proj, sum_up, sum_down, sum_gains = done[:6]
        new_qkv, new_out, new_proj, new_up, new_down, new_gains = done[6:12]
        row_qkv_new, row_out_new, row_proj_new, row_up_new, row_down_new = [done[12]] + [r[0] for r in done[13:17]]
        col_qkv_new, col_out_new, col_proj_new, col_up_new, col_down_new = done[17:22]
        gain_var_new, output_low, projected, input_grad = done[22:]
        return (
            output_low[None], projected[None], input_grad[None],
            sum_qkv, sum_out, sum_up, sum_down, sum_proj, sum_gains,
            new_qkv, new_out, new_up, new_down, new_proj, new_gains,
            row_qkv_new, col_qkv_new, row_out_new, col_out_new, row_up_new, col_up_new,
            row_down_new, col_down_new, row_proj_new, col_proj_new, gain_var_new,
        )
    ext_back = dot(ext_key_grad, weight_qkv[1], NT) + dot(ext_value_grad, weight_qkv[2], NT)
    halo_back = ext_back[:WINDOW].astype(low)
    grads_qkv = [
        dot(normed, query_grad, TN).astype(low),
        dot(ext_normed, ext_key_grad, TN).astype(low),
        dot(ext_normed, ext_value_grad, TN).astype(low),
    ]
    returned = []
    for distance in range(1, hop_total + 1):
        need = min(rows_dev, WINDOW - (distance - 1) * rows_dev)
        upper = WINDOW - (distance - 1) * rows_dev
        returned.append(from_behind(halo_back[upper - need : upper], "seq", -distance))
    sums = [lax.psum_scatter(g, AXES, scatter_dimension=0, tiled=True).astype(f32) for g in grads_qkv]
    sum_qkv = jnp.stack(sums)
    normed_grad = ext_back[WINDOW:] + dot(query_grad, weight_qkv[0], NT)
    for block in returned:
        need = block.shape[0]
        normed_grad = normed_grad.at[rows_dev - need :].add(block.astype(f32))
    _, norm_one_back = jax.vjp(norm_rows, inputs, gain_full[0])
    input_norm_grad, gain_one_grad = norm_one_back(normed_grad)
    input_grad = (resid_grad + input_norm_grad).astype(low)

    decay = 1.0 - STEP ** (-0.8)
    square_qkv = sum_qkv * sum_qkv + TINY_SQUARE
    square_out = sum_out * sum_out + TINY_SQUARE
    square_up = sum_up * sum_up + TINY_SQUARE
    square_down = sum_down * sum_down + TINY_SQUARE
    square_proj = sum_proj * sum_proj + TINY_SQUARE
    row_qkv_new = decay * row_qkv + (1.0 - decay) * jnp.mean(square_qkv, axis=-1)
    row_out_new = decay * row_out + (1.0 - decay) * jnp.mean(square_out, axis=-1)
    row_up_new = decay * row_up + (1.0 - decay) * jnp.mean(square_up, axis=-1)
    row_down_new = decay * row_down + (1.0 - decay) * jnp.mean(square_down, axis=-1)
    row_proj_new = decay * row_proj + (1.0 - decay) * jnp.mean(square_proj, axis=-1)
    row_sums = jnp.concatenate(
        [
            jnp.sum(row_qkv_new, axis=1),
            jnp.sum(row_out_new)[None],
            jnp.sum(row_up_new)[None],
            jnp.sum(row_down_new)[None],
            jnp.sum(row_proj_new)[None],
        ]
    )
    stats = [
        jnp.sum(square_qkv, axis=1).reshape(-1),
        jnp.sum(square_out, axis=0),
        jnp.sum(square_up, axis=0),
        jnp.sum(square_down, axis=0),
        jnp.sum(square_proj, axis=0),
        gain_one_grad,
        gain_two_grad,
        row_sums,
    ]
    flat = jnp.concatenate(stats)
    used = flat.shape[0]
    padded = -(-used // 1024) * 1024
    flat = jnp.pad(flat, (0, padded - used)).reshape(padded // 128, 128)
    flat = sum_all(flat, sizes).reshape(-1)
    totals, at = [], 0
    for part in stats:
        totals.append(flat[at : at + part.shape[0]])
        at += part.shape[0]
    col_qkv_total, col_out_total, col_up_total, col_down_total, col_proj_total, gain_one, gain_two, row_totals = totals
    col_qkv_total = col_qkv_total.reshape(3, width)
    mine = lax.axis_index("seq") * lax.axis_size("item") + lax.axis_index("item")
    sum_gains = lax.dynamic_slice_in_dim(jnp.stack([gain_one, gain_two]), mine * shard, shard, 1)
    row_counts = jnp.array([width, width, width, width, width, ff, width], f32)
    row_means = row_totals / row_counts
    new_qkv, col_qkv_new = finish_update(
        w_qkv, sum_qkv, row_qkv_new, col_qkv, col_qkv_total, width, row_means[:3][:, None, None], decay
    )
    new_out, col_out_new = finish_update(w_out, sum_out, row_out_new, col_out, col_out_total, width, row_means[3], decay)
    new_up, col_up_new = finish_update(w_up, sum_up, row_up_new, col_up, col_up_total, width, row_means[4], decay)
    new_down, col_down_new = finish_update(
        w_down, sum_down, row_down_new, col_down, col_down_total, ff, row_means[5], decay
    )
    new_proj, col_proj_new = finish_update(
        w_proj, sum_proj, row_proj_new, col_proj, col_proj_total, width, row_means[6], decay
    )
    gain_var_new = decay * gain_var + (1.0 - decay) * (sum_gains * sum_gains + TINY_SQUARE)
    new_gains = gains - GAIN_RATE * sum_gains * lax.rsqrt(gain_var_new)
    return (
        output_low[None], projected[None], input_grad[None],
        sum_qkv, sum_out, sum_up, sum_down, sum_proj, sum_gains,
        new_qkv, new_out, new_up, new_down, new_proj, new_gains,
        row_qkv_new, col_qkv_new, row_out_new, col_out_new, row_up_new, col_up_new,
        row_down_new, col_down_new, row_proj_new, col_proj_new, gain_var_new,
    )


def solution(mesh):
    in_specs = (
        P("item", "seq", None),
        P("item", None),
        P("item", "seq"),
        P("item", "seq"),
        P("item", "seq", None),
        P("item", "seq", None),
        P(None, ("seq", "item"), None),
        P(("seq", "item"), None),
        P(("seq", "item"), None),
        P(("seq", "item"), None),
        P(("seq", "item"), None),
        P(None, ("seq", "item")),
        P(None, ("seq", "item")),
        P(),
        P(("seq", "item")),
        P(),
        P(("seq", "item")),
        P(),
        P(("seq", "item")),
        P(),
        P(("seq", "item")),
        P(),
        P(None, ("seq", "item")),
    )
    out_specs = (
        P("item", "seq", None),
        P("item", "seq", None),
        P("item", "seq", None),
        P(None, ("seq", "item"), None),
        P(("seq", "item"), None),
        P(("seq", "item"), None),
        P(("seq", "item"), None),
        P(("seq", "item"), None),
        P(None, ("seq", "item")),
        P(None, ("seq", "item"), None),
        P(("seq", "item"), None),
        P(("seq", "item"), None),
        P(("seq", "item"), None),
        P(("seq", "item"), None),
        P(None, ("seq", "item")),
        P(None, ("seq", "item")),
        P(),
        P(("seq", "item")),
        P(),
        P(("seq", "item")),
        P(),
        P(("seq", "item")),
        P(),
        P(("seq", "item")),
        P(),
        P(None, ("seq", "item")),
    )
    return jax.shard_map(local, mesh=mesh, in_specs=in_specs, out_specs=out_specs, check_vma=False)
```

```python
import functools
import jax
import jax.numpy as jnp
from jax import lax
from jax.experimental import pallas as pl
from jax.experimental.pallas import tpu as pltpu
from jax.sharding import PartitionSpec as P

WINDOW = 1536
HEADS = 12
NEG = -1e30
EPSILON = 1e-06
TINY_SQUARE = 1e-30
WEIGHT_RATE = 0.02
GAIN_RATE = 0.2
STEP = 10
QB = 256
NT = (((1,), (1,)), ((), ()))
TN = (((0,), (0,)), ((), ()))
f32 = jnp.float32
bf = jnp.bfloat16


def dot(a, b, dims=None):
    if dims is None:
        return jnp.dot(a, b, preferred_element_type=f32)
    return lax.dot_general(a, b, dims, preferred_element_type=f32)


def halves(x):
    lane = lax.broadcasted_iota(jnp.int32, x.shape, 1)
    zero = jnp.zeros_like(x)
    return jnp.where(lane < 64, x, zero), jnp.where(lane < 64, zero, x)


def fwd_kernel(lo_ref, q_ref, k_ref, v_ref, o_ref, lse_ref, bias):
    hp, qb = pl.program_id(0), pl.program_id(1)
    span = WINDOW + QB

    @pl.when(hp == 0)
    def _():
        base = qb * QB
        kpos = base + lax.broadcasted_iota(jnp.int32, (QB, span), 1)
        qpos = WINDOW + base + lax.broadcasted_iota(jnp.int32, (QB, span), 0)
        ok = (kpos >= lo_ref[...]) & (kpos <= qpos)
        bias[qb] = jnp.where(ok, 0.0, NEG)

    start = pl.multiple_of(qb * QB, QB)
    kw = k_ref[pl.ds(start, span), :]
    vw = v_ref[pl.ds(start, span), :]
    outs, lses = [], []
    for qh in halves(q_ref[...]):
        s = dot(qh, kw, NT) + bias[qb]
        m = jnp.max(s, axis=1, keepdims=True)
        p = jnp.exp(s - m)
        l = jnp.sum(p, axis=1, keepdims=True)
        outs.append(dot(p.astype(bf), vw) * (1.0 / l))
        lses.append(m + jnp.log(l))
    lane = lax.broadcasted_iota(jnp.int32, (QB, 128), 1)
    o_ref[...] = jnp.where(lane < 64, outs[0], outs[1]).astype(bf)
    both = jnp.where(lane == 0, lses[0], lses[1])
    lse_ref[0] = both.T[:8]


def attend(q, k, v, lo):
    rows, width = q.shape
    ext = k.shape[0]
    nq, nh = rows // QB, width // 128
    return pl.pallas_call(
        fwd_kernel,
        grid=(nh, nq),
        in_specs=[
            pl.BlockSpec((QB, 1), lambda h, i: (i, 0)),
            pl.BlockSpec((QB, 128), lambda h, i: (i, h)),
            pl.BlockSpec((ext, 128), lambda h, i: (0, h)),
            pl.BlockSpec((ext, 128), lambda h, i: (0, h)),
        ],
        out_specs=[
            pl.BlockSpec((QB, 128), lambda h, i: (i, h)),
            pl.BlockSpec((1, 8, QB), lambda h, i: (h, 0, i)),
        ],
        out_shape=[
            jax.ShapeDtypeStruct((rows, width), bf),
            jax.ShapeDtypeStruct((nh, 8, rows), f32),
        ],
        scratch_shapes=[pltpu.VMEM((nq, QB, WINDOW + QB), f32)],
        compiler_params=pltpu.CompilerParams(vmem_limit_bytes=50 * 2**20),
        cost_estimate=pl.CostEstimate(flops=4 * rows * 1792 * 768 * 3, bytes_accessed=14 * 2**20, transcendentals=0),
        name="attend",
    )(lo, q, k, v)


AXES = ("seq", "item")
MESH = pl.DeviceIdType.MESH


def grid_of(seq, item):
    side = 1
    while side * side * 4 <= seq:
        side *= 2
    return (seq // side, side, item // 2)


def my_place(dims):
    seq, item = lax.axis_index("seq"), lax.axis_index("item")
    return (seq // dims[1], lax.rem(seq, dims[1]), item // 2, lax.rem(item, 2))


def device_at(dims, place):
    z, y, x, c = place
    return (z * dims[1] + y, x * 2 + c)


def moved(dims, place, dim, by):
    to = list(place)
    to[dim] = lax.rem(place[dim] + by, dims[dim])
    return tuple(to)


def sibling(place):
    return place[:3] + (1 - place[3],)


def peers(dims, place):
    found = [sibling(place)]
    for dim in range(3):
        found += [moved(dims, place, dim, by) for by in range(1, dims[dim])]
    return [device_at(dims, p) for p in found]


def meet(targets):
    barrier = pltpu.get_barrier_semaphore()
    for target in targets:
        pl.semaphore_signal(barrier, inc=1, device_id=target, device_id_type=MESH)
    pl.semaphore_wait(barrier, len(targets))


class Spread:
    def __init__(self, dims, place, own, out, rows, cols, order, send, recv):
        self.dims, self.place, self.own, self.out = dims, place, own, out
        self.rows, self.cols, self.order = rows, cols, order
        self.send, self.recv = send, recv

    def span(self, core):
        half = self.out.shape[-1] // 2
        return pl.ds(pl.multiple_of(core * half + self.cols[0], 128), self.cols[1])

    def region(self, stage, by=0, core=None):
        held = self.order[:stage]
        at = []
        for dim in range(3):
            if dim in held:
                at.append(slice(None))
            elif by and dim == self.order[stage]:
                at.append(lax.rem(self.place[dim] + self.dims[dim] - by, self.dims[dim]))
            else:
                at.append(self.place[dim])
        core = self.place[3] if core is None else core
        return self.out.at[tuple(at) + (self.rows, self.span(core))]

    def slots(self, stage):
        first = sum(self.dims[d] - 1 for d in self.order[:stage])
        return [(by, first + by - 1) for by in range(1, self.dims[self.order[stage]])]

    def hops(self, stage):
        for by, slot in self.slots(stage):
            block = self.region(stage)
            source = self.own.at[self.rows, self.span(self.place[3])] if stage == 0 else block
            target = device_at(self.dims, moved(self.dims, self.place, self.order[stage], by))
            yield pltpu.make_async_remote_copy(
                src_ref=source, dst_ref=block, send_sem=self.send.at[slot], recv_sem=self.recv.at[slot],
                device_id=target, device_id_type=MESH,
            )

    def shares(self, stage, core=None):
        count = sum(d - 1 for d in self.dims)
        for by, slot in self.slots(stage):
            block = self.region(stage, by, core)
            yield pltpu.make_async_remote_copy(
                src_ref=block, dst_ref=block, send_sem=self.send.at[count + slot], recv_sem=self.recv.at[count + slot],
                device_id=device_at(self.dims, sibling(self.place)), device_id_type=MESH,
            )

    def begin(self, stage):
        for copy in self.hops(stage):
            copy.start()

    def advance(self, stage, go_on=True):
        for copy in self.hops(stage):
            copy.wait_recv()
        if stage < 2 and go_on:
            self.begin(stage + 1)
        for copy in self.shares(stage):
            copy.start()

    def finish(self, stages=(0, 1, 2)):
        for stage in stages:
            for copy in self.hops(stage):
                copy.wait_send()
            for copy in self.shares(stage):
                copy.wait_send()
            for copy in self.shares(stage, 1 - self.place[3]):
                copy.wait_recv()


def keep_own(own, out, place, sem):
    return pltpu.make_async_copy(own, out.at[place[0], place[1], place[2]], sem)


def copies_of(dims):
    return 2 * sum(d - 1 for d in dims)


def halves_of(shape):
    rows, cols = shape
    half = cols // 2
    if half % 256 == 0:
        return [((0, rows), (0, half // 2)), ((0, rows), (half // 2, half // 2))]
    cut = rows // 32 * 16
    return [((at, count), (0, half)) for at, count in ((0, cut), (cut, rows - cut)) if count]


ORDERS = ((0, 1, 2), (0, 2, 1))


def pieces_of(dims, place, owns, outs, shapes, send, recv):
    made, at = [], 0
    for k, (own, out, shape) in enumerate(zip(owns, outs, shapes)):
        turn = k % 2
        pieces = []
        for order, (rows, cols) in zip(ORDERS[turn:] + ORDERS[:turn], halves_of(shape)):
            pieces.append(Spread(dims, place, own, out, pl.ds(*rows), cols, order, send.at[at], recv.at[at]))
            at += 1
        made.append(pieces)
    return made


def begin(pieces):
    for piece in pieces:
        piece.begin(0)


def advance(pieces, stage):
    for piece in pieces:
        piece.advance(stage)


def lower_bounds(lengths_ref, pos, offset):
    begin = jnp.zeros_like(pos)
    end = jnp.int32(0)
    for j in range(lengths_ref.shape[1]):
        end = end + lengths_ref[0, j]
        begin = jnp.where(end <= pos, end, begin)
    return jnp.maximum(begin, pos - (WINDOW - 1)) - offset + WINDOW


def norm_block(values, gain):
    x = values.astype(f32)
    return (x * lax.rsqrt(jnp.mean(x * x, axis=-1, keepdims=True) + EPSILON) * gain).astype(bf)


REST_EVENTS = {
    (0, 0, 0): ((2, 0),),
    (1, 0, 2): ((2, 1),),
    (1, 1, 2): ((3, 0),),
    (1, 3, 0): ((0, 0), (2, 2)),
    (1, 4, 2): ((3, 1), (0, 1)),
}


def front_kernel(dims, shapes, count, lengths_ref, x_ref, gains_ref, qkv_ref, out_ref_, proj_ref, up_ref, down_ref, *refs):
    names = iter(refs)
    take = lambda k: [next(names) for _ in range(k)]
    o_ref, lse_ref, q_out, k_out, v_out, n_out = take(6)
    w_outs = take(4)
    rest_outs = take(4)
    halo, staging, normed, q_scr, k_scr, v_scr, gain_scr, gain_own, bias, own_mixed, own_top, own_total = take(12)
    wide, blocks = take(8), take(8)
    first = take(4)
    swap_send, swap_recv, send, recv, keep_sem, halo_send, halo_recv, out_sem = take(8)

    place = my_place(dims)
    c = place[3]
    seq, item = lax.axis_index("seq"), lax.axis_index("item")
    rows, width = x_ref.shape
    hops = -(-WINDOW // rows)
    around = [(lax.rem(seq + d, count), item) for d in range(1, hops + 1)]
    behind = [(lax.rem(seq + count - d, count), item) for d in range(1, hops + 1)]
    with jax.named_scope("meet"):
        meet(peers(dims, place) + around + behind)

    mate = device_at(dims, sibling(place))
    shard = gains_ref.shape[1]
    gain_own[...] = jnp.zeros_like(gain_own)
    gain_own[0:2, 0:shard] = gains_ref[...]
    mine = seq * (dims[2] * 2) + item
    gain_own[...] = pltpu.roll(gain_own[...], mine * shard, 1)
    shards = [qkv_ref.at[0], qkv_ref.at[1], qkv_ref.at[2], gain_own, out_ref_, proj_ref, up_ref, down_ref]
    swaps = []
    for k in range(8):
        half = shapes[k][0] // 2
        part = wide[k].at[pl.ds(pl.multiple_of(c * half, 8), half)]
        part[...] = shards[k][...]
        swaps.append(
            pltpu.make_async_remote_copy(
                src_ref=shards[k], dst_ref=part, send_sem=swap_send.at[k], recv_sem=swap_recv.at[k],
                device_id=mate, device_id_type=MESH,
            )
        )
        swaps[k].start()
    outs = first + rest_outs
    keeps = [keep_own(blocks[k], outs[k], place, keep_sem.at[k]) for k in range(8)]
    pieces = pieces_of(dims, place, blocks, outs, shapes, send, recv)

    def ready(k):
        swaps[k].wait()
        blocks[k][...] = wide[k][...].astype(bf)
        keeps[k].start()

    odd = place[1] == 1
    lower, upper = WINDOW - rows, 2 * rows - WINDOW
    part = rows // 4

    def hop(send_slot, slot, source, target, device):
        return pltpu.make_async_remote_copy(
            src_ref=source, dst_ref=target, send_sem=halo_send.at[send_slot], recv_sem=halo_recv.at[slot],
            device_id=device, device_id_type=MESH,
        )

    cuts = [(0, 2 * part), (2 * part, part), (3 * part, part)]
    direct = [
        hop(n, n, x_ref.at[pl.ds(at, size)], halo.at[pl.ds(lower + at, size)], around[0])
        for n, (at, size) in enumerate(cuts)
    ]
    far = hop(3, 3, x_ref.at[pl.ds(upper, lower)], halo.at[pl.ds(0, lower)], around[1])
    aside = hop(4, 4, x_ref.at[pl.ds(0, 2 * part)], staging, behind[0])
    onward = hop(5, 0, staging, halo.at[pl.ds(lower, 2 * part)], around[1])
    has_next, has_far = seq + 1 < count, seq + 2 < count
    odd_next = jnp.logical_and(odd, has_next)
    even_next = jnp.logical_and(jnp.logical_not(odd), has_next)
    relays = jnp.logical_and(jnp.logical_not(odd), has_far)

    with jax.named_scope("swap"):
        for k in (3, 0, 1, 2):
            ready(k)
            begin(pieces[k])
        pl.when(odd_next)(aside.start)
        pl.when(even_next)(direct[2].start)
    with jax.named_scope("swap_rest"):
        for k in (4, 5, 6, 7):
            ready(k)
        for k in range(8):
            keeps[k].wait()
    with jax.named_scope("first_0"):
        for k in (3, 0, 1, 2):
            advance(pieces[k], 0)
        begin(pieces[6])
    with jax.named_scope("first_1"):
        for k in (3, 0, 1, 2):
            advance(pieces[k], 1)
        pl.when(has_far)(far.start)
        pl.when(has_next)(direct[1].start)
        pl.when(odd_next)(direct[2].start)
        pl.when(even_next)(direct[0].start)
    with jax.named_scope("relay"):

        @pl.when(relays)
        def _():
            aside.wait_recv()
            onward.start()

        for k in (7, 4, 5):
            begin(pieces[k])

    with jax.named_scope("first_2"):
        for k in (3, 0, 1, 2):
            advance(pieces[k], 2)
    with jax.named_scope("first_end"):
        for k in range(4):
            for piece in pieces[k]:
                piece.finish()
    total = first[3][...].astype(f32).reshape(dims[0] * dims[1] * dims[2] * 2, 8, width)
    gain_scr[...] = jnp.sum(total, axis=0)

    weights = [first[k] for k in range(3)]

    def project(slot, at):
        return dot(normed[at, :], weights[slot][...].reshape(width, width)).astype(bf)

    def own_rows(i, carry):
        at = pl.ds(pl.multiple_of(i * QB, QB), QB)
        ext = pl.ds(pl.multiple_of(WINDOW + i * QB, QB), QB)
        normed[ext, :] = norm_block(x_ref[at, :], gain_scr[0:1])
        q_scr[at, :] = project(0, ext) * jnp.asarray(0.125, bf)
        k_scr[ext, :] = project(1, ext)
        v_scr[ext, :] = project(2, ext)
        return carry

    def halo_rows(i, carry):
        at = pl.ds(pl.multiple_of(i * QB, QB), QB)
        pos = seq * rows - WINDOW + i * QB + lax.broadcasted_iota(jnp.int32, (QB, width), 0)
        block = jnp.where(pos >= 0, halo[at, :].astype(f32), 0.0)
        normed[at, :] = norm_block(block, gain_scr[0:1])
        k_scr[at, :] = project(1, at)
        v_scr[at, :] = project(2, at)
        return carry

    nq, pairs = rows // QB, width // 128

    def events(stage, hp, qb):
        for (part, pair, block), moves in REST_EVENTS.items():
            if (part, block) != (stage, qb):
                continue

            @pl.when(hp == pair)
            def _():
                for k, what in moves:
                    with jax.named_scope("rest_%d_%d" % (k, what + 1)):
                        advance(pieces[4 + k], what)

    lane = lax.broadcasted_iota(jnp.int32, (QB, 128), 1)

    def masks(qb):
        pos = seq * rows + qb * QB + lax.broadcasted_iota(jnp.int32, (QB, 1), 0)
        lo = lower_bounds(lengths_ref, pos, seq * rows)
        kpos = qb * QB + lax.broadcasted_iota(jnp.int32, (QB, WINDOW + QB), 1)
        qpos = WINDOW + qb * QB + lax.broadcasted_iota(jnp.int32, (QB, WINDOW + QB), 0)
        bias[qb] = jnp.where((kpos >= lo) & (kpos <= qpos), 0.0, NEG)

    low_half = lane < 64

    def both(pair):
        return jnp.where(low_half, pair[0], pair[1])

    def attend_to(at, keys, lanes, mask):
        kw, vw = k_scr[keys, lanes], v_scr[keys, lanes]
        tops, totals, found = [], [], []
        for qh in halves(q_scr[at, lanes]):
            s = dot(qh, kw, NT) + mask
            m = jnp.max(s, axis=1, keepdims=True)
            p = jnp.exp(s - m)
            tops.append(m)
            totals.append(jnp.sum(p, axis=1, keepdims=True))
            found.append(dot(p.astype(bf), vw))
        return both(tops), both(totals), both(found)

    def own_keys(hp, carry):
        lanes = pl.ds(pl.multiple_of(hp * 128, 128), 128)
        for qb in range(nq):
            events(0, hp, qb)
            at, keys = pl.ds(qb * QB, QB), pl.ds(WINDOW, (qb + 1) * QB)
            top, total, mixed = attend_to(at, keys, lanes, bias[qb, :, WINDOW - qb * QB :])
            own_top[hp, at, :] = top
            own_total[hp, at, :] = total
            own_mixed[at, lanes] = mixed
        return carry

    def halo_keys(hp, carry):
        lanes = pl.ds(pl.multiple_of(hp * 128, 128), 128)
        for qb in range(nq):
            events(1, hp, qb)
            at, keys = pl.ds(qb * QB, QB), pl.ds(qb * QB, WINDOW - qb * QB)
            top, total, mixed = attend_to(at, keys, lanes, bias[qb, :, : WINDOW - qb * QB])
            before = own_top[hp, at, :]
            highest = jnp.maximum(before, top)
            by_own, by_halo = jnp.exp(before - highest), jnp.exp(top - highest)
            total = own_total[hp, at, :] * by_own + total * by_halo
            mixed = own_mixed[at, lanes] * by_own + mixed * by_halo
            o_ref[at, lanes] = (mixed * (1.0 / total)).astype(bf)
            logs = (highest + jnp.log(total)).T
            lse_ref[hp, 0:1, at] = logs[0:1]
            lse_ref[hp, 1:2, at] = logs[64:65]
        return carry

    with jax.named_scope("own_rows"):
        lax.fori_loop(0, nq, own_rows, 0)
        for qb in range(nq):
            masks(qb)
    with jax.named_scope("own_keys"):
        lax.fori_loop(0, pairs, own_keys, 0)
    with jax.named_scope("wait_halo"):

        @pl.when(seq >= 1)
        def _():
            for copy in direct:
                copy.wait_recv()

        pl.when(seq >= 2)(far.wait_recv)
    with jax.named_scope("halo_rows"):
        lax.fori_loop(0, WINDOW // QB, halo_rows, 0)
    saved = [
        pltpu.make_async_copy(a, b, out_sem.at[n])
        for n, (a, b) in enumerate(
            zip([q_scr, k_scr, v_scr, normed] + first[:3] + [gain_scr], [q_out, k_out, v_out, n_out] + w_outs)
        )
    ]
    for copy in saved:
        copy.start()
    with jax.named_scope("halo_keys"):
        lax.fori_loop(0, pairs, halo_keys, 0)
    with jax.named_scope("rest_end"):
        for piece in pieces[5]:
            piece.advance(0, False)
        for k in (7, 4):
            advance(pieces[k], 2)
        for k in range(4, 8):
            for piece in pieces[k]:
                piece.finish((0,) if k == 5 else (0, 1, 2))
        pl.when(has_far)(far.wait_send)
        pl.when(has_next)(direct[1].wait_send)
        pl.when(has_next)(direct[2].wait_send)
        pl.when(even_next)(direct[0].wait_send)
        pl.when(odd_next)(aside.wait_send)
        pl.when(relays)(onward.wait_send)
        for copy in saved:
            copy.wait()


def front(lengths, x, gains, w_qkv, others, dims, count):
    rows, width = x.shape
    shard = w_qkv.shape[1]
    ext = WINDOW + rows
    shapes = [(2 * shard, width)] * 3 + [(16, width)] + [(2 * w.shape[0], w.shape[1]) for w in others]
    copies = copies_of(dims)
    vmem = pl.BlockSpec(memory_space=pltpu.VMEM)
    hbm = pl.BlockSpec(memory_space=pl.ANY)
    dma = pltpu.SemaphoreType.DMA
    count_pieces = sum(len(halves_of(s)) for s in shapes)
    nh, nq = width // 128, rows // QB
    sds = jax.ShapeDtypeStruct
    got = pl.pallas_call(
        functools.partial(front_kernel, dims, shapes, count),
        in_specs=[pl.BlockSpec(memory_space=pltpu.SMEM)] + [vmem] * 7,
        out_specs=[vmem] * 2 + [hbm] * 12,
        out_shape=[
            sds((rows, width), bf), sds((nh, 8, rows), f32),
            sds((rows, width), bf), sds((ext, width), bf), sds((ext, width), bf), sds((ext, width), bf),
        ]
        + [sds(dims + shapes[0], bf)] * 3 + [sds((8, width), f32)]
        + [sds(dims + s, bf) for s in shapes[4:]],
        scratch_shapes=[
            pltpu.VMEM((WINDOW, width), bf), pltpu.VMEM((rows // 2, width), bf), pltpu.VMEM((ext, width), bf),
            pltpu.VMEM((rows, width), bf),
            pltpu.VMEM((ext, width), bf), pltpu.VMEM((ext, width), bf), pltpu.VMEM((8, width), f32),
            pltpu.VMEM((8, width), f32), pltpu.VMEM((nq, QB, WINDOW + QB), f32),
            pltpu.VMEM((rows, width), f32), pltpu.VMEM((nh, rows, 128), f32), pltpu.VMEM((nh, rows, 128), f32),
        ]
        + [pltpu.VMEM(s, f32) for s in shapes]
        + [pltpu.VMEM(s, bf) for s in shapes]
        + [pltpu.VMEM(dims + s, bf) for s in shapes[:4]]
        + [
            dma((8,)), dma((8,)), dma((count_pieces, copies)), dma((count_pieces, copies)), dma((8,)),
            dma((6,)), dma((5,)), dma((8,)),
        ],
        compiler_params=pltpu.CompilerParams(
            collective_id=1, has_side_effects=True, vmem_limit_bytes=60 * 2**20
        ),
        cost_estimate=pl.CostEstimate(flops=4 * rows * 1792 * 768 * 3, bytes_accessed=14 * 2**20, transcendentals=0),
        name="front",
    )(lengths, x, gains, w_qkv, *others)
    return got


def piece_cuts(shape):
    return [(pl.ds(*rows), pl.ds(*cols)) for rows, cols in halves_of(shape)]


class Collapse:
    def __init__(self, dims, place, shape, turn, grad, out, buffers, send, recv):
        self.dims, self.place, self.shape = dims, place, shape
        self.grad, self.out, self.send, self.recv = grad, out, send, recv
        self.acc, self.box0, self.box1, self.box2, self.box3, self.fin, self.box4 = buffers
        z, y, x, c = place
        far_x, far_y = device_at(dims, (z, y, 1 - x, c)), device_at(dims, (z, 1 - y, x, c))
        every = slice(None)
        by_x = [(far_x, (every, every, 1 - x), (every, every, x)), (far_y, (every, 1 - y, x), (every, y, x))]
        by_y = [(far_y, (every, 1 - y, every), (every, y, every)), (far_x, (every, y, 1 - x), (every, y, x))]
        ways = [by_x, by_y] if turn == 0 else [by_y, by_x]
        self.pieces = list(zip(piece_cuts(shape), ways))

    def columns(self, core):
        half = self.shape[1] // 2
        return pl.ds(pl.multiple_of(core * half, 128), half)

    def copy(self, slot, source, target, device):
        return pltpu.make_async_remote_copy(
            src_ref=source, dst_ref=target, send_sem=self.send.at[slot], recv_sem=self.recv.at[slot],
            device_id=device, device_id_type=MESH,
        )

    def copies(self, stage):
        z, y, x, c = self.place
        mate = device_at(self.dims, sibling(self.place))
        every = slice(None)
        if stage == 0:
            source = self.grad.at[every, every, every, every, self.columns(1 - c)]
            return [self.copy(0, source, self.box0, mate)]
        if stage == 4:
            half = self.shape[0] // 2
            source = self.fin.at[pl.ds(pl.multiple_of((1 - c) * half, 8), half)]
            return [self.copy(1, source, self.box4, mate)]
        made = []
        for at, (cut, ways) in enumerate(self.pieces):
            first = 2 + at * (2 + self.dims[0] - 1)
            if stage in (1, 2):
                device, give, _ = ways[stage - 1]
                box = (self.box1 if stage == 1 else self.box2).at[(every,) * (3 - stage) + cut]
                made.append(self.copy(first + stage - 1, self.acc.at[give + cut], box, device))
            else:
                for by in range(1, self.dims[0]):
                    to = lax.rem(z + by, self.dims[0])
                    made.append(
                        self.copy(
                            first + 1 + by, self.acc.at[(to, y, x) + cut], self.box3.at[(by - 1,) + cut],
                            device_at(self.dims, (to, y, x, c)),
                        )
                    )
        return made

    def local(self, sem):
        if self.grad.shape == self.acc.shape:
            return pltpu.make_async_copy(self.grad, self.acc, sem)
        every = slice(None)
        source = self.grad.at[every, every, every, every, self.columns(self.place[3])]
        return pltpu.make_async_copy(source, self.acc, sem)

    def start(self, stage):
        for copy in self.copies(stage):
            copy.start()

    def add(self, stage):
        for copy in self.copies(stage):
            copy.wait_recv()
        z, y, x, c = self.place
        dims = self.dims
        if stage == 0:

            def body(i, carry):
                a, b, d = i // (dims[1] * dims[2]), lax.rem(i // dims[2], dims[1]), lax.rem(i, dims[2])
                self.acc[a, b, d] = self.acc[a, b, d] + self.box0[a, b, d]
                return carry

            lax.fori_loop(0, dims[0] * dims[1] * dims[2], body, 0)
        elif stage == 1:
            for cut, ways in self.pieces:
                by_x = not isinstance(ways[0][2][2], slice)

                def body(i, carry):
                    a, b = i // 2, lax.rem(i, 2)
                    at = ((a, b, x) if by_x else (a, y, b)) + cut
                    self.acc[at] = self.acc[at] + self.box1[(a, b) + cut]
                    return carry

                lax.fori_loop(0, dims[0] * 2, body, 0)
        elif stage == 2:

            def body(a, carry):
                self.acc[a, y, x] = self.acc[a, y, x] + self.box2[a]
                return carry

            lax.fori_loop(0, dims[0], body, 0)
        elif stage == 3:
            total = self.acc[z, y, x].astype(f32)
            for by in range(1, dims[0]):
                total = total + self.box3[by - 1].astype(f32)
            self.fin[...] = total
        else:
            half = self.shape[0] // 2
            mine = self.fin[pl.ds(pl.multiple_of(c * half, 8), half)]
            other = self.box4[...]
            width = self.shape[1] // 2
            self.out[:, :width] = jnp.where(c == 0, mine, other)
            self.out[:, width:] = jnp.where(c == 0, other, mine)

    def finish(self, stages=(0, 1, 2, 3, 4)):
        for stage in stages:
            for copy in self.copies(stage):
                copy.wait_send()


class EarlyCollapse(Collapse):
    def trade(self, given, send, recv):
        mate = device_at(self.dims, sibling(self.place))
        self.swaps = [
            pltpu.make_async_remote_copy(
                src_ref=given.at[j], dst_ref=self.box0.at[j], send_sem=send.at[j], recv_sem=recv.at[j],
                device_id=mate, device_id_type=MESH,
            )
            for j in range(self.dims[0])
        ]

    def copies(self, stage):
        return self.swaps if stage == 0 else super().copies(stage)


def collapse_scratch(dims, shapes, resumed=()):
    found = []
    for k, (rows, cols) in enumerate(shapes):
        half = cols // 2
        first = (16, 128) if k in resumed else None
        found += [
            pltpu.VMEM(dims + (rows, half), bf),
            pltpu.VMEM(first or dims + (rows, half), bf),
            pltpu.VMEM(first or (dims[0], 2, rows, half), bf),
            pltpu.VMEM((dims[0], rows, half), bf),
            pltpu.VMEM((dims[0] - 1, rows, half), bf),
            pltpu.VMEM((rows, half), f32),
            pltpu.VMEM((rows // 2, half), f32),
        ]
    dma = pltpu.SemaphoreType.DMA
    n = len(shapes)
    slots = 2 + 2 * (2 + dims[0] - 1)
    return found + [dma((n, slots)), dma((n, slots)), dma((n,))]


def collapses_of(dims, place, shapes, grads, outs, scratch):
    n = len(shapes)
    send, recv, local_sem = scratch[7 * n :]
    made = [
        Collapse(dims, place, shapes[k], k % 2, grads[k], outs[k], scratch[7 * k : 7 * k + 7], send.at[k], recv.at[k])
        for k in range(n)
    ]
    return made, [made[k].local(local_sem.at[k]) for k in range(n)]


def run_collapse(sums, locals_, k, stage):
    if stage < 0:
        locals_[k].start()
        sums[k].start(0)
        return
    if stage == 0:
        locals_[k].wait()
    sums[k].add(stage)
    if stage < 4:
        sums[k].start(stage + 1)


def back_kernel(lo_ref, q_ref, do_ref, o_ref, lse_ref, k_ref, v_ref, dq_ref, dk_ref, dv_ref, bias, dk_acc, dv_acc):
    hp, qb = pl.program_id(0), pl.program_id(1)
    span = WINDOW + QB
    start = pl.multiple_of(qb * QB, QB)

    @pl.when(hp == 0)
    def _():
        base = qb * QB
        kpos = base + lax.broadcasted_iota(jnp.int32, (span, QB), 0)
        qpos = WINDOW + base + lax.broadcasted_iota(jnp.int32, (span, QB), 1)
        ok = (kpos >= lo_ref[...]) & (kpos <= qpos)
        bias[qb] = jnp.where(ok, 0.0, NEG)

    @pl.when(qb == 0)
    def _():
        dk_acc[...] = jnp.zeros_like(dk_acc)
        dv_acc[...] = jnp.zeros_like(dv_acc)

    q_heads = halves(q_ref[...])
    do = do_ref[...]
    d_heads = halves(do)
    prod = do.astype(f32) * o_ref[...].astype(f32)
    row = lax.broadcasted_iota(jnp.int32, (8, 128), 0)
    lane = lax.broadcasted_iota(jnp.int32, (8, 128), 1)
    pick = jnp.where(row == lane // 64, 1.0, 0.0).astype(f32)
    delta = lax.dot_general(pick, prod, NT, precision=lax.Precision.HIGHEST, preferred_element_type=f32)
    lse = lse_ref[0]
    at = pl.ds(start, span)
    kw, vw = k_ref[at, :], v_ref[at, :]
    low_p, low_s, dq = [], [], []
    for h in range(2):
        s = dot(kw, q_heads[h], NT) + bias[qb]
        p = jnp.exp(s - lse[h : h + 1])
        dp = dot(vw, d_heads[h], NT)
        ds = (p * (dp - delta[h : h + 1])).astype(bf)
        low_p.append(p.astype(bf))
        low_s.append(ds)
        dq.append(dot(ds, kw, TN))
    dv_acc[at, :] += dot(jnp.concatenate(low_p, axis=1), jnp.concatenate(d_heads, axis=0))
    dk_acc[at, :] += dot(jnp.concatenate(low_s, axis=1), jnp.concatenate(q_heads, axis=0))
    lane = lax.broadcasted_iota(jnp.int32, (QB, 128), 1)
    dq_ref[...] = (jnp.where(lane < 64, dq[0], dq[1]) * 0.125).astype(bf)

    @pl.when(qb == pl.num_programs(1) - 1)
    def _():
        dk_ref[...] = dk_acc[...].astype(bf)
        dv_ref[...] = dv_acc[...].astype(bf)


def attend_back(q, do, o, lse, k, v, lo_row):
    rows, width = q.shape
    ext = k.shape[0]
    nq, nh = rows // QB, width // 128
    blk = pl.BlockSpec((QB, 128), lambda h, i: (i, h))
    full = pl.BlockSpec((ext, 128), lambda h, i: (0, h))
    return pl.pallas_call(
        back_kernel,
        grid=(nh, nq),
        in_specs=[pl.BlockSpec((1, QB), lambda h, i: (0, i)), blk, blk, blk]
        + [pl.BlockSpec((1, 8, QB), lambda h, i: (h, 0, i)), full, full],
        out_specs=[blk, full, full],
        out_shape=[
            jax.ShapeDtypeStruct((rows, width), bf),
            jax.ShapeDtypeStruct((ext, width), bf),
            jax.ShapeDtypeStruct((ext, width), bf),
        ],
        scratch_shapes=[
            pltpu.VMEM((nq, WINDOW + QB, QB), f32),
            pltpu.VMEM((ext, 128), f32),
            pltpu.VMEM((ext, 128), f32),
        ],
        compiler_params=pltpu.CompilerParams(vmem_limit_bytes=56 * 2**20),
        name="attend_back",
    )(lo_row, q, do, o, lse, k, v)


SUM_EVENTS = {
    (0, 1): ((2, 2), (1, 0), (0, 0)),
    (0, 3): ((1, 1), (0, 1), (2, 3)),
    (0, 4): ((1, 2), (0, 2), (2, 4)),
    (1, 2): ((1, 4), (0, 4)),
}


def back_kernel_paired(dims, shapes, count, lengths_ref, lse_ref, delta_ref, *refs):
    n = len(shapes)
    names = iter(refs)
    take = lambda k: [next(names) for _ in range(k)]
    sources = take(6)
    grads = take(n)
    dq_out, dk_out, dv_out, near_out, rest_out = take(5)
    sums_out = take(n)
    q, do, k, v, wk, wv = buffers = take(6)
    dk, dv, dq_acc, dk_acc, dv_acc, bias = take(6)
    load_sem, out_sem, back_send, back_recv = take(4)
    scratch = list(names)

    place = my_place(dims)
    seq, item = lax.axis_index("seq"), lax.axis_index("item")
    rows, width = q.shape
    nq, pairs = rows // QB, width // 128
    loads = [pltpu.make_async_copy(a, b, load_sem.at[m]) for m, (a, b) in enumerate(zip(sources, buffers))]
    for load in loads:
        load.start()
    ahead, behind = (lax.rem(seq + 1, count), item), (lax.rem(seq + count - 1, count), item)
    with jax.named_scope("masks"):
        for qb in range(nq):
            pos = seq * rows + qb * QB + lax.broadcasted_iota(jnp.int32, (1, QB), 1)
            lo = lower_bounds(lengths_ref, pos, seq * rows)
            kpos = qb * QB + lax.broadcasted_iota(jnp.int32, (WINDOW + QB, QB), 0)
            qpos = WINDOW + qb * QB + lax.broadcasted_iota(jnp.int32, (WINDOW + QB, QB), 1)
            bias[qb] = jnp.where((kpos >= lo) & (kpos <= qpos), 0.0, NEG).astype(bf)
    with jax.named_scope("meet"):
        meet(peers(dims, place) + [ahead, behind])
    sums, locals_ = collapses_of(dims, place, shapes, grads, sums_out, scratch)
    locals_[2].start()
    for a in (1, 0):
        run_collapse(sums, locals_, a, -1)

    with jax.named_scope("load"):
        locals_[2].wait()
        sums[2].start(2)
        for load in loads[:4]:
            load.wait()

    def events(part, hp):
        for (when, pair), moves in SUM_EVENTS.items():
            if when != part:
                continue

            @pl.when(hp == pair)
            def _():
                for a, stage in moves:
                    with jax.named_scope("reduce_%d_%d" % (a, stage + 1)):
                        run_collapse(sums, locals_, a, stage)

    lane = lax.broadcasted_iota(jnp.int32, (QB, 128), 1)

    def block(hp, lanes, at, keys, mask):
        q_heads, d_heads = halves(q[at, lanes]), halves(do[at, lanes])
        lse, delta = lse_ref[hp, :, at], delta_ref[hp, :, at]
        kw, vw = k[keys, lanes], v[keys, lanes]
        low_p, low_s, found = [], [], []
        for h in range(2):
            s = dot(kw, q_heads[h], NT) + mask.astype(f32)
            p = jnp.exp(s - lse[h : h + 1])
            dp = dot(vw, d_heads[h], NT)
            ds = (p * (dp - delta[h : h + 1])).astype(bf)
            low_p.append(p.astype(bf))
            low_s.append(ds)
            found.append(dot(ds, kw, TN))
        dv_part = dot(jnp.concatenate(low_p, axis=1), jnp.concatenate(d_heads, axis=0))
        dk_part = dot(jnp.concatenate(low_s, axis=1), jnp.concatenate(q_heads, axis=0))
        return jnp.where(lane < 64, found[0], found[1]), dk_part, dv_part

    early = nq // 2
    reach = early * QB

    def halo_keys(hp, carry):
        events(0, hp)
        lanes = pl.ds(pl.multiple_of(hp * 128, 128), 128)
        for qb in reversed(range(nq)):
            at, size = pl.ds(qb * QB, QB), WINDOW + QB if qb < early else WINDOW - qb * QB
            keys = pl.ds(qb * QB, size)
            dq_part, dk_part, dv_part = block(hp, lanes, at, keys, bias[qb, :size, :])
            if qb < early:
                q[at, lanes] = (dq_part * 0.125).astype(bf)
            else:
                dq_acc[pl.ds(qb * QB - reach, QB), lanes] = dq_part
            if qb == nq - 1:
                dk_acc[...] = jnp.zeros_like(dk_acc)
                dv_acc[...] = jnp.zeros_like(dv_acc)
            dk_acc[keys, :] += dk_part
            dv_acc[keys, :] += dv_part
        dk[0 : WINDOW + reach, lanes] = dk_acc[...].astype(bf)
        dv[0 : WINDOW + reach, lanes] = dv_acc[...].astype(bf)
        return carry

    with jax.named_scope("halo_keys"):
        lax.fori_loop(0, pairs, halo_keys, 0)

    def halo_rows(i, carry):
        at = pl.ds(pl.multiple_of(i * QB, QB), QB)
        total = dot(dk[at, :], wk[...].reshape(width, width), NT) + dot(dv[at, :], wv[...].reshape(width, width), NT)
        k[at, :] = total.astype(bf)
        return carry

    lower, part = WINDOW - rows, rows // 4
    returned = [
        pltpu.make_async_remote_copy(
            src_ref=k.at[pl.ds(lower + m * part, part)], dst_ref=near_out.at[pl.ds(m * part, part)],
            send_sem=back_send.at[m], recv_sem=back_recv.at[m], device_id=behind, device_id_type=MESH,
        )
        for m in range(3)
    ]
    with jax.named_scope("halo_rows"):
        for load in loads[4:]:
            load.wait()
        for m in range(3):
            lax.fori_loop((lower + m * part) // QB, (lower + (m + 1) * part) // QB, halo_rows, 0)
            pl.when(seq >= 1)(returned[m].start)
        lax.fori_loop(0, lower // QB, halo_rows, 0)
        lax.fori_loop((lower + 3 * part) // QB, WINDOW // QB, halo_rows, 0)
        rest = [
            pltpu.make_async_copy(k.at[pl.ds(0, lower)], rest_out.at[pl.ds(0, lower)], out_sem.at[0]),
            pltpu.make_async_copy(k.at[pl.ds(lower + 3 * part, part)], rest_out.at[pl.ds(lower, part)], out_sem.at[1]),
        ]
        rest += [
            pltpu.make_async_copy(a.at[pl.ds(0, WINDOW)], b.at[pl.ds(0, WINDOW)], out_sem.at[2 + m])
            for m, (a, b) in enumerate([(dk, dk_out), (dv, dv_out)])
        ]
        for copy in rest:
            copy.start()
    for a in (1, 0):
        with jax.named_scope("reduce_%d_4" % a):
            run_collapse(sums, locals_, a, 3)

    def own_keys(hp, carry):
        events(1, hp)
        lanes = pl.ds(pl.multiple_of(hp * 128, 128), 128)
        for qb in reversed(range(early, nq)):
            at, size = pl.ds(qb * QB, QB), (qb + 1) * QB
            keys, own = pl.ds(WINDOW, size), pl.ds(0, size)
            dq_part, dk_part, dv_part = block(hp, lanes, at, keys, bias[qb, WINDOW - qb * QB :, :])
            q[at, lanes] = ((dq_acc[pl.ds(qb * QB - reach, QB), lanes] + dq_part) * 0.125).astype(bf)
            if qb == nq - 1:
                dk_acc[own, :] = dk_part
                dv_acc[own, :] = dv_part
            else:
                dk_acc[own, :] += dk_part
                dv_acc[own, :] += dv_part
        for total, kept in ((dk_acc, dk), (dv_acc, dv)):
            first, second = pl.ds(WINDOW, reach), pl.ds(WINDOW + reach, rows - reach)
            kept[first, lanes] = (total[0:reach, :] + kept[first, lanes].astype(f32)).astype(bf)
            kept[second, lanes] = total[reach:rows, :].astype(bf)
        return carry

    with jax.named_scope("own_keys"):
        lax.fori_loop(0, pairs, own_keys, 0)
    own = pl.ds(WINDOW, rows)
    stores = rest + [
        pltpu.make_async_copy(a, b, out_sem.at[4 + m])
        for m, (a, b) in enumerate([(q, dq_out), (dk.at[own], dk_out.at[own]), (dv.at[own], dv_out.at[own])])
    ]
    for store in stores[4:]:
        store.start()
    with jax.named_scope("finish"):
        for one in sums[:2]:
            one.finish()
        sums[2].finish((2, 3, 4))
        for store in stores:
            store.wait()

        for copy in returned:
            pl.when(seq >= 1)(copy.wait_send)
            pl.when(seq + 1 < count)(copy.wait_recv)


def back(lengths, lse, delta, arrays, grads, dims, count):
    q, do, k, v, wk, wv = arrays
    rows, width = q.shape
    ext = k.shape[0]
    nq = rows // QB
    shapes = [g.shape[3:] for g in grads]
    shapes[2] = (shapes[2][0], 2 * shapes[2][1])
    vmem = pl.BlockSpec(memory_space=pltpu.VMEM)
    hbm = pl.BlockSpec(memory_space=pl.ANY)
    dma = pltpu.SemaphoreType.DMA
    sds = jax.ShapeDtypeStruct
    part = rows // 4
    got = pl.pallas_call(
        functools.partial(back_kernel_paired, dims, shapes, count),
        in_specs=[pl.BlockSpec(memory_space=pltpu.SMEM), vmem, vmem] + [hbm] * (6 + len(grads)),
        out_specs=[hbm] * 5 + [vmem] * len(grads),
        out_shape=[
            sds((rows, width), bf), sds((ext, width), bf), sds((ext, width), bf),
            sds((3 * part, width), bf), sds((WINDOW - 3 * part, width), bf),
        ]
        + [sds((r // 2, c), f32) for r, c in shapes],
        scratch_shapes=[pltpu.VMEM(a.shape, bf) for a in arrays]
        + [
            pltpu.VMEM((ext, width), bf), pltpu.VMEM((ext, width), bf), pltpu.VMEM((rows // 2, width), f32),
            pltpu.VMEM((WINDOW + rows // 2, 128), f32), pltpu.VMEM((WINDOW + rows // 2, 128), f32),
            pltpu.VMEM((nq, WINDOW + QB, QB), bf),
            dma((6,)), dma((7,)), dma((3,)), dma((3,)),
        ]
        + collapse_scratch(dims, shapes, (2,)),
        compiler_params=pltpu.CompilerParams(
            collective_id=3, has_side_effects=True, vmem_limit_bytes=63 * 2**20
        ),
        name="back",
    )(lengths, lse, delta, *arrays, *grads)
    return got[:5], got[5:]


GELU_A, GELU_B = 0.7978845608028654, 0.044715
MB = 512
PROJ_STEPS = (0, 1)
GATHER_STEP = 0
DOWN_STEP = 1


def middle_kernel(dims, proj_shape, wd_shape, bound_ref, cont_ref, gain_ref, *refs):
    names = iter(refs)
    take = lambda k: [next(names) for _ in range(k)]
    sources = take(8)
    y_out, p_out, dr_out, do_out, gain_out, delta_out, sum_proj, g_out, g_up, down_out = take(10)
    x, o, cot, pcot, wo, wu, wd, wp = buffers = take(8)
    n2, r1, act, slope, low_c, dyl, stage, grad_proj = take(8)
    load_sem, stage_sem, out_sem, send, recv = take(5)
    down_given, down_send, down_recv, trade_send, trade_recv, proj_send, proj_recv = take(7)
    down_buffers = take(3)
    scratch = list(names)

    place = my_place(dims)
    z, y, x_, c = place
    line = (slice(None), y, x_)
    pairs = list(zip(sources[:7], buffers[:7])) + [(sources[7].at[line], wp.at[line])]
    loads = [pltpu.make_async_copy(a, b, load_sem.at[k]) for k, (a, b) in enumerate(pairs)]
    for k in (0, 1, 4, 7, 5, 6, 3, 2):
        loads[k].start()
    with jax.named_scope("meet"):
        meet(peers(dims, place))
    total = EarlyCollapse(dims, place, proj_shape, 0, None, sum_proj, scratch[:7], scratch[7].at[0], scratch[8].at[0])
    total.trade(grad_proj, proj_send, proj_recv)

    def move_on(stage):
        total.add(stage)
        if stage < 4:
            total.start(stage + 1)


    down = EarlyCollapse(
        dims, place, wd_shape, 0, None, None, down_buffers + [None] * 4, down_send, down_recv
    )
    down.trade(down_given, trade_send, trade_recv)

    rows, width = x.shape
    chunks = wu.shape[1] // width
    gain = gain_ref[1:2]
    pieces = [
        Spread(dims, place, None, wp, pl.ds(*at), cols, order, send.at[k], recv.at[k])
        for k, (order, (at, cols)) in enumerate(zip(ORDERS, halves_of(wp.shape[3:])))
    ]
    def residual(i, carry):
        at = pl.ds(pl.multiple_of(i * MB, MB), MB)
        r = x[at, :].astype(f32) + dot(o[at, :], wo[...])
        r1[at, :] = r
        scale = lax.rsqrt(jnp.mean(r * r, axis=-1, keepdims=True) + EPSILON)
        n2[at, :] = (r * scale * gain).astype(bf)
        return carry

    with jax.named_scope("load"):
        loads[7].wait()
        for piece in pieces:
            piece.begin(1)
        for k in (0, 1, 4):
            loads[k].wait()
        lax.fori_loop(0, rows // MB, residual, 0)
        for k in (2, 3, 5, 6):
            loads[k].wait()

    def edge_of(at):
        edge = (bound_ref[:, at] * (1 - cont_ref[:, at])).astype(f32)
        return jnp.broadcast_to(edge, (8, MB)).T[:, 0:1]

    def forward(i, carry):
        at = pl.ds(pl.multiple_of(i * MB, MB), MB)
        y = r1[at, :]
        for j in range(chunks):
            cols = slice(j * width, (j + 1) * width)
            u = dot(n2[at, :], wu[:, cols])
            square = u * u
            t = jnp.tanh(GELU_A * (u + GELU_B * square * u))
            half = 0.5 * (1.0 + t)
            act[at, cols] = (u * half).astype(bf)
            slope[at, cols] = (half + 0.5 * u * (1.0 - t * t) * (GELU_A + 3.0 * GELU_A * GELU_B * square)).astype(bf)
            y = y + dot(act[at, cols], wd[cols, :])
        low_c[at, :] = (edge_of(at) * pcot[at, :].astype(f32)).astype(bf)
        dr_out[at, :] = cot[at, :].astype(f32)
        cot[at, :] = y.astype(bf)

        @pl.when(i == GATHER_STEP)
        def _():
            with jax.named_scope("proj_1"):
                for piece in pieces:
                    piece.advance(1)

        return carry

    def project(i, carry):
        at = pl.ds(pl.multiple_of(i * MB, MB), MB)
        weight = wp[...].reshape(width, wp.shape[-1])
        d = dr_out[at, :] + dot(low_c[at, :], weight, NT)
        dr_out[at, :] = d
        dyl[at, :] = d.astype(bf)
        pcot[at, :] = (edge_of(at) * dot(cot[at, :], weight)).astype(bf)
        return carry

    with jax.named_scope("forward"):
        lax.fori_loop(0, rows // MB, forward, 0)
    with jax.named_scope("proj_2"):
        for piece in pieces:
            piece.advance(2)
        for piece in pieces:
            piece.finish((1, 2))
    with jax.named_scope("project"):
        lax.fori_loop(0, rows // MB, project, 0)
    stores = [pltpu.make_async_copy(cot, y_out, out_sem.at[0]), pltpu.make_async_copy(pcot, p_out, out_sem.at[1])]
    for store in stores:
        store.start()

    flying = {}

    def emit(target, left, right):
        block = width // 2
        for j in range(left.shape[1] // block):
            for k in range(right.shape[1] // width):
                slot = emit.count % 2
                emit.count += 1
                if slot in flying:
                    flying[slot].wait()
                rows_at, cols_at = slice(j * block, (j + 1) * block), slice(k * width, (k + 1) * width)
                stage[slot] = dot(left[:, rows_at], right[:, cols_at], TN).astype(bf)
                copy = pltpu.make_async_copy(
                    stage.at[slot], target.at[pl.ds(j * block, block), pl.ds(k * width, width)], stage_sem.at[slot]
                )
                copy.start()
                flying[slot] = copy

    emit.count = 0
    with jax.named_scope("grad_proj"):
        half = proj_shape[1] // 2
        for target, core in ((grad_proj, 1 - c), (scratch[0], c)):
            cols = pl.ds(pl.multiple_of(core * half, 128), half)
            target[...] = dot(cot[...], low_c[:, cols], TN).astype(bf).reshape(target.shape)
            if target is grad_proj:
                total.start(0)
    with jax.named_scope("grad_down"):
        acc, half = down_buffers[0], width // 2
        for j in range(chunks):
            got = dot(act[:, j * width : (j + 1) * width], dyl[...], TN).astype(bf)
            left, right = got[:, :half], got[:, half:]
            acc[j] = jnp.where(c == 0, left, right).reshape(acc.shape[1:])
            down_given[j] = jnp.where(c == 0, right, left).reshape(acc.shape[1:])
            down.swaps[j].start()

    row = lax.broadcasted_iota(jnp.int32, (16, width), 0)
    lane = lax.broadcasted_iota(jnp.int32, (16, width), 1)
    heads = jnp.where(row == lane // 64, 1.0, 0.0).astype(f32)

    def backward(i, carry):
        for step, when in enumerate(PROJ_STEPS):

            @pl.when(i == when)
            def _():
                with jax.named_scope("reduce_%d" % step):
                    move_on(step)
        @pl.when(i == DOWN_STEP)
        def _():
            with jax.named_scope("down_0"):
                down.add(0)
                down.start(1)

        at = pl.ds(pl.multiple_of(i * MB, MB), MB)
        dn = jnp.zeros((MB, width), f32)
        for j in range(chunks):
            cols = slice(j * width, (j + 1) * width)
            du = (dot(dyl[at, :], wd[cols, :], NT) * slope[at, cols].astype(f32)).astype(bf)
            slope[at, cols] = du
            dn = dn + dot(du, wu[:, cols], NT)
        r = r1[at, :]
        scale = lax.rsqrt(jnp.mean(r * r, axis=-1, keepdims=True) + EPSILON)
        unit = r * scale
        by_gain = dn * gain
        inner = jnp.mean(by_gain * unit, axis=-1, keepdims=True)
        dr = dr_out[at, :] + scale * (by_gain - unit * inner)
        dr_out[at, :] = dr
        low_dr = dr.astype(bf)
        dyl[at, :] = low_dr
        low_do = dot(low_dr, wo[...], NT).astype(bf)
        x[at, :] = low_do
        delta = lax.dot_general(
            heads, low_do.astype(f32) * o[at, :].astype(f32), NT,
            precision=lax.Precision.HIGHEST, preferred_element_type=f32,
        )
        for hp in range(width // 128):
            delta_out[hp, 0:2, at] = delta[2 * hp : 2 * hp + 2]
        return carry + jnp.sum(dn * unit, axis=0, keepdims=True)

    with jax.named_scope("backward"):
        gain_out[...] = lax.fori_loop(0, rows // MB, backward, jnp.zeros((1, width), f32))
    stores.append(pltpu.make_async_copy(x, do_out, out_sem.at[2]))
    stores[-1].start()
    with jax.named_scope("grad_out"):
        move_on(2)
        emit(g_out, o, dyl)
    with jax.named_scope("grad_up"):
        emit(g_up, n2, slope)
    with jax.named_scope("down_1"):
        down.add(1)
        stores.append(pltpu.make_async_copy(down_buffers[0], down_out, out_sem.at[3]))
        stores[-1].start()
    with jax.named_scope("finish"):
        for stage in (3, 4):
            move_on(stage)
        for copy in list(flying.values()) + stores:
            copy.wait()
        total.finish()
        down.finish((0, 1))


def middle(bound, cont, gain, arrays, dims):
    x, o, cot, pcot, wo, wu, wd, wp = arrays
    rows, width = x.shape
    ff, proj = wu.shape[1], wp.shape[-1]
    copies = copies_of(dims)
    pair = width // (dims[0] * dims[1] * dims[2])
    tall = ff // (dims[0] * dims[1] * dims[2])
    down_acc = dims + (tall, width // 2)
    vmem = pl.BlockSpec(memory_space=pltpu.VMEM)
    hbm = pl.BlockSpec(memory_space=pl.ANY)
    dma = pltpu.SemaphoreType.DMA
    sds = jax.ShapeDtypeStruct
    return pl.pallas_call(
        functools.partial(middle_kernel, dims, (pair, proj), (tall, width)),
        in_specs=[vmem] * 3 + [hbm] * 8,
        out_specs=[hbm, hbm, vmem, hbm, vmem, vmem, vmem, hbm, hbm, hbm],
        out_shape=[
            sds((rows, width), bf), sds((rows, proj), bf), sds((rows, width), f32), sds((rows, width), bf),
            sds((1, width), f32), sds((width // 128, 8, rows), f32), sds((pair // 2, proj), f32),
            sds(wo.shape, bf), sds(wu.shape, bf), sds(down_acc, bf),
        ],
        scratch_shapes=[pltpu.VMEM(a.shape, bf) for a in arrays]
        + [
            pltpu.VMEM((rows, width), bf), pltpu.VMEM((rows, width), f32), pltpu.VMEM((rows, ff), bf),
            pltpu.VMEM((rows, ff), bf), pltpu.VMEM((rows, proj), bf), pltpu.VMEM((rows, width), bf),
            pltpu.VMEM((2, width // 2, width), bf), pltpu.VMEM(dims + (pair, proj // 2), bf),
            dma((8,)), dma((2,)), dma((4,)), dma((2, copies)), dma((2, copies)),
            pltpu.VMEM(down_acc, bf), dma((12,)), dma((12,)), dma((dims[0],)), dma((dims[0],)),
            dma((dims[0],)), dma((dims[0],)),
            pltpu.VMEM(down_acc, bf), pltpu.VMEM(down_acc, bf), pltpu.VMEM((dims[0], 2, tall, width // 2), bf),
        ]
        + collapse_scratch(dims, [(pair, proj)]),
        compiler_params=pltpu.CompilerParams(
            collective_id=2, has_side_effects=True, vmem_limit_bytes=63 * 2**20
        ),
        name="middle",
    )(bound, cont, gain, *arrays)


ROW_OUT, ROW_UP, ROW_PROJ, ROW_DOWN, ROW_GAIN, ROW_MEAN = 3, 4, 8, 10, 11, 13
STAT_ROWS = 16
DECAY = 1.0 - STEP ** (-0.8)


def exchange_rounds(dims, place):
    z, y, x, c = place
    plane = [(1, 0), (0, 1), (1, 1)]
    rounds = [
        ([sibling(place)], c),
        ([(z, lax.rem(y + dy, 2), lax.rem(x + dx, 2), c) for dy, dx in plane], y * 2 + x),
        ([moved(dims, place, 0, by) for by in range(1, dims[0])], z),
    ]
    return [([device_at(dims, p) for p in others], number) for others, number in rounds]


def put_stats(stats, row, total, square_sum, old_rows, lane, columns):
    width = stats.shape[1]
    for j in range(total.shape[1] // width):
        stats[row + j : row + j + 1, :] = total[:, j * width : (j + 1) * width]
    value = DECAY * jnp.sum(old_rows, axis=1, keepdims=True) + (1.0 - DECAY) / columns * square_sum
    at = lax.broadcasted_iota(jnp.int32, (1, width), 1)
    stats[ROW_MEAN : ROW_MEAN + 1, :] += jnp.where(at == lane, value, 0.0)


def last_kernel(
    dims, shapes, count, x_hbm, resid_hbm, gain_ref, gain_two_ref,
    dq_hbm, dk_hbm, dv_hbm, n_hbm, wq_hbm, wk_hbm, wv_hbm, near_hbm, rest_hbm,
    sum_out, sum_proj, sum_up, sum_down, row_qkv, row_out, row_proj, row_up, row_down, *refs,
):
    names = iter(refs)
    take = lambda k: [next(names) for _ in range(k)]
    grad_ref, total_ref = take(2)
    sums_out = take(3)
    dq, dk, dv, normed, flipped, wq, wk, wv = take(8)
    own_back, near, rest, box, stats, inbox, x_ref, resid_ref = take(8)
    grads = take(3)
    load_sem, back_send, back_recv, stat_send, stat_recv = take(5)
    scratch = list(names)

    place = my_place(dims)
    seq, item = lax.axis_index("seq"), lax.axis_index("item")
    rows, width = x_ref.shape
    loads = [
        pltpu.make_async_copy(a, b, load_sem.at[n])
        for n, (a, b) in enumerate(
            [
                (rest_hbm, rest), (n_hbm, normed), (dk_hbm, dk), (dv_hbm, dv), (dq_hbm, dq),
                (wk_hbm, wk), (wv_hbm, wv), (wq_hbm, wq), (near_hbm, near),
                (x_hbm, x_ref), (resid_hbm, resid_ref),
            ]
        )
    ]
    for load in loads:
        load.start()
    ahead = [(lax.rem(seq + d, count), item) for d in (1, 2)]
    behind = [(lax.rem(seq + count - d, count), item) for d in (1, 2)]
    with jax.named_scope("meet"):
        meet(peers(dims, place) + ahead + behind + [device_at(dims, place[:1] + (1 - place[1], 1 - place[2], place[3]))])
    far = WINDOW - rows
    near_rows, far_rows = pl.ds(far, rest.shape[0] - far), pl.ds(0, far)
    returned = [
        pltpu.make_async_remote_copy(
            src_ref=rest.at[part], dst_ref=box.at[part], send_sem=back_send.at[m], recv_sem=back_recv.at[m],
            device_id=behind[m], device_id_type=MESH,
        )
        for m, part in enumerate((near_rows, far_rows))
    ]
    loads[0].wait()
    for m in range(2):
        pl.when(seq >= m + 1)(returned[m].start)

    def back_of(at):
        return dot(dk[at, :], wk[...].reshape(width, width), NT) + dot(dv[at, :], wv[...].reshape(width, width), NT)

    sums, locals_ = collapses_of(dims, place, shapes, grads, sums_out, scratch)
    with jax.named_scope("weight_gradients"):
        loads[1].wait()
        flipped[...] = normed[...].T
        for k, part in ((1, dk), (2, dv), (0, dq)):
            loads[(4, 2, 3)[k]].wait()
            base = WINDOW if k == 0 else 0
            got = dot(flipped[:, base:], part[...])
            grads[k][...] = got.astype(bf).reshape(grads[k].shape)
            run_collapse(sums, locals_, k, -1)
            if k != 1:
                run_collapse(sums, locals_, 1 if k == 2 else 2, 0)

    def own_block(i, carry):
        at = pl.ds(pl.multiple_of(i * QB, QB), QB)
        ext = pl.ds(pl.multiple_of(WINDOW + i * QB, QB), QB)
        own_back[at, :] = back_of(ext) + dot(dq[at, :], wq[...].reshape(width, width), NT)
        return carry

    with jax.named_scope("own_rows"):
        for load in loads[5:]:
            load.wait()
        lax.fori_loop(0, rows // QB, own_block, 0)

    stats[0] = jnp.zeros_like(stats[0])
    held = stats.at[0]
    held[ROW_GAIN + 1 : ROW_GAIN + 2, :] = gain_two_ref[...]

    def add_stats(row, grad, old_rows, lane):
        square = grad * grad + TINY_SQUARE
        total = jnp.sum(square, axis=0, keepdims=True)
        put_stats(held, row, total, jnp.sum(total, axis=1, keepdims=True), old_rows, lane, grad.shape[1])

    with jax.named_scope("small_sums"):
        add_stats(ROW_OUT, sum_out[...], row_out[...], 3)
        add_stats(ROW_UP, sum_up[...], row_up[...], 4)
        add_stats(ROW_PROJ, sum_proj[...], row_proj[...], 5)
        add_stats(ROW_DOWN, sum_down[...], row_down[...], 6)

    for stage in range(5):
        with jax.named_scope("reduce_%d" % stage):
            for k in (1, 2, 0) if stage else (0,):
                run_collapse(sums, locals_, k, stage)
    for k in range(3):
        add_stats(k, sums_out[k][...], row_qkv[k : k + 1, :], k)

    with jax.named_scope("rows_returned"):

        @pl.when(seq + 1 < count)
        def _():
            returned[0].wait_recv()
            size = near.shape[0]
            own_back[0:size, :] += near[...].astype(f32)
            own_back[size:, :] += box[near_rows, :].astype(f32)

        @pl.when(seq + 2 < count)
        def _():
            returned[1].wait_recv()
            own_back[rows - far :, :] += box[far_rows, :].astype(f32)

    gain = gain_ref[0:1]

    def input_block(i, total):
        at = pl.ds(pl.multiple_of(i * QB, QB), QB)
        x = x_ref[at, :].astype(f32)
        scale = lax.rsqrt(jnp.mean(x * x, axis=-1, keepdims=True) + EPSILON)
        back = own_back[at, :]
        unit = x * scale
        by_gain = back * gain
        inner = jnp.mean(by_gain * unit, axis=-1, keepdims=True)
        grad_ref[at, :] = (resid_ref[at, :] + scale * (by_gain - unit * inner)).astype(bf)
        return total + jnp.sum(back * unit, axis=0, keepdims=True)

    with jax.named_scope("input_gradient"):
        total = lax.fori_loop(0, rows // QB, input_block, jnp.zeros((1, width), f32))
    held[ROW_GAIN : ROW_GAIN + 1, :] = total

    rounds = exchange_rounds(dims, place)
    z, y, x, c = place
    senders = [
        [1 - c],
        [lax.rem(y + dy, 2) * 2 + lax.rem(x + dx, 2) for dy, dx in ((1, 0), (0, 1), (1, 1))],
        [lax.rem(z + dims[0] - by, dims[0]) for by in range(1, dims[0])],
    ]

    with jax.named_scope("exchange_sums"):
        slot = 0
        for stage, (others, number) in enumerate(rounds):
            copies = []
            for other in others:
                copies.append(
                    pltpu.make_async_remote_copy(
                        src_ref=stats.at[stage], dst_ref=inbox.at[slot],
                        send_sem=stat_send.at[slot], recv_sem=stat_recv.at[slot],
                        device_id=other, device_id_type=MESH,
                    )
                )
                copies[-1].start()
                slot += 1
            for copy in copies:
                copy.wait()
            base = slot - len(others)
            total = jnp.zeros_like(stats[0])
            for member in range(len(others) + 1):
                term = stats[stage]
                for m in range(len(others)):
                    term = jnp.where(senders[stage][m] == member, inbox[base + m], term)
                total = total + term
            stats[stage + 1] = total
        total_ref[...] = stats[len(rounds)]
    for one in sums:
        one.finish()
    for m in range(2):
        pl.when(seq >= m + 1)(returned[m].wait_send)


def last(x, resid_grad, gain, gain_two, dq, dk, dv, normed, weights, returned, sums, old_rows, dims, count):
    rows, width = x.shape
    ext = normed.shape[0]
    shapes = [w.shape[3:] for w in weights]
    slots = 4 + dims[0] - 1
    vmem = pl.BlockSpec(memory_space=pltpu.VMEM)
    hbm = pl.BlockSpec(memory_space=pl.ANY)
    dma = pltpu.SemaphoreType.DMA
    sds = jax.ShapeDtypeStruct
    got = pl.pallas_call(
        functools.partial(last_kernel, dims, shapes, count),
        in_specs=[hbm] * 2 + [vmem] * 2 + [hbm] * 9 + [vmem] * 9,
        out_specs=[vmem] * 5,
        out_shape=[sds((rows, width), bf), sds((STAT_ROWS, width), f32)] + [sds((r // 2, c), f32) for r, c in shapes],
        scratch_shapes=[
            pltpu.VMEM((rows, width), bf), pltpu.VMEM((ext, width), bf), pltpu.VMEM((ext, width), bf),
            pltpu.VMEM((ext, width), bf), pltpu.VMEM((width, ext), bf),
        ]
        + [pltpu.VMEM(w.shape, bf) for w in weights]
        + [pltpu.VMEM((rows, width), f32)]
        + [pltpu.VMEM(a.shape, bf) for a in (*returned, returned[1])]
        + [pltpu.VMEM((4, STAT_ROWS, width), f32), pltpu.VMEM((slots, STAT_ROWS, width), f32)]
        + [pltpu.VMEM((rows, width), bf), pltpu.VMEM((rows, width), f32)]
        + [pltpu.VMEM(w.shape, bf) for w in weights]
        + [dma((11,)), dma((2,)), dma((2,)), dma((slots,)), dma((slots,))]
        + collapse_scratch(dims, shapes),
        compiler_params=pltpu.CompilerParams(
            collective_id=4, has_side_effects=True, vmem_limit_bytes=61 * 2**20
        ),
        name="last",
    )(x, resid_grad, gain, gain_two, dq, dk, dv, normed, *weights, *returned, *sums, *old_rows)
    return got[0], got[1], got[2:]


def update_kernel(
    place_ref, total_ref, gains_ref, gain_var_ref,
    w_qkv, w_out, w_proj, w_up, w_down, s_q, s_k, s_v, s_out, s_proj, s_up, s_down,
    row_qkv, row_out, row_proj, row_up, row_down, col_qkv, col_out, col_proj, col_up, col_down,
    y_ref, p_ref, d_ref, g_qkv, g_out, g_proj, g_up, g_down, g_gains, n_qkv, n_out, n_proj, n_up, n_down, n_gains,
    r_qkv, r_out, r_proj, r_up, r_down, c_qkv, c_out, c_proj, c_up, c_down, gain_var_new,
    y_out, p_out, d_out, flat, tall, y_held, p_held, d_held, pass_sem,
):
    held = (y_held, p_held, d_held)
    taken = [pltpu.make_async_copy(a, b, pass_sem.at[n]) for n, (a, b) in enumerate(zip((y_ref, p_ref, d_ref), held))]
    passed = [pltpu.make_async_copy(a, b, pass_sem.at[3 + n]) for n, (a, b) in enumerate(zip(held, (y_out, p_out, d_out)))]
    for copy in taken:
        copy.start()
    shard = row_out.shape[1]
    shard_down = row_down.shape[1]
    width = total_ref.shape[1]
    flat[...] = jnp.zeros_like(flat)
    flat[0:3, :shard] = row_qkv[...]
    flat[3:4, :shard] = row_out[...]
    flat[4:5, :shard] = row_up[...]
    flat[5:6, :shard] = row_proj[...]
    flat[6:7, :shard_down] = row_down[...]
    olds = flat[...].T
    tall[...] = jnp.zeros_like(tall)

    def one(weight, grad, lane, row, old_col, rows_all, g_out_, n_out_, c_out_):
        count, columns = grad.shape
        square = grad * grad + TINY_SQUARE
        row_new = DECAY * olds[:count, lane : lane + 1] + (1.0 - DECAY) * jnp.mean(square, axis=1, keepdims=True)
        tall[:count, lane : lane + 1] = row_new
        parts = [total_ref[row + j : row + j + 1, :] for j in range(columns // width)]
        col_total = parts[0] if len(parts) == 1 else jnp.concatenate(parts, axis=1)
        col_new = DECAY * old_col + (1.0 - DECAY) * col_total / rows_all
        mean = total_ref[ROW_MEAN : ROW_MEAN + 1, lane : lane + 1] / rows_all
        second = row_new * col_new / mean
        g_out_[...] = grad
        n_out_[...] = weight - WEIGHT_RATE * grad * lax.rsqrt(second)
        c_out_[...] = col_new.reshape(c_out_.shape)

    for k, grad in enumerate((s_q, s_k, s_v)):
        one(w_qkv[k], grad[...], k, k, col_qkv[k : k + 1, :], width, g_qkv.at[k], n_qkv.at[k], c_qkv.at[k : k + 1])
    ff = col_up.shape[0]
    one(w_out[...], s_out[...], 3, ROW_OUT, col_out[...].reshape(1, width), width, g_out, n_out, c_out)
    one(w_up[...], s_up[...], 4, ROW_UP, col_up[...].reshape(1, ff), width, g_up, n_up, c_up)
    one(w_proj[...], s_proj[...], 5, ROW_PROJ, col_proj[...].reshape(1, -1), width, g_proj, n_proj, c_proj)
    one(w_down[...], s_down[...], 6, ROW_DOWN, col_down[...].reshape(1, width), ff, g_down, n_down, c_down)
    for copy, onward in zip(taken, passed):
        copy.wait()
        onward.start()
    news = tall[...].T
    r_qkv[...] = news[0:3, :shard]
    r_out[...] = news[3:4, :shard]
    r_up[...] = news[4:5, :shard]
    r_proj[...] = news[5:6, :shard]
    r_down[...] = news[6:7, :shard_down]

    gain_sums = pltpu.roll(total_ref[8:16, :], width - place_ref[0] * shard, 1)
    sums = gain_sums[ROW_GAIN - 8 : ROW_GAIN - 6, :shard]
    var = DECAY * gain_var_ref[...] + (1.0 - DECAY) * (sums * sums + TINY_SQUARE)
    g_gains[...] = sums
    gain_var_new[...] = var
    n_gains[...] = gains_ref[...] - GAIN_RATE * sums * lax.rsqrt(var)
    for copy in passed:
        copy.wait()


def update(place, totals, gains, gain_var, weights, sums, rows, cols, results):
    vmem = pl.BlockSpec(memory_space=pltpu.VMEM)
    like = lambda arrays: [jax.ShapeDtypeStruct(a.shape, f32) for a in arrays]
    outs = like(weights) + like([gains]) + like(weights) + like([gains]) + like(rows) + like(cols) + like([gain_var])
    hbm = pl.BlockSpec(memory_space=pl.ANY)
    return pl.pallas_call(
        update_kernel,
        in_specs=[pl.BlockSpec(memory_space=pltpu.SMEM)] + [vmem] * (3 + 5 + 7 + 5 + 5) + [hbm] * 3,
        out_specs=[vmem] * len(outs) + [hbm] * 3,
        out_shape=outs + [jax.ShapeDtypeStruct(a.shape, a.dtype) for a in results],
        scratch_shapes=[pltpu.VMEM((8, 128), f32), pltpu.VMEM((128, 8), f32)]
        + [pltpu.VMEM(a.shape, a.dtype) for a in results]
        + [pltpu.SemaphoreType.DMA((6,))],
        compiler_params=pltpu.CompilerParams(vmem_limit_bytes=63 * 2**20),
        name="update",
    )(place, totals, gains, gain_var, *weights, *sums, *rows, *cols, *results)


def sum_kernel(sizes, x_ref, o_ref, inbox, send_sem, recv_sem):
    place = {name: lax.axis_index(name) for name, _ in sizes}
    partners = []
    for name, size in sizes:
        bit = 1
        while bit < size:
            mine = place[name]
            low = lax.rem(mine // bit, 2)
            other = mine + bit * (1 - 2 * low)
            partners.append(tuple(other if n == name else place[n] for n in ("seq", "item")))
            bit *= 2
    barrier = pltpu.get_barrier_semaphore()
    for partner in partners:
        pl.semaphore_signal(barrier, inc=1, device_id=partner, device_id_type=MESH)
    pl.semaphore_wait(barrier, len(partners))
    o_ref[0] = x_ref[...]
    for stage, partner in enumerate(partners):
        copy = pltpu.make_async_remote_copy(
            src_ref=o_ref.at[stage],
            dst_ref=inbox.at[stage],
            send_sem=send_sem.at[stage],
            recv_sem=recv_sem.at[stage],
            device_id=partner,
            device_id_type=MESH,
        )
        copy.start()
        copy.wait()
        o_ref[stage + 1] = o_ref[stage] + inbox[stage]


def sum_all(x, sizes):
    stages = sum(size.bit_length() - 1 for _, size in sizes)
    held = pl.pallas_call(
        functools.partial(sum_kernel, sizes),
        out_shape=jax.ShapeDtypeStruct((stages + 1,) + x.shape, x.dtype),
        in_specs=[pl.BlockSpec(memory_space=pltpu.VMEM)],
        out_specs=pl.BlockSpec(memory_space=pltpu.VMEM),
        scratch_shapes=[
            pltpu.VMEM((stages,) + x.shape, x.dtype),
            pltpu.SemaphoreType.DMA((stages,)),
            pltpu.SemaphoreType.DMA((stages,)),
        ],
        compiler_params=pltpu.CompilerParams(collective_id=0, has_side_effects=True),
        name="sum_all",
    )(x)
    return held[stages]


def from_behind(block, axis, distance):
    devices = range(lax.axis_size(axis))
    route = [(i - distance, i) for i in devices if i - distance in devices]
    return lax.ppermute(block, axis, route)


def norm_rows(values, gain):
    return values * lax.rsqrt(jnp.mean(values * values, axis=-1, keepdims=True) + EPSILON) * gain


def gelu_tanh(values):
    return (
        0.5
        * values
        * (1.0 + jnp.tanh(0.7978845608028654 * (values + 0.044715 * values * values * values)))
    )


def finish_update(weight, grad, row_new, col_state, col_total, rows_all, row_mean, decay):
    col_new = decay * col_state + (1.0 - decay) * col_total / rows_all
    second = row_new[..., :, None] * col_new[..., None, :] / row_mean
    return (weight - WEIGHT_RATE * grad * lax.rsqrt(second), col_new)


def local(
    byte_rows, item_lengths, cont_mask, bound_mask, out_cot, proj_cot,
    w_qkv, w_out, w_up, w_down, w_proj, gains,
    row_qkv, col_qkv, row_out, col_out, row_up, col_up, row_down, col_down, row_proj, col_proj, gain_var,
):
    sizes = tuple((name, lax.axis_size(name)) for name in ("item", "seq"))
    count = lax.axis_size("item") * lax.axis_size("seq")
    rows_dev, width = byte_rows.shape[1:]
    ff = w_up.shape[1]
    shard = width // count
    low = bf

    dims = grid_of(lax.axis_size("seq"), lax.axis_size("item"))
    paired = dims == (4, 2, 2) and shard % 8 == 0 and rows_dev < WINDOW <= 2 * rows_dev
    inputs_low = byte_rows[0]
    if paired:
        got = front(item_lengths, inputs_low, gains, w_qkv, (w_out, w_proj, w_up, w_down), dims, lax.axis_size("seq"))
        attended, lse, queries, ext_keys, ext_values, ext_normed = got[:6]
        split_qkv = got[6:9]
        gain_full = got[9]
        weight_out, weight_up, weight_down = [w.reshape(-1, w.shape[-1]) for w in (got[10], got[12], got[13])]
        part_proj = got[11]
    else:
        inputs = inputs_low.astype(f32)
        weight_qkv = lax.all_gather(w_qkv.astype(low), AXES, axis=1, tiled=True)
        gain_full = lax.all_gather(gains.astype(low), AXES, axis=1, tiled=True).astype(f32)
        weight_out, weight_proj, weight_up, weight_down = [
            lax.all_gather(w.astype(low), AXES, axis=0, tiled=True) for w in (w_out, w_proj, w_up, w_down)
        ]

    hop_total = -(-WINDOW // rows_dev)
    if not paired:
        offset = lax.axis_index("seq") * rows_dev
        ends = jnp.cumsum(item_lengths[0], dtype=jnp.int32)
        pos = offset + jnp.arange(rows_dev, dtype=jnp.int32)
        begin_at = jnp.max(jnp.where(ends[None, :] <= pos[:, None], ends[None, :], 0), axis=1)
        lo = jnp.maximum(begin_at, pos - WINDOW + 1) - offset + WINDOW
        halo = []
        for distance in range(hop_total, 0, -1):
            need = min(rows_dev, WINDOW - (distance - 1) * rows_dev)
            halo.append(from_behind(inputs_low[rows_dev - need :], "seq", distance))
        normed = norm_rows(inputs, gain_full[0]).astype(low)
        halo_normed = norm_rows(jnp.concatenate(halo, axis=0).astype(f32), gain_full[0]).astype(low)
        ext_normed = jnp.concatenate([halo_normed, normed], axis=0)
        queries = dot(normed, weight_qkv[0]).astype(low) * jnp.asarray(0.125, low)
        ext_keys = dot(ext_normed, weight_qkv[1]).astype(low)
        ext_values = dot(ext_normed, weight_qkv[2]).astype(low)
        attended, lse = attend(queries, ext_keys, ext_values, lo[:, None])

    if paired:
        output_low, projected, resid_grad, attended_grad, gain_two_grad, delta, sum_proj, *low_grads = middle(
            bound_mask, cont_mask, gain_full,
            (inputs_low, attended, out_cot[0], proj_cot[0], weight_out, weight_up, weight_down, part_proj), dims,
        )
        apart = [g.reshape(dims + (-1, g.shape[-1])) for g in low_grads]
        (query_grad, ext_key_grad, ext_value_grad, *returned), (sum_out, sum_up, sum_down) = back(
            item_lengths, lse, delta, (queries, attended_grad, ext_keys, ext_values, split_qkv[1], split_qkv[2]),
            apart, dims, lax.axis_size("seq"),
        )
        sums = [sum_out, sum_proj, sum_up, sum_down]
    else:
        resid = inputs + dot(attended, weight_out)
        normed_two = norm_rows(resid, gain_full[1]).astype(low)
        hidden_pre = dot(normed_two, weight_up)
        activated = gelu_tanh(hidden_pre).astype(low)
        output = resid + dot(activated, weight_down)
        output_low = output.astype(low)
        boundary = (bound_mask[0] * (1 - cont_mask[0])).astype(f32)[:, None]
        projected = (boundary * dot(output_low, weight_proj)).astype(low)
        proj_grad = (boundary * proj_cot[0].astype(f32)).astype(low)
        grad_proj = dot(output_low, proj_grad, TN)
        output_grad = out_cot[0].astype(f32) + dot(proj_grad, weight_proj, NT)
        output_grad_low = output_grad.astype(low)
        grad_down = dot(activated, output_grad_low, TN)
        act_grad = dot(output_grad_low, weight_down, NT)
        _, gelu_back = jax.vjp(gelu_tanh, hidden_pre)
        pre_grad = gelu_back(act_grad)[0].astype(low)
        grad_up = dot(normed_two, pre_grad, TN)
        normed_two_grad = dot(pre_grad, weight_up, NT)
        _, norm_two_back = jax.vjp(norm_rows, resid, gain_full[1])
        resid_norm_grad, gain_two_grad = norm_two_back(normed_two_grad)
        resid_grad = output_grad + resid_norm_grad
        resid_grad_low = resid_grad.astype(low)
        grad_out = dot(attended, resid_grad_low, TN)
        attended_grad = dot(resid_grad_low, weight_out, NT).astype(low)

        low_grads = [g.astype(low) for g in (grad_out, grad_proj, grad_up, grad_down)]
        query_grad, ext_key_grad, ext_value_grad = attend_back(
            queries, attended_grad, attended, lse, ext_keys, ext_values, lo[None, :]
        )
        sums = [lax.psum_scatter(g, AXES, scatter_dimension=0, tiled=True).astype(f32) for g in low_grads]
        sum_out, sum_proj, sum_up, sum_down = sums
    if paired:
        rows = [row_qkv, row_out[None], row_proj[None], row_up[None], row_down[None]]
        cols = [col_qkv, col_out, col_proj, col_up, col_down]
        input_grad, totals, sums_qkv = last(
            inputs_low, resid_grad, gain_full, gain_two_grad, query_grad, ext_key_grad, ext_value_grad,
            ext_normed, split_qkv, returned, sums, rows, dims, lax.axis_size("seq"),
        )
        mine = lax.axis_index("seq") * lax.axis_size("item") + lax.axis_index("item")
        done = update(
            mine[None].astype(jnp.int32), totals, gains, gain_var,
            (w_qkv, w_out, w_proj, w_up, w_down), (*sums_qkv, *sums), rows, cols,
            (output_low, projected, input_grad),
        )
        sum_qkv, sum_out, sum_proj, sum_up, sum_down, sum_gains = done[:6]
        new_qkv, new_out, new_proj, new_up, new_down, new_gains = done[6:12]
        row_qkv_new, row_out_new, row_proj_new, row_up_new, row_down_new = [done[12]] + [r[0] for r in done[13:17]]
        col_qkv_new, col_out_new, col_proj_new, col_up_new, col_down_new = done[17:22]
        gain_var_new, output_low, projected, input_grad = done[22:]
        return (
            output_low[None], projected[None], input_grad[None],
            sum_qkv, sum_out, sum_up, sum_down, sum_proj, sum_gains,
            new_qkv, new_out, new_up, new_down, new_proj, new_gains,
            row_qkv_new, col_qkv_new, row_out_new, col_out_new, row_up_new, col_up_new,
            row_down_new, col_down_new, row_proj_new, col_proj_new, gain_var_new,
        )
    ext_back = dot(ext_key_grad, weight_qkv[1], NT) + dot(ext_value_grad, weight_qkv[2], NT)
    halo_back = ext_back[:WINDOW].astype(low)
    grads_qkv = [
        dot(normed, query_grad, TN).astype(low),
        dot(ext_normed, ext_key_grad, TN).astype(low),
        dot(ext_normed, ext_value_grad, TN).astype(low),
    ]
    returned = []
    for distance in range(1, hop_total + 1):
        need = min(rows_dev, WINDOW - (distance - 1) * rows_dev)
        upper = WINDOW - (distance - 1) * rows_dev
        returned.append(from_behind(halo_back[upper - need : upper], "seq", -distance))
    sums = [lax.psum_scatter(g, AXES, scatter_dimension=0, tiled=True).astype(f32) for g in grads_qkv]
    sum_qkv = jnp.stack(sums)
    normed_grad = ext_back[WINDOW:] + dot(query_grad, weight_qkv[0], NT)
    for block in returned:
        need = block.shape[0]
        normed_grad = normed_grad.at[rows_dev - need :].add(block.astype(f32))
    _, norm_one_back = jax.vjp(norm_rows, inputs, gain_full[0])
    input_norm_grad, gain_one_grad = norm_one_back(normed_grad)
    input_grad = (resid_grad + input_norm_grad).astype(low)

    decay = 1.0 - STEP ** (-0.8)
    square_qkv = sum_qkv * sum_qkv + TINY_SQUARE
    square_out = sum_out * sum_out + TINY_SQUARE
    square_up = sum_up * sum_up + TINY_SQUARE
    square_down = sum_down * sum_down + TINY_SQUARE
    square_proj = sum_proj * sum_proj + TINY_SQUARE
    row_qkv_new = decay * row_qkv + (1.0 - decay) * jnp.mean(square_qkv, axis=-1)
    row_out_new = decay * row_out + (1.0 - decay) * jnp.mean(square_out, axis=-1)
    row_up_new = decay * row_up + (1.0 - decay) * jnp.mean(square_up, axis=-1)
    row_down_new = decay * row_down + (1.0 - decay) * jnp.mean(square_down, axis=-1)
    row_proj_new = decay * row_proj + (1.0 - decay) * jnp.mean(square_proj, axis=-1)
    row_sums = jnp.concatenate(
        [
            jnp.sum(row_qkv_new, axis=1),
            jnp.sum(row_out_new)[None],
            jnp.sum(row_up_new)[None],
            jnp.sum(row_down_new)[None],
            jnp.sum(row_proj_new)[None],
        ]
    )
    stats = [
        jnp.sum(square_qkv, axis=1).reshape(-1),
        jnp.sum(square_out, axis=0),
        jnp.sum(square_up, axis=0),
        jnp.sum(square_down, axis=0),
        jnp.sum(square_proj, axis=0),
        gain_one_grad,
        gain_two_grad,
        row_sums,
    ]
    flat = jnp.concatenate(stats)
    used = flat.shape[0]
    padded = -(-used // 1024) * 1024
    flat = jnp.pad(flat, (0, padded - used)).reshape(padded // 128, 128)
    flat = sum_all(flat, sizes).reshape(-1)
    totals, at = [], 0
    for part in stats:
        totals.append(flat[at : at + part.shape[0]])
        at += part.shape[0]
    col_qkv_total, col_out_total, col_up_total, col_down_total, col_proj_total, gain_one, gain_two, row_totals = totals
    col_qkv_total = col_qkv_total.reshape(3, width)
    mine = lax.axis_index("seq") * lax.axis_size("item") + lax.axis_index("item")
    sum_gains = lax.dynamic_slice_in_dim(jnp.stack([gain_one, gain_two]), mine * shard, shard, 1)
    row_counts = jnp.array([width, width, width, width, width, ff, width], f32)
    row_means = row_totals / row_counts
    new_qkv, col_qkv_new = finish_update(
        w_qkv, sum_qkv, row_qkv_new, col_qkv, col_qkv_total, width, row_means[:3][:, None, None], decay
    )
    new_out, col_out_new = finish_update(w_out, sum_out, row_out_new, col_out, col_out_total, width, row_means[3], decay)
    new_up, col_up_new = finish_update(w_up, sum_up, row_up_new, col_up, col_up_total, width, row_means[4], decay)
    new_down, col_down_new = finish_update(
        w_down, sum_down, row_down_new, col_down, col_down_total, ff, row_means[5], decay
    )
    new_proj, col_proj_new = finish_update(
        w_proj, sum_proj, row_proj_new, col_proj, col_proj_total, width, row_means[6], decay
    )
    gain_var_new = decay * gain_var + (1.0 - decay) * (sum_gains * sum_gains + TINY_SQUARE)
    new_gains = gains - GAIN_RATE * sum_gains * lax.rsqrt(gain_var_new)
    return (
        output_low[None], projected[None], input_grad[None],
        sum_qkv, sum_out, sum_up, sum_down, sum_proj, sum_gains,
        new_qkv, new_out, new_up, new_down, new_proj, new_gains,
        row_qkv_new, col_qkv_new, row_out_new, col_out_new, row_up_new, col_up_new,
        row_down_new, col_down_new, row_proj_new, col_proj_new, gain_var_new,
    )


def solution(mesh):
    in_specs = (
        P("item", "seq", None),
        P("item", None),
        P("item", "seq"),
        P("item", "seq"),
        P("item", "seq", None),
        P("item", "seq", None),
        P(None, ("seq", "item"), None),
        P(("seq", "item"), None),
        P(("seq", "item"), None),
        P(("seq", "item"), None),
        P(("seq", "item"), None),
        P(None, ("seq", "item")),
        P(None, ("seq", "item")),
        P(),
        P(("seq", "item")),
        P(),
        P(("seq", "item")),
        P(),
        P(("seq", "item")),
        P(),
        P(("seq", "item")),
        P(),
        P(None, ("seq", "item")),
    )
    out_specs = (
        P("item", "seq", None),
        P("item", "seq", None),
        P("item", "seq", None),
        P(None, ("seq", "item"), None),
        P(("seq", "item"), None),
        P(("seq", "item"), None),
        P(("seq", "item"), None),
        P(("seq", "item"), None),
        P(None, ("seq", "item")),
        P(None, ("seq", "item"), None),
        P(("seq", "item"), None),
        P(("seq", "item"), None),
        P(("seq", "item"), None),
        P(("seq", "item"), None),
        P(None, ("seq", "item")),
        P(None, ("seq", "item")),
        P(),
        P(("seq", "item")),
        P(),
        P(("seq", "item")),
        P(),
        P(("seq", "item")),
        P(),
        P(("seq", "item")),
        P(),
        P(None, ("seq", "item")),
    )
    return jax.shard_map(local, mesh=mesh, in_specs=in_specs, out_specs=out_specs, check_vma=False)
```

```python
import functools
import jax
import jax.numpy as jnp
from jax import lax
from jax.experimental import pallas as pl
from jax.experimental.pallas import tpu as pltpu
from jax.sharding import PartitionSpec as P

WINDOW = 1536
HEADS = 12
NEG = -1e30
EPSILON = 1e-06
TINY_SQUARE = 1e-30
WEIGHT_RATE = 0.02
GAIN_RATE = 0.2
STEP = 10
QB = 256
NT = (((1,), (1,)), ((), ()))
TN = (((0,), (0,)), ((), ()))
f32 = jnp.float32
bf = jnp.bfloat16


def dot(a, b, dims=None):
    if dims is None:
        return jnp.dot(a, b, preferred_element_type=f32)
    return lax.dot_general(a, b, dims, preferred_element_type=f32)


def halves(x):
    lane = lax.broadcasted_iota(jnp.int32, x.shape, 1)
    zero = jnp.zeros_like(x)
    return jnp.where(lane < 64, x, zero), jnp.where(lane < 64, zero, x)


def fwd_kernel(lo_ref, q_ref, k_ref, v_ref, o_ref, lse_ref, bias):
    hp, qb = pl.program_id(0), pl.program_id(1)
    span = WINDOW + QB

    @pl.when(hp == 0)
    def _():
        base = qb * QB
        kpos = base + lax.broadcasted_iota(jnp.int32, (QB, span), 1)
        qpos = WINDOW + base + lax.broadcasted_iota(jnp.int32, (QB, span), 0)
        ok = (kpos >= lo_ref[...]) & (kpos <= qpos)
        bias[qb] = jnp.where(ok, 0.0, NEG)

    start = pl.multiple_of(qb * QB, QB)
    kw = k_ref[pl.ds(start, span), :]
    vw = v_ref[pl.ds(start, span), :]
    outs, lses = [], []
    for qh in halves(q_ref[...]):
        s = dot(qh, kw, NT) + bias[qb]
        m = jnp.max(s, axis=1, keepdims=True)
        p = jnp.exp(s - m)
        l = jnp.sum(p, axis=1, keepdims=True)
        outs.append(dot(p.astype(bf), vw) * (1.0 / l))
        lses.append(m + jnp.log(l))
    lane = lax.broadcasted_iota(jnp.int32, (QB, 128), 1)
    o_ref[...] = jnp.where(lane < 64, outs[0], outs[1]).astype(bf)
    both = jnp.where(lane == 0, lses[0], lses[1])
    lse_ref[0] = both.T[:8]


def attend(q, k, v, lo):
    rows, width = q.shape
    ext = k.shape[0]
    nq, nh = rows // QB, width // 128
    return pl.pallas_call(
        fwd_kernel,
        grid=(nh, nq),
        in_specs=[
            pl.BlockSpec((QB, 1), lambda h, i: (i, 0)),
            pl.BlockSpec((QB, 128), lambda h, i: (i, h)),
            pl.BlockSpec((ext, 128), lambda h, i: (0, h)),
            pl.BlockSpec((ext, 128), lambda h, i: (0, h)),
        ],
        out_specs=[
            pl.BlockSpec((QB, 128), lambda h, i: (i, h)),
            pl.BlockSpec((1, 8, QB), lambda h, i: (h, 0, i)),
        ],
        out_shape=[
            jax.ShapeDtypeStruct((rows, width), bf),
            jax.ShapeDtypeStruct((nh, 8, rows), f32),
        ],
        scratch_shapes=[pltpu.VMEM((nq, QB, WINDOW + QB), f32)],
        compiler_params=pltpu.CompilerParams(vmem_limit_bytes=50 * 2**20),
        cost_estimate=pl.CostEstimate(flops=4 * rows * 1792 * 768 * 3, bytes_accessed=14 * 2**20, transcendentals=0),
        name="attend",
    )(lo, q, k, v)


AXES = ("seq", "item")
MESH = pl.DeviceIdType.MESH


def grid_of(seq, item):
    side = 1
    while side * side * 4 <= seq:
        side *= 2
    return (seq // side, side, item // 2)


def my_place(dims):
    seq, item = lax.axis_index("seq"), lax.axis_index("item")
    return (seq // dims[1], lax.rem(seq, dims[1]), item // 2, lax.rem(item, 2))


def device_at(dims, place):
    z, y, x, c = place
    return (z * dims[1] + y, x * 2 + c)


def moved(dims, place, dim, by):
    to = list(place)
    to[dim] = lax.rem(place[dim] + by, dims[dim])
    return tuple(to)


def sibling(place):
    return place[:3] + (1 - place[3],)


def peers(dims, place):
    found = [sibling(place)]
    for dim in range(3):
        found += [moved(dims, place, dim, by) for by in range(1, dims[dim])]
    return [device_at(dims, p) for p in found]


def meet(targets):
    barrier = pltpu.get_barrier_semaphore()
    for target in targets:
        pl.semaphore_signal(barrier, inc=1, device_id=target, device_id_type=MESH)
    pl.semaphore_wait(barrier, len(targets))


class Spread:
    def __init__(self, dims, place, own, out, rows, cols, order, send, recv):
        self.dims, self.place, self.own, self.out = dims, place, own, out
        self.rows, self.cols, self.order = rows, cols, order
        self.send, self.recv = send, recv

    def span(self, core):
        half = self.out.shape[-1] // 2
        return pl.ds(pl.multiple_of(core * half + self.cols[0], 128), self.cols[1])

    def region(self, stage, by=0, core=None):
        held = self.order[:stage]
        at = []
        for dim in range(3):
            if dim in held:
                at.append(slice(None))
            elif by and dim == self.order[stage]:
                at.append(lax.rem(self.place[dim] + self.dims[dim] - by, self.dims[dim]))
            else:
                at.append(self.place[dim])
        core = self.place[3] if core is None else core
        return self.out.at[tuple(at) + (self.rows, self.span(core))]

    def slots(self, stage):
        first = sum(self.dims[d] - 1 for d in self.order[:stage])
        return [(by, first + by - 1) for by in range(1, self.dims[self.order[stage]])]

    def hops(self, stage):
        for by, slot in self.slots(stage):
            block = self.region(stage)
            source = self.own.at[self.rows, self.span(self.place[3])] if stage == 0 else block
            target = device_at(self.dims, moved(self.dims, self.place, self.order[stage], by))
            yield pltpu.make_async_remote_copy(
                src_ref=source, dst_ref=block, send_sem=self.send.at[slot], recv_sem=self.recv.at[slot],
                device_id=target, device_id_type=MESH,
            )

    def shares(self, stage, core=None):
        count = sum(d - 1 for d in self.dims)
        for by, slot in self.slots(stage):
            block = self.region(stage, by, core)
            yield pltpu.make_async_remote_copy(
                src_ref=block, dst_ref=block, send_sem=self.send.at[count + slot], recv_sem=self.recv.at[count + slot],
                device_id=device_at(self.dims, sibling(self.place)), device_id_type=MESH,
            )

    def begin(self, stage):
        for copy in self.hops(stage):
            copy.start()

    def advance(self, stage, go_on=True):
        for copy in self.hops(stage):
            copy.wait_recv()
        if stage < 2 and go_on:
            self.begin(stage + 1)
        for copy in self.shares(stage):
            copy.start()

    def finish(self, stages=(0, 1, 2)):
        for stage in stages:
            for copy in self.hops(stage):
                copy.wait_send()
            for copy in self.shares(stage):
                copy.wait_send()
            for copy in self.shares(stage, 1 - self.place[3]):
                copy.wait_recv()


def keep_own(own, out, place, sem):
    return pltpu.make_async_copy(own, out.at[place[0], place[1], place[2]], sem)


def copies_of(dims):
    return 2 * sum(d - 1 for d in dims)


def halves_of(shape):
    rows, cols = shape
    half = cols // 2
    if half % 256 == 0:
        return [((0, rows), (0, half // 2)), ((0, rows), (half // 2, half // 2))]
    cut = rows // 32 * 16
    return [((at, count), (0, half)) for at, count in ((0, cut), (cut, rows - cut)) if count]


ORDERS = ((0, 1, 2), (0, 2, 1))


def pieces_of(dims, place, owns, outs, shapes, send, recv):
    made, at = [], 0
    for k, (own, out, shape) in enumerate(zip(owns, outs, shapes)):
        turn = k % 2
        pieces = []
        for order, (rows, cols) in zip(ORDERS[turn:] + ORDERS[:turn], halves_of(shape)):
            pieces.append(Spread(dims, place, own, out, pl.ds(*rows), cols, order, send.at[at], recv.at[at]))
            at += 1
        made.append(pieces)
    return made


def begin(pieces):
    for piece in pieces:
        piece.begin(0)


def advance(pieces, stage):
    for piece in pieces:
        piece.advance(stage)


def lower_bounds(lengths_ref, pos, offset):
    begin = jnp.zeros_like(pos)
    end = jnp.int32(0)
    for j in range(lengths_ref.shape[1]):
        end = end + lengths_ref[0, j]
        begin = jnp.where(end <= pos, end, begin)
    return jnp.maximum(begin, pos - (WINDOW - 1)) - offset + WINDOW


def norm_block(values, gain):
    x = values.astype(f32)
    return (x * lax.rsqrt(jnp.mean(x * x, axis=-1, keepdims=True) + EPSILON) * gain).astype(bf)


REST_EVENTS = {
    (0, 0, 0): ((2, 0),),
    (1, 0, 2): ((2, 1),),
    (1, 1, 2): ((3, 0),),
    (1, 3, 0): ((0, 0), (2, 2)),
    (1, 4, 2): ((3, 1), (0, 1)),
}


def front_kernel(dims, shapes, count, lengths_ref, x_ref, gains_ref, qkv_ref, out_ref_, proj_ref, up_ref, down_ref, *refs):
    names = iter(refs)
    take = lambda k: [next(names) for _ in range(k)]
    o_ref, lse_ref, q_out, k_out, v_out, n_out = take(6)
    w_outs = take(4)
    rest_outs = take(4)
    (flip_out,) = take(1)
    halo, staging, normed, q_scr, k_scr, v_scr, gain_scr, gain_own, bias, own_mixed, own_top, own_total, flipped = take(13)
    wide, blocks = take(8), take(8)
    first = take(4)
    swap_send, swap_recv, send, recv, keep_sem, halo_send, halo_recv, out_sem = take(8)

    place = my_place(dims)
    c = place[3]
    seq, item = lax.axis_index("seq"), lax.axis_index("item")
    rows, width = x_ref.shape
    hops = -(-WINDOW // rows)
    around = [(lax.rem(seq + d, count), item) for d in range(1, hops + 1)]
    behind = [(lax.rem(seq + count - d, count), item) for d in range(1, hops + 1)]
    with jax.named_scope("meet"):
        meet(peers(dims, place) + around + behind)

    mate = device_at(dims, sibling(place))
    shard = gains_ref.shape[1]
    gain_own[...] = jnp.zeros_like(gain_own)
    gain_own[0:2, 0:shard] = gains_ref[...]
    mine = seq * (dims[2] * 2) + item
    gain_own[...] = pltpu.roll(gain_own[...], mine * shard, 1)
    shards = [qkv_ref.at[0], qkv_ref.at[1], qkv_ref.at[2], gain_own, out_ref_, proj_ref, up_ref, down_ref]
    swaps = []
    for k in range(8):
        half = shapes[k][0] // 2
        part = wide[k].at[pl.ds(pl.multiple_of(c * half, 8), half)]
        part[...] = shards[k][...]
        swaps.append(
            pltpu.make_async_remote_copy(
                src_ref=shards[k], dst_ref=part, send_sem=swap_send.at[k], recv_sem=swap_recv.at[k],
                device_id=mate, device_id_type=MESH,
            )
        )
        swaps[k].start()
    outs = first + rest_outs
    keeps = [keep_own(blocks[k], outs[k], place, keep_sem.at[k]) for k in range(8)]
    pieces = pieces_of(dims, place, blocks, outs, shapes, send, recv)

    def ready(k):
        swaps[k].wait()
        blocks[k][...] = wide[k][...].astype(bf)
        keeps[k].start()

    odd = place[1] == 1
    lower, upper = WINDOW - rows, 2 * rows - WINDOW
    part = rows // 4

    def hop(send_slot, slot, source, target, device):
        return pltpu.make_async_remote_copy(
            src_ref=source, dst_ref=target, send_sem=halo_send.at[send_slot], recv_sem=halo_recv.at[slot],
            device_id=device, device_id_type=MESH,
        )

    cuts = [(0, 2 * part), (2 * part, part), (3 * part, part)]
    direct = [
        hop(n, n, x_ref.at[pl.ds(at, size)], halo.at[pl.ds(lower + at, size)], around[0])
        for n, (at, size) in enumerate(cuts)
    ]
    far = hop(3, 3, x_ref.at[pl.ds(upper, lower)], halo.at[pl.ds(0, lower)], around[1])
    aside = hop(4, 4, x_ref.at[pl.ds(0, 2 * part)], staging, behind[0])
    onward = hop(5, 0, staging, halo.at[pl.ds(lower, 2 * part)], around[1])
    has_next, has_far = seq + 1 < count, seq + 2 < count
    odd_next = jnp.logical_and(odd, has_next)
    even_next = jnp.logical_and(jnp.logical_not(odd), has_next)
    relays = jnp.logical_and(jnp.logical_not(odd), has_far)

    with jax.named_scope("swap"):
        for k in (3, 0, 1, 2):
            ready(k)
            begin(pieces[k])
        pl.when(odd_next)(aside.start)
        pl.when(even_next)(direct[2].start)
    with jax.named_scope("swap_rest"):
        for k in (4, 5, 6, 7):
            ready(k)
        for k in range(8):
            keeps[k].wait()
    with jax.named_scope("first_0"):
        for k in (3, 0, 1, 2):
            advance(pieces[k], 0)
        begin(pieces[6])
    with jax.named_scope("first_1"):
        for k in (3, 0, 1, 2):
            advance(pieces[k], 1)
        pl.when(has_far)(far.start)
        pl.when(has_next)(direct[1].start)
        pl.when(odd_next)(direct[2].start)
        pl.when(even_next)(direct[0].start)
    with jax.named_scope("relay"):

        @pl.when(relays)
        def _():
            aside.wait_recv()
            onward.start()

        for k in (7, 4, 5):
            begin(pieces[k])

    with jax.named_scope("first_2"):
        for k in (3, 0, 1, 2):
            advance(pieces[k], 2)
    with jax.named_scope("first_end"):
        for k in range(4):
            for piece in pieces[k]:
                piece.finish()
    total = first[3][...].astype(f32).reshape(dims[0] * dims[1] * dims[2] * 2, 8, width)
    gain_scr[...] = jnp.sum(total, axis=0)

    weights = [first[k] for k in range(3)]

    def project(slot, at):
        return dot(normed[at, :], weights[slot][...].reshape(width, width)).astype(bf)

    def own_rows(i, carry):
        at = pl.ds(pl.multiple_of(i * QB, QB), QB)
        ext = pl.ds(pl.multiple_of(WINDOW + i * QB, QB), QB)
        normed[ext, :] = norm_block(x_ref[at, :], gain_scr[0:1])
        q_scr[at, :] = project(0, ext) * jnp.asarray(0.125, bf)
        k_scr[ext, :] = project(1, ext)
        v_scr[ext, :] = project(2, ext)
        return carry

    def halo_rows(i, carry):
        at = pl.ds(pl.multiple_of(i * QB, QB), QB)
        pos = seq * rows - WINDOW + i * QB + lax.broadcasted_iota(jnp.int32, (QB, width), 0)
        block = jnp.where(pos >= 0, halo[at, :].astype(f32), 0.0)
        normed[at, :] = norm_block(block, gain_scr[0:1])
        k_scr[at, :] = project(1, at)
        v_scr[at, :] = project(2, at)
        return carry

    nq, pairs = rows // QB, width // 128

    def events(stage, hp, qb):
        for (part, pair, block), moves in REST_EVENTS.items():
            if (part, block) != (stage, qb):
                continue

            @pl.when(hp == pair)
            def _():
                for k, what in moves:
                    with jax.named_scope("rest_%d_%d" % (k, what + 1)):
                        advance(pieces[4 + k], what)

    lane = lax.broadcasted_iota(jnp.int32, (QB, 128), 1)

    def masks(qb):
        pos = seq * rows + qb * QB + lax.broadcasted_iota(jnp.int32, (QB, 1), 0)
        lo = lower_bounds(lengths_ref, pos, seq * rows)
        kpos = qb * QB + lax.broadcasted_iota(jnp.int32, (QB, WINDOW + QB), 1)
        qpos = WINDOW + qb * QB + lax.broadcasted_iota(jnp.int32, (QB, WINDOW + QB), 0)
        bias[qb] = jnp.where((kpos >= lo) & (kpos <= qpos), 0.0, NEG)

    low_half = lane < 64

    def both(pair):
        return jnp.where(low_half, pair[0], pair[1])

    def attend_to(at, keys, lanes, mask):
        kw, vw = k_scr[keys, lanes], v_scr[keys, lanes]
        tops, totals, found = [], [], []
        for qh in halves(q_scr[at, lanes]):
            s = dot(qh, kw, NT) + mask
            m = jnp.max(s, axis=1, keepdims=True)
            p = jnp.exp(s - m)
            tops.append(m)
            totals.append(jnp.sum(p, axis=1, keepdims=True))
            found.append(dot(p.astype(bf), vw))
        return both(tops), both(totals), both(found)

    def own_keys(hp, carry):
        lanes = pl.ds(pl.multiple_of(hp * 128, 128), 128)
        for qb in range(nq):
            events(0, hp, qb)
            at, keys = pl.ds(qb * QB, QB), pl.ds(WINDOW, (qb + 1) * QB)
            top, total, mixed = attend_to(at, keys, lanes, bias[qb, :, WINDOW - qb * QB :])
            own_top[hp, at, :] = top
            own_total[hp, at, :] = total
            own_mixed[at, lanes] = mixed
        return carry

    def halo_keys(hp, carry):
        lanes = pl.ds(pl.multiple_of(hp * 128, 128), 128)
        for qb in range(nq):
            events(1, hp, qb)
            at, keys = pl.ds(qb * QB, QB), pl.ds(qb * QB, WINDOW - qb * QB)
            top, total, mixed = attend_to(at, keys, lanes, bias[qb, :, : WINDOW - qb * QB])
            before = own_top[hp, at, :]
            highest = jnp.maximum(before, top)
            by_own, by_halo = jnp.exp(before - highest), jnp.exp(top - highest)
            total = own_total[hp, at, :] * by_own + total * by_halo
            mixed = own_mixed[at, lanes] * by_own + mixed * by_halo
            o_ref[at, lanes] = (mixed * (1.0 / total)).astype(bf)
            logs = (highest + jnp.log(total)).T
            lse_ref[hp, 0:1, at] = logs[0:1]
            lse_ref[hp, 1:2, at] = logs[64:65]
        return carry

    with jax.named_scope("own_rows"):
        lax.fori_loop(0, nq, own_rows, 0)
        for qb in range(nq):
            masks(qb)
    with jax.named_scope("own_keys"):
        lax.fori_loop(0, pairs, own_keys, 0)
    with jax.named_scope("wait_halo"):

        @pl.when(seq >= 1)
        def _():
            for copy in direct:
                copy.wait_recv()

        pl.when(seq >= 2)(far.wait_recv)
    with jax.named_scope("halo_rows"):
        lax.fori_loop(0, WINDOW // QB, halo_rows, 0)
    saved = [
        pltpu.make_async_copy(a, b, out_sem.at[n])
        for n, (a, b) in enumerate(
            zip([q_scr, k_scr, v_scr, normed] + first[:3] + [gain_scr], [q_out, k_out, v_out, n_out] + w_outs)
        )
    ]
    for copy in saved:
        copy.start()
    with jax.named_scope("halo_keys"):
        lax.fori_loop(0, pairs, halo_keys, 0)
    with jax.named_scope("flip_keys"):
        flipped[...] = k_scr[...].T
        saved.append(pltpu.make_async_copy(flipped, flip_out, out_sem.at[8]))
        saved[-1].start()
    with jax.named_scope("rest_end"):
        for piece in pieces[5]:
            piece.advance(0, False)
        for k in (7, 4):
            advance(pieces[k], 2)
        for k in range(4, 8):
            for piece in pieces[k]:
                piece.finish((0,) if k == 5 else (0, 1, 2))
        pl.when(has_far)(far.wait_send)
        pl.when(has_next)(direct[1].wait_send)
        pl.when(has_next)(direct[2].wait_send)
        pl.when(even_next)(direct[0].wait_send)
        pl.when(odd_next)(aside.wait_send)
        pl.when(relays)(onward.wait_send)
        for copy in saved:
            copy.wait()


def front(lengths, x, gains, w_qkv, others, dims, count):
    rows, width = x.shape
    shard = w_qkv.shape[1]
    ext = WINDOW + rows
    shapes = [(2 * shard, width)] * 3 + [(16, width)] + [(2 * w.shape[0], w.shape[1]) for w in others]
    copies = copies_of(dims)
    vmem = pl.BlockSpec(memory_space=pltpu.VMEM)
    hbm = pl.BlockSpec(memory_space=pl.ANY)
    dma = pltpu.SemaphoreType.DMA
    count_pieces = sum(len(halves_of(s)) for s in shapes)
    nh, nq = width // 128, rows // QB
    sds = jax.ShapeDtypeStruct
    got = pl.pallas_call(
        functools.partial(front_kernel, dims, shapes, count),
        in_specs=[pl.BlockSpec(memory_space=pltpu.SMEM)] + [vmem] * 7,
        out_specs=[vmem] * 2 + [hbm] * 13,
        out_shape=[
            sds((rows, width), bf), sds((nh, 8, rows), f32),
            sds((rows, width), bf), sds((ext, width), bf), sds((ext, width), bf), sds((ext, width), bf),
        ]
        + [sds(dims + shapes[0], bf)] * 3 + [sds((8, width), f32)]
        + [sds(dims + s, bf) for s in shapes[4:]] + [sds((width, ext), bf)],
        scratch_shapes=[
            pltpu.VMEM((WINDOW, width), bf), pltpu.VMEM((rows // 2, width), bf), pltpu.VMEM((ext, width), bf),
            pltpu.VMEM((rows, width), bf),
            pltpu.VMEM((ext, width), bf), pltpu.VMEM((ext, width), bf), pltpu.VMEM((8, width), f32),
            pltpu.VMEM((8, width), f32), pltpu.VMEM((nq, QB, WINDOW + QB), f32),
            pltpu.VMEM((rows, width), f32), pltpu.VMEM((nh, rows, 128), f32), pltpu.VMEM((nh, rows, 128), f32),
            pltpu.VMEM((width, ext), bf),
        ]
        + [pltpu.VMEM(s, f32) for s in shapes]
        + [pltpu.VMEM(s, bf) for s in shapes]
        + [pltpu.VMEM(dims + s, bf) for s in shapes[:4]]
        + [
            dma((8,)), dma((8,)), dma((count_pieces, copies)), dma((count_pieces, copies)), dma((8,)),
            dma((6,)), dma((5,)), dma((9,)),
        ],
        compiler_params=pltpu.CompilerParams(
            collective_id=1, has_side_effects=True, vmem_limit_bytes=63 * 2**20
        ),
        cost_estimate=pl.CostEstimate(flops=4 * rows * 1792 * 768 * 3, bytes_accessed=14 * 2**20, transcendentals=0),
        name="front",
    )(lengths, x, gains, w_qkv, *others)
    return got


def piece_cuts(shape):
    return [(pl.ds(*rows), pl.ds(*cols)) for rows, cols in halves_of(shape)]


class Collapse:
    def __init__(self, dims, place, shape, turn, grad, out, buffers, send, recv):
        self.dims, self.place, self.shape = dims, place, shape
        self.grad, self.out, self.send, self.recv = grad, out, send, recv
        self.acc, self.box0, self.box1, self.box2, self.box3, self.fin, self.box4 = buffers
        z, y, x, c = place
        far_x, far_y = device_at(dims, (z, y, 1 - x, c)), device_at(dims, (z, 1 - y, x, c))
        every = slice(None)
        by_x = [(far_x, (every, every, 1 - x), (every, every, x)), (far_y, (every, 1 - y, x), (every, y, x))]
        by_y = [(far_y, (every, 1 - y, every), (every, y, every)), (far_x, (every, y, 1 - x), (every, y, x))]
        ways = [by_x, by_y] if turn == 0 else [by_y, by_x]
        self.pieces = list(zip(piece_cuts(shape), ways))

    def columns(self, core):
        half = self.shape[1] // 2
        return pl.ds(pl.multiple_of(core * half, 128), half)

    def copy(self, slot, source, target, device):
        return pltpu.make_async_remote_copy(
            src_ref=source, dst_ref=target, send_sem=self.send.at[slot], recv_sem=self.recv.at[slot],
            device_id=device, device_id_type=MESH,
        )

    def copies(self, stage):
        z, y, x, c = self.place
        mate = device_at(self.dims, sibling(self.place))
        every = slice(None)
        if stage == 0:
            source = self.grad.at[every, every, every, every, self.columns(1 - c)]
            return [self.copy(0, source, self.box0, mate)]
        if stage == 4:
            half = self.shape[0] // 2
            source = self.fin.at[pl.ds(pl.multiple_of((1 - c) * half, 8), half)]
            return [self.copy(1, source, self.box4, mate)]
        made = []
        for at, (cut, ways) in enumerate(self.pieces):
            first = 2 + at * (2 + self.dims[0] - 1)
            if stage in (1, 2):
                device, give, _ = ways[stage - 1]
                box = (self.box1 if stage == 1 else self.box2).at[(every,) * (3 - stage) + cut]
                made.append(self.copy(first + stage - 1, self.acc.at[give + cut], box, device))
            else:
                for by in range(1, self.dims[0]):
                    to = lax.rem(z + by, self.dims[0])
                    made.append(
                        self.copy(
                            first + 1 + by, self.acc.at[(to, y, x) + cut], self.box3.at[(by - 1,) + cut],
                            device_at(self.dims, (to, y, x, c)),
                        )
                    )
        return made

    def local(self, sem):
        if self.grad.shape == self.acc.shape:
            return pltpu.make_async_copy(self.grad, self.acc, sem)
        every = slice(None)
        source = self.grad.at[every, every, every, every, self.columns(self.place[3])]
        return pltpu.make_async_copy(source, self.acc, sem)

    def start(self, stage):
        for copy in self.copies(stage):
            copy.start()

    def add(self, stage):
        for copy in self.copies(stage):
            copy.wait_recv()
        z, y, x, c = self.place
        dims = self.dims
        if stage == 0:

            def body(i, carry):
                a, b, d = i // (dims[1] * dims[2]), lax.rem(i // dims[2], dims[1]), lax.rem(i, dims[2])
                self.acc[a, b, d] = self.acc[a, b, d] + self.box0[a, b, d]
                return carry

            lax.fori_loop(0, dims[0] * dims[1] * dims[2], body, 0)
        elif stage == 1:
            for cut, ways in self.pieces:
                by_x = not isinstance(ways[0][2][2], slice)

                def body(i, carry):
                    a, b = i // 2, lax.rem(i, 2)
                    at = ((a, b, x) if by_x else (a, y, b)) + cut
                    self.acc[at] = self.acc[at] + self.box1[(a, b) + cut]
                    return carry

                lax.fori_loop(0, dims[0] * 2, body, 0)
        elif stage == 2:

            def body(a, carry):
                self.acc[a, y, x] = self.acc[a, y, x] + self.box2[a]
                return carry

            lax.fori_loop(0, dims[0], body, 0)
        elif stage == 3:
            total = self.acc[z, y, x].astype(f32)
            for by in range(1, dims[0]):
                total = total + self.box3[by - 1].astype(f32)
            self.fin[...] = total
        else:
            half = self.shape[0] // 2
            mine = self.fin[pl.ds(pl.multiple_of(c * half, 8), half)]
            other = self.box4[...]
            width = self.shape[1] // 2
            self.out[:, :width] = jnp.where(c == 0, mine, other)
            self.out[:, width:] = jnp.where(c == 0, other, mine)

    def finish(self, stages=(0, 1, 2, 3, 4)):
        for stage in stages:
            for copy in self.copies(stage):
                copy.wait_send()


class EarlyCollapse(Collapse):
    def trade(self, given, send, recv):
        mate = device_at(self.dims, sibling(self.place))
        self.swaps = [
            pltpu.make_async_remote_copy(
                src_ref=given.at[j], dst_ref=self.box0.at[j], send_sem=send.at[j], recv_sem=recv.at[j],
                device_id=mate, device_id_type=MESH,
            )
            for j in range(self.dims[0])
        ]

    def copies(self, stage):
        return self.swaps if stage == 0 else super().copies(stage)


def collapse_scratch(dims, shapes, resumed=()):
    found = []
    for k, (rows, cols) in enumerate(shapes):
        half = cols // 2
        first = (16, 128) if k in resumed else None
        found += [
            pltpu.VMEM(dims + (rows, half), bf),
            pltpu.VMEM(first or dims + (rows, half), bf),
            pltpu.VMEM(first or (dims[0], 2, rows, half), bf),
            pltpu.VMEM((dims[0], rows, half), bf),
            pltpu.VMEM((dims[0] - 1, rows, half), bf),
            pltpu.VMEM((rows, half), f32),
            pltpu.VMEM((rows // 2, half), f32),
        ]
    dma = pltpu.SemaphoreType.DMA
    n = len(shapes)
    slots = 2 + 2 * (2 + dims[0] - 1)
    return found + [dma((n, slots)), dma((n, slots)), dma((n,))]


def collapses_of(dims, place, shapes, grads, outs, scratch):
    n = len(shapes)
    send, recv, local_sem = scratch[7 * n :]
    made = [
        Collapse(dims, place, shapes[k], k % 2, grads[k], outs[k], scratch[7 * k : 7 * k + 7], send.at[k], recv.at[k])
        for k in range(n)
    ]
    return made, [made[k].local(local_sem.at[k]) for k in range(n)]


def run_collapse(sums, locals_, k, stage):
    if stage < 0:
        locals_[k].start()
        sums[k].start(0)
        return
    if stage == 0:
        locals_[k].wait()
    sums[k].add(stage)
    if stage < 4:
        sums[k].start(stage + 1)


def back_kernel(lo_ref, q_ref, do_ref, o_ref, lse_ref, k_ref, v_ref, dq_ref, dk_ref, dv_ref, bias, dk_acc, dv_acc):
    hp, qb = pl.program_id(0), pl.program_id(1)
    span = WINDOW + QB
    start = pl.multiple_of(qb * QB, QB)

    @pl.when(hp == 0)
    def _():
        base = qb * QB
        kpos = base + lax.broadcasted_iota(jnp.int32, (span, QB), 0)
        qpos = WINDOW + base + lax.broadcasted_iota(jnp.int32, (span, QB), 1)
        ok = (kpos >= lo_ref[...]) & (kpos <= qpos)
        bias[qb] = jnp.where(ok, 0.0, NEG)

    @pl.when(qb == 0)
    def _():
        dk_acc[...] = jnp.zeros_like(dk_acc)
        dv_acc[...] = jnp.zeros_like(dv_acc)

    q_heads = halves(q_ref[...])
    do = do_ref[...]
    d_heads = halves(do)
    prod = do.astype(f32) * o_ref[...].astype(f32)
    row = lax.broadcasted_iota(jnp.int32, (8, 128), 0)
    lane = lax.broadcasted_iota(jnp.int32, (8, 128), 1)
    pick = jnp.where(row == lane // 64, 1.0, 0.0).astype(f32)
    delta = lax.dot_general(pick, prod, NT, precision=lax.Precision.HIGHEST, preferred_element_type=f32)
    lse = lse_ref[0]
    at = pl.ds(start, span)
    kw, vw = k_ref[at, :], v_ref[at, :]
    low_p, low_s, dq = [], [], []
    for h in range(2):
        s = dot(kw, q_heads[h], NT) + bias[qb]
        p = jnp.exp(s - lse[h : h + 1])
        dp = dot(vw, d_heads[h], NT)
        ds = (p * (dp - delta[h : h + 1])).astype(bf)
        low_p.append(p.astype(bf))
        low_s.append(ds)
        dq.append(dot(ds, kw, TN))
    dv_acc[at, :] += dot(jnp.concatenate(low_p, axis=1), jnp.concatenate(d_heads, axis=0))
    dk_acc[at, :] += dot(jnp.concatenate(low_s, axis=1), jnp.concatenate(q_heads, axis=0))
    lane = lax.broadcasted_iota(jnp.int32, (QB, 128), 1)
    dq_ref[...] = (jnp.where(lane < 64, dq[0], dq[1]) * 0.125).astype(bf)

    @pl.when(qb == pl.num_programs(1) - 1)
    def _():
        dk_ref[...] = dk_acc[...].astype(bf)
        dv_ref[...] = dv_acc[...].astype(bf)


def attend_back(q, do, o, lse, k, v, lo_row):
    rows, width = q.shape
    ext = k.shape[0]
    nq, nh = rows // QB, width // 128
    blk = pl.BlockSpec((QB, 128), lambda h, i: (i, h))
    full = pl.BlockSpec((ext, 128), lambda h, i: (0, h))
    return pl.pallas_call(
        back_kernel,
        grid=(nh, nq),
        in_specs=[pl.BlockSpec((1, QB), lambda h, i: (0, i)), blk, blk, blk]
        + [pl.BlockSpec((1, 8, QB), lambda h, i: (h, 0, i)), full, full],
        out_specs=[blk, full, full],
        out_shape=[
            jax.ShapeDtypeStruct((rows, width), bf),
            jax.ShapeDtypeStruct((ext, width), bf),
            jax.ShapeDtypeStruct((ext, width), bf),
        ],
        scratch_shapes=[
            pltpu.VMEM((nq, WINDOW + QB, QB), f32),
            pltpu.VMEM((ext, 128), f32),
            pltpu.VMEM((ext, 128), f32),
        ],
        compiler_params=pltpu.CompilerParams(vmem_limit_bytes=56 * 2**20),
        name="attend_back",
    )(lo_row, q, do, o, lse, k, v)


SUM_EVENTS = {
    (0, 1): ((2, 2), (1, 0), (0, 0)),
    (0, 3): ((1, 1), (2, 3)),
    (0, 4): ((0, 1), (1, 2), (2, 4)),
    (0, 5): ((0, 2),),
    (1, 2): ((1, 4), (0, 4)),
}


def back_kernel_paired(dims, shapes, count, lengths_ref, lse_ref, delta_ref, *refs):
    n = len(shapes)
    names = iter(refs)
    take = lambda k: [next(names) for _ in range(k)]
    sources = take(7)
    grads = take(n)
    dq_out, dk_out, dv_out, near_out, rest_out = take(5)
    sums_out = take(n)
    q, do, k, v, flipped, wk, wv = buffers = take(7)
    dk, dv, dq_acc, dk_acc, dv_acc, bias = take(6)
    load_sem, out_sem, back_send, back_recv = take(4)
    scratch = list(names)

    place = my_place(dims)
    seq, item = lax.axis_index("seq"), lax.axis_index("item")
    rows, width = q.shape
    nq, pairs = rows // QB, width // 128
    loads = [pltpu.make_async_copy(a, b, load_sem.at[m]) for m, (a, b) in enumerate(zip(sources, buffers))]
    for load in loads:
        load.start()
    ahead, behind = (lax.rem(seq + 1, count), item), (lax.rem(seq + count - 1, count), item)
    with jax.named_scope("masks"):
        for qb in range(nq):
            pos = seq * rows + qb * QB + lax.broadcasted_iota(jnp.int32, (1, QB), 1)
            lo = lower_bounds(lengths_ref, pos, seq * rows)
            kpos = qb * QB + lax.broadcasted_iota(jnp.int32, (WINDOW + QB, QB), 0)
            qpos = WINDOW + qb * QB + lax.broadcasted_iota(jnp.int32, (WINDOW + QB, QB), 1)
            bias[qb] = jnp.where((kpos >= lo) & (kpos <= qpos), 0.0, NEG).astype(bf)
    with jax.named_scope("meet"):
        meet(peers(dims, place) + [ahead, behind])
    sums, locals_ = collapses_of(dims, place, shapes, grads, sums_out, scratch)
    locals_[2].start()

    with jax.named_scope("load"):
        locals_[2].wait()
        sums[2].start(2)
        for load in loads[:5]:
            load.wait()
        for a in (1, 0):
            run_collapse(sums, locals_, a, -1)

    def events(part, hp):
        for (when, pair), moves in SUM_EVENTS.items():
            if when != part:
                continue

            @pl.when(hp == pair)
            def _():
                for a, stage in moves:
                    with jax.named_scope("reduce_%d_%d" % (a, stage + 1)):
                        run_collapse(sums, locals_, a, stage)

    half = lax.broadcasted_iota(jnp.int32, (128, QB), 0)

    def block(hp, lanes, at, keys, mask):
        q_heads, d_heads = halves(q[at, lanes]), halves(do[at, lanes])
        lse, delta = lse_ref[hp, :, at], delta_ref[hp, :, at]
        kw, vw = k[keys, lanes], v[keys, lanes]
        low_p, low_s, found = [], [], []
        for h in range(2):
            s = dot(kw, q_heads[h], NT) + mask.astype(f32)
            p = jnp.exp(s - lse[h : h + 1])
            dp = dot(vw, d_heads[h], NT)
            ds = (p * (dp - delta[h : h + 1])).astype(bf)
            low_p.append(p.astype(bf))
            low_s.append(ds)
            found.append(dot(flipped[lanes, keys], ds))
        dv_part = dot(jnp.concatenate(low_p, axis=1), jnp.concatenate(d_heads, axis=0))
        dk_part = dot(jnp.concatenate(low_s, axis=1), jnp.concatenate(q_heads, axis=0))
        return jnp.where(half < 64, found[0], found[1]).T, dk_part, dv_part

    early = nq // 2
    reach = early * QB

    def halo_keys(hp, carry):
        events(0, hp)
        lanes = pl.ds(pl.multiple_of(hp * 128, 128), 128)
        for qb in range(nq):
            at, size = pl.ds(qb * QB, QB), WINDOW + QB if qb < early else WINDOW - qb * QB
            keys = pl.ds(qb * QB, size)
            dq_part, dk_part, dv_part = block(hp, lanes, at, keys, bias[qb, :size, :])
            if qb < early:
                q[at, lanes] = (dq_part * 0.125).astype(bf)
            else:
                dq_acc[pl.ds(qb * QB - reach, QB), lanes] = dq_part
            for total, part in ((dk_acc, dk_part), (dv_acc, dv_part)):
                if qb == 0:
                    total[keys, :] = part
                    total[size:, :] = jnp.zeros((total.shape[0] - size, 128), f32)
                else:
                    total[keys, :] += part
        dk[0 : WINDOW + reach, lanes] = dk_acc[...].astype(bf)
        dv[0 : WINDOW + reach, lanes] = dv_acc[...].astype(bf)
        return carry

    with jax.named_scope("halo_keys"):
        lax.fori_loop(0, pairs, halo_keys, 0)

    def halo_rows(i, carry):
        at = pl.ds(pl.multiple_of(i * QB, QB), QB)
        total = dot(dk[at, :], wk[...].reshape(width, width), NT) + dot(dv[at, :], wv[...].reshape(width, width), NT)
        k[at, :] = total.astype(bf)
        return carry

    lower, part = WINDOW - rows, rows // 4
    returned = [
        pltpu.make_async_remote_copy(
            src_ref=k.at[pl.ds(lower + m * part, part)], dst_ref=near_out.at[pl.ds(m * part, part)],
            send_sem=back_send.at[m], recv_sem=back_recv.at[m], device_id=behind, device_id_type=MESH,
        )
        for m in range(3)
    ]
    with jax.named_scope("halo_rows"):
        for load in loads[5:]:
            load.wait()
        for m in range(3):
            lax.fori_loop((lower + m * part) // QB, (lower + (m + 1) * part) // QB, halo_rows, 0)
            pl.when(seq >= 1)(returned[m].start)
        lax.fori_loop(0, lower // QB, halo_rows, 0)
        lax.fori_loop((lower + 3 * part) // QB, WINDOW // QB, halo_rows, 0)
        rest = [
            pltpu.make_async_copy(k.at[pl.ds(0, lower)], rest_out.at[pl.ds(0, lower)], out_sem.at[0]),
            pltpu.make_async_copy(k.at[pl.ds(lower + 3 * part, part)], rest_out.at[pl.ds(lower, part)], out_sem.at[1]),
        ]
        rest += [
            pltpu.make_async_copy(a.at[pl.ds(0, WINDOW)], b.at[pl.ds(0, WINDOW)], out_sem.at[2 + m])
            for m, (a, b) in enumerate([(dk, dk_out), (dv, dv_out)])
        ]
        for copy in rest:
            copy.start()
    for a in (1, 0):
        with jax.named_scope("reduce_%d_4" % a):
            run_collapse(sums, locals_, a, 3)

    def own_keys(hp, carry):
        events(1, hp)
        lanes = pl.ds(pl.multiple_of(hp * 128, 128), 128)
        for qb in reversed(range(early, nq)):
            at, size = pl.ds(qb * QB, QB), (qb + 1) * QB
            keys, own = pl.ds(WINDOW, size), pl.ds(0, size)
            dq_part, dk_part, dv_part = block(hp, lanes, at, keys, bias[qb, WINDOW - qb * QB :, :])
            q[at, lanes] = ((dq_acc[pl.ds(qb * QB - reach, QB), lanes] + dq_part) * 0.125).astype(bf)
            if qb == nq - 1:
                dk_acc[own, :] = dk_part
                dv_acc[own, :] = dv_part
            else:
                dk_acc[own, :] += dk_part
                dv_acc[own, :] += dv_part
        for total, kept in ((dk_acc, dk), (dv_acc, dv)):
            first, second = pl.ds(WINDOW, reach), pl.ds(WINDOW + reach, rows - reach)
            kept[first, lanes] = (total[0:reach, :] + kept[first, lanes].astype(f32)).astype(bf)
            kept[second, lanes] = total[reach:rows, :].astype(bf)
        return carry

    with jax.named_scope("own_keys"):
        lax.fori_loop(0, pairs, own_keys, 0)
    own = pl.ds(WINDOW, rows)
    stores = rest + [
        pltpu.make_async_copy(a, b, out_sem.at[4 + m])
        for m, (a, b) in enumerate([(q, dq_out), (dk.at[own], dk_out.at[own]), (dv.at[own], dv_out.at[own])])
    ]
    for store in stores[4:]:
        store.start()
    with jax.named_scope("finish"):
        for one in sums[:2]:
            one.finish()
        sums[2].finish((2, 3, 4))
        for store in stores:
            store.wait()

        for copy in returned:
            pl.when(seq >= 1)(copy.wait_send)
            pl.when(seq + 1 < count)(copy.wait_recv)


def back(lengths, lse, delta, arrays, grads, dims, count):
    q, do, k, v, flipped, wk, wv = arrays
    rows, width = q.shape
    ext = k.shape[0]
    nq = rows // QB
    shapes = [g.shape[3:] for g in grads]
    shapes[2] = (shapes[2][0], 2 * shapes[2][1])
    vmem = pl.BlockSpec(memory_space=pltpu.VMEM)
    hbm = pl.BlockSpec(memory_space=pl.ANY)
    dma = pltpu.SemaphoreType.DMA
    sds = jax.ShapeDtypeStruct
    part = rows // 4
    got = pl.pallas_call(
        functools.partial(back_kernel_paired, dims, shapes, count),
        in_specs=[pl.BlockSpec(memory_space=pltpu.SMEM), vmem, vmem] + [hbm] * (7 + len(grads)),
        out_specs=[hbm] * 5 + [vmem] * len(grads),
        out_shape=[
            sds((rows, width), bf), sds((ext, width), bf), sds((ext, width), bf),
            sds((3 * part, width), bf), sds((WINDOW - 3 * part, width), bf),
        ]
        + [sds((r // 2, c), f32) for r, c in shapes],
        scratch_shapes=[pltpu.VMEM(a.shape, bf) for a in arrays]
        + [
            pltpu.VMEM((ext, width), bf), pltpu.VMEM((ext, width), bf), pltpu.VMEM((rows // 2, width), f32),
            pltpu.VMEM((WINDOW + rows // 2, 128), f32), pltpu.VMEM((WINDOW + rows // 2, 128), f32),
            pltpu.VMEM((nq, WINDOW + QB, QB), bf),
            dma((7,)), dma((7,)), dma((3,)), dma((3,)),
        ]
        + collapse_scratch(dims, shapes, (2,)),
        compiler_params=pltpu.CompilerParams(
            collective_id=3, has_side_effects=True, vmem_limit_bytes=63 * 2**20
        ),
        name="back",
    )(lengths, lse, delta, *arrays, *grads)
    return got[:5], got[5:]


GELU_A, GELU_B = 0.7978845608028654, 0.044715
MB = 512
PROJ_STEPS = (0, 1)
GATHER_STEP = 0
DOWN_STEP = 1


def middle_kernel(dims, proj_shape, wd_shape, bound_ref, cont_ref, gain_ref, *refs):
    names = iter(refs)
    take = lambda k: [next(names) for _ in range(k)]
    sources = take(8)
    y_out, p_out, dr_out, do_out, gain_out, delta_out, sum_proj, g_out, g_up, down_out = take(10)
    x, o, cot, pcot, wo, wu, wd, wp = buffers = take(8)
    n2, r1, act, slope, low_c, dyl, stage, grad_proj = take(8)
    load_sem, stage_sem, out_sem, send, recv = take(5)
    down_given, down_send, down_recv, trade_send, trade_recv, proj_send, proj_recv = take(7)
    down_buffers = take(3)
    scratch = list(names)

    place = my_place(dims)
    z, y, x_, c = place
    line = (slice(None), y, x_)
    pairs = list(zip(sources[:7], buffers[:7])) + [(sources[7].at[line], wp.at[line])]
    loads = [pltpu.make_async_copy(a, b, load_sem.at[k]) for k, (a, b) in enumerate(pairs)]
    for k in (0, 1, 4, 7, 5, 6, 3, 2):
        loads[k].start()
    with jax.named_scope("meet"):
        meet(peers(dims, place))
    total = EarlyCollapse(dims, place, proj_shape, 0, None, sum_proj, scratch[:7], scratch[7].at[0], scratch[8].at[0])
    total.trade(grad_proj, proj_send, proj_recv)

    def move_on(stage):
        total.add(stage)
        if stage < 4:
            total.start(stage + 1)


    down = EarlyCollapse(
        dims, place, wd_shape, 0, None, None, down_buffers + [None] * 4, down_send, down_recv
    )
    down.trade(down_given, trade_send, trade_recv)

    rows, width = x.shape
    chunks = wu.shape[1] // width
    gain = gain_ref[1:2]
    pieces = [
        Spread(dims, place, None, wp, pl.ds(*at), cols, order, send.at[k], recv.at[k])
        for k, (order, (at, cols)) in enumerate(zip(ORDERS, halves_of(wp.shape[3:])))
    ]
    def residual(i, carry):
        at = pl.ds(pl.multiple_of(i * MB, MB), MB)
        r = x[at, :].astype(f32) + dot(o[at, :], wo[...])
        r1[at, :] = r
        scale = lax.rsqrt(jnp.mean(r * r, axis=-1, keepdims=True) + EPSILON)
        n2[at, :] = (r * scale * gain).astype(bf)
        return carry

    with jax.named_scope("load"):
        loads[7].wait()
        for piece in pieces:
            piece.begin(1)
        for k in (0, 1, 4):
            loads[k].wait()
        lax.fori_loop(0, rows // MB, residual, 0)
        for k in (2, 3, 5, 6):
            loads[k].wait()

    def edge_of(at):
        edge = (bound_ref[:, at] * (1 - cont_ref[:, at])).astype(f32)
        return jnp.broadcast_to(edge, (8, MB)).T[:, 0:1]

    def forward(i, carry):
        at = pl.ds(pl.multiple_of(i * MB, MB), MB)
        y = r1[at, :]
        for j in range(chunks):
            cols = slice(j * width, (j + 1) * width)
            u = dot(n2[at, :], wu[:, cols])
            square = u * u
            t = jnp.tanh(GELU_A * (u + GELU_B * square * u))
            half = 0.5 * (1.0 + t)
            act[at, cols] = (u * half).astype(bf)
            slope[at, cols] = (half + 0.5 * u * (1.0 - t * t) * (GELU_A + 3.0 * GELU_A * GELU_B * square)).astype(bf)
            y = y + dot(act[at, cols], wd[cols, :])
        low_c[at, :] = (edge_of(at) * pcot[at, :].astype(f32)).astype(bf)
        dr_out[at, :] = cot[at, :].astype(f32)
        cot[at, :] = y.astype(bf)

        @pl.when(i == GATHER_STEP)
        def _():
            with jax.named_scope("proj_1"):
                for piece in pieces:
                    piece.advance(1)

        return carry

    def project(i, carry):
        at = pl.ds(pl.multiple_of(i * MB, MB), MB)
        weight = wp[...].reshape(width, wp.shape[-1])
        d = dr_out[at, :] + dot(low_c[at, :], weight, NT)
        dr_out[at, :] = d
        dyl[at, :] = d.astype(bf)
        pcot[at, :] = (edge_of(at) * dot(cot[at, :], weight)).astype(bf)
        return carry

    with jax.named_scope("forward"):
        lax.fori_loop(0, rows // MB, forward, 0)
    with jax.named_scope("proj_2"):
        for piece in pieces:
            piece.advance(2)
        for piece in pieces:
            piece.finish((1, 2))
    with jax.named_scope("project"):
        lax.fori_loop(0, rows // MB, project, 0)
    stores = [pltpu.make_async_copy(cot, y_out, out_sem.at[0]), pltpu.make_async_copy(pcot, p_out, out_sem.at[1])]
    for store in stores:
        store.start()

    flying = {}

    def emit(target, left, right):
        block = width // 2
        for j in range(left.shape[1] // block):
            for k in range(right.shape[1] // width):
                slot = emit.count % 2
                emit.count += 1
                if slot in flying:
                    flying[slot].wait()
                rows_at, cols_at = slice(j * block, (j + 1) * block), slice(k * width, (k + 1) * width)
                stage[slot] = dot(left[:, rows_at], right[:, cols_at], TN).astype(bf)
                copy = pltpu.make_async_copy(
                    stage.at[slot], target.at[pl.ds(j * block, block), pl.ds(k * width, width)], stage_sem.at[slot]
                )
                copy.start()
                flying[slot] = copy

    emit.count = 0
    with jax.named_scope("grad_proj"):
        half = proj_shape[1] // 2
        for target, core in ((grad_proj, 1 - c), (scratch[0], c)):
            cols = pl.ds(pl.multiple_of(core * half, 128), half)
            target[...] = dot(cot[...], low_c[:, cols], TN).astype(bf).reshape(target.shape)
            if target is grad_proj:
                total.start(0)
    with jax.named_scope("grad_down"):
        acc, half = down_buffers[0], width // 2
        for j in range(chunks):
            got = dot(act[:, j * width : (j + 1) * width], dyl[...], TN).astype(bf)
            left, right = got[:, :half], got[:, half:]
            acc[j] = jnp.where(c == 0, left, right).reshape(acc.shape[1:])
            down_given[j] = jnp.where(c == 0, right, left).reshape(acc.shape[1:])
            down.swaps[j].start()

    row = lax.broadcasted_iota(jnp.int32, (16, width), 0)
    lane = lax.broadcasted_iota(jnp.int32, (16, width), 1)
    heads = jnp.where(row == lane // 64, 1.0, 0.0).astype(f32)

    def backward(i, carry):
        for step, when in enumerate(PROJ_STEPS):

            @pl.when(i == when)
            def _():
                with jax.named_scope("reduce_%d" % step):
                    move_on(step)
        @pl.when(i == DOWN_STEP)
        def _():
            with jax.named_scope("down_0"):
                down.add(0)
                down.start(1)

        at = pl.ds(pl.multiple_of(i * MB, MB), MB)
        dn = jnp.zeros((MB, width), f32)
        for j in range(chunks):
            cols = slice(j * width, (j + 1) * width)
            du = (dot(dyl[at, :], wd[cols, :], NT) * slope[at, cols].astype(f32)).astype(bf)
            slope[at, cols] = du
            dn = dn + dot(du, wu[:, cols], NT)
        r = r1[at, :]
        scale = lax.rsqrt(jnp.mean(r * r, axis=-1, keepdims=True) + EPSILON)
        unit = r * scale
        by_gain = dn * gain
        inner = jnp.mean(by_gain * unit, axis=-1, keepdims=True)
        dr = dr_out[at, :] + scale * (by_gain - unit * inner)
        dr_out[at, :] = dr
        low_dr = dr.astype(bf)
        dyl[at, :] = low_dr
        low_do = dot(low_dr, wo[...], NT).astype(bf)
        x[at, :] = low_do
        delta = lax.dot_general(
            heads, low_do.astype(f32) * o[at, :].astype(f32), NT,
            precision=lax.Precision.HIGHEST, preferred_element_type=f32,
        )
        for hp in range(width // 128):
            delta_out[hp, 0:2, at] = delta[2 * hp : 2 * hp + 2]
        return carry + jnp.sum(dn * unit, axis=0, keepdims=True)

    with jax.named_scope("backward"):
        gain_out[...] = lax.fori_loop(0, rows // MB, backward, jnp.zeros((1, width), f32))
    stores.append(pltpu.make_async_copy(x, do_out, out_sem.at[2]))
    stores[-1].start()
    with jax.named_scope("grad_out"):
        move_on(2)
        emit(g_out, o, dyl)
    with jax.named_scope("grad_up"):
        emit(g_up, n2, slope)
    with jax.named_scope("down_1"):
        down.add(1)
        stores.append(pltpu.make_async_copy(down_buffers[0], down_out, out_sem.at[3]))
        stores[-1].start()
    with jax.named_scope("finish"):
        for stage in (3, 4):
            move_on(stage)
        for copy in list(flying.values()) + stores:
            copy.wait()
        total.finish()
        down.finish((0, 1))


def middle(bound, cont, gain, arrays, dims):
    x, o, cot, pcot, wo, wu, wd, wp = arrays
    rows, width = x.shape
    ff, proj = wu.shape[1], wp.shape[-1]
    copies = copies_of(dims)
    pair = width // (dims[0] * dims[1] * dims[2])
    tall = ff // (dims[0] * dims[1] * dims[2])
    down_acc = dims + (tall, width // 2)
    vmem = pl.BlockSpec(memory_space=pltpu.VMEM)
    hbm = pl.BlockSpec(memory_space=pl.ANY)
    dma = pltpu.SemaphoreType.DMA
    sds = jax.ShapeDtypeStruct
    return pl.pallas_call(
        functools.partial(middle_kernel, dims, (pair, proj), (tall, width)),
        in_specs=[vmem] * 3 + [hbm] * 8,
        out_specs=[hbm, hbm, vmem, hbm, vmem, vmem, vmem, hbm, hbm, hbm],
        out_shape=[
            sds((rows, width), bf), sds((rows, proj), bf), sds((rows, width), f32), sds((rows, width), bf),
            sds((1, width), f32), sds((width // 128, 8, rows), f32), sds((pair // 2, proj), f32),
            sds(wo.shape, bf), sds(wu.shape, bf), sds(down_acc, bf),
        ],
        scratch_shapes=[pltpu.VMEM(a.shape, bf) for a in arrays]
        + [
            pltpu.VMEM((rows, width), bf), pltpu.VMEM((rows, width), f32), pltpu.VMEM((rows, ff), bf),
            pltpu.VMEM((rows, ff), bf), pltpu.VMEM((rows, proj), bf), pltpu.VMEM((rows, width), bf),
            pltpu.VMEM((2, width // 2, width), bf), pltpu.VMEM(dims + (pair, proj // 2), bf),
            dma((8,)), dma((2,)), dma((4,)), dma((2, copies)), dma((2, copies)),
            pltpu.VMEM(down_acc, bf), dma((12,)), dma((12,)), dma((dims[0],)), dma((dims[0],)),
            dma((dims[0],)), dma((dims[0],)),
            pltpu.VMEM(down_acc, bf), pltpu.VMEM(down_acc, bf), pltpu.VMEM((dims[0], 2, tall, width // 2), bf),
        ]
        + collapse_scratch(dims, [(pair, proj)]),
        compiler_params=pltpu.CompilerParams(
            collective_id=2, has_side_effects=True, vmem_limit_bytes=63 * 2**20
        ),
        name="middle",
    )(bound, cont, gain, *arrays)


ROW_OUT, ROW_UP, ROW_PROJ, ROW_DOWN, ROW_GAIN, ROW_MEAN = 3, 4, 8, 10, 11, 13
STAT_ROWS = 16
DECAY = 1.0 - STEP ** (-0.8)


def exchange_rounds(dims, place):
    z, y, x, c = place
    plane = [(1, 0), (0, 1), (1, 1)]
    rounds = [
        ([sibling(place)], c),
        ([(z, lax.rem(y + dy, 2), lax.rem(x + dx, 2), c) for dy, dx in plane], y * 2 + x),
        ([moved(dims, place, 0, by) for by in range(1, dims[0])], z),
    ]
    return [([device_at(dims, p) for p in others], number) for others, number in rounds]


def put_stats(stats, row, total, square_sum, old_rows, lane, columns):
    width = stats.shape[1]
    for j in range(total.shape[1] // width):
        stats[row + j : row + j + 1, :] = total[:, j * width : (j + 1) * width]
    value = DECAY * jnp.sum(old_rows, axis=1, keepdims=True) + (1.0 - DECAY) / columns * square_sum
    at = lax.broadcasted_iota(jnp.int32, (1, width), 1)
    stats[ROW_MEAN : ROW_MEAN + 1, :] += jnp.where(at == lane, value, 0.0)


def last_kernel(
    dims, shapes, count, x_hbm, resid_hbm, gain_ref, gain_two_ref,
    dq_hbm, dk_hbm, dv_hbm, n_hbm, wq_hbm, wk_hbm, wv_hbm, near_hbm, rest_hbm,
    sum_out, sum_proj, sum_up, sum_down, row_qkv, row_out, row_proj, row_up, row_down, *refs,
):
    names = iter(refs)
    take = lambda k: [next(names) for _ in range(k)]
    grad_ref, total_ref = take(2)
    sums_out = take(3)
    dq, dk, dv, normed, flipped, wq, wk, wv = take(8)
    own_back, near, rest, box, stats, inbox, x_ref, resid_ref = take(8)
    grads = take(3)
    load_sem, back_send, back_recv, stat_send, stat_recv = take(5)
    scratch = list(names)

    place = my_place(dims)
    seq, item = lax.axis_index("seq"), lax.axis_index("item")
    rows, width = x_ref.shape
    loads = [
        pltpu.make_async_copy(a, b, load_sem.at[n])
        for n, (a, b) in enumerate(
            [
                (rest_hbm, rest), (n_hbm, normed), (dk_hbm, dk), (dv_hbm, dv), (dq_hbm, dq),
                (wk_hbm, wk), (wv_hbm, wv), (wq_hbm, wq), (near_hbm, near),
                (x_hbm, x_ref), (resid_hbm, resid_ref),
            ]
        )
    ]
    for load in loads:
        load.start()
    ahead = [(lax.rem(seq + d, count), item) for d in (1, 2)]
    behind = [(lax.rem(seq + count - d, count), item) for d in (1, 2)]
    with jax.named_scope("meet"):
        meet(peers(dims, place) + ahead + behind + [device_at(dims, place[:1] + (1 - place[1], 1 - place[2], place[3]))])
    far = WINDOW - rows
    near_rows, far_rows = pl.ds(far, rest.shape[0] - far), pl.ds(0, far)
    returned = [
        pltpu.make_async_remote_copy(
            src_ref=rest.at[part], dst_ref=box.at[part], send_sem=back_send.at[m], recv_sem=back_recv.at[m],
            device_id=behind[m], device_id_type=MESH,
        )
        for m, part in enumerate((near_rows, far_rows))
    ]
    loads[0].wait()
    for m in range(2):
        pl.when(seq >= m + 1)(returned[m].start)

    def back_of(at):
        return dot(dk[at, :], wk[...].reshape(width, width), NT) + dot(dv[at, :], wv[...].reshape(width, width), NT)

    sums, locals_ = collapses_of(dims, place, shapes, grads, sums_out, scratch)
    with jax.named_scope("weight_gradients"):
        loads[1].wait()
        flipped[...] = normed[...].T
        for k, part in ((1, dk), (2, dv), (0, dq)):
            loads[(4, 2, 3)[k]].wait()
            base = WINDOW if k == 0 else 0
            got = dot(flipped[:, base:], part[...])
            grads[k][...] = got.astype(bf).reshape(grads[k].shape)
            run_collapse(sums, locals_, k, -1)
            if k != 1:
                run_collapse(sums, locals_, 1 if k == 2 else 2, 0)

    def own_block(i, carry):
        at = pl.ds(pl.multiple_of(i * QB, QB), QB)
        ext = pl.ds(pl.multiple_of(WINDOW + i * QB, QB), QB)
        own_back[at, :] = back_of(ext) + dot(dq[at, :], wq[...].reshape(width, width), NT)
        return carry

    with jax.named_scope("own_rows"):
        for load in loads[5:]:
            load.wait()
        lax.fori_loop(0, rows // QB, own_block, 0)

    stats[0] = jnp.zeros_like(stats[0])
    held = stats.at[0]
    held[ROW_GAIN + 1 : ROW_GAIN + 2, :] = gain_two_ref[...]

    def add_stats(row, grad, old_rows, lane):
        square = grad * grad + TINY_SQUARE
        total = jnp.sum(square, axis=0, keepdims=True)
        put_stats(held, row, total, jnp.sum(total, axis=1, keepdims=True), old_rows, lane, grad.shape[1])

    with jax.named_scope("small_sums"):
        add_stats(ROW_OUT, sum_out[...], row_out[...], 3)
        add_stats(ROW_UP, sum_up[...], row_up[...], 4)
        add_stats(ROW_PROJ, sum_proj[...], row_proj[...], 5)
        add_stats(ROW_DOWN, sum_down[...], row_down[...], 6)

    for stage in range(5):
        with jax.named_scope("reduce_%d" % stage):
            for k in (1, 2, 0) if stage else (0,):
                run_collapse(sums, locals_, k, stage)
    for k in range(3):
        add_stats(k, sums_out[k][...], row_qkv[k : k + 1, :], k)

    with jax.named_scope("rows_returned"):

        @pl.when(seq + 1 < count)
        def _():
            returned[0].wait_recv()
            size = near.shape[0]
            own_back[0:size, :] += near[...].astype(f32)
            own_back[size:, :] += box[near_rows, :].astype(f32)

        @pl.when(seq + 2 < count)
        def _():
            returned[1].wait_recv()
            own_back[rows - far :, :] += box[far_rows, :].astype(f32)

    gain = gain_ref[0:1]

    def input_block(i, total):
        at = pl.ds(pl.multiple_of(i * QB, QB), QB)
        x = x_ref[at, :].astype(f32)
        scale = lax.rsqrt(jnp.mean(x * x, axis=-1, keepdims=True) + EPSILON)
        back = own_back[at, :]
        unit = x * scale
        by_gain = back * gain
        inner = jnp.mean(by_gain * unit, axis=-1, keepdims=True)
        grad_ref[at, :] = (resid_ref[at, :] + scale * (by_gain - unit * inner)).astype(bf)
        return total + jnp.sum(back * unit, axis=0, keepdims=True)

    with jax.named_scope("input_gradient"):
        total = lax.fori_loop(0, rows // QB, input_block, jnp.zeros((1, width), f32))
    held[ROW_GAIN : ROW_GAIN + 1, :] = total

    rounds = exchange_rounds(dims, place)
    z, y, x, c = place
    senders = [
        [1 - c],
        [lax.rem(y + dy, 2) * 2 + lax.rem(x + dx, 2) for dy, dx in ((1, 0), (0, 1), (1, 1))],
        [lax.rem(z + dims[0] - by, dims[0]) for by in range(1, dims[0])],
    ]

    with jax.named_scope("exchange_sums"):
        slot = 0
        for stage, (others, number) in enumerate(rounds):
            copies = []
            for other in others:
                copies.append(
                    pltpu.make_async_remote_copy(
                        src_ref=stats.at[stage], dst_ref=inbox.at[slot],
                        send_sem=stat_send.at[slot], recv_sem=stat_recv.at[slot],
                        device_id=other, device_id_type=MESH,
                    )
                )
                copies[-1].start()
                slot += 1
            for copy in copies:
                copy.wait()
            base = slot - len(others)
            total = jnp.zeros_like(stats[0])
            for member in range(len(others) + 1):
                term = stats[stage]
                for m in range(len(others)):
                    term = jnp.where(senders[stage][m] == member, inbox[base + m], term)
                total = total + term
            stats[stage + 1] = total
        total_ref[...] = stats[len(rounds)]
    for one in sums:
        one.finish()
    for m in range(2):
        pl.when(seq >= m + 1)(returned[m].wait_send)


def last(x, resid_grad, gain, gain_two, dq, dk, dv, normed, weights, returned, sums, old_rows, dims, count):
    rows, width = x.shape
    ext = normed.shape[0]
    shapes = [w.shape[3:] for w in weights]
    slots = 4 + dims[0] - 1
    vmem = pl.BlockSpec(memory_space=pltpu.VMEM)
    hbm = pl.BlockSpec(memory_space=pl.ANY)
    dma = pltpu.SemaphoreType.DMA
    sds = jax.ShapeDtypeStruct
    got = pl.pallas_call(
        functools.partial(last_kernel, dims, shapes, count),
        in_specs=[hbm] * 2 + [vmem] * 2 + [hbm] * 9 + [vmem] * 9,
        out_specs=[vmem] * 5,
        out_shape=[sds((rows, width), bf), sds((STAT_ROWS, width), f32)] + [sds((r // 2, c), f32) for r, c in shapes],
        scratch_shapes=[
            pltpu.VMEM((rows, width), bf), pltpu.VMEM((ext, width), bf), pltpu.VMEM((ext, width), bf),
            pltpu.VMEM((ext, width), bf), pltpu.VMEM((width, ext), bf),
        ]
        + [pltpu.VMEM(w.shape, bf) for w in weights]
        + [pltpu.VMEM((rows, width), f32)]
        + [pltpu.VMEM(a.shape, bf) for a in (*returned, returned[1])]
        + [pltpu.VMEM((4, STAT_ROWS, width), f32), pltpu.VMEM((slots, STAT_ROWS, width), f32)]
        + [pltpu.VMEM((rows, width), bf), pltpu.VMEM((rows, width), f32)]
        + [pltpu.VMEM(w.shape, bf) for w in weights]
        + [dma((11,)), dma((2,)), dma((2,)), dma((slots,)), dma((slots,))]
        + collapse_scratch(dims, shapes),
        compiler_params=pltpu.CompilerParams(
            collective_id=4, has_side_effects=True, vmem_limit_bytes=61 * 2**20
        ),
        name="last",
    )(x, resid_grad, gain, gain_two, dq, dk, dv, normed, *weights, *returned, *sums, *old_rows)
    return got[0], got[1], got[2:]


def update_kernel(
    place_ref, total_ref, gains_ref, gain_var_ref,
    w_qkv, w_out, w_proj, w_up, w_down, s_q, s_k, s_v, s_out, s_proj, s_up, s_down,
    row_qkv, row_out, row_proj, row_up, row_down, col_qkv, col_out, col_proj, col_up, col_down,
    y_ref, p_ref, d_ref, g_qkv, g_out, g_proj, g_up, g_down, g_gains, n_qkv, n_out, n_proj, n_up, n_down, n_gains,
    r_qkv, r_out, r_proj, r_up, r_down, c_qkv, c_out, c_proj, c_up, c_down, gain_var_new,
    y_out, p_out, d_out, flat, tall, y_held, p_held, d_held, pass_sem,
):
    held = (y_held, p_held, d_held)
    taken = [pltpu.make_async_copy(a, b, pass_sem.at[n]) for n, (a, b) in enumerate(zip((y_ref, p_ref, d_ref), held))]
    passed = [pltpu.make_async_copy(a, b, pass_sem.at[3 + n]) for n, (a, b) in enumerate(zip(held, (y_out, p_out, d_out)))]
    for copy in taken:
        copy.start()
    shard = row_out.shape[1]
    shard_down = row_down.shape[1]
    width = total_ref.shape[1]
    flat[...] = jnp.zeros_like(flat)
    flat[0:3, :shard] = row_qkv[...]
    flat[3:4, :shard] = row_out[...]
    flat[4:5, :shard] = row_up[...]
    flat[5:6, :shard] = row_proj[...]
    flat[6:7, :shard_down] = row_down[...]
    olds = flat[...].T
    tall[...] = jnp.zeros_like(tall)

    def one(weight, grad, lane, row, old_col, rows_all, g_out_, n_out_, c_out_):
        count, columns = grad.shape
        square = grad * grad + TINY_SQUARE
        row_new = DECAY * olds[:count, lane : lane + 1] + (1.0 - DECAY) * jnp.mean(square, axis=1, keepdims=True)
        tall[:count, lane : lane + 1] = row_new
        parts = [total_ref[row + j : row + j + 1, :] for j in range(columns // width)]
        col_total = parts[0] if len(parts) == 1 else jnp.concatenate(parts, axis=1)
        col_new = DECAY * old_col + (1.0 - DECAY) * col_total / rows_all
        mean = total_ref[ROW_MEAN : ROW_MEAN + 1, lane : lane + 1] / rows_all
        second = row_new * col_new / mean
        g_out_[...] = grad
        n_out_[...] = weight - WEIGHT_RATE * grad * lax.rsqrt(second)
        c_out_[...] = col_new.reshape(c_out_.shape)

    for k, grad in enumerate((s_q, s_k, s_v)):
        one(w_qkv[k], grad[...], k, k, col_qkv[k : k + 1, :], width, g_qkv.at[k], n_qkv.at[k], c_qkv.at[k : k + 1])
    ff = col_up.shape[0]
    one(w_out[...], s_out[...], 3, ROW_OUT, col_out[...].reshape(1, width), width, g_out, n_out, c_out)
    one(w_up[...], s_up[...], 4, ROW_UP, col_up[...].reshape(1, ff), width, g_up, n_up, c_up)
    one(w_proj[...], s_proj[...], 5, ROW_PROJ, col_proj[...].reshape(1, -1), width, g_proj, n_proj, c_proj)
    one(w_down[...], s_down[...], 6, ROW_DOWN, col_down[...].reshape(1, width), ff, g_down, n_down, c_down)
    for copy, onward in zip(taken, passed):
        copy.wait()
        onward.start()
    news = tall[...].T
    r_qkv[...] = news[0:3, :shard]
    r_out[...] = news[3:4, :shard]
    r_up[...] = news[4:5, :shard]
    r_proj[...] = news[5:6, :shard]
    r_down[...] = news[6:7, :shard_down]

    gain_sums = pltpu.roll(total_ref[8:16, :], width - place_ref[0] * shard, 1)
    sums = gain_sums[ROW_GAIN - 8 : ROW_GAIN - 6, :shard]
    var = DECAY * gain_var_ref[...] + (1.0 - DECAY) * (sums * sums + TINY_SQUARE)
    g_gains[...] = sums
    gain_var_new[...] = var
    n_gains[...] = gains_ref[...] - GAIN_RATE * sums * lax.rsqrt(var)
    for copy in passed:
        copy.wait()


def update(place, totals, gains, gain_var, weights, sums, rows, cols, results):
    vmem = pl.BlockSpec(memory_space=pltpu.VMEM)
    like = lambda arrays: [jax.ShapeDtypeStruct(a.shape, f32) for a in arrays]
    outs = like(weights) + like([gains]) + like(weights) + like([gains]) + like(rows) + like(cols) + like([gain_var])
    hbm = pl.BlockSpec(memory_space=pl.ANY)
    return pl.pallas_call(
        update_kernel,
        in_specs=[pl.BlockSpec(memory_space=pltpu.SMEM)] + [vmem] * (3 + 5 + 7 + 5 + 5) + [hbm] * 3,
        out_specs=[vmem] * len(outs) + [hbm] * 3,
        out_shape=outs + [jax.ShapeDtypeStruct(a.shape, a.dtype) for a in results],
        scratch_shapes=[pltpu.VMEM((8, 128), f32), pltpu.VMEM((128, 8), f32)]
        + [pltpu.VMEM(a.shape, a.dtype) for a in results]
        + [pltpu.SemaphoreType.DMA((6,))],
        compiler_params=pltpu.CompilerParams(vmem_limit_bytes=63 * 2**20),
        name="update",
    )(place, totals, gains, gain_var, *weights, *sums, *rows, *cols, *results)


def sum_kernel(sizes, x_ref, o_ref, inbox, send_sem, recv_sem):
    place = {name: lax.axis_index(name) for name, _ in sizes}
    partners = []
    for name, size in sizes:
        bit = 1
        while bit < size:
            mine = place[name]
            low = lax.rem(mine // bit, 2)
            other = mine + bit * (1 - 2 * low)
            partners.append(tuple(other if n == name else place[n] for n in ("seq", "item")))
            bit *= 2
    barrier = pltpu.get_barrier_semaphore()
    for partner in partners:
        pl.semaphore_signal(barrier, inc=1, device_id=partner, device_id_type=MESH)
    pl.semaphore_wait(barrier, len(partners))
    o_ref[0] = x_ref[...]
    for stage, partner in enumerate(partners):
        copy = pltpu.make_async_remote_copy(
            src_ref=o_ref.at[stage],
            dst_ref=inbox.at[stage],
            send_sem=send_sem.at[stage],
            recv_sem=recv_sem.at[stage],
            device_id=partner,
            device_id_type=MESH,
        )
        copy.start()
        copy.wait()
        o_ref[stage + 1] = o_ref[stage] + inbox[stage]


def sum_all(x, sizes):
    stages = sum(size.bit_length() - 1 for _, size in sizes)
    held = pl.pallas_call(
        functools.partial(sum_kernel, sizes),
        out_shape=jax.ShapeDtypeStruct((stages + 1,) + x.shape, x.dtype),
        in_specs=[pl.BlockSpec(memory_space=pltpu.VMEM)],
        out_specs=pl.BlockSpec(memory_space=pltpu.VMEM),
        scratch_shapes=[
            pltpu.VMEM((stages,) + x.shape, x.dtype),
            pltpu.SemaphoreType.DMA((stages,)),
            pltpu.SemaphoreType.DMA((stages,)),
        ],
        compiler_params=pltpu.CompilerParams(collective_id=0, has_side_effects=True),
        name="sum_all",
    )(x)
    return held[stages]


def from_behind(block, axis, distance):
    devices = range(lax.axis_size(axis))
    route = [(i - distance, i) for i in devices if i - distance in devices]
    return lax.ppermute(block, axis, route)


def norm_rows(values, gain):
    return values * lax.rsqrt(jnp.mean(values * values, axis=-1, keepdims=True) + EPSILON) * gain


def gelu_tanh(values):
    return (
        0.5
        * values
        * (1.0 + jnp.tanh(0.7978845608028654 * (values + 0.044715 * values * values * values)))
    )


def finish_update(weight, grad, row_new, col_state, col_total, rows_all, row_mean, decay):
    col_new = decay * col_state + (1.0 - decay) * col_total / rows_all
    second = row_new[..., :, None] * col_new[..., None, :] / row_mean
    return (weight - WEIGHT_RATE * grad * lax.rsqrt(second), col_new)


def local(
    byte_rows, item_lengths, cont_mask, bound_mask, out_cot, proj_cot,
    w_qkv, w_out, w_up, w_down, w_proj, gains,
    row_qkv, col_qkv, row_out, col_out, row_up, col_up, row_down, col_down, row_proj, col_proj, gain_var,
):
    sizes = tuple((name, lax.axis_size(name)) for name in ("item", "seq"))
    count = lax.axis_size("item") * lax.axis_size("seq")
    rows_dev, width = byte_rows.shape[1:]
    ff = w_up.shape[1]
    shard = width // count
    low = bf

    dims = grid_of(lax.axis_size("seq"), lax.axis_size("item"))
    paired = dims == (4, 2, 2) and shard % 8 == 0 and rows_dev < WINDOW <= 2 * rows_dev
    inputs_low = byte_rows[0]
    if paired:
        got = front(item_lengths, inputs_low, gains, w_qkv, (w_out, w_proj, w_up, w_down), dims, lax.axis_size("seq"))
        attended, lse, queries, ext_keys, ext_values, ext_normed = got[:6]
        split_qkv = got[6:9]
        gain_full = got[9]
        weight_out, weight_up, weight_down = [w.reshape(-1, w.shape[-1]) for w in (got[10], got[12], got[13])]
        part_proj, flipped_keys = got[11], got[14]
    else:
        inputs = inputs_low.astype(f32)
        weight_qkv = lax.all_gather(w_qkv.astype(low), AXES, axis=1, tiled=True)
        gain_full = lax.all_gather(gains.astype(low), AXES, axis=1, tiled=True).astype(f32)
        weight_out, weight_proj, weight_up, weight_down = [
            lax.all_gather(w.astype(low), AXES, axis=0, tiled=True) for w in (w_out, w_proj, w_up, w_down)
        ]

    hop_total = -(-WINDOW // rows_dev)
    if not paired:
        offset = lax.axis_index("seq") * rows_dev
        ends = jnp.cumsum(item_lengths[0], dtype=jnp.int32)
        pos = offset + jnp.arange(rows_dev, dtype=jnp.int32)
        begin_at = jnp.max(jnp.where(ends[None, :] <= pos[:, None], ends[None, :], 0), axis=1)
        lo = jnp.maximum(begin_at, pos - WINDOW + 1) - offset + WINDOW
        halo = []
        for distance in range(hop_total, 0, -1):
            need = min(rows_dev, WINDOW - (distance - 1) * rows_dev)
            halo.append(from_behind(inputs_low[rows_dev - need :], "seq", distance))
        normed = norm_rows(inputs, gain_full[0]).astype(low)
        halo_normed = norm_rows(jnp.concatenate(halo, axis=0).astype(f32), gain_full[0]).astype(low)
        ext_normed = jnp.concatenate([halo_normed, normed], axis=0)
        queries = dot(normed, weight_qkv[0]).astype(low) * jnp.asarray(0.125, low)
        ext_keys = dot(ext_normed, weight_qkv[1]).astype(low)
        ext_values = dot(ext_normed, weight_qkv[2]).astype(low)
        attended, lse = attend(queries, ext_keys, ext_values, lo[:, None])

    if paired:
        output_low, projected, resid_grad, attended_grad, gain_two_grad, delta, sum_proj, *low_grads = middle(
            bound_mask, cont_mask, gain_full,
            (inputs_low, attended, out_cot[0], proj_cot[0], weight_out, weight_up, weight_down, part_proj), dims,
        )
        apart = [g.reshape(dims + (-1, g.shape[-1])) for g in low_grads]
        (query_grad, ext_key_grad, ext_value_grad, *returned), (sum_out, sum_up, sum_down) = back(
            item_lengths, lse, delta, (queries, attended_grad, ext_keys, ext_values, flipped_keys, split_qkv[1], split_qkv[2]),
            apart, dims, lax.axis_size("seq"),
        )
        sums = [sum_out, sum_proj, sum_up, sum_down]
    else:
        resid = inputs + dot(attended, weight_out)
        normed_two = norm_rows(resid, gain_full[1]).astype(low)
        hidden_pre = dot(normed_two, weight_up)
        activated = gelu_tanh(hidden_pre).astype(low)
        output = resid + dot(activated, weight_down)
        output_low = output.astype(low)
        boundary = (bound_mask[0] * (1 - cont_mask[0])).astype(f32)[:, None]
        projected = (boundary * dot(output_low, weight_proj)).astype(low)
        proj_grad = (boundary * proj_cot[0].astype(f32)).astype(low)
        grad_proj = dot(output_low, proj_grad, TN)
        output_grad = out_cot[0].astype(f32) + dot(proj_grad, weight_proj, NT)
        output_grad_low = output_grad.astype(low)
        grad_down = dot(activated, output_grad_low, TN)
        act_grad = dot(output_grad_low, weight_down, NT)
        _, gelu_back = jax.vjp(gelu_tanh, hidden_pre)
        pre_grad = gelu_back(act_grad)[0].astype(low)
        grad_up = dot(normed_two, pre_grad, TN)
        normed_two_grad = dot(pre_grad, weight_up, NT)
        _, norm_two_back = jax.vjp(norm_rows, resid, gain_full[1])
        resid_norm_grad, gain_two_grad = norm_two_back(normed_two_grad)
        resid_grad = output_grad + resid_norm_grad
        resid_grad_low = resid_grad.astype(low)
        grad_out = dot(attended, resid_grad_low, TN)
        attended_grad = dot(resid_grad_low, weight_out, NT).astype(low)

        low_grads = [g.astype(low) for g in (grad_out, grad_proj, grad_up, grad_down)]
        query_grad, ext_key_grad, ext_value_grad = attend_back(
            queries, attended_grad, attended, lse, ext_keys, ext_values, lo[None, :]
        )
        sums = [lax.psum_scatter(g, AXES, scatter_dimension=0, tiled=True).astype(f32) for g in low_grads]
        sum_out, sum_proj, sum_up, sum_down = sums
    if paired:
        rows = [row_qkv, row_out[None], row_proj[None], row_up[None], row_down[None]]
        cols = [col_qkv, col_out, col_proj, col_up, col_down]
        input_grad, totals, sums_qkv = last(
            inputs_low, resid_grad, gain_full, gain_two_grad, query_grad, ext_key_grad, ext_value_grad,
            ext_normed, split_qkv, returned, sums, rows, dims, lax.axis_size("seq"),
        )
        mine = lax.axis_index("seq") * lax.axis_size("item") + lax.axis_index("item")
        done = update(
            mine[None].astype(jnp.int32), totals, gains, gain_var,
            (w_qkv, w_out, w_proj, w_up, w_down), (*sums_qkv, *sums), rows, cols,
            (output_low, projected, input_grad),
        )
        sum_qkv, sum_out, sum_proj, sum_up, sum_down, sum_gains = done[:6]
        new_qkv, new_out, new_proj, new_up, new_down, new_gains = done[6:12]
        row_qkv_new, row_out_new, row_proj_new, row_up_new, row_down_new = [done[12]] + [r[0] for r in done[13:17]]
        col_qkv_new, col_out_new, col_proj_new, col_up_new, col_down_new = done[17:22]
        gain_var_new, output_low, projected, input_grad = done[22:]
        return (
            output_low[None], projected[None], input_grad[None],
            sum_qkv, sum_out, sum_up, sum_down, sum_proj, sum_gains,
            new_qkv, new_out, new_up, new_down, new_proj, new_gains,
            row_qkv_new, col_qkv_new, row_out_new, col_out_new, row_up_new, col_up_new,
            row_down_new, col_down_new, row_proj_new, col_proj_new, gain_var_new,
        )
    ext_back = dot(ext_key_grad, weight_qkv[1], NT) + dot(ext_value_grad, weight_qkv[2], NT)
    halo_back = ext_back[:WINDOW].astype(low)
    grads_qkv = [
        dot(normed, query_grad, TN).astype(low),
        dot(ext_normed, ext_key_grad, TN).astype(low),
        dot(ext_normed, ext_value_grad, TN).astype(low),
    ]
    returned = []
    for distance in range(1, hop_total + 1):
        need = min(rows_dev, WINDOW - (distance - 1) * rows_dev)
        upper = WINDOW - (distance - 1) * rows_dev
        returned.append(from_behind(halo_back[upper - need : upper], "seq", -distance))
    sums = [lax.psum_scatter(g, AXES, scatter_dimension=0, tiled=True).astype(f32) for g in grads_qkv]
    sum_qkv = jnp.stack(sums)
    normed_grad = ext_back[WINDOW:] + dot(query_grad, weight_qkv[0], NT)
    for block in returned:
        need = block.shape[0]
        normed_grad = normed_grad.at[rows_dev - need :].add(block.astype(f32))
    _, norm_one_back = jax.vjp(norm_rows, inputs, gain_full[0])
    input_norm_grad, gain_one_grad = norm_one_back(normed_grad)
    input_grad = (resid_grad + input_norm_grad).astype(low)

    decay = 1.0 - STEP ** (-0.8)
    square_qkv = sum_qkv * sum_qkv + TINY_SQUARE
    square_out = sum_out * sum_out + TINY_SQUARE
    square_up = sum_up * sum_up + TINY_SQUARE
    square_down = sum_down * sum_down + TINY_SQUARE
    square_proj = sum_proj * sum_proj + TINY_SQUARE
    row_qkv_new = decay * row_qkv + (1.0 - decay) * jnp.mean(square_qkv, axis=-1)
    row_out_new = decay * row_out + (1.0 - decay) * jnp.mean(square_out, axis=-1)
    row_up_new = decay * row_up + (1.0 - decay) * jnp.mean(square_up, axis=-1)
    row_down_new = decay * row_down + (1.0 - decay) * jnp.mean(square_down, axis=-1)
    row_proj_new = decay * row_proj + (1.0 - decay) * jnp.mean(square_proj, axis=-1)
    row_sums = jnp.concatenate(
        [
            jnp.sum(row_qkv_new, axis=1),
            jnp.sum(row_out_new)[None],
            jnp.sum(row_up_new)[None],
            jnp.sum(row_down_new)[None],
            jnp.sum(row_proj_new)[None],
        ]
    )
    stats = [
        jnp.sum(square_qkv, axis=1).reshape(-1),
        jnp.sum(square_out, axis=0),
        jnp.sum(square_up, axis=0),
        jnp.sum(square_down, axis=0),
        jnp.sum(square_proj, axis=0),
        gain_one_grad,
        gain_two_grad,
        row_sums,
    ]
    flat = jnp.concatenate(stats)
    used = flat.shape[0]
    padded = -(-used // 1024) * 1024
    flat = jnp.pad(flat, (0, padded - used)).reshape(padded // 128, 128)
    flat = sum_all(flat, sizes).reshape(-1)
    totals, at = [], 0
    for part in stats:
        totals.append(flat[at : at + part.shape[0]])
        at += part.shape[0]
    col_qkv_total, col_out_total, col_up_total, col_down_total, col_proj_total, gain_one, gain_two, row_totals = totals
    col_qkv_total = col_qkv_total.reshape(3, width)
    mine = lax.axis_index("seq") * lax.axis_size("item") + lax.axis_index("item")
    sum_gains = lax.dynamic_slice_in_dim(jnp.stack([gain_one, gain_two]), mine * shard, shard, 1)
    row_counts = jnp.array([width, width, width, width, width, ff, width], f32)
    row_means = row_totals / row_counts
    new_qkv, col_qkv_new = finish_update(
        w_qkv, sum_qkv, row_qkv_new, col_qkv, col_qkv_total, width, row_means[:3][:, None, None], decay
    )
    new_out, col_out_new = finish_update(w_out, sum_out, row_out_new, col_out, col_out_total, width, row_means[3], decay)
    new_up, col_up_new = finish_update(w_up, sum_up, row_up_new, col_up, col_up_total, width, row_means[4], decay)
    new_down, col_down_new = finish_update(
        w_down, sum_down, row_down_new, col_down, col_down_total, ff, row_means[5], decay
    )
    new_proj, col_proj_new = finish_update(
        w_proj, sum_proj, row_proj_new, col_proj, col_proj_total, width, row_means[6], decay
    )
    gain_var_new = decay * gain_var + (1.0 - decay) * (sum_gains * sum_gains + TINY_SQUARE)
    new_gains = gains - GAIN_RATE * sum_gains * lax.rsqrt(gain_var_new)
    return (
        output_low[None], projected[None], input_grad[None],
        sum_qkv, sum_out, sum_up, sum_down, sum_proj, sum_gains,
        new_qkv, new_out, new_up, new_down, new_proj, new_gains,
        row_qkv_new, col_qkv_new, row_out_new, col_out_new, row_up_new, col_up_new,
        row_down_new, col_down_new, row_proj_new, col_proj_new, gain_var_new,
    )


def solution(mesh):
    in_specs = (
        P("item", "seq", None),
        P("item", None),
        P("item", "seq"),
        P("item", "seq"),
        P("item", "seq", None),
        P("item", "seq", None),
        P(None, ("seq", "item"), None),
        P(("seq", "item"), None),
        P(("seq", "item"), None),
        P(("seq", "item"), None),
        P(("seq", "item"), None),
        P(None, ("seq", "item")),
        P(None, ("seq", "item")),
        P(),
        P(("seq", "item")),
        P(),
        P(("seq", "item")),
        P(),
        P(("seq", "item")),
        P(),
        P(("seq", "item")),
        P(),
        P(None, ("seq", "item")),
    )
    out_specs = (
        P("item", "seq", None),
        P("item", "seq", None),
        P("item", "seq", None),
        P(None, ("seq", "item"), None),
        P(("seq", "item"), None),
        P(("seq", "item"), None),
        P(("seq", "item"), None),
        P(("seq", "item"), None),
        P(None, ("seq", "item")),
        P(None, ("seq", "item"), None),
        P(("seq", "item"), None),
        P(("seq", "item"), None),
        P(("seq", "item"), None),
        P(("seq", "item"), None),
        P(None, ("seq", "item")),
        P(None, ("seq", "item")),
        P(),
        P(("seq", "item")),
        P(),
        P(("seq", "item")),
        P(),
        P(("seq", "item")),
        P(),
        P(("seq", "item")),
        P(),
        P(None, ("seq", "item")),
    )
    return jax.shard_map(local, mesh=mesh, in_specs=in_specs, out_specs=out_specs, check_vma=False)
```

```python
import functools
import jax
import jax.numpy as jnp
from jax import lax
from jax.experimental import pallas as pl
from jax.experimental.pallas import tpu as pltpu
from jax.sharding import PartitionSpec as P

WINDOW = 1536
HEADS = 12
NEG = -1e30
EPSILON = 1e-06
TINY_SQUARE = 1e-30
WEIGHT_RATE = 0.02
GAIN_RATE = 0.2
STEP = 10
QB = 256
NT = (((1,), (1,)), ((), ()))
TN = (((0,), (0,)), ((), ()))
f32 = jnp.float32
bf = jnp.bfloat16


def dot(a, b, dims=None):
    if dims is None:
        return jnp.dot(a, b, preferred_element_type=f32)
    return lax.dot_general(a, b, dims, preferred_element_type=f32)


def halves(x):
    lane = lax.broadcasted_iota(jnp.int32, x.shape, 1)
    zero = jnp.zeros_like(x)
    return jnp.where(lane < 64, x, zero), jnp.where(lane < 64, zero, x)


def fwd_kernel(lo_ref, q_ref, k_ref, v_ref, o_ref, lse_ref, bias):
    hp, qb = pl.program_id(0), pl.program_id(1)
    span = WINDOW + QB

    @pl.when(hp == 0)
    def _():
        base = qb * QB
        kpos = base + lax.broadcasted_iota(jnp.int32, (QB, span), 1)
        qpos = WINDOW + base + lax.broadcasted_iota(jnp.int32, (QB, span), 0)
        ok = (kpos >= lo_ref[...]) & (kpos <= qpos)
        bias[qb] = jnp.where(ok, 0.0, NEG)

    start = pl.multiple_of(qb * QB, QB)
    kw = k_ref[pl.ds(start, span), :]
    vw = v_ref[pl.ds(start, span), :]
    outs, lses = [], []
    for qh in halves(q_ref[...]):
        s = dot(qh, kw, NT) + bias[qb]
        m = jnp.max(s, axis=1, keepdims=True)
        p = jnp.exp(s - m)
        l = jnp.sum(p, axis=1, keepdims=True)
        outs.append(dot(p.astype(bf), vw) * (1.0 / l))
        lses.append(m + jnp.log(l))
    lane = lax.broadcasted_iota(jnp.int32, (QB, 128), 1)
    o_ref[...] = jnp.where(lane < 64, outs[0], outs[1]).astype(bf)
    both = jnp.where(lane == 0, lses[0], lses[1])
    lse_ref[0] = both.T[:8]


def attend(q, k, v, lo):
    rows, width = q.shape
    ext = k.shape[0]
    nq, nh = rows // QB, width // 128
    return pl.pallas_call(
        fwd_kernel,
        grid=(nh, nq),
        in_specs=[
            pl.BlockSpec((QB, 1), lambda h, i: (i, 0)),
            pl.BlockSpec((QB, 128), lambda h, i: (i, h)),
            pl.BlockSpec((ext, 128), lambda h, i: (0, h)),
            pl.BlockSpec((ext, 128), lambda h, i: (0, h)),
        ],
        out_specs=[
            pl.BlockSpec((QB, 128), lambda h, i: (i, h)),
            pl.BlockSpec((1, 8, QB), lambda h, i: (h, 0, i)),
        ],
        out_shape=[
            jax.ShapeDtypeStruct((rows, width), bf),
            jax.ShapeDtypeStruct((nh, 8, rows), f32),
        ],
        scratch_shapes=[pltpu.VMEM((nq, QB, WINDOW + QB), f32)],
        compiler_params=pltpu.CompilerParams(vmem_limit_bytes=50 * 2**20),
        cost_estimate=pl.CostEstimate(flops=4 * rows * 1792 * 768 * 3, bytes_accessed=14 * 2**20, transcendentals=0),
        name="attend",
    )(lo, q, k, v)


AXES = ("seq", "item")
MESH = pl.DeviceIdType.MESH


def grid_of(seq, item):
    side = 1
    while side * side * 4 <= seq:
        side *= 2
    return (seq // side, side, item // 2)


def my_place(dims):
    seq, item = lax.axis_index("seq"), lax.axis_index("item")
    return (seq // dims[1], lax.rem(seq, dims[1]), item // 2, lax.rem(item, 2))


def device_at(dims, place):
    z, y, x, c = place
    return (z * dims[1] + y, x * 2 + c)


def moved(dims, place, dim, by):
    to = list(place)
    to[dim] = lax.rem(place[dim] + by, dims[dim])
    return tuple(to)


def sibling(place):
    return place[:3] + (1 - place[3],)


def peers(dims, place):
    found = [sibling(place)]
    for dim in range(3):
        found += [moved(dims, place, dim, by) for by in range(1, dims[dim])]
    return [device_at(dims, p) for p in found]


def meet(targets):
    barrier = pltpu.get_barrier_semaphore()
    for target in targets:
        pl.semaphore_signal(barrier, inc=1, device_id=target, device_id_type=MESH)
    pl.semaphore_wait(barrier, len(targets))


class Spread:
    def __init__(self, dims, place, own, out, rows, cols, order, send, recv):
        self.dims, self.place, self.own, self.out = dims, place, own, out
        self.rows, self.cols, self.order = rows, cols, order
        self.send, self.recv = send, recv

    def span(self, core):
        half = self.out.shape[-1] // 2
        return pl.ds(pl.multiple_of(core * half + self.cols[0], 128), self.cols[1])

    def region(self, stage, by=0, core=None):
        held = self.order[:stage]
        at = []
        for dim in range(3):
            if dim in held:
                at.append(slice(None))
            elif by and dim == self.order[stage]:
                at.append(lax.rem(self.place[dim] + self.dims[dim] - by, self.dims[dim]))
            else:
                at.append(self.place[dim])
        core = self.place[3] if core is None else core
        return self.out.at[tuple(at) + (self.rows, self.span(core))]

    def slots(self, stage):
        first = sum(self.dims[d] - 1 for d in self.order[:stage])
        return [(by, first + by - 1) for by in range(1, self.dims[self.order[stage]])]

    def hops(self, stage):
        for by, slot in self.slots(stage):
            block = self.region(stage)
            source = self.own.at[self.rows, self.span(self.place[3])] if stage == 0 else block
            target = device_at(self.dims, moved(self.dims, self.place, self.order[stage], by))
            yield pltpu.make_async_remote_copy(
                src_ref=source, dst_ref=block, send_sem=self.send.at[slot], recv_sem=self.recv.at[slot],
                device_id=target, device_id_type=MESH,
            )

    def shares(self, stage, core=None):
        count = sum(d - 1 for d in self.dims)
        for by, slot in self.slots(stage):
            block = self.region(stage, by, core)
            yield pltpu.make_async_remote_copy(
                src_ref=block, dst_ref=block, send_sem=self.send.at[count + slot], recv_sem=self.recv.at[count + slot],
                device_id=device_at(self.dims, sibling(self.place)), device_id_type=MESH,
            )

    def begin(self, stage):
        for copy in self.hops(stage):
            copy.start()

    def advance(self, stage, go_on=True):
        for copy in self.hops(stage):
            copy.wait_recv()
        if stage < 2 and go_on:
            self.begin(stage + 1)
        for copy in self.shares(stage):
            copy.start()

    def finish(self, stages=(0, 1, 2)):
        for stage in stages:
            for copy in self.hops(stage):
                copy.wait_send()
            for copy in self.shares(stage):
                copy.wait_send()
            for copy in self.shares(stage, 1 - self.place[3]):
                copy.wait_recv()


def keep_own(own, out, place, sem):
    return pltpu.make_async_copy(own, out.at[place[0], place[1], place[2]], sem)


def copies_of(dims):
    return 2 * sum(d - 1 for d in dims)


def halves_of(shape):
    rows, cols = shape
    half = cols // 2
    if half % 256 == 0:
        return [((0, rows), (0, half // 2)), ((0, rows), (half // 2, half // 2))]
    cut = rows // 32 * 16
    return [((at, count), (0, half)) for at, count in ((0, cut), (cut, rows - cut)) if count]


ORDERS = ((0, 1, 2), (0, 2, 1))


def pieces_of(dims, place, owns, outs, shapes, send, recv):
    made, at = [], 0
    for k, (own, out, shape) in enumerate(zip(owns, outs, shapes)):
        turn = k % 2
        pieces = []
        for order, (rows, cols) in zip(ORDERS[turn:] + ORDERS[:turn], halves_of(shape)):
            pieces.append(Spread(dims, place, own, out, pl.ds(*rows), cols, order, send.at[at], recv.at[at]))
            at += 1
        made.append(pieces)
    return made


def begin(pieces):
    for piece in pieces:
        piece.begin(0)


def advance(pieces, stage):
    for piece in pieces:
        piece.advance(stage)


def lower_bounds(lengths_ref, pos, offset):
    begin = jnp.zeros_like(pos)
    end = jnp.int32(0)
    for j in range(lengths_ref.shape[1]):
        end = end + lengths_ref[0, j]
        begin = jnp.where(end <= pos, end, begin)
    return jnp.maximum(begin, pos - (WINDOW - 1)) - offset + WINDOW


def norm_block(values, gain):
    x = values.astype(f32)
    return (x * lax.rsqrt(jnp.mean(x * x, axis=-1, keepdims=True) + EPSILON) * gain).astype(bf)


REST_EVENTS = {
    (0, 0, 0): ((2, 0),),
    (1, 0, 2): ((2, 1),),
    (1, 1, 2): ((3, 0),),
    (1, 3, 0): ((0, 0), (2, 2)),
    (1, 4, 2): ((3, 1), (0, 1)),
}


def front_kernel(dims, shapes, count, lengths_ref, x_ref, gains_ref, qkv_ref, out_ref_, proj_ref, up_ref, down_ref, *refs):
    names = iter(refs)
    take = lambda k: [next(names) for _ in range(k)]
    o_ref, lse_ref, q_out, k_out, v_out, n_out = take(6)
    w_outs = take(4)
    rest_outs = take(4)
    (flip_out,) = take(1)
    halo, staging, normed, q_scr, k_scr, v_scr, gain_scr, gain_own, bias, own_mixed, own_top, own_total, flipped = take(13)
    wide, blocks = take(8), take(8)
    first = take(4)
    swap_send, swap_recv, send, recv, keep_sem, halo_send, halo_recv, out_sem = take(8)

    place = my_place(dims)
    c = place[3]
    seq, item = lax.axis_index("seq"), lax.axis_index("item")
    rows, width = x_ref.shape
    hops = -(-WINDOW // rows)
    around = [(lax.rem(seq + d, count), item) for d in range(1, hops + 1)]
    behind = [(lax.rem(seq + count - d, count), item) for d in range(1, hops + 1)]
    with jax.named_scope("meet"):
        meet(peers(dims, place) + around + behind)

    mate = device_at(dims, sibling(place))
    shard = gains_ref.shape[1]
    gain_own[...] = jnp.zeros_like(gain_own)
    gain_own[0:2, 0:shard] = gains_ref[...]
    mine = seq * (dims[2] * 2) + item
    gain_own[...] = pltpu.roll(gain_own[...], mine * shard, 1)
    shards = [qkv_ref.at[0], qkv_ref.at[1], qkv_ref.at[2], gain_own, out_ref_, proj_ref, up_ref, down_ref]
    swaps = []
    for k in range(8):
        half = shapes[k][0] // 2
        part = wide[k].at[pl.ds(pl.multiple_of(c * half, 8), half)]
        part[...] = shards[k][...]
        swaps.append(
            pltpu.make_async_remote_copy(
                src_ref=shards[k], dst_ref=part, send_sem=swap_send.at[k], recv_sem=swap_recv.at[k],
                device_id=mate, device_id_type=MESH,
            )
        )
        swaps[k].start()
    outs = first + rest_outs
    keeps = [keep_own(blocks[k], outs[k], place, keep_sem.at[k]) for k in range(8)]
    pieces = pieces_of(dims, place, blocks, outs, shapes, send, recv)

    def ready(k):
        swaps[k].wait()
        blocks[k][...] = wide[k][...].astype(bf)
        keeps[k].start()

    odd = place[1] == 1
    lower, upper = WINDOW - rows, 2 * rows - WINDOW
    part = rows // 4

    def hop(send_slot, slot, source, target, device):
        return pltpu.make_async_remote_copy(
            src_ref=source, dst_ref=target, send_sem=halo_send.at[send_slot], recv_sem=halo_recv.at[slot],
            device_id=device, device_id_type=MESH,
        )

    cuts = [(0, 2 * part), (2 * part, part), (3 * part, part)]
    direct = [
        hop(n, n, x_ref.at[pl.ds(at, size)], halo.at[pl.ds(lower + at, size)], around[0])
        for n, (at, size) in enumerate(cuts)
    ]
    far = hop(3, 3, x_ref.at[pl.ds(upper, lower)], halo.at[pl.ds(0, lower)], around[1])
    aside = hop(4, 4, x_ref.at[pl.ds(0, 2 * part)], staging, behind[0])
    onward = hop(5, 0, staging, halo.at[pl.ds(lower, 2 * part)], around[1])
    has_next, has_far = seq + 1 < count, seq + 2 < count
    odd_next = jnp.logical_and(odd, has_next)
    even_next = jnp.logical_and(jnp.logical_not(odd), has_next)
    relays = jnp.logical_and(jnp.logical_not(odd), has_far)

    with jax.named_scope("swap"):
        for k in (3, 0, 1, 2):
            ready(k)
            begin(pieces[k])
        pl.when(odd_next)(aside.start)
        pl.when(even_next)(direct[2].start)
    with jax.named_scope("swap_rest"):
        for k in (4, 5, 6, 7):
            ready(k)
        for k in range(8):
            keeps[k].wait()
    with jax.named_scope("first_0"):
        for k in (3, 0, 1, 2):
            advance(pieces[k], 0)
        begin(pieces[6])
    with jax.named_scope("first_1"):
        for k in (3, 0, 1, 2):
            advance(pieces[k], 1)
        pl.when(has_far)(far.start)
        pl.when(has_next)(direct[1].start)
        pl.when(odd_next)(direct[2].start)
        pl.when(even_next)(direct[0].start)
    with jax.named_scope("relay"):

        @pl.when(relays)
        def _():
            aside.wait_recv()
            onward.start()

        for k in (7, 4, 5):
            begin(pieces[k])

    with jax.named_scope("first_2"):
        for k in (3, 0, 1, 2):
            advance(pieces[k], 2)
    with jax.named_scope("first_end"):
        for k in range(4):
            for piece in pieces[k]:
                piece.finish()
    total = first[3][...].astype(f32).reshape(dims[0] * dims[1] * dims[2] * 2, 8, width)
    gain_scr[...] = jnp.sum(total, axis=0)

    weights = [first[k] for k in range(3)]

    def project(slot, at):
        return dot(normed[at, :], weights[slot][...].reshape(width, width)).astype(bf)

    def own_rows(i, carry):
        at = pl.ds(pl.multiple_of(i * QB, QB), QB)
        ext = pl.ds(pl.multiple_of(WINDOW + i * QB, QB), QB)
        normed[ext, :] = norm_block(x_ref[at, :], gain_scr[0:1])
        q_scr[at, :] = project(0, ext) * jnp.asarray(0.125, bf)
        k_scr[ext, :] = project(1, ext)
        v_scr[ext, :] = project(2, ext)
        return carry

    def halo_rows(i, carry):
        at = pl.ds(pl.multiple_of(i * QB, QB), QB)
        pos = seq * rows - WINDOW + i * QB + lax.broadcasted_iota(jnp.int32, (QB, width), 0)
        block = jnp.where(pos >= 0, halo[at, :].astype(f32), 0.0)
        normed[at, :] = norm_block(block, gain_scr[0:1])
        k_scr[at, :] = project(1, at)
        v_scr[at, :] = project(2, at)
        return carry

    nq, pairs = rows // QB, width // 128

    def events(stage, hp, qb):
        for (part, pair, block), moves in REST_EVENTS.items():
            if (part, block) != (stage, qb):
                continue

            @pl.when(hp == pair)
            def _():
                for k, what in moves:
                    with jax.named_scope("rest_%d_%d" % (k, what + 1)):
                        advance(pieces[4 + k], what)

    lane = lax.broadcasted_iota(jnp.int32, (QB, 128), 1)

    def masks(qb):
        pos = seq * rows + qb * QB + lax.broadcasted_iota(jnp.int32, (QB, 1), 0)
        lo = lower_bounds(lengths_ref, pos, seq * rows)
        kpos = qb * QB + lax.broadcasted_iota(jnp.int32, (QB, WINDOW + QB), 1)
        qpos = WINDOW + qb * QB + lax.broadcasted_iota(jnp.int32, (QB, WINDOW + QB), 0)
        bias[qb] = jnp.where((kpos >= lo) & (kpos <= qpos), 0.0, NEG)

    low_half = lane < 64

    def both(pair):
        return jnp.where(low_half, pair[0], pair[1])

    def attend_to(at, keys, lanes, mask):
        kw, vw = k_scr[keys, lanes], v_scr[keys, lanes]
        tops, totals, found = [], [], []
        for qh in halves(q_scr[at, lanes]):
            s = dot(qh, kw, NT) + mask
            m = jnp.max(s, axis=1, keepdims=True)
            p = jnp.exp(s - m)
            tops.append(m)
            totals.append(jnp.sum(p, axis=1, keepdims=True))
            found.append(dot(p.astype(bf), vw))
        return both(tops), both(totals), both(found)

    def own_keys(hp, carry):
        lanes = pl.ds(pl.multiple_of(hp * 128, 128), 128)
        for qb in range(nq):
            events(0, hp, qb)
            at, keys = pl.ds(qb * QB, QB), pl.ds(WINDOW, (qb + 1) * QB)
            top, total, mixed = attend_to(at, keys, lanes, bias[qb, :, WINDOW - qb * QB :])
            own_top[hp, at, :] = top
            own_total[hp, at, :] = total
            own_mixed[at, lanes] = mixed
        return carry

    def halo_keys(hp, carry):
        lanes = pl.ds(pl.multiple_of(hp * 128, 128), 128)
        for qb in range(nq):
            events(1, hp, qb)
            at, keys = pl.ds(qb * QB, QB), pl.ds(qb * QB, WINDOW - qb * QB)
            top, total, mixed = attend_to(at, keys, lanes, bias[qb, :, : WINDOW - qb * QB])
            before = own_top[hp, at, :]
            highest = jnp.maximum(before, top)
            by_own, by_halo = jnp.exp(before - highest), jnp.exp(top - highest)
            total = own_total[hp, at, :] * by_own + total * by_halo
            mixed = own_mixed[at, lanes] * by_own + mixed * by_halo
            o_ref[at, lanes] = (mixed * (1.0 / total)).astype(bf)
            logs = (highest + jnp.log(total)).T
            lse_ref[hp, 0:1, at] = logs[0:1]
            lse_ref[hp, 1:2, at] = logs[64:65]
        return carry

    with jax.named_scope("own_rows"):
        lax.fori_loop(0, nq, own_rows, 0)
        for qb in range(nq):
            masks(qb)
    with jax.named_scope("own_keys"):
        lax.fori_loop(0, pairs, own_keys, 0)
    with jax.named_scope("wait_halo"):

        @pl.when(seq >= 1)
        def _():
            for copy in direct:
                copy.wait_recv()

        pl.when(seq >= 2)(far.wait_recv)
    with jax.named_scope("halo_rows"):
        lax.fori_loop(0, WINDOW // QB, halo_rows, 0)
    saved = [
        pltpu.make_async_copy(a, b, out_sem.at[n])
        for n, (a, b) in enumerate(
            zip([q_scr, k_scr, v_scr, normed] + first[:3] + [gain_scr], [q_out, k_out, v_out, n_out] + w_outs)
        )
    ]
    for copy in saved:
        copy.start()
    with jax.named_scope("halo_keys"):
        lax.fori_loop(0, pairs, halo_keys, 0)
    with jax.named_scope("flip_keys"):
        flipped[...] = k_scr[...].T
        saved.append(pltpu.make_async_copy(flipped, flip_out, out_sem.at[8]))
        saved[-1].start()
    with jax.named_scope("rest_end"):
        for piece in pieces[5]:
            piece.advance(0, False)
        for k in (7, 4):
            advance(pieces[k], 2)
        for k in range(4, 8):
            for piece in pieces[k]:
                piece.finish((0,) if k == 5 else (0, 1, 2))
        pl.when(has_far)(far.wait_send)
        pl.when(has_next)(direct[1].wait_send)
        pl.when(has_next)(direct[2].wait_send)
        pl.when(even_next)(direct[0].wait_send)
        pl.when(odd_next)(aside.wait_send)
        pl.when(relays)(onward.wait_send)
        for copy in saved:
            copy.wait()


def front(lengths, x, gains, w_qkv, others, dims, count):
    rows, width = x.shape
    shard = w_qkv.shape[1]
    ext = WINDOW + rows
    shapes = [(2 * shard, width)] * 3 + [(16, width)] + [(2 * w.shape[0], w.shape[1]) for w in others]
    copies = copies_of(dims)
    vmem = pl.BlockSpec(memory_space=pltpu.VMEM)
    hbm = pl.BlockSpec(memory_space=pl.ANY)
    dma = pltpu.SemaphoreType.DMA
    count_pieces = sum(len(halves_of(s)) for s in shapes)
    nh, nq = width // 128, rows // QB
    sds = jax.ShapeDtypeStruct
    got = pl.pallas_call(
        functools.partial(front_kernel, dims, shapes, count),
        in_specs=[pl.BlockSpec(memory_space=pltpu.SMEM)] + [vmem] * 7,
        out_specs=[vmem] * 2 + [hbm] * 13,
        out_shape=[
            sds((rows, width), bf), sds((nh, 8, rows), f32),
            sds((rows, width), bf), sds((ext, width), bf), sds((ext, width), bf), sds((ext, width), bf),
        ]
        + [sds(dims + shapes[0], bf)] * 3 + [sds((8, width), f32)]
        + [sds(dims + s, bf) for s in shapes[4:]] + [sds((width, ext), bf)],
        scratch_shapes=[
            pltpu.VMEM((WINDOW, width), bf), pltpu.VMEM((rows // 2, width), bf), pltpu.VMEM((ext, width), bf),
            pltpu.VMEM((rows, width), bf),
            pltpu.VMEM((ext, width), bf), pltpu.VMEM((ext, width), bf), pltpu.VMEM((8, width), f32),
            pltpu.VMEM((8, width), f32), pltpu.VMEM((nq, QB, WINDOW + QB), f32),
            pltpu.VMEM((rows, width), f32), pltpu.VMEM((nh, rows, 128), f32), pltpu.VMEM((nh, rows, 128), f32),
            pltpu.VMEM((width, ext), bf),
        ]
        + [pltpu.VMEM(s, f32) for s in shapes]
        + [pltpu.VMEM(s, bf) for s in shapes]
        + [pltpu.VMEM(dims + s, bf) for s in shapes[:4]]
        + [
            dma((8,)), dma((8,)), dma((count_pieces, copies)), dma((count_pieces, copies)), dma((8,)),
            dma((6,)), dma((5,)), dma((9,)),
        ],
        compiler_params=pltpu.CompilerParams(
            collective_id=1, has_side_effects=True, vmem_limit_bytes=63 * 2**20
        ),
        cost_estimate=pl.CostEstimate(flops=4 * rows * 1792 * 768 * 3, bytes_accessed=14 * 2**20, transcendentals=0),
        name="front",
    )(lengths, x, gains, w_qkv, *others)
    return got


def piece_cuts(shape):
    return [(pl.ds(*rows), pl.ds(*cols)) for rows, cols in halves_of(shape)]


class Collapse:
    def __init__(self, dims, place, shape, turn, grad, out, buffers, send, recv):
        self.dims, self.place, self.shape = dims, place, shape
        self.grad, self.out, self.send, self.recv = grad, out, send, recv
        self.acc, self.box0, self.box1, self.box2, self.box3, self.fin, self.box4 = buffers
        z, y, x, c = place
        far_x, far_y = device_at(dims, (z, y, 1 - x, c)), device_at(dims, (z, 1 - y, x, c))
        every = slice(None)
        by_x = [(far_x, (every, every, 1 - x), (every, every, x)), (far_y, (every, 1 - y, x), (every, y, x))]
        by_y = [(far_y, (every, 1 - y, every), (every, y, every)), (far_x, (every, y, 1 - x), (every, y, x))]
        ways = [by_x, by_y] if turn == 0 else [by_y, by_x]
        self.pieces = list(zip(piece_cuts(shape), ways))

    def columns(self, core):
        half = self.shape[1] // 2
        return pl.ds(pl.multiple_of(core * half, 128), half)

    def copy(self, slot, source, target, device):
        return pltpu.make_async_remote_copy(
            src_ref=source, dst_ref=target, send_sem=self.send.at[slot], recv_sem=self.recv.at[slot],
            device_id=device, device_id_type=MESH,
        )

    def copies(self, stage):
        z, y, x, c = self.place
        mate = device_at(self.dims, sibling(self.place))
        every = slice(None)
        if stage == 0:
            source = self.grad.at[every, every, every, every, self.columns(1 - c)]
            return [self.copy(0, source, self.box0, mate)]
        if stage == 4:
            half = self.shape[0] // 2
            source = self.fin.at[pl.ds(pl.multiple_of((1 - c) * half, 8), half)]
            return [self.copy(1, source, self.box4, mate)]
        made = []
        for at, (cut, ways) in enumerate(self.pieces):
            first = 2 + at * (2 + self.dims[0] - 1)
            if stage in (1, 2):
                device, give, _ = ways[stage - 1]
                box = (self.box1 if stage == 1 else self.box2).at[(every,) * (3 - stage) + cut]
                made.append(self.copy(first + stage - 1, self.acc.at[give + cut], box, device))
            else:
                for by in range(1, self.dims[0]):
                    to = lax.rem(z + by, self.dims[0])
                    made.append(
                        self.copy(
                            first + 1 + by, self.acc.at[(to, y, x) + cut], self.box3.at[(by - 1,) + cut],
                            device_at(self.dims, (to, y, x, c)),
                        )
                    )
        return made

    def local(self, sem):
        if self.grad.shape == self.acc.shape:
            return pltpu.make_async_copy(self.grad, self.acc, sem)
        every = slice(None)
        source = self.grad.at[every, every, every, every, self.columns(self.place[3])]
        return pltpu.make_async_copy(source, self.acc, sem)

    def start(self, stage):
        for copy in self.copies(stage):
            copy.start()

    def add(self, stage):
        for copy in self.copies(stage):
            copy.wait_recv()
        z, y, x, c = self.place
        dims = self.dims
        if stage == 0:

            def body(i, carry):
                a, b, d = i // (dims[1] * dims[2]), lax.rem(i // dims[2], dims[1]), lax.rem(i, dims[2])
                self.acc[a, b, d] = self.acc[a, b, d] + self.box0[a, b, d]
                return carry

            lax.fori_loop(0, dims[0] * dims[1] * dims[2], body, 0)
        elif stage == 1:
            for cut, ways in self.pieces:
                by_x = not isinstance(ways[0][2][2], slice)

                def body(i, carry):
                    a, b = i // 2, lax.rem(i, 2)
                    at = ((a, b, x) if by_x else (a, y, b)) + cut
                    self.acc[at] = self.acc[at] + self.box1[(a, b) + cut]
                    return carry

                lax.fori_loop(0, dims[0] * 2, body, 0)
        elif stage == 2:

            def body(a, carry):
                self.acc[a, y, x] = self.acc[a, y, x] + self.box2[a]
                return carry

            lax.fori_loop(0, dims[0], body, 0)
        elif stage == 3:
            total = self.acc[z, y, x].astype(f32)
            for by in range(1, dims[0]):
                total = total + self.box3[by - 1].astype(f32)
            self.fin[...] = total
        else:
            half = self.shape[0] // 2
            mine = self.fin[pl.ds(pl.multiple_of(c * half, 8), half)]
            other = self.box4[...]
            width = self.shape[1] // 2
            self.out[:, :width] = jnp.where(c == 0, mine, other)
            self.out[:, width:] = jnp.where(c == 0, other, mine)

    def finish(self, stages=(0, 1, 2, 3, 4)):
        for stage in stages:
            for copy in self.copies(stage):
                copy.wait_send()


class EarlyCollapse(Collapse):
    def trade(self, given, send, recv):
        mate = device_at(self.dims, sibling(self.place))
        self.swaps = [
            pltpu.make_async_remote_copy(
                src_ref=given.at[j], dst_ref=self.box0.at[j], send_sem=send.at[j], recv_sem=recv.at[j],
                device_id=mate, device_id_type=MESH,
            )
            for j in range(self.dims[0])
        ]

    def copies(self, stage):
        return self.swaps if stage == 0 else super().copies(stage)


def collapse_scratch(dims, shapes, resumed=()):
    found = []
    for k, (rows, cols) in enumerate(shapes):
        half = cols // 2
        first = (16, 128) if k in resumed else None
        found += [
            pltpu.VMEM(dims + (rows, half), bf),
            pltpu.VMEM(first or dims + (rows, half), bf),
            pltpu.VMEM(first or (dims[0], 2, rows, half), bf),
            pltpu.VMEM((dims[0], rows, half), bf),
            pltpu.VMEM((dims[0] - 1, rows, half), bf),
            pltpu.VMEM((rows, half), f32),
            pltpu.VMEM((rows // 2, half), f32),
        ]
    dma = pltpu.SemaphoreType.DMA
    n = len(shapes)
    slots = 2 + 2 * (2 + dims[0] - 1)
    return found + [dma((n, slots)), dma((n, slots)), dma((n,))]


def collapses_of(dims, place, shapes, grads, outs, scratch):
    n = len(shapes)
    send, recv, local_sem = scratch[7 * n :]
    made = [
        Collapse(dims, place, shapes[k], k % 2, grads[k], outs[k], scratch[7 * k : 7 * k + 7], send.at[k], recv.at[k])
        for k in range(n)
    ]
    return made, [made[k].local(local_sem.at[k]) for k in range(n)]


def run_collapse(sums, locals_, k, stage):
    if stage < 0:
        locals_[k].start()
        sums[k].start(0)
        return
    if stage == 0:
        locals_[k].wait()
    sums[k].add(stage)
    if stage < 4:
        sums[k].start(stage + 1)


def back_kernel(lo_ref, q_ref, do_ref, o_ref, lse_ref, k_ref, v_ref, dq_ref, dk_ref, dv_ref, bias, dk_acc, dv_acc):
    hp, qb = pl.program_id(0), pl.program_id(1)
    span = WINDOW + QB
    start = pl.multiple_of(qb * QB, QB)

    @pl.when(hp == 0)
    def _():
        base = qb * QB
        kpos = base + lax.broadcasted_iota(jnp.int32, (span, QB), 0)
        qpos = WINDOW + base + lax.broadcasted_iota(jnp.int32, (span, QB), 1)
        ok = (kpos >= lo_ref[...]) & (kpos <= qpos)
        bias[qb] = jnp.where(ok, 0.0, NEG)

    @pl.when(qb == 0)
    def _():
        dk_acc[...] = jnp.zeros_like(dk_acc)
        dv_acc[...] = jnp.zeros_like(dv_acc)

    q_heads = halves(q_ref[...])
    do = do_ref[...]
    d_heads = halves(do)
    prod = do.astype(f32) * o_ref[...].astype(f32)
    row = lax.broadcasted_iota(jnp.int32, (8, 128), 0)
    lane = lax.broadcasted_iota(jnp.int32, (8, 128), 1)
    pick = jnp.where(row == lane // 64, 1.0, 0.0).astype(f32)
    delta = lax.dot_general(pick, prod, NT, precision=lax.Precision.HIGHEST, preferred_element_type=f32)
    lse = lse_ref[0]
    at = pl.ds(start, span)
    kw, vw = k_ref[at, :], v_ref[at, :]
    low_p, low_s, dq = [], [], []
    for h in range(2):
        s = dot(kw, q_heads[h], NT) + bias[qb]
        p = jnp.exp(s - lse[h : h + 1])
        dp = dot(vw, d_heads[h], NT)
        ds = (p * (dp - delta[h : h + 1])).astype(bf)
        low_p.append(p.astype(bf))
        low_s.append(ds)
        dq.append(dot(ds, kw, TN))
    dv_acc[at, :] += dot(jnp.concatenate(low_p, axis=1), jnp.concatenate(d_heads, axis=0))
    dk_acc[at, :] += dot(jnp.concatenate(low_s, axis=1), jnp.concatenate(q_heads, axis=0))
    lane = lax.broadcasted_iota(jnp.int32, (QB, 128), 1)
    dq_ref[...] = (jnp.where(lane < 64, dq[0], dq[1]) * 0.125).astype(bf)

    @pl.when(qb == pl.num_programs(1) - 1)
    def _():
        dk_ref[...] = dk_acc[...].astype(bf)
        dv_ref[...] = dv_acc[...].astype(bf)


def attend_back(q, do, o, lse, k, v, lo_row):
    rows, width = q.shape
    ext = k.shape[0]
    nq, nh = rows // QB, width // 128
    blk = pl.BlockSpec((QB, 128), lambda h, i: (i, h))
    full = pl.BlockSpec((ext, 128), lambda h, i: (0, h))
    return pl.pallas_call(
        back_kernel,
        grid=(nh, nq),
        in_specs=[pl.BlockSpec((1, QB), lambda h, i: (0, i)), blk, blk, blk]
        + [pl.BlockSpec((1, 8, QB), lambda h, i: (h, 0, i)), full, full],
        out_specs=[blk, full, full],
        out_shape=[
            jax.ShapeDtypeStruct((rows, width), bf),
            jax.ShapeDtypeStruct((ext, width), bf),
            jax.ShapeDtypeStruct((ext, width), bf),
        ],
        scratch_shapes=[
            pltpu.VMEM((nq, WINDOW + QB, QB), f32),
            pltpu.VMEM((ext, 128), f32),
            pltpu.VMEM((ext, 128), f32),
        ],
        compiler_params=pltpu.CompilerParams(vmem_limit_bytes=56 * 2**20),
        name="attend_back",
    )(lo_row, q, do, o, lse, k, v)


SUM_EVENTS = {
    (0, 1): ((2, 2), (1, 0), (0, 0)),
    (0, 3): ((1, 1), (2, 3)),
    (0, 4): ((0, 1), (1, 2), (2, 4)),
    (0, 5): ((0, 2),),
    (1, 2): ((1, 4), (0, 4)),
}


def back_kernel_paired(dims, shapes, count, lengths_ref, lse_ref, delta_ref, *refs):
    n = len(shapes)
    names = iter(refs)
    take = lambda k: [next(names) for _ in range(k)]
    sources = take(7)
    grads = take(n)
    dq_out, dk_out, dv_out, near_out, rest_out = take(5)
    sums_out = take(n)
    q, do, k, v, flipped, wk, wv = buffers = take(7)
    dk, dv, dq_acc, dk_acc, dv_acc, bias = take(6)
    load_sem, out_sem, back_send, back_recv = take(4)
    scratch = list(names)

    place = my_place(dims)
    seq, item = lax.axis_index("seq"), lax.axis_index("item")
    rows, width = q.shape
    nq, pairs = rows // QB, width // 128
    loads = [pltpu.make_async_copy(a, b, load_sem.at[m]) for m, (a, b) in enumerate(zip(sources, buffers))]
    for load in loads[:5]:
        load.start()
    ahead, behind = (lax.rem(seq + 1, count), item), (lax.rem(seq + count - 1, count), item)
    with jax.named_scope("masks"):
        for qb in range(nq):
            pos = seq * rows + qb * QB + lax.broadcasted_iota(jnp.int32, (1, QB), 1)
            lo = lower_bounds(lengths_ref, pos, seq * rows)
            kpos = qb * QB + lax.broadcasted_iota(jnp.int32, (WINDOW + QB, QB), 0)
            qpos = WINDOW + qb * QB + lax.broadcasted_iota(jnp.int32, (WINDOW + QB, QB), 1)
            bias[qb] = jnp.where((kpos >= lo) & (kpos <= qpos), 0.0, NEG).astype(bf)
    with jax.named_scope("meet"):
        meet(peers(dims, place) + [ahead, behind])
    sums, locals_ = collapses_of(dims, place, shapes, grads, sums_out, scratch)
    locals_[2].start()

    with jax.named_scope("load"):
        locals_[2].wait()
        sums[2].start(2)
        for load in loads[:5]:
            load.wait()
        for a in (1, 0):
            run_collapse(sums, locals_, a, -1)
        for load in loads[5:]:
            load.start()

    def events(part, hp):
        for (when, pair), moves in SUM_EVENTS.items():
            if when != part:
                continue

            @pl.when(hp == pair)
            def _():
                for a, stage in moves:
                    with jax.named_scope("reduce_%d_%d" % (a, stage + 1)):
                        run_collapse(sums, locals_, a, stage)

    half = lax.broadcasted_iota(jnp.int32, (128, QB), 0)

    def block(hp, lanes, at, keys, mask):
        q_heads, d_heads = halves(q[at, lanes]), halves(do[at, lanes])
        lse, delta = lse_ref[hp, :, at], delta_ref[hp, :, at]
        kw, vw = k[keys, lanes], v[keys, lanes]
        low_p, low_s, found = [], [], []
        for h in range(2):
            s = dot(kw, q_heads[h], NT) + mask.astype(f32)
            p = jnp.exp(s - lse[h : h + 1])
            dp = dot(vw, d_heads[h], NT)
            ds = (p * (dp - delta[h : h + 1])).astype(bf)
            low_p.append(p.astype(bf))
            low_s.append(ds)
            found.append(dot(flipped[lanes, keys], ds))
        dv_part = dot(jnp.concatenate(low_p, axis=1), jnp.concatenate(d_heads, axis=0))
        dk_part = dot(jnp.concatenate(low_s, axis=1), jnp.concatenate(q_heads, axis=0))
        return jnp.where(half < 64, found[0], found[1]).T, dk_part, dv_part

    early = nq // 2
    reach = early * QB

    def halo_keys(hp, carry):
        events(0, hp)
        lanes = pl.ds(pl.multiple_of(hp * 128, 128), 128)
        for qb in range(nq):
            at, size = pl.ds(qb * QB, QB), WINDOW + QB if qb < early else WINDOW - qb * QB
            keys = pl.ds(qb * QB, size)
            dq_part, dk_part, dv_part = block(hp, lanes, at, keys, bias[qb, :size, :])
            if qb < early:
                q[at, lanes] = (dq_part * 0.125).astype(bf)
            else:
                dq_acc[pl.ds(qb * QB - reach, QB), lanes] = dq_part
            for total, part in ((dk_acc, dk_part), (dv_acc, dv_part)):
                if qb == 0:
                    total[keys, :] = part
                    total[size:, :] = jnp.zeros((total.shape[0] - size, 128), f32)
                else:
                    total[keys, :] += part
        dk[0 : WINDOW + reach, lanes] = dk_acc[...].astype(bf)
        dv[0 : WINDOW + reach, lanes] = dv_acc[...].astype(bf)
        return carry

    with jax.named_scope("halo_keys"):
        lax.fori_loop(0, pairs, halo_keys, 0)

    def halo_rows(i, carry):
        at = pl.ds(pl.multiple_of(i * QB, QB), QB)
        total = dot(dk[at, :], wk[...].reshape(width, width), NT) + dot(dv[at, :], wv[...].reshape(width, width), NT)
        k[at, :] = total.astype(bf)
        return carry

    lower, part = WINDOW - rows, rows // 4
    returned = [
        pltpu.make_async_remote_copy(
            src_ref=k.at[pl.ds(lower + m * part, part)], dst_ref=near_out.at[pl.ds(m * part, part)],
            send_sem=back_send.at[m], recv_sem=back_recv.at[m], device_id=behind, device_id_type=MESH,
        )
        for m in range(3)
    ]
    with jax.named_scope("halo_rows"):
        for load in loads[5:]:
            load.wait()
        for m in range(3):
            lax.fori_loop((lower + m * part) // QB, (lower + (m + 1) * part) // QB, halo_rows, 0)
            pl.when(seq >= 1)(returned[m].start)
        lax.fori_loop(0, lower // QB, halo_rows, 0)
        lax.fori_loop((lower + 3 * part) // QB, WINDOW // QB, halo_rows, 0)
        rest = [
            pltpu.make_async_copy(k.at[pl.ds(0, lower)], rest_out.at[pl.ds(0, lower)], out_sem.at[0]),
            pltpu.make_async_copy(k.at[pl.ds(lower + 3 * part, part)], rest_out.at[pl.ds(lower, part)], out_sem.at[1]),
        ]
        rest += [
            pltpu.make_async_copy(a.at[pl.ds(0, WINDOW)], b.at[pl.ds(0, WINDOW)], out_sem.at[2 + m])
            for m, (a, b) in enumerate([(dk, dk_out), (dv, dv_out)])
        ]
        for copy in rest:
            copy.start()
    for a in (1, 0):
        with jax.named_scope("reduce_%d_4" % a):
            run_collapse(sums, locals_, a, 3)

    def own_keys(hp, carry):
        events(1, hp)
        lanes = pl.ds(pl.multiple_of(hp * 128, 128), 128)
        for qb in reversed(range(early, nq)):
            at, size = pl.ds(qb * QB, QB), (qb + 1) * QB
            keys, own = pl.ds(WINDOW, size), pl.ds(0, size)
            dq_part, dk_part, dv_part = block(hp, lanes, at, keys, bias[qb, WINDOW - qb * QB :, :])
            q[at, lanes] = ((dq_acc[pl.ds(qb * QB - reach, QB), lanes] + dq_part) * 0.125).astype(bf)
            if qb == nq - 1:
                dk_acc[own, :] = dk_part
                dv_acc[own, :] = dv_part
            else:
                dk_acc[own, :] += dk_part
                dv_acc[own, :] += dv_part
        for total, kept in ((dk_acc, dk), (dv_acc, dv)):
            first, second = pl.ds(WINDOW, reach), pl.ds(WINDOW + reach, rows - reach)
            kept[first, lanes] = (total[0:reach, :] + kept[first, lanes].astype(f32)).astype(bf)
            kept[second, lanes] = total[reach:rows, :].astype(bf)
        return carry

    with jax.named_scope("own_keys"):
        lax.fori_loop(0, pairs, own_keys, 0)
    own = pl.ds(WINDOW, rows)
    stores = rest + [
        pltpu.make_async_copy(a, b, out_sem.at[4 + m])
        for m, (a, b) in enumerate([(q, dq_out), (dk.at[own], dk_out.at[own]), (dv.at[own], dv_out.at[own])])
    ]
    for store in stores[4:]:
        store.start()
    with jax.named_scope("finish"):
        for one in sums[:2]:
            one.finish()
        sums[2].finish((2, 3, 4))
        for store in stores:
            store.wait()

        for copy in returned:
            pl.when(seq >= 1)(copy.wait_send)
            pl.when(seq + 1 < count)(copy.wait_recv)


def back(lengths, lse, delta, arrays, grads, dims, count):
    q, do, k, v, flipped, wk, wv = arrays
    rows, width = q.shape
    ext = k.shape[0]
    nq = rows // QB
    shapes = [g.shape[3:] for g in grads]
    shapes[2] = (shapes[2][0], 2 * shapes[2][1])
    vmem = pl.BlockSpec(memory_space=pltpu.VMEM)
    hbm = pl.BlockSpec(memory_space=pl.ANY)
    dma = pltpu.SemaphoreType.DMA
    sds = jax.ShapeDtypeStruct
    part = rows // 4
    got = pl.pallas_call(
        functools.partial(back_kernel_paired, dims, shapes, count),
        in_specs=[pl.BlockSpec(memory_space=pltpu.SMEM), vmem, vmem] + [hbm] * (7 + len(grads)),
        out_specs=[hbm] * 5 + [vmem] * len(grads),
        out_shape=[
            sds((rows, width), bf), sds((ext, width), bf), sds((ext, width), bf),
            sds((3 * part, width), bf), sds((WINDOW - 3 * part, width), bf),
        ]
        + [sds((r // 2, c), f32) for r, c in shapes],
        scratch_shapes=[pltpu.VMEM(a.shape, bf) for a in arrays]
        + [
            pltpu.VMEM((ext, width), bf), pltpu.VMEM((ext, width), bf), pltpu.VMEM((rows // 2, width), f32),
            pltpu.VMEM((WINDOW + rows // 2, 128), f32), pltpu.VMEM((WINDOW + rows // 2, 128), f32),
            pltpu.VMEM((nq, WINDOW + QB, QB), bf),
            dma((7,)), dma((7,)), dma((3,)), dma((3,)),
        ]
        + collapse_scratch(dims, shapes, (2,)),
        compiler_params=pltpu.CompilerParams(
            collective_id=3, has_side_effects=True, vmem_limit_bytes=63 * 2**20
        ),
        name="back",
    )(lengths, lse, delta, *arrays, *grads)
    return got[:5], got[5:]


GELU_A, GELU_B = 0.7978845608028654, 0.044715
MB = 512
PROJ_STEPS = (0, 1)
GATHER_STEP = 0
DOWN_STEP = 1


def middle_kernel(dims, proj_shape, wd_shape, bound_ref, cont_ref, gain_ref, *refs):
    names = iter(refs)
    take = lambda k: [next(names) for _ in range(k)]
    sources = take(8)
    y_out, p_out, dr_out, do_out, gain_out, delta_out, sum_proj, g_out, g_up, down_out = take(10)
    x, o, cot, pcot, wo, wu, wd, wp = buffers = take(8)
    n2, r1, act, slope, low_c, dyl, stage, grad_proj = take(8)
    load_sem, stage_sem, out_sem, send, recv = take(5)
    down_given, down_send, down_recv, trade_send, trade_recv, proj_send, proj_recv = take(7)
    down_buffers = take(3)
    scratch = list(names)

    place = my_place(dims)
    z, y, x_, c = place
    line = (slice(None), y, x_)
    pairs = list(zip(sources[:7], buffers[:7])) + [(sources[7].at[line], wp.at[line])]
    loads = [pltpu.make_async_copy(a, b, load_sem.at[k]) for k, (a, b) in enumerate(pairs)]
    for k in (0, 1, 4, 7, 5, 6, 3, 2):
        loads[k].start()
    with jax.named_scope("meet"):
        meet(peers(dims, place))
    total = EarlyCollapse(dims, place, proj_shape, 0, None, sum_proj, scratch[:7], scratch[7].at[0], scratch[8].at[0])
    total.trade(grad_proj, proj_send, proj_recv)

    def move_on(stage):
        total.add(stage)
        if stage < 4:
            total.start(stage + 1)


    down = EarlyCollapse(
        dims, place, wd_shape, 0, None, None, down_buffers + [None] * 4, down_send, down_recv
    )
    down.trade(down_given, trade_send, trade_recv)

    rows, width = x.shape
    chunks = wu.shape[1] // width
    gain = gain_ref[1:2]
    pieces = [
        Spread(dims, place, None, wp, pl.ds(*at), cols, order, send.at[k], recv.at[k])
        for k, (order, (at, cols)) in enumerate(zip(ORDERS, halves_of(wp.shape[3:])))
    ]
    def residual(i, carry):
        at = pl.ds(pl.multiple_of(i * MB, MB), MB)
        r = x[at, :].astype(f32) + dot(o[at, :], wo[...])
        r1[at, :] = r
        scale = lax.rsqrt(jnp.mean(r * r, axis=-1, keepdims=True) + EPSILON)
        n2[at, :] = (r * scale * gain).astype(bf)
        return carry

    with jax.named_scope("load"):
        loads[7].wait()
        for piece in pieces:
            piece.begin(1)
        for k in (0, 1, 4):
            loads[k].wait()
        lax.fori_loop(0, rows // MB, residual, 0)
        for k in (2, 3, 5, 6):
            loads[k].wait()

    def edge_of(at):
        edge = (bound_ref[:, at] * (1 - cont_ref[:, at])).astype(f32)
        return jnp.broadcast_to(edge, (8, MB)).T[:, 0:1]

    def forward(i, carry):
        at = pl.ds(pl.multiple_of(i * MB, MB), MB)
        y = r1[at, :]
        for j in range(chunks):
            cols = slice(j * width, (j + 1) * width)
            u = dot(n2[at, :], wu[:, cols])
            square = u * u
            t = jnp.tanh(GELU_A * (u + GELU_B * square * u))
            half = 0.5 * (1.0 + t)
            act[at, cols] = (u * half).astype(bf)
            slope[at, cols] = (half + 0.5 * u * (1.0 - t * t) * (GELU_A + 3.0 * GELU_A * GELU_B * square)).astype(bf)
            y = y + dot(act[at, cols], wd[cols, :])
        low_c[at, :] = (edge_of(at) * pcot[at, :].astype(f32)).astype(bf)
        dr_out[at, :] = cot[at, :].astype(f32)
        cot[at, :] = y.astype(bf)

        @pl.when(i == GATHER_STEP)
        def _():
            with jax.named_scope("proj_1"):
                for piece in pieces:
                    piece.advance(1)

        return carry

    def project(i, carry):
        at = pl.ds(pl.multiple_of(i * MB, MB), MB)
        weight = wp[...].reshape(width, wp.shape[-1])
        d = dr_out[at, :] + dot(low_c[at, :], weight, NT)
        dr_out[at, :] = d
        dyl[at, :] = d.astype(bf)
        pcot[at, :] = (edge_of(at) * dot(cot[at, :], weight)).astype(bf)
        return carry

    with jax.named_scope("forward"):
        lax.fori_loop(0, rows // MB, forward, 0)
    with jax.named_scope("proj_2"):
        for piece in pieces:
            piece.advance(2)
        for piece in pieces:
            piece.finish((1, 2))
    with jax.named_scope("project"):
        lax.fori_loop(0, rows // MB, project, 0)
    stores = [pltpu.make_async_copy(cot, y_out, out_sem.at[0]), pltpu.make_async_copy(pcot, p_out, out_sem.at[1])]
    for store in stores:
        store.start()

    flying = {}

    def emit(target, left, right):
        block = width // 2
        for j in range(left.shape[1] // block):
            for k in range(right.shape[1] // width):
                slot = emit.count % 2
                emit.count += 1
                if slot in flying:
                    flying[slot].wait()
                rows_at, cols_at = slice(j * block, (j + 1) * block), slice(k * width, (k + 1) * width)
                stage[slot] = dot(left[:, rows_at], right[:, cols_at], TN).astype(bf)
                copy = pltpu.make_async_copy(
                    stage.at[slot], target.at[pl.ds(j * block, block), pl.ds(k * width, width)], stage_sem.at[slot]
                )
                copy.start()
                flying[slot] = copy

    emit.count = 0
    with jax.named_scope("grad_proj"):
        half = proj_shape[1] // 2
        for target, core in ((grad_proj, 1 - c), (scratch[0], c)):
            cols = pl.ds(pl.multiple_of(core * half, 128), half)
            target[...] = dot(cot[...], low_c[:, cols], TN).astype(bf).reshape(target.shape)
            if target is grad_proj:
                total.start(0)
    with jax.named_scope("grad_down"):
        acc, half = down_buffers[0], width // 2
        for j in range(chunks):
            got = dot(act[:, j * width : (j + 1) * width], dyl[...], TN).astype(bf)
            left, right = got[:, :half], got[:, half:]
            acc[j] = jnp.where(c == 0, left, right).reshape(acc.shape[1:])
            down_given[j] = jnp.where(c == 0, right, left).reshape(acc.shape[1:])
            down.swaps[j].start()

    row = lax.broadcasted_iota(jnp.int32, (16, width), 0)
    lane = lax.broadcasted_iota(jnp.int32, (16, width), 1)
    heads = jnp.where(row == lane // 64, 1.0, 0.0).astype(f32)

    def backward(i, carry):
        for step, when in enumerate(PROJ_STEPS):

            @pl.when(i == when)
            def _():
                with jax.named_scope("reduce_%d" % step):
                    move_on(step)
        @pl.when(i == DOWN_STEP)
        def _():
            with jax.named_scope("down_0"):
                down.add(0)
                down.start(1)

        at = pl.ds(pl.multiple_of(i * MB, MB), MB)
        dn = jnp.zeros((MB, width), f32)
        for j in range(chunks):
            cols = slice(j * width, (j + 1) * width)
            du = (dot(dyl[at, :], wd[cols, :], NT) * slope[at, cols].astype(f32)).astype(bf)
            slope[at, cols] = du
            dn = dn + dot(du, wu[:, cols], NT)
        r = r1[at, :]
        scale = lax.rsqrt(jnp.mean(r * r, axis=-1, keepdims=True) + EPSILON)
        unit = r * scale
        by_gain = dn * gain
        inner = jnp.mean(by_gain * unit, axis=-1, keepdims=True)
        dr = dr_out[at, :] + scale * (by_gain - unit * inner)
        dr_out[at, :] = dr
        low_dr = dr.astype(bf)
        dyl[at, :] = low_dr
        low_do = dot(low_dr, wo[...], NT).astype(bf)
        x[at, :] = low_do
        delta = lax.dot_general(
            heads, low_do.astype(f32) * o[at, :].astype(f32), NT,
            precision=lax.Precision.HIGHEST, preferred_element_type=f32,
        )
        for hp in range(width // 128):
            delta_out[hp, 0:2, at] = delta[2 * hp : 2 * hp + 2]
        return carry + jnp.sum(dn * unit, axis=0, keepdims=True)

    with jax.named_scope("backward"):
        gain_out[...] = lax.fori_loop(0, rows // MB, backward, jnp.zeros((1, width), f32))
    stores.append(pltpu.make_async_copy(x, do_out, out_sem.at[2]))
    stores[-1].start()
    with jax.named_scope("grad_out"):
        move_on(2)
        emit(g_out, o, dyl)
    with jax.named_scope("grad_up"):
        emit(g_up, n2, slope)
    with jax.named_scope("down_1"):
        down.add(1)
        stores.append(pltpu.make_async_copy(down_buffers[0], down_out, out_sem.at[3]))
        stores[-1].start()
    with jax.named_scope("finish"):
        for stage in (3, 4):
            move_on(stage)
        for copy in list(flying.values()) + stores:
            copy.wait()
        total.finish()
        down.finish((0, 1))


def middle(bound, cont, gain, arrays, dims):
    x, o, cot, pcot, wo, wu, wd, wp = arrays
    rows, width = x.shape
    ff, proj = wu.shape[1], wp.shape[-1]
    copies = copies_of(dims)
    pair = width // (dims[0] * dims[1] * dims[2])
    tall = ff // (dims[0] * dims[1] * dims[2])
    down_acc = dims + (tall, width // 2)
    vmem = pl.BlockSpec(memory_space=pltpu.VMEM)
    hbm = pl.BlockSpec(memory_space=pl.ANY)
    dma = pltpu.SemaphoreType.DMA
    sds = jax.ShapeDtypeStruct
    return pl.pallas_call(
        functools.partial(middle_kernel, dims, (pair, proj), (tall, width)),
        in_specs=[vmem] * 3 + [hbm] * 8,
        out_specs=[hbm, hbm, vmem, hbm, vmem, vmem, vmem, hbm, hbm, hbm],
        out_shape=[
            sds((rows, width), bf), sds((rows, proj), bf), sds((rows, width), f32), sds((rows, width), bf),
            sds((1, width), f32), sds((width // 128, 8, rows), f32), sds((pair // 2, proj), f32),
            sds(wo.shape, bf), sds(wu.shape, bf), sds(down_acc, bf),
        ],
        scratch_shapes=[pltpu.VMEM(a.shape, bf) for a in arrays]
        + [
            pltpu.VMEM((rows, width), bf), pltpu.VMEM((rows, width), f32), pltpu.VMEM((rows, ff), bf),
            pltpu.VMEM((rows, ff), bf), pltpu.VMEM((rows, proj), bf), pltpu.VMEM((rows, width), bf),
            pltpu.VMEM((2, width // 2, width), bf), pltpu.VMEM(dims + (pair, proj // 2), bf),
            dma((8,)), dma((2,)), dma((4,)), dma((2, copies)), dma((2, copies)),
            pltpu.VMEM(down_acc, bf), dma((12,)), dma((12,)), dma((dims[0],)), dma((dims[0],)),
            dma((dims[0],)), dma((dims[0],)),
            pltpu.VMEM(down_acc, bf), pltpu.VMEM(down_acc, bf), pltpu.VMEM((dims[0], 2, tall, width // 2), bf),
        ]
        + collapse_scratch(dims, [(pair, proj)]),
        compiler_params=pltpu.CompilerParams(
            collective_id=2, has_side_effects=True, vmem_limit_bytes=63 * 2**20
        ),
        name="middle",
    )(bound, cont, gain, *arrays)


ROW_OUT, ROW_UP, ROW_PROJ, ROW_DOWN, ROW_GAIN, ROW_MEAN = 3, 4, 8, 10, 11, 13
STAT_ROWS = 16
DECAY = 1.0 - STEP ** (-0.8)


def exchange_rounds(dims, place):
    z, y, x, c = place
    plane = [(1, 0), (0, 1), (1, 1)]
    rounds = [
        ([sibling(place)], c),
        ([(z, lax.rem(y + dy, 2), lax.rem(x + dx, 2), c) for dy, dx in plane], y * 2 + x),
        ([moved(dims, place, 0, by) for by in range(1, dims[0])], z),
    ]
    return [([device_at(dims, p) for p in others], number) for others, number in rounds]


def put_stats(stats, row, total, square_sum, old_rows, lane, columns):
    width = stats.shape[1]
    for j in range(total.shape[1] // width):
        stats[row + j : row + j + 1, :] = total[:, j * width : (j + 1) * width]
    value = DECAY * jnp.sum(old_rows, axis=1, keepdims=True) + (1.0 - DECAY) / columns * square_sum
    at = lax.broadcasted_iota(jnp.int32, (1, width), 1)
    stats[ROW_MEAN : ROW_MEAN + 1, :] += jnp.where(at == lane, value, 0.0)


def last_kernel(
    dims, shapes, count, x_hbm, resid_hbm, gain_ref, gain_two_ref,
    dq_hbm, dk_hbm, dv_hbm, n_hbm, wq_hbm, wk_hbm, wv_hbm, near_hbm, rest_hbm,
    sum_out, sum_proj, sum_up, sum_down, row_qkv, row_out, row_proj, row_up, row_down, *refs,
):
    names = iter(refs)
    take = lambda k: [next(names) for _ in range(k)]
    grad_ref, total_ref = take(2)
    sums_out = take(3)
    dq, dk, dv, normed, flipped, wq, wk, wv = take(8)
    own_back, near, rest, box, stats, inbox, x_ref, resid_ref = take(8)
    grads = take(3)
    load_sem, back_send, back_recv, stat_send, stat_recv = take(5)
    scratch = list(names)

    place = my_place(dims)
    seq, item = lax.axis_index("seq"), lax.axis_index("item")
    rows, width = x_ref.shape
    loads = [
        pltpu.make_async_copy(a, b, load_sem.at[n])
        for n, (a, b) in enumerate(
            [
                (rest_hbm, rest), (n_hbm, normed), (dk_hbm, dk), (dv_hbm, dv), (dq_hbm, dq),
                (wk_hbm, wk), (wv_hbm, wv), (wq_hbm, wq), (near_hbm, near),
                (x_hbm, x_ref), (resid_hbm, resid_ref),
            ]
        )
    ]
    for load in loads:
        load.start()
    ahead = [(lax.rem(seq + d, count), item) for d in (1, 2)]
    behind = [(lax.rem(seq + count - d, count), item) for d in (1, 2)]
    with jax.named_scope("meet"):
        meet(peers(dims, place) + ahead + behind + [device_at(dims, place[:1] + (1 - place[1], 1 - place[2], place[3]))])
    far = WINDOW - rows
    near_rows, far_rows = pl.ds(far, rest.shape[0] - far), pl.ds(0, far)
    returned = [
        pltpu.make_async_remote_copy(
            src_ref=rest.at[part], dst_ref=box.at[part], send_sem=back_send.at[m], recv_sem=back_recv.at[m],
            device_id=behind[m], device_id_type=MESH,
        )
        for m, part in enumerate((near_rows, far_rows))
    ]
    loads[0].wait()
    for m in range(2):
        pl.when(seq >= m + 1)(returned[m].start)

    def back_of(at):
        return dot(dk[at, :], wk[...].reshape(width, width), NT) + dot(dv[at, :], wv[...].reshape(width, width), NT)

    sums, locals_ = collapses_of(dims, place, shapes, grads, sums_out, scratch)
    with jax.named_scope("weight_gradients"):
        loads[1].wait()
        flipped[...] = normed[...].T
        for k, part in ((1, dk), (2, dv), (0, dq)):
            loads[(4, 2, 3)[k]].wait()
            base = WINDOW if k == 0 else 0
            got = dot(flipped[:, base:], part[...])
            grads[k][...] = got.astype(bf).reshape(grads[k].shape)
            run_collapse(sums, locals_, k, -1)
            if k != 1:
                run_collapse(sums, locals_, 1 if k == 2 else 2, 0)

    def own_block(i, carry):
        at = pl.ds(pl.multiple_of(i * QB, QB), QB)
        ext = pl.ds(pl.multiple_of(WINDOW + i * QB, QB), QB)
        own_back[at, :] = back_of(ext) + dot(dq[at, :], wq[...].reshape(width, width), NT)
        return carry

    with jax.named_scope("own_rows"):
        for load in loads[5:]:
            load.wait()
        lax.fori_loop(0, rows // QB, own_block, 0)

    stats[0] = jnp.zeros_like(stats[0])
    held = stats.at[0]
    held[ROW_GAIN + 1 : ROW_GAIN + 2, :] = gain_two_ref[...]

    def add_stats(row, grad, old_rows, lane):
        square = grad * grad + TINY_SQUARE
        total = jnp.sum(square, axis=0, keepdims=True)
        put_stats(held, row, total, jnp.sum(total, axis=1, keepdims=True), old_rows, lane, grad.shape[1])

    with jax.named_scope("small_sums"):
        add_stats(ROW_OUT, sum_out[...], row_out[...], 3)
        add_stats(ROW_UP, sum_up[...], row_up[...], 4)
        add_stats(ROW_PROJ, sum_proj[...], row_proj[...], 5)
        add_stats(ROW_DOWN, sum_down[...], row_down[...], 6)

    for stage in range(5):
        with jax.named_scope("reduce_%d" % stage):
            for k in (1, 2, 0) if stage else (0,):
                run_collapse(sums, locals_, k, stage)
    for k in range(3):
        add_stats(k, sums_out[k][...], row_qkv[k : k + 1, :], k)

    with jax.named_scope("rows_returned"):

        @pl.when(seq + 1 < count)
        def _():
            returned[0].wait_recv()
            size = near.shape[0]
            own_back[0:size, :] += near[...].astype(f32)
            own_back[size:, :] += box[near_rows, :].astype(f32)

        @pl.when(seq + 2 < count)
        def _():
            returned[1].wait_recv()
            own_back[rows - far :, :] += box[far_rows, :].astype(f32)

    gain = gain_ref[0:1]

    def input_block(i, total):
        at = pl.ds(pl.multiple_of(i * QB, QB), QB)
        x = x_ref[at, :].astype(f32)
        scale = lax.rsqrt(jnp.mean(x * x, axis=-1, keepdims=True) + EPSILON)
        back = own_back[at, :]
        unit = x * scale
        by_gain = back * gain
        inner = jnp.mean(by_gain * unit, axis=-1, keepdims=True)
        grad_ref[at, :] = (resid_ref[at, :] + scale * (by_gain - unit * inner)).astype(bf)
        return total + jnp.sum(back * unit, axis=0, keepdims=True)

    with jax.named_scope("input_gradient"):
        total = lax.fori_loop(0, rows // QB, input_block, jnp.zeros((1, width), f32))
    held[ROW_GAIN : ROW_GAIN + 1, :] = total

    rounds = exchange_rounds(dims, place)
    z, y, x, c = place
    senders = [
        [1 - c],
        [lax.rem(y + dy, 2) * 2 + lax.rem(x + dx, 2) for dy, dx in ((1, 0), (0, 1), (1, 1))],
        [lax.rem(z + dims[0] - by, dims[0]) for by in range(1, dims[0])],
    ]

    with jax.named_scope("exchange_sums"):
        slot = 0
        for stage, (others, number) in enumerate(rounds):
            copies = []
            for other in others:
                copies.append(
                    pltpu.make_async_remote_copy(
                        src_ref=stats.at[stage], dst_ref=inbox.at[slot],
                        send_sem=stat_send.at[slot], recv_sem=stat_recv.at[slot],
                        device_id=other, device_id_type=MESH,
                    )
                )
                copies[-1].start()
                slot += 1
            for copy in copies:
                copy.wait()
            base = slot - len(others)
            total = jnp.zeros_like(stats[0])
            for member in range(len(others) + 1):
                term = stats[stage]
                for m in range(len(others)):
                    term = jnp.where(senders[stage][m] == member, inbox[base + m], term)
                total = total + term
            stats[stage + 1] = total
        total_ref[...] = stats[len(rounds)]
    for one in sums:
        one.finish()
    for m in range(2):
        pl.when(seq >= m + 1)(returned[m].wait_send)


def last(x, resid_grad, gain, gain_two, dq, dk, dv, normed, weights, returned, sums, old_rows, dims, count):
    rows, width = x.shape
    ext = normed.shape[0]
    shapes = [w.shape[3:] for w in weights]
    slots = 4 + dims[0] - 1
    vmem = pl.BlockSpec(memory_space=pltpu.VMEM)
    hbm = pl.BlockSpec(memory_space=pl.ANY)
    dma = pltpu.SemaphoreType.DMA
    sds = jax.ShapeDtypeStruct
    got = pl.pallas_call(
        functools.partial(last_kernel, dims, shapes, count),
        in_specs=[hbm] * 2 + [vmem] * 2 + [hbm] * 9 + [vmem] * 9,
        out_specs=[vmem] * 5,
        out_shape=[sds((rows, width), bf), sds((STAT_ROWS, width), f32)] + [sds((r // 2, c), f32) for r, c in shapes],
        scratch_shapes=[
            pltpu.VMEM((rows, width), bf), pltpu.VMEM((ext, width), bf), pltpu.VMEM((ext, width), bf),
            pltpu.VMEM((ext, width), bf), pltpu.VMEM((width, ext), bf),
        ]
        + [pltpu.VMEM(w.shape, bf) for w in weights]
        + [pltpu.VMEM((rows, width), f32)]
        + [pltpu.VMEM(a.shape, bf) for a in (*returned, returned[1])]
        + [pltpu.VMEM((4, STAT_ROWS, width), f32), pltpu.VMEM((slots, STAT_ROWS, width), f32)]
        + [pltpu.VMEM((rows, width), bf), pltpu.VMEM((rows, width), f32)]
        + [pltpu.VMEM(w.shape, bf) for w in weights]
        + [dma((11,)), dma((2,)), dma((2,)), dma((slots,)), dma((slots,))]
        + collapse_scratch(dims, shapes),
        compiler_params=pltpu.CompilerParams(
            collective_id=4, has_side_effects=True, vmem_limit_bytes=61 * 2**20
        ),
        name="last",
    )(x, resid_grad, gain, gain_two, dq, dk, dv, normed, *weights, *returned, *sums, *old_rows)
    return got[0], got[1], got[2:]


def update_kernel(
    place_ref, total_ref, gains_ref, gain_var_ref,
    w_qkv, w_out, w_proj, w_up, w_down, s_q, s_k, s_v, s_out, s_proj, s_up, s_down,
    row_qkv, row_out, row_proj, row_up, row_down, col_qkv, col_out, col_proj, col_up, col_down,
    y_ref, p_ref, d_ref, g_qkv, g_out, g_proj, g_up, g_down, g_gains, n_qkv, n_out, n_proj, n_up, n_down, n_gains,
    r_qkv, r_out, r_proj, r_up, r_down, c_qkv, c_out, c_proj, c_up, c_down, gain_var_new,
    y_out, p_out, d_out, flat, tall, y_held, p_held, d_held, pass_sem,
):
    held = (y_held, p_held, d_held)
    taken = [pltpu.make_async_copy(a, b, pass_sem.at[n]) for n, (a, b) in enumerate(zip((y_ref, p_ref, d_ref), held))]
    passed = [pltpu.make_async_copy(a, b, pass_sem.at[3 + n]) for n, (a, b) in enumerate(zip(held, (y_out, p_out, d_out)))]
    for copy in taken:
        copy.start()
    shard = row_out.shape[1]
    shard_down = row_down.shape[1]
    width = total_ref.shape[1]
    flat[...] = jnp.zeros_like(flat)
    flat[0:3, :shard] = row_qkv[...]
    flat[3:4, :shard] = row_out[...]
    flat[4:5, :shard] = row_up[...]
    flat[5:6, :shard] = row_proj[...]
    flat[6:7, :shard_down] = row_down[...]
    olds = flat[...].T
    tall[...] = jnp.zeros_like(tall)

    def one(weight, grad, lane, row, old_col, rows_all, g_out_, n_out_, c_out_):
        count, columns = grad.shape
        square = grad * grad + TINY_SQUARE
        row_new = DECAY * olds[:count, lane : lane + 1] + (1.0 - DECAY) * jnp.mean(square, axis=1, keepdims=True)
        tall[:count, lane : lane + 1] = row_new
        parts = [total_ref[row + j : row + j + 1, :] for j in range(columns // width)]
        col_total = parts[0] if len(parts) == 1 else jnp.concatenate(parts, axis=1)
        col_new = DECAY * old_col + (1.0 - DECAY) * col_total / rows_all
        mean = total_ref[ROW_MEAN : ROW_MEAN + 1, lane : lane + 1] / rows_all
        second = row_new * col_new / mean
        g_out_[...] = grad
        n_out_[...] = weight - WEIGHT_RATE * grad * lax.rsqrt(second)
        c_out_[...] = col_new.reshape(c_out_.shape)

    for k, grad in enumerate((s_q, s_k, s_v)):
        one(w_qkv[k], grad[...], k, k, col_qkv[k : k + 1, :], width, g_qkv.at[k], n_qkv.at[k], c_qkv.at[k : k + 1])
    ff = col_up.shape[0]
    one(w_out[...], s_out[...], 3, ROW_OUT, col_out[...].reshape(1, width), width, g_out, n_out, c_out)
    one(w_up[...], s_up[...], 4, ROW_UP, col_up[...].reshape(1, ff), width, g_up, n_up, c_up)
    one(w_proj[...], s_proj[...], 5, ROW_PROJ, col_proj[...].reshape(1, -1), width, g_proj, n_proj, c_proj)
    one(w_down[...], s_down[...], 6, ROW_DOWN, col_down[...].reshape(1, width), ff, g_down, n_down, c_down)
    for copy, onward in zip(taken, passed):
        copy.wait()
        onward.start()
    news = tall[...].T
    r_qkv[...] = news[0:3, :shard]
    r_out[...] = news[3:4, :shard]
    r_up[...] = news[4:5, :shard]
    r_proj[...] = news[5:6, :shard]
    r_down[...] = news[6:7, :shard_down]

    gain_sums = pltpu.roll(total_ref[8:16, :], width - place_ref[0] * shard, 1)
    sums = gain_sums[ROW_GAIN - 8 : ROW_GAIN - 6, :shard]
    var = DECAY * gain_var_ref[...] + (1.0 - DECAY) * (sums * sums + TINY_SQUARE)
    g_gains[...] = sums
    gain_var_new[...] = var
    n_gains[...] = gains_ref[...] - GAIN_RATE * sums * lax.rsqrt(var)
    for copy in passed:
        copy.wait()


def update(place, totals, gains, gain_var, weights, sums, rows, cols, results):
    vmem = pl.BlockSpec(memory_space=pltpu.VMEM)
    like = lambda arrays: [jax.ShapeDtypeStruct(a.shape, f32) for a in arrays]
    outs = like(weights) + like([gains]) + like(weights) + like([gains]) + like(rows) + like(cols) + like([gain_var])
    hbm = pl.BlockSpec(memory_space=pl.ANY)
    return pl.pallas_call(
        update_kernel,
        in_specs=[pl.BlockSpec(memory_space=pltpu.SMEM)] + [vmem] * (3 + 5 + 7 + 5 + 5) + [hbm] * 3,
        out_specs=[vmem] * len(outs) + [hbm] * 3,
        out_shape=outs + [jax.ShapeDtypeStruct(a.shape, a.dtype) for a in results],
        scratch_shapes=[pltpu.VMEM((8, 128), f32), pltpu.VMEM((128, 8), f32)]
        + [pltpu.VMEM(a.shape, a.dtype) for a in results]
        + [pltpu.SemaphoreType.DMA((6,))],
        compiler_params=pltpu.CompilerParams(vmem_limit_bytes=63 * 2**20),
        name="update",
    )(place, totals, gains, gain_var, *weights, *sums, *rows, *cols, *results)


def sum_kernel(sizes, x_ref, o_ref, inbox, send_sem, recv_sem):
    place = {name: lax.axis_index(name) for name, _ in sizes}
    partners = []
    for name, size in sizes:
        bit = 1
        while bit < size:
            mine = place[name]
            low = lax.rem(mine // bit, 2)
            other = mine + bit * (1 - 2 * low)
            partners.append(tuple(other if n == name else place[n] for n in ("seq", "item")))
            bit *= 2
    barrier = pltpu.get_barrier_semaphore()
    for partner in partners:
        pl.semaphore_signal(barrier, inc=1, device_id=partner, device_id_type=MESH)
    pl.semaphore_wait(barrier, len(partners))
    o_ref[0] = x_ref[...]
    for stage, partner in enumerate(partners):
        copy = pltpu.make_async_remote_copy(
            src_ref=o_ref.at[stage],
            dst_ref=inbox.at[stage],
            send_sem=send_sem.at[stage],
            recv_sem=recv_sem.at[stage],
            device_id=partner,
            device_id_type=MESH,
        )
        copy.start()
        copy.wait()
        o_ref[stage + 1] = o_ref[stage] + inbox[stage]


def sum_all(x, sizes):
    stages = sum(size.bit_length() - 1 for _, size in sizes)
    held = pl.pallas_call(
        functools.partial(sum_kernel, sizes),
        out_shape=jax.ShapeDtypeStruct((stages + 1,) + x.shape, x.dtype),
        in_specs=[pl.BlockSpec(memory_space=pltpu.VMEM)],
        out_specs=pl.BlockSpec(memory_space=pltpu.VMEM),
        scratch_shapes=[
            pltpu.VMEM((stages,) + x.shape, x.dtype),
            pltpu.SemaphoreType.DMA((stages,)),
            pltpu.SemaphoreType.DMA((stages,)),
        ],
        compiler_params=pltpu.CompilerParams(collective_id=0, has_side_effects=True),
        name="sum_all",
    )(x)
    return held[stages]


def from_behind(block, axis, distance):
    devices = range(lax.axis_size(axis))
    route = [(i - distance, i) for i in devices if i - distance in devices]
    return lax.ppermute(block, axis, route)


def norm_rows(values, gain):
    return values * lax.rsqrt(jnp.mean(values * values, axis=-1, keepdims=True) + EPSILON) * gain


def gelu_tanh(values):
    return (
        0.5
        * values
        * (1.0 + jnp.tanh(0.7978845608028654 * (values + 0.044715 * values * values * values)))
    )


def finish_update(weight, grad, row_new, col_state, col_total, rows_all, row_mean, decay):
    col_new = decay * col_state + (1.0 - decay) * col_total / rows_all
    second = row_new[..., :, None] * col_new[..., None, :] / row_mean
    return (weight - WEIGHT_RATE * grad * lax.rsqrt(second), col_new)


def local(
    byte_rows, item_lengths, cont_mask, bound_mask, out_cot, proj_cot,
    w_qkv, w_out, w_up, w_down, w_proj, gains,
    row_qkv, col_qkv, row_out, col_out, row_up, col_up, row_down, col_down, row_proj, col_proj, gain_var,
):
    sizes = tuple((name, lax.axis_size(name)) for name in ("item", "seq"))
    count = lax.axis_size("item") * lax.axis_size("seq")
    rows_dev, width = byte_rows.shape[1:]
    ff = w_up.shape[1]
    shard = width // count
    low = bf

    dims = grid_of(lax.axis_size("seq"), lax.axis_size("item"))
    paired = dims == (4, 2, 2) and shard % 8 == 0 and rows_dev < WINDOW <= 2 * rows_dev
    inputs_low = byte_rows[0]
    if paired:
        got = front(item_lengths, inputs_low, gains, w_qkv, (w_out, w_proj, w_up, w_down), dims, lax.axis_size("seq"))
        attended, lse, queries, ext_keys, ext_values, ext_normed = got[:6]
        split_qkv = got[6:9]
        gain_full = got[9]
        weight_out, weight_up, weight_down = [w.reshape(-1, w.shape[-1]) for w in (got[10], got[12], got[13])]
        part_proj, flipped_keys = got[11], got[14]
    else:
        inputs = inputs_low.astype(f32)
        weight_qkv = lax.all_gather(w_qkv.astype(low), AXES, axis=1, tiled=True)
        gain_full = lax.all_gather(gains.astype(low), AXES, axis=1, tiled=True).astype(f32)
        weight_out, weight_proj, weight_up, weight_down = [
            lax.all_gather(w.astype(low), AXES, axis=0, tiled=True) for w in (w_out, w_proj, w_up, w_down)
        ]

    hop_total = -(-WINDOW // rows_dev)
    if not paired:
        offset = lax.axis_index("seq") * rows_dev
        ends = jnp.cumsum(item_lengths[0], dtype=jnp.int32)
        pos = offset + jnp.arange(rows_dev, dtype=jnp.int32)
        begin_at = jnp.max(jnp.where(ends[None, :] <= pos[:, None], ends[None, :], 0), axis=1)
        lo = jnp.maximum(begin_at, pos - WINDOW + 1) - offset + WINDOW
        halo = []
        for distance in range(hop_total, 0, -1):
            need = min(rows_dev, WINDOW - (distance - 1) * rows_dev)
            halo.append(from_behind(inputs_low[rows_dev - need :], "seq", distance))
        normed = norm_rows(inputs, gain_full[0]).astype(low)
        halo_normed = norm_rows(jnp.concatenate(halo, axis=0).astype(f32), gain_full[0]).astype(low)
        ext_normed = jnp.concatenate([halo_normed, normed], axis=0)
        queries = dot(normed, weight_qkv[0]).astype(low) * jnp.asarray(0.125, low)
        ext_keys = dot(ext_normed, weight_qkv[1]).astype(low)
        ext_values = dot(ext_normed, weight_qkv[2]).astype(low)
        attended, lse = attend(queries, ext_keys, ext_values, lo[:, None])

    if paired:
        output_low, projected, resid_grad, attended_grad, gain_two_grad, delta, sum_proj, *low_grads = middle(
            bound_mask, cont_mask, gain_full,
            (inputs_low, attended, out_cot[0], proj_cot[0], weight_out, weight_up, weight_down, part_proj), dims,
        )
        apart = [g.reshape(dims + (-1, g.shape[-1])) for g in low_grads]
        (query_grad, ext_key_grad, ext_value_grad, *returned), (sum_out, sum_up, sum_down) = back(
            item_lengths, lse, delta, (queries, attended_grad, ext_keys, ext_values, flipped_keys, split_qkv[1], split_qkv[2]),
            apart, dims, lax.axis_size("seq"),
        )
        sums = [sum_out, sum_proj, sum_up, sum_down]
    else:
        resid = inputs + dot(attended, weight_out)
        normed_two = norm_rows(resid, gain_full[1]).astype(low)
        hidden_pre = dot(normed_two, weight_up)
        activated = gelu_tanh(hidden_pre).astype(low)
        output = resid + dot(activated, weight_down)
        output_low = output.astype(low)
        boundary = (bound_mask[0] * (1 - cont_mask[0])).astype(f32)[:, None]
        projected = (boundary * dot(output_low, weight_proj)).astype(low)
        proj_grad = (boundary * proj_cot[0].astype(f32)).astype(low)
        grad_proj = dot(output_low, proj_grad, TN)
        output_grad = out_cot[0].astype(f32) + dot(proj_grad, weight_proj, NT)
        output_grad_low = output_grad.astype(low)
        grad_down = dot(activated, output_grad_low, TN)
        act_grad = dot(output_grad_low, weight_down, NT)
        _, gelu_back = jax.vjp(gelu_tanh, hidden_pre)
        pre_grad = gelu_back(act_grad)[0].astype(low)
        grad_up = dot(normed_two, pre_grad, TN)
        normed_two_grad = dot(pre_grad, weight_up, NT)
        _, norm_two_back = jax.vjp(norm_rows, resid, gain_full[1])
        resid_norm_grad, gain_two_grad = norm_two_back(normed_two_grad)
        resid_grad = output_grad + resid_norm_grad
        resid_grad_low = resid_grad.astype(low)
        grad_out = dot(attended, resid_grad_low, TN)
        attended_grad = dot(resid_grad_low, weight_out, NT).astype(low)

        low_grads = [g.astype(low) for g in (grad_out, grad_proj, grad_up, grad_down)]
        query_grad, ext_key_grad, ext_value_grad = attend_back(
            queries, attended_grad, attended, lse, ext_keys, ext_values, lo[None, :]
        )
        sums = [lax.psum_scatter(g, AXES, scatter_dimension=0, tiled=True).astype(f32) for g in low_grads]
        sum_out, sum_proj, sum_up, sum_down = sums
    if paired:
        rows = [row_qkv, row_out[None], row_proj[None], row_up[None], row_down[None]]
        cols = [col_qkv, col_out, col_proj, col_up, col_down]
        input_grad, totals, sums_qkv = last(
            inputs_low, resid_grad, gain_full, gain_two_grad, query_grad, ext_key_grad, ext_value_grad,
            ext_normed, split_qkv, returned, sums, rows, dims, lax.axis_size("seq"),
        )
        mine = lax.axis_index("seq") * lax.axis_size("item") + lax.axis_index("item")
        done = update(
            mine[None].astype(jnp.int32), totals, gains, gain_var,
            (w_qkv, w_out, w_proj, w_up, w_down), (*sums_qkv, *sums), rows, cols,
            (output_low, projected, input_grad),
        )
        sum_qkv, sum_out, sum_proj, sum_up, sum_down, sum_gains = done[:6]
        new_qkv, new_out, new_proj, new_up, new_down, new_gains = done[6:12]
        row_qkv_new, row_out_new, row_proj_new, row_up_new, row_down_new = [done[12]] + [r[0] for r in done[13:17]]
        col_qkv_new, col_out_new, col_proj_new, col_up_new, col_down_new = done[17:22]
        gain_var_new, output_low, projected, input_grad = done[22:]
        return (
            output_low[None], projected[None], input_grad[None],
            sum_qkv, sum_out, sum_up, sum_down, sum_proj, sum_gains,
            new_qkv, new_out, new_up, new_down, new_proj, new_gains,
            row_qkv_new, col_qkv_new, row_out_new, col_out_new, row_up_new, col_up_new,
            row_down_new, col_down_new, row_proj_new, col_proj_new, gain_var_new,
        )
    ext_back = dot(ext_key_grad, weight_qkv[1], NT) + dot(ext_value_grad, weight_qkv[2], NT)
    halo_back = ext_back[:WINDOW].astype(low)
    grads_qkv = [
        dot(normed, query_grad, TN).astype(low),
        dot(ext_normed, ext_key_grad, TN).astype(low),
        dot(ext_normed, ext_value_grad, TN).astype(low),
    ]
    returned = []
    for distance in range(1, hop_total + 1):
        need = min(rows_dev, WINDOW - (distance - 1) * rows_dev)
        upper = WINDOW - (distance - 1) * rows_dev
        returned.append(from_behind(halo_back[upper - need : upper], "seq", -distance))
    sums = [lax.psum_scatter(g, AXES, scatter_dimension=0, tiled=True).astype(f32) for g in grads_qkv]
    sum_qkv = jnp.stack(sums)
    normed_grad = ext_back[WINDOW:] + dot(query_grad, weight_qkv[0], NT)
    for block in returned:
        need = block.shape[0]
        normed_grad = normed_grad.at[rows_dev - need :].add(block.astype(f32))
    _, norm_one_back = jax.vjp(norm_rows, inputs, gain_full[0])
    input_norm_grad, gain_one_grad = norm_one_back(normed_grad)
    input_grad = (resid_grad + input_norm_grad).astype(low)

    decay = 1.0 - STEP ** (-0.8)
    square_qkv = sum_qkv * sum_qkv + TINY_SQUARE
    square_out = sum_out * sum_out + TINY_SQUARE
    square_up = sum_up * sum_up + TINY_SQUARE
    square_down = sum_down * sum_down + TINY_SQUARE
    square_proj = sum_proj * sum_proj + TINY_SQUARE
    row_qkv_new = decay * row_qkv + (1.0 - decay) * jnp.mean(square_qkv, axis=-1)
    row_out_new = decay * row_out + (1.0 - decay) * jnp.mean(square_out, axis=-1)
    row_up_new = decay * row_up + (1.0 - decay) * jnp.mean(square_up, axis=-1)
    row_down_new = decay * row_down + (1.0 - decay) * jnp.mean(square_down, axis=-1)
    row_proj_new = decay * row_proj + (1.0 - decay) * jnp.mean(square_proj, axis=-1)
    row_sums = jnp.concatenate(
        [
            jnp.sum(row_qkv_new, axis=1),
            jnp.sum(row_out_new)[None],
            jnp.sum(row_up_new)[None],
            jnp.sum(row_down_new)[None],
            jnp.sum(row_proj_new)[None],
        ]
    )
    stats = [
        jnp.sum(square_qkv, axis=1).reshape(-1),
        jnp.sum(square_out, axis=0),
        jnp.sum(square_up, axis=0),
        jnp.sum(square_down, axis=0),
        jnp.sum(square_proj, axis=0),
        gain_one_grad,
        gain_two_grad,
        row_sums,
    ]
    flat = jnp.concatenate(stats)
    used = flat.shape[0]
    padded = -(-used // 1024) * 1024
    flat = jnp.pad(flat, (0, padded - used)).reshape(padded // 128, 128)
    flat = sum_all(flat, sizes).reshape(-1)
    totals, at = [], 0
    for part in stats:
        totals.append(flat[at : at + part.shape[0]])
        at += part.shape[0]
    col_qkv_total, col_out_total, col_up_total, col_down_total, col_proj_total, gain_one, gain_two, row_totals = totals
    col_qkv_total = col_qkv_total.reshape(3, width)
    mine = lax.axis_index("seq") * lax.axis_size("item") + lax.axis_index("item")
    sum_gains = lax.dynamic_slice_in_dim(jnp.stack([gain_one, gain_two]), mine * shard, shard, 1)
    row_counts = jnp.array([width, width, width, width, width, ff, width], f32)
    row_means = row_totals / row_counts
    new_qkv, col_qkv_new = finish_update(
        w_qkv, sum_qkv, row_qkv_new, col_qkv, col_qkv_total, width, row_means[:3][:, None, None], decay
    )
    new_out, col_out_new = finish_update(w_out, sum_out, row_out_new, col_out, col_out_total, width, row_means[3], decay)
    new_up, col_up_new = finish_update(w_up, sum_up, row_up_new, col_up, col_up_total, width, row_means[4], decay)
    new_down, col_down_new = finish_update(
        w_down, sum_down, row_down_new, col_down, col_down_total, ff, row_means[5], decay
    )
    new_proj, col_proj_new = finish_update(
        w_proj, sum_proj, row_proj_new, col_proj, col_proj_total, width, row_means[6], decay
    )
    gain_var_new = decay * gain_var + (1.0 - decay) * (sum_gains * sum_gains + TINY_SQUARE)
    new_gains = gains - GAIN_RATE * sum_gains * lax.rsqrt(gain_var_new)
    return (
        output_low[None], projected[None], input_grad[None],
        sum_qkv, sum_out, sum_up, sum_down, sum_proj, sum_gains,
        new_qkv, new_out, new_up, new_down, new_proj, new_gains,
        row_qkv_new, col_qkv_new, row_out_new, col_out_new, row_up_new, col_up_new,
        row_down_new, col_down_new, row_proj_new, col_proj_new, gain_var_new,
    )


def solution(mesh):
    in_specs = (
        P("item", "seq", None),
        P("item", None),
        P("item", "seq"),
        P("item", "seq"),
        P("item", "seq", None),
        P("item", "seq", None),
        P(None, ("seq", "item"), None),
        P(("seq", "item"), None),
        P(("seq", "item"), None),
        P(("seq", "item"), None),
        P(("seq", "item"), None),
        P(None, ("seq", "item")),
        P(None, ("seq", "item")),
        P(),
        P(("seq", "item")),
        P(),
        P(("seq", "item")),
        P(),
        P(("seq", "item")),
        P(),
        P(("seq", "item")),
        P(),
        P(None, ("seq", "item")),
    )
    out_specs = (
        P("item", "seq", None),
        P("item", "seq", None),
        P("item", "seq", None),
        P(None, ("seq", "item"), None),
        P(("seq", "item"), None),
        P(("seq", "item"), None),
        P(("seq", "item"), None),
        P(("seq", "item"), None),
        P(None, ("seq", "item")),
        P(None, ("seq", "item"), None),
        P(("seq", "item"), None),
        P(("seq", "item"), None),
        P(("seq", "item"), None),
        P(("seq", "item"), None),
        P(None, ("seq", "item")),
        P(None, ("seq", "item")),
        P(),
        P(("seq", "item")),
        P(),
        P(("seq", "item")),
        P(),
        P(("seq", "item")),
        P(),
        P(("seq", "item")),
        P(),
        P(None, ("seq", "item")),
    )
    return jax.shard_map(local, mesh=mesh, in_specs=in_specs, out_specs=out_specs, check_vma=False)
```
